32 devices in a mesh: hyp: 2 (over y), prow: 4 (over x, core), pcol: 4 (over z).
Axes of the slice: x: 2, y: 2, z: 4, core: 2. Of those that a mesh axis runs over, the one named last changes fastest.
Arguments:
- sigma_rows: bfloat16 [2, 2048, 2048], P('hyp', 'prow', 'pcol'), may hold values from -1 to 1, as said below
- panel: bfloat16 [2, 2048, 2, 384], P('hyp', ('prow', 'pcol')), may hold values from -0.59765625 to 0.59765625
- live_block_rows: int32 [2, 16], P(None, ('prow', 'pcol')), may hold values from 1 to 128, 1536 in all within a row
- inv_diag: bfloat16 [2, 2, 384, 384], P('hyp', None, ('prow', 'pcol')), may hold values from -0.3125 to 0.3125
- quad_weight: float32 [2], P('hyp'), may hold values from 0.05 to 0.5
Outputs:
- sigma_panel: bfloat16 [2, 2048, 2, 384], P('hyp', ('prow', 'pcol'))
- marginal: float32 [2, 384, 384], replicated
The draws below stay inside these ranges and needn't reach their ends.
Inputs may be any that keep to these rules, and one draw needn't show every extreme that they name: `sigma_rows`: each quadrature point's matrix is symmetric.
All inputs are finite; a program needn't handle non-finite values. No bound on the sum of `live_block_rows` on one device may be relied on, other than what follows from the above.
Results may differ from the reference program's by a relative error of at most 0.0004.
Values may be sent and summed in bfloat16 or wider, within the bound.
No kernel may reach another device: no remote copies, remote signals or barrier semaphores. Data moves between devices by JAX's collectives and lax.ppermute only.
A program may use at most 64 MiB of HBM per device.

```python
import math
import jax
import jax.numpy as jnp
import numpy as np
from jax import lax

W = 384
NS = 2
BLOCK = 128
NB = 16
R = 2048
HYP = 2


def draw_sigma_rows(key, part):
    pairing = jax.random.permutation(jax.random.fold_in(key, 7), NB)
    blocks = jnp.arange(R, dtype=jnp.int32) // BLOCK
    spike = 1.0 + 3.0 * (pairing[blocks][:, None] == blocks[None, :]).astype(jnp.float32)
    spread = math.sqrt(2.0) * (R // 4) ** (-0.5)

    def one_point(point_key):
        values = jax.random.normal(point_key, (R, R), jnp.float32)
        values = values * spread * spike
        values = 0.5 * (values + values.T)
        return jnp.clip(values, -1.0, 1.0).astype(jnp.bfloat16)
    point_keys = jax.random.split(jax.random.fold_in(key, 11), HYP)
    return lax.map(one_point, point_keys)


def block_scale(rng, shape, cuts, smallest, high):
    def one(axis_at, parts):
        steps = jax.random.uniform(jax.random.fold_in(jax.random.fold_in(rng, 6), axis_at), (parts,), jnp.float32, smallest / len(cuts), high / len(cuts))
        return jnp.repeat(jnp.exp(steps), shape[axis_at] // parts).reshape((-1,) + (1,) * (len(shape) - axis_at - 1))

    factor_of = one(*cuts[0])
    for cut in cuts[1:]:
        factor_of = factor_of * one(*cut)
    return factor_of


def split_up(count, total, most, lean):
    loads = [(1 << 20) // math.isqrt(grade ** lean) + 1 for grade in range(2, count + 1)]
    rest, given = total - most - (count - 1), [1] * (count - 1)
    while rest > 0:
        free = [i for i in range(count - 1) if given[i] < most]
        mass, remaining = sum([loads[i] for i in free]), rest
        for i in free:
            more = min(most - given[i], max(1, remaining * loads[i] // mass), rest)
            given[i] = given[i] + more
            rest = rest - more
    return np.array([most] + given)


def ragged(key, count, total, limit, skew):
    if count == 2:
        one = jax.random.randint(key, (), max(1, total - limit), min(limit, total - 1) + 1)
        return jnp.stack([one, total - one])
    tallies = jnp.asarray(split_up(count, total, limit, skew), jnp.int32)
    pairs = (count - 1) // 2
    giver, taker = tallies[1:1 + 2 * pairs:2], tallies[2:2 + 2 * pairs:2]
    room = jnp.minimum(giver - 1, limit - taker)
    passed = jax.random.randint(jax.random.fold_in(key, 1), (pairs,), 0, 1 << 20) % (room + 1)
    tallies = tallies.at[1:1 + 2 * pairs:2].set(giver - passed).at[2:2 + 2 * pairs:2].set(taker + passed)
    return tallies[jax.random.permutation(jax.random.fold_in(key, 2), count)]


def normal_values(key, extent, scale, limit, cuts=(), kind=jnp.bfloat16):
    entries = jax.random.normal(key, extent, jnp.float32) * scale
    if len(cuts) > 0:
        entries = block_scale(key, extent, cuts, -0.22, 0.18) * entries
    return jnp.clip(entries, min=-limit, max=limit).astype(kind)


def setup_inputs(seed: int = 0) -> dict:
    streams_of = jax.random.split(jax.random.key(seed), 6)
    sigma_rows = draw_sigma_rows(jax.random.fold_in(streams_of[5], 71), 0)
    panel = normal_values(streams_of[1], (HYP, R, NS, W), 0.1, 0.59765625, ((0, 2), (1, 16)))
    live_block_rows = jax.vmap(lambda own: ragged(own, NB, NB * BLOCK * 3 // 4, BLOCK, 2))(jax.random.split(streams_of[2], NS)).reshape((NS, NB)).astype(jnp.int32)
    inv_diag = normal_values(streams_of[3], (HYP, NS, W, W), W ** -0.5, 0.3125, ((0, 2), (2, 16)))
    quad_weight = jnp.clip(jnp.exp(math.log(0.5) - 2.3025851 * jax.random.uniform(streams_of[4], (HYP,), jnp.float32) ** block_scale(streams_of[4], (HYP,), ((0, 2),), -0.2, 0.2)), 0.05, 0.5)
    return {"sigma_rows": sigma_rows, "panel": panel, "live_block_rows": live_block_rows, "inv_diag": inv_diag, "quad_weight": quad_weight}


def reference(sigma_rows, panel, live_block_rows, inv_diag, quad_weight):
    offsets = jnp.arange(R, dtype=jnp.int32) % BLOCK
    block_index = jnp.arange(R, dtype=jnp.int32) // BLOCK
    active = (offsets[None, :] < live_block_rows[:, block_index]).T
    masked_panel = jnp.where(active[None, :, :, None], panel, jnp.zeros_like(panel)).astype(jnp.bfloat16)

    def one_group(operands):
        covariance_block, single_masked_panel, inverse = operands
        applied = jnp.dot(covariance_block, single_masked_panel.reshape(R, NS * W), preferred_element_type=jnp.float32)
        applied_full = applied.reshape(R, NS, W)
        half_applied_product = applied_full.astype(jnp.bfloat16)
        panel_out = jnp.where(active[:, :, None], -half_applied_product, jnp.zeros_like(half_applied_product))
        coupling_block = jnp.einsum("vwg,vwe->wge", single_masked_panel.astype(jnp.float32), applied_full, precision=lax.Precision.HIGHEST)
        diagonal = jnp.einsum("skp,skq->spq", inverse.astype(jnp.float32), inverse.astype(jnp.float32), precision=lax.Precision.HIGHEST)
        return panel_out, coupling_block + diagonal

    sigma_panel, diagonal = lax.map(one_group, (sigma_rows, masked_panel, inv_diag))
    marginal = jnp.einsum("h,hspq->spq", quad_weight, diagonal, precision=lax.Precision.HIGHEST)
    return sigma_panel, marginal
```

```python
import functools

import jax
import jax.numpy as jnp
from jax import lax
from jax.experimental import pallas as pl
from jax.experimental.pallas import tpu as pltpu
from jax.sharding import PartitionSpec as P

LANES = 128
VMEM = pl.BlockSpec(memory_space=pltpu.VMEM)
SMEM = pl.BlockSpec(memory_space=pltpu.SMEM)


def call(kernel, outs, specs, *operands, scratch=()):
    many = isinstance(outs, (list, tuple))
    return pl.pallas_call(
        kernel,
        out_shape=outs,
        in_specs=specs,
        out_specs=[VMEM] * len(outs) if many else VMEM,
        scratch_shapes=scratch,
        compiler_params=pltpu.CompilerParams(vmem_limit_bytes=32 * 2**20),
    )(*operands)


def transposed_dot(left, right):
    return lax.dot_general(
        left, right, (((0,), (0,)), ((), ())), preferred_element_type=jnp.float32
    )


def tiles(width):
    count = width // LANES
    return [(a, b) for a in range(count) for b in range(a, count)]


def general(sigma_rows, panel, live_block_rows, inv_diag, quad_weight):
    height, count, width = panel.shape[1:]
    offsets = lax.broadcasted_iota(jnp.int32, (height, count), 0)
    active = offsets < live_block_rows[:, 0][None, :]
    masked = jnp.where(active[:, :, None], panel[0], jnp.zeros_like(panel[0]))
    extent = height * lax.axis_size("prow")
    gathered = lax.all_gather(masked, ("prow", "pcol"), axis=0, tiled=True)
    start = lax.axis_index("pcol") * sigma_rows.shape[2]
    column_panel = lax.dynamic_slice_in_dim(gathered, start, sigma_rows.shape[2], 0)
    applied = lax.psum_scatter(
        jnp.dot(
            sigma_rows[0],
            column_panel.reshape(sigma_rows.shape[2], count * width),
            preferred_element_type=jnp.float32,
        ),
        "pcol",
        scatter_dimension=0,
        tiled=True,
    ).reshape(height, count, width)
    half = applied.astype(jnp.bfloat16)
    sigma_panel = jnp.where(active[:, :, None], -half, jnp.zeros_like(half))[None]
    coupling = jnp.einsum(
        "vwg,vwe->wge",
        masked.astype(jnp.float32),
        applied,
        precision=lax.Precision.HIGHEST,
    )
    diagonal = jnp.einsum(
        "skp,skq->spq", inv_diag[0], inv_diag[0], preferred_element_type=jnp.float32
    )
    marginal = lax.psum(quad_weight[0] * (coupling + diagonal), ("hyp", "prow", "pcol"))
    return sigma_panel, marginal


def apply_kernel(height, place, own_sigma, far_sigma, *refs):
    blocks, applied, own_rows, panel = refs[:12], refs[12], refs[13], refs[14]
    column, family = place[0], place[1]
    inner = (column == 1) | (column == 2)
    spots = (column, place[2], place[3], place[4])
    extent = 4 * height
    for one in range(2):
        own, near, second_in, second_out, third_in, third_out = blocks[6 * one : 6 * one + 6]
        second = jnp.where(inner, second_in[...], second_out[...])
        third = jnp.where(inner, third_in[...], third_out[...])
        for spot, value in zip(spots, (own[...], near[...], second, third)):
            start = pl.multiple_of(one * extent + spot * height, height)
            panel[pl.ds(start, height), :] = value
    total = transposed_dot(own_sigma[0], panel[pl.ds(0, extent), :])
    total += transposed_dot(far_sigma[0], panel[pl.ds(extent, extent), :])
    applied[...] = total
    own_rows[...] = panel[pl.ds(pl.multiple_of(family * extent, extent), extent), :]


def couple_kernel(height, place, weight, mine, other, rows, inverse_a, inverse_b, *refs):
    outs, keep, send, packed = refs[:4], refs[4], refs[5], refs[6]
    column, point = place[0], place[5]
    applied = mine[...] + other[...]
    high = applied.astype(jnp.bfloat16)
    low = (applied - high.astype(jnp.float32)).astype(jnp.bfloat16)
    packed_half = -high
    scale = weight[0]
    width = applied.shape[1]
    at = 0
    for first in range(width // LANES):
        left = rows[:, first * LANES : (first + 1) * LANES]
        part = transposed_dot(left, high[:, first * LANES :])
        part += transposed_dot(left, low[:, first * LANES :])
        for inverse in (inverse_a, inverse_b):
            part += transposed_dot(
                inverse[:, first * LANES : (first + 1) * LANES], inverse[:, first * LANES :]
            )
        part = scale * part
        for block in range(part.shape[1] // LANES):
            packed[pl.ds(at * LANES, LANES), :] = part[:, block * LANES : (block + 1) * LANES]
            at += 1
    half = packed.shape[0] // 2
    keep[...] = packed[pl.ds(pl.multiple_of(point * half, LANES), half), :]
    send[...] = packed[pl.ds(pl.multiple_of((1 - point) * half, LANES), half), :]
    for block in range(4):
        for step in range(4):
            @pl.when(lax.rem(column + step, 4) == block)
            def _():
                outs[step][...] = packed_half[block * height : (block + 1) * height]


def split_kernel(place, keep, came, *refs):
    outs, whole = refs[:4], refs[4]
    whole[...] = keep[...] + came[...]
    size = outs[0].shape[0]
    for step in range(4):
        spot = place[0] if step == 0 else place[5 + step]
        outs[step][...] = whole[pl.ds(pl.multiple_of(spot * size, 8), size), :]


def sum_kernel(a, b, c, d, out):
    out[...] = (a[...] + b[...]) + (c[...] + d[...])


def join_kernel(place, *refs):
    out = refs[4]
    size = refs[0].shape[0]
    for step in range(4):
        spot = place[0] if step == 0 else place[5 + step]
        out[pl.ds(pl.multiple_of(spot * size, 8), size), :] = refs[step][...]


def spread_kernel(place, *refs):
    out = refs[8]
    width = out.shape[1]
    lead = place[9] == 1
    point, side = place[5], place[10]
    per = len(tiles(width)) // 2
    for half in range(2):
        for node in range(2):
            at_point = half == point
            at_side = node == side
            for same_point in range(2):
                for same_side in range(2):
                    source = (1 - same_point) + 2 * (1 - same_side)
                    for from_lead in range(2):
                        ref = refs[source] if from_lead else refs[4 + source]
                        hit = (at_point == bool(same_point)) & (at_side == bool(same_side))

                        @pl.when(hit & (lead == bool(from_lead)))
                        def _():
                            for index in range(per):
                                a, b = tiles(width)[half * per + index]
                                tile = ref[index * LANES : (index + 1) * LANES, :]
                                out[node, a * LANES : (a + 1) * LANES, b * LANES : (b + 1) * LANES] = tile
                                if a != b:
                                    out[node, b * LANES : (b + 1) * LANES, a * LANES : (a + 1) * LANES] = tile.T


def square(sigma_rows, panel, live_block_rows, inv_diag, quad_weight):
    height, count, width = panel.shape[1:]
    grid = lax.axis_size("pcol")
    points = lax.axis_size("hyp")
    cores = lax.axis_size("prow") // count
    row, column, point = lax.axis_index("prow"), lax.axis_index("pcol"), lax.axis_index("hyp")
    side, core = row // cores, row % cores
    f32, bf16 = jnp.float32, jnp.bfloat16
    shape = jax.ShapeDtypeStruct

    def lead(side, column):
        return side * cores + column % cores

    def move(x, pairs):
        flat = [(a * grid + b, c * grid + d) for (a, b), (c, d) in pairs]
        return lax.ppermute(x, ("prow", "pcol"), flat)

    def along_columns(x, pairs):
        return lax.ppermute(x, "pcol", pairs)

    def across_points(x):
        pairs = []
        for h in range(points):
            for s in range(count):
                for c in range(grid):
                    tail = lead(s, c) * grid + c
                    size = count * cores * grid
                    pairs.append((h * size + tail, (1 - h) * size + tail))
        return lax.ppermute(x, ("hyp", "prow", "pcol"), pairs)

    sides = [(r, (r + cores) % (count * cores)) for r in range(count * cores)]
    leads = [(s, c) for s in range(count) for c in range(grid)]
    to_lead = [((s * cores + 1 - c % cores, c), (lead(s, c), c)) for s, c in leads]
    from_lead = [(b, a) for a, b in to_lead]
    second = jnp.where(column < 2, 2, 1)
    third = jnp.where(column < 2, 3, 0)
    place = jnp.stack(
        [
            column,
            (side != column // cores).astype(jnp.int32),
            column ^ 1,
            second,
            third,
            point,
            column ^ 1,
            column ^ 2,
            column ^ 3,
            (core == column % cores).astype(jnp.int32),
            side,
        ]
    ).astype(jnp.int32)

    far_sigma = lax.ppermute(sigma_rows, "prow", sides)

    offsets = lax.broadcasted_iota(jnp.int32, (height, count), 0)
    active = offsets < live_block_rows[:, 0][None, :]
    masked = jnp.where(active[:, :, None], panel[0], jnp.zeros_like(panel[0]))
    masked = jnp.transpose(masked, (1, 0, 2))
    own = lax.dynamic_index_in_dim(masked, side, 0, keepdims=False)
    give = lax.dynamic_index_in_dim(masked, 1 - side, 0, keepdims=False)
    got = lax.ppermute(give, "prow", sides)
    own_inverse = lax.dynamic_index_in_dim(inv_diag[0], side, 0, keepdims=False)
    got_inverse = lax.ppermute(
        lax.dynamic_index_in_dim(inv_diag[0], 1 - side, 0, keepdims=False), "prow", sides
    )
    inverse = jnp.concatenate([own_inverse, got_inverse], 0)
    other_inverse = move(inverse, to_lead)

    blocks = []
    for block in (own, got):
        near = along_columns(block, [(0, 1), (1, 0), (2, 3), (3, 2)])
        second_in = along_columns(block, [(1, 2), (2, 1)])
        third_in = along_columns(near, [(1, 2), (2, 1)])
        second_out = along_columns(second_in, [(1, 0), (2, 3)])
        third_out = along_columns(third_in, [(1, 0), (2, 3)])
        blocks += [block, near, second_in, second_out, third_in, third_out]

    extent = sigma_rows.shape[2]
    applied, rows = call(
        functools.partial(apply_kernel, height),
        [shape((extent, width), f32), shape((extent, width), bf16)],
        [SMEM] + [VMEM] * 14,
        place,
        sigma_rows,
        far_sigma,
        *blocks,
        scratch=[pltpu.VMEM((2 * extent, width), bf16)],
    )
    other = move(applied, to_lead)

    packed = len(tiles(width)) * LANES
    *pieces, keep, send = call(
        functools.partial(couple_kernel, height),
        [shape((height, width), bf16)] * 4 + [shape((packed // 2, LANES), f32)] * 2,
        [SMEM, SMEM] + [VMEM] * 5,
        place,
        quad_weight,
        applied,
        other,
        rows,
        inverse,
        other_inverse,
        scratch=[pltpu.VMEM((packed, LANES), f32)],
    )

    came = across_points(send)
    steps = [
        [((lead(s, c), c), (lead(s, c ^ step), c ^ step)) for s, c in leads] for step in (1, 2, 3)
    ]
    size = packed // 2 // grid
    part = call(
        split_kernel,
        [shape((size, LANES), f32)] * 4,
        [SMEM, VMEM, VMEM],
        place,
        keep,
        came,
        scratch=[pltpu.VMEM((packed // 2, LANES), f32)],
    )
    arrived = [move(x, pairs) for x, pairs in zip(part[1:], steps)]
    done = call(sum_kernel, shape((size, LANES), f32), [VMEM] * 4, part[0], *arrived)
    others = [move(done, pairs) for pairs in steps]
    own_half = call(
        join_kernel,
        shape((packed // 2, LANES), f32),
        [SMEM] + [VMEM] * 4,
        place,
        done,
        *others,
    )
    cross = [((lead(s, c), c), (lead(1 - s, c), c)) for s, c in leads]
    point_half = across_points(own_half)
    side_half = move(own_half, cross)
    both_half = move(point_half, cross)
    halves = [own_half, point_half, side_half, both_half]
    copies = [move(x, from_lead) for x in halves]
    marginal = call(
        spread_kernel,
        shape((count, width, width), f32),
        [SMEM] + [VMEM] * 8,
        place,
        *halves,
        *copies,
    )

    landed = []
    for s in range(count):
        total = None
        for step in range(4):
            pairs = [((lead(s, c), c), (c, (c + step) % grid)) for c in range(grid)]
            value = move(pieces[step], pairs)
            total = value if total is None else total + value
        landed.append(total)
    sigma_panel = jnp.stack(landed, 1)
    sigma_panel = jnp.where(active[:, :, None], sigma_panel, jnp.zeros_like(sigma_panel))
    return sigma_panel[None], marginal


def solution(mesh):
    sizes = dict(mesh.shape)

    def on_device(sigma_rows, panel, live_block_rows, inv_diag, quad_weight):
        height, count, width = panel.shape[1:]
        grid = sizes["pcol"]
        fits = (
            sizes["hyp"] == 2
            and grid == 4
            and sizes["prow"] == grid
            and count == 2
            and sigma_rows.shape[1] == sigma_rows.shape[2] == grid * height
            and width % LANES == 0
            and len(tiles(width)) % 2 == 0
            and len(tiles(width)) // 2 * LANES % (8 * grid) == 0
        )
        body = square if fits else general
        return body(sigma_rows, panel, live_block_rows, inv_diag, quad_weight)

    in_specs = (
        P("hyp", "prow", "pcol"),
        P("hyp", ("prow", "pcol"), None, None),
        P(None, ("prow", "pcol")),
        P("hyp", None, ("prow", "pcol"), None),
        P("hyp"),
    )
    out_specs = (P("hyp", ("prow", "pcol"), None, None), P())
    return jax.shard_map(
        on_device, mesh=mesh, in_specs=in_specs, out_specs=out_specs, check_vma=False
    )
```

```python
import functools

import jax
import jax.numpy as jnp
from jax import lax
from jax.experimental import pallas as pl
from jax.experimental.pallas import tpu as pltpu
from jax.sharding import PartitionSpec as P

LANES = 128
VMEM = pl.BlockSpec(memory_space=pltpu.VMEM)
SMEM = pl.BlockSpec(memory_space=pltpu.SMEM)


def call(kernel, outs, specs, *operands, scratch=()):
    many = isinstance(outs, (list, tuple))
    return pl.pallas_call(
        kernel,
        out_shape=outs,
        in_specs=specs,
        out_specs=[VMEM] * len(outs) if many else VMEM,
        scratch_shapes=scratch,
        compiler_params=pltpu.CompilerParams(vmem_limit_bytes=32 * 2**20),
    )(*operands)


def transposed_dot(left, right):
    return lax.dot_general(
        left, right, (((0,), (0,)), ((), ())), preferred_element_type=jnp.float32
    )


def tiles(width):
    count = width // LANES
    return [(a, b) for a in range(count) for b in range(a, count)]


def general(sigma_rows, panel, live_block_rows, inv_diag, quad_weight):
    height, count, width = panel.shape[1:]
    offsets = lax.broadcasted_iota(jnp.int32, (height, count), 0)
    active = offsets < live_block_rows[:, 0][None, :]
    masked = jnp.where(active[:, :, None], panel[0], jnp.zeros_like(panel[0]))
    extent = height * lax.axis_size("prow")
    gathered = lax.all_gather(masked, ("prow", "pcol"), axis=0, tiled=True)
    start = lax.axis_index("pcol") * sigma_rows.shape[2]
    column_panel = lax.dynamic_slice_in_dim(gathered, start, sigma_rows.shape[2], 0)
    applied = lax.psum_scatter(
        jnp.dot(
            sigma_rows[0],
            column_panel.reshape(sigma_rows.shape[2], count * width),
            preferred_element_type=jnp.float32,
        ),
        "pcol",
        scatter_dimension=0,
        tiled=True,
    ).reshape(height, count, width)
    half = applied.astype(jnp.bfloat16)
    sigma_panel = jnp.where(active[:, :, None], -half, jnp.zeros_like(half))[None]
    coupling = jnp.einsum(
        "vwg,vwe->wge",
        masked.astype(jnp.float32),
        applied,
        precision=lax.Precision.HIGHEST,
    )
    diagonal = jnp.einsum(
        "skp,skq->spq", inv_diag[0], inv_diag[0], preferred_element_type=jnp.float32
    )
    marginal = lax.psum(quad_weight[0] * (coupling + diagonal), ("hyp", "prow", "pcol"))
    return sigma_panel, marginal


def apply_kernel(place, own_sigma, far_sigma, rows, applied):
    side = place[0]
    applied[...] = transposed_dot(own_sigma[0], rows[side])
    applied[...] += transposed_dot(far_sigma[0], rows[1 - side])


def couple_kernel(place, weight, mine, other, rows, inverse_a, inverse_b, *refs):
    half_out, keep, send, packed = refs
    core, column = place[1], place[2]
    finishes = column % 2 == core
    width = mine.shape[1]
    firsts = range(width // LANES)

    def store(first, part, at):
        for block in range(part.shape[1] // LANES):
            packed[pl.ds((at + block) * LANES, LANES), :] = (
                weight[0] * part[:, block * LANES : (block + 1) * LANES]
            )

    at = 0
    for first in firsts:
        part = jnp.zeros((LANES, width - first * LANES), jnp.float32)
        for inverse in (inverse_a, inverse_b):
            part += transposed_dot(
                inverse[:, first * LANES : (first + 1) * LANES], inverse[:, first * LANES :]
            )
        store(first, part, at)
        at += width // LANES - first

    @pl.when(finishes)
    def _():
        applied = mine[...] + other[...]
        high = applied.astype(jnp.bfloat16)
        low = (applied - high.astype(jnp.float32)).astype(jnp.bfloat16)
        half_out[...] = (-high).reshape(half_out.shape)
        panel = rows[column // 2]
        at = 0
        for first in firsts:
            left = panel[:, first * LANES : (first + 1) * LANES]
            part = transposed_dot(left, high[:, first * LANES :])
            part += transposed_dot(left, low[:, first * LANES :])
            for block in range(part.shape[1] // LANES):
                packed[pl.ds((at + block) * LANES, LANES), :] += (
                    weight[0] * part[:, block * LANES : (block + 1) * LANES]
                )
            at += width // LANES - first

    @pl.when(jnp.logical_not(finishes))
    def _():
        half_out[...] = jnp.zeros_like(half_out)

    half = packed.shape[0] // 2
    keep[...] = packed[pl.ds(pl.multiple_of(core * half, LANES), half), :]
    send[...] = packed[pl.ds(pl.multiple_of((1 - core) * half, LANES), half), :]


def add_kernel(a, b, out):
    out[...] = (a[...] + b[...]).reshape(out.shape)


def total_kernel(parts, out):
    total = jnp.sum(parts[...], axis=0)
    for copy in range(out.shape[0]):
        out[copy] = total


def spread_kernel(place, own, across, own_other, across_other, out):
    width = out.shape[1]
    blocks = tiles(width)
    per = len(blocks) // 2
    for core in range(2):
        for refs, same_core in (((own, across), True), ((own_other, across_other), False)):

            @pl.when((place[1] == core) == same_core)
            def _():
                for ref, node in zip(refs, (place[0], 1 - place[0])):
                    for index in range(per):
                        a, b = blocks[core * per + index]
                        tile = ref[index * LANES : (index + 1) * LANES, :]
                        out[node, a * LANES : (a + 1) * LANES, b * LANES : (b + 1) * LANES] = tile
                        if a != b:
                            out[node, b * LANES : (b + 1) * LANES, a * LANES : (a + 1) * LANES] = tile.T


def square(sigma_rows, panel, live_block_rows, inv_diag, quad_weight):
    height, count, width = panel.shape[1:]
    grid = lax.axis_size("pcol")
    points = lax.axis_size("hyp")
    cores = lax.axis_size("core")
    side, core, column = (lax.axis_index(name) for name in ("side", "core", "pcol"))
    f32, bf16 = jnp.float32, jnp.bfloat16
    shape = jax.ShapeDtypeStruct
    place = jnp.stack([side, core, column]).astype(jnp.int32)
    swap = [(0, 1), (1, 0)]
    pick = functools.partial(lax.dynamic_index_in_dim, axis=0, keepdims=False)

    far_sigma = lax.ppermute(sigma_rows, "side", swap)

    offsets = lax.broadcasted_iota(jnp.int32, (height, count), 0)
    active = offsets < live_block_rows[:, 0][None, :]
    masked = jnp.where(active[:, :, None], panel[0], jnp.zeros_like(panel[0]))
    masked = jnp.transpose(masked, (1, 0, 2))
    copies = jnp.broadcast_to(masked[:, None], (count, grid, height, width))
    rows = lax.all_to_all(
        copies.reshape(count * grid, height, width), ("side", "pcol"), 0, 0, tiled=True
    ).reshape(count, grid * height, width)
    own_inverse = pick(inv_diag[0], side)
    got_inverse = lax.ppermute(pick(inv_diag[0], 1 - side), "side", swap)

    extent = sigma_rows.shape[2]
    applied = call(
        apply_kernel,
        shape((extent, width), f32),
        [SMEM] + [VMEM] * 3,
        place,
        sigma_rows,
        far_sigma,
        rows,
    )
    to_lead = [((1 - c % cores) * grid + c, c % cores * grid + c) for c in range(grid)]
    other = lax.ppermute(applied, ("core", "pcol"), to_lead)

    packed = len(tiles(width)) * LANES
    half, keep, send = call(
        couple_kernel,
        [shape((grid, height, width), bf16)] + [shape((packed // 2, LANES), f32)] * 2,
        [SMEM, SMEM] + [VMEM] * 5,
        place,
        quad_weight,
        applied,
        other,
        rows,
        own_inverse,
        got_inverse,
        scratch=[pltpu.VMEM((packed, LANES), f32)],
    )
    came = lax.ppermute(send, "core", swap)
    shares = points * grid
    size = packed // 2 // shares
    parts = call(
        add_kernel, shape((shares, size, LANES), f32), [VMEM] * 2, keep, came
    )
    parts = lax.all_to_all(parts, ("hyp", "pcol"), 0, 0, tiled=True)
    total = call(total_kernel, shape((shares, size, LANES), f32), [VMEM], parts)
    own = lax.all_to_all(total, ("hyp", "pcol"), 0, 0, tiled=True)
    own = own.reshape(packed // 2, LANES)
    across = lax.ppermute(own, "side", swap)
    own_other = lax.ppermute(own, "core", swap)
    across_other = lax.ppermute(across, "core", swap)
    marginal = call(
        spread_kernel,
        shape((count, width, width), f32),
        [SMEM] + [VMEM] * 4,
        place,
        own,
        across,
        own_other,
        across_other,
    )

    landed = lax.all_to_all(half, "pcol", 0, 0, tiled=True)
    mine = pick(landed, core + cores * side)
    theirs = lax.ppermute(pick(landed, core + cores * (1 - side)), "side", swap)
    first = jnp.where(side == 0, mine, theirs)
    last = jnp.where(side == 0, theirs, mine)
    sigma_panel = jnp.stack([first, last], 1)
    sigma_panel = jnp.where(active[:, :, None], sigma_panel, jnp.zeros_like(sigma_panel))
    return sigma_panel[None], marginal


def solution(mesh):
    sizes = dict(mesh.shape)
    prow, pcol = ("prow",), ("pcol",)

    def on_device(sigma_rows, panel, live_block_rows, inv_diag, quad_weight):
        body = square if split else general
        return body(sigma_rows, panel, live_block_rows, inv_diag, quad_weight)

    split = sizes["hyp"] == 2 and sizes["pcol"] == 4 and sizes["prow"] == 4
    if split:
        prow = ("side", "core")
        mesh = jax.sharding.Mesh(
            mesh.devices.reshape(sizes["hyp"], 2, 2, sizes["pcol"]),
            ("hyp", "side", "core", "pcol"),
        )
    in_specs = (
        P("hyp", prow, pcol),
        P("hyp", prow + pcol, None, None),
        P(None, prow + pcol),
        P("hyp", None, prow + pcol, None),
        P("hyp"),
    )
    out_specs = (P("hyp", prow + pcol, None, None), P())
    return jax.shard_map(
        on_device, mesh=mesh, in_specs=in_specs, out_specs=out_specs, check_vma=False
    )
```

```python
import functools

import jax
import jax.numpy as jnp
from jax import lax
from jax.experimental import pallas as pl
from jax.experimental.pallas import tpu as pltpu
from jax.sharding import PartitionSpec as P

LANES = 128
VMEM = pl.BlockSpec(memory_space=pltpu.VMEM)
SMEM = pl.BlockSpec(memory_space=pltpu.SMEM)


def call(kernel, outs, specs, *operands, scratch=()):
    many = isinstance(outs, (list, tuple))
    return pl.pallas_call(
        kernel,
        out_shape=outs,
        in_specs=specs,
        out_specs=[VMEM] * len(outs) if many else VMEM,
        scratch_shapes=scratch,
        compiler_params=pltpu.CompilerParams(vmem_limit_bytes=32 * 2**20),
    )(*operands)


def transposed_dot(left, right):
    return lax.dot_general(
        left, right, (((0,), (0,)), ((), ())), preferred_element_type=jnp.float32
    )


def tiles(width):
    count = width // LANES
    return [(a, b) for a in range(count) for b in range(a, count)]


def general(sigma_rows, panel, live_block_rows, inv_diag, quad_weight):
    height, count, width = panel.shape[1:]
    offsets = lax.broadcasted_iota(jnp.int32, (height, count), 0)
    active = offsets < live_block_rows[:, 0][None, :]
    masked = jnp.where(active[:, :, None], panel[0], jnp.zeros_like(panel[0]))
    extent = height * lax.axis_size("prow")
    gathered = lax.all_gather(masked, ("prow", "pcol"), axis=0, tiled=True)
    start = lax.axis_index("pcol") * sigma_rows.shape[2]
    column_panel = lax.dynamic_slice_in_dim(gathered, start, sigma_rows.shape[2], 0)
    applied = lax.psum_scatter(
        jnp.dot(
            sigma_rows[0],
            column_panel.reshape(sigma_rows.shape[2], count * width),
            preferred_element_type=jnp.float32,
        ),
        "pcol",
        scatter_dimension=0,
        tiled=True,
    ).reshape(height, count, width)
    half = applied.astype(jnp.bfloat16)
    sigma_panel = jnp.where(active[:, :, None], -half, jnp.zeros_like(half))[None]
    coupling = jnp.einsum(
        "vwg,vwe->wge",
        masked.astype(jnp.float32),
        applied,
        precision=lax.Precision.HIGHEST,
    )
    diagonal = jnp.einsum(
        "skp,skq->spq", inv_diag[0], inv_diag[0], preferred_element_type=jnp.float32
    )
    marginal = lax.psum(quad_weight[0] * (coupling + diagonal), ("hyp", "prow", "pcol"))
    return sigma_panel, marginal


def mask_kernel(place, live, panel, inverse, own, give, own_inverse, give_inverse):
    first = place[0] == 0
    row = lax.broadcasted_iota(jnp.int32, own.shape, 0)
    rows = panel[0]
    zero = jnp.zeros(own.shape, own.dtype)
    one, two = (jnp.where(row < live[s, 0], rows[:, s, :], zero) for s in range(2))
    own[...] = jnp.where(first, one, two)
    give[...] = jnp.where(first, two, one)
    own_inverse[...] = inverse[0, place[0]]
    give_inverse[...] = inverse[0, 1 - place[0]]


def scaled_blocks(weight, product, out):
    at = 0
    for first in range(out.shape[0]):
        part = product(first)
        for block in range(part.shape[1] // LANES):
            out[at] = weight * part[:, block * LANES : (block + 1) * LANES]
            at += 1
        if at == out.shape[0]:
            return


def inverse_kernel(weight, own, got, out):
    def product(first):
        lanes = pl.ds(first * LANES, LANES)
        rest = pl.ds(first * LANES, own.shape[1] - first * LANES)
        return transposed_dot(own[:, lanes], own[:, rest]) + transposed_dot(got[:, lanes], got[:, rest])

    scaled_blocks(weight[0], product, out)


def apply_kernel(place, own_sigma, far_sigma, *refs):
    blocks, (keep, send, keep_rows, send_rows, panel) = refs[:8], refs[8:]
    core, column = place[1], place[2]
    height = blocks[0].shape[0]
    for index, block in enumerate(blocks):
        spot = jnp.bitwise_xor(column, index % 4)
        panel[index // 4, pl.ds(pl.multiple_of(spot * height, height), height), :] = block[...]
    half = keep.shape[0]
    family = jnp.where(column // 2 == place[0], 0, 1)
    for out, out_rows, part in ((send, send_rows, 1 - core), (keep, keep_rows, core)):
        spot = pl.ds(pl.multiple_of(part * half, half), half)
        out_rows[...] = panel[family, spot, :]
        total = transposed_dot(own_sigma[0, :, spot], panel[0])
        out[...] = total + transposed_dot(far_sigma[0, :, spot], panel[1])


def couple_kernel(place, weight, mine, other, keep_rows, got_rows, inverse, *refs):
    out_a, out_b, keep, send, packed = refs
    core, column = place[1], place[2]
    applied = mine[...] + other[...]
    high = applied.astype(jnp.bfloat16)
    low = (applied - high.astype(jnp.float32)).astype(jnp.bfloat16)
    rows = jnp.where(column % 2 == core, keep_rows[...], got_rows[...])

    def product(first):
        left = rows[:, first * LANES : (first + 1) * LANES]
        rest = slice(first * LANES, None)
        return transposed_dot(left, high[:, rest]) + transposed_dot(left, low[:, rest])

    scaled_blocks(weight[0], product, packed)
    half = packed.shape[0] // 2
    for out, part in ((send, 1 - core), (keep, core)):
        out[...] = packed[pl.ds(part * half, half)] + inverse[pl.ds(part * half, half)]
    height = out_a.shape[0]
    near = core == column // 2
    for out, steps in ((out_a, (0, 3)), (out_b, (1, 2))):
        spot = jnp.where(near, jnp.bitwise_xor(column, steps[0]), jnp.bitwise_xor(column, steps[1]))
        first = spot % 2 == 0
        out[...] = jnp.where(first, -high[:height], -high[height:])


def share_kernel(place, keep, came, *refs):
    outs, whole = refs[:8], refs[8]
    whole[...] = keep[...].reshape(whole.shape) + came[...].reshape(whole.shape)
    size = outs[0].shape[0]
    for index, out in enumerate(outs):
        spot = jnp.bitwise_xor(place[3], index)
        out[...] = whole[pl.ds(pl.multiple_of(spot * size, 8), size), :]


def sum_kernel(*refs):
    parts, out = refs[:8], refs[8]
    sums = [part[...] for part in parts]
    while len(sums) > 1:
        sums = [left + right for left, right in zip(sums[::2], sums[1::2])]
    out[...] = sums[0]


def join_kernel(place, *refs):
    parts, out = refs[:8], refs[8]
    size = parts[0].shape[0]
    for index, part in enumerate(parts):
        spot = jnp.bitwise_xor(place[3], index)
        out[pl.ds(pl.multiple_of(spot * size, 8), size), :] = part[...]


def spread_kernel(place, own, across, own_other, across_other, out):
    width = out.shape[1]
    blocks = tiles(width)
    per = len(blocks) // 2
    for core in range(2):
        for refs, same_core in (((own, across), True), ((own_other, across_other), False)):

            @pl.when((place[1] == core) == same_core)
            def _():
                for ref, node in zip(refs, (place[0], 1 - place[0])):
                    for index in range(per):
                        a, b = blocks[core * per + index]
                        tile = ref[index * LANES : (index + 1) * LANES, :]
                        out[node, a * LANES : (a + 1) * LANES, b * LANES : (b + 1) * LANES] = tile
                        if a != b:
                            out[node, b * LANES : (b + 1) * LANES, a * LANES : (a + 1) * LANES] = tile.T


def finish_kernel(place, live, a, b, out):
    row = lax.broadcasted_iota(jnp.int32, a.shape, 0)
    for s, block in enumerate((a, b)):
        out[0, :, s, :] = jnp.where(row < live[s, 0], block[...], jnp.zeros(a.shape, a.dtype))


AXES = ("hyp", "side", "core", "pcol")


def square(sigma_rows, panel, live_block_rows, inv_diag, quad_weight):
    height, count, width = panel.shape[1:]
    grid = lax.axis_size("pcol")
    points = lax.axis_size("hyp")
    point, side, core, column = (lax.axis_index(name) for name in AXES)
    f32, bf16 = jnp.float32, jnp.bfloat16
    shape = jax.ShapeDtypeStruct
    place = jnp.stack([side, core, column, point * grid + column]).astype(jnp.int32)
    total = points * 2 * 2 * grid

    def swap(x, point=0, side=0, core=0, column=0):
        mask = ((point * 2 + side) * 2 + core) * grid + column
        return lax.ppermute(x, AXES, [(i, i ^ mask) for i in range(total)])

    block = shape((height, width), bf16)
    rows = shape(inv_diag.shape[2:], bf16)
    far_sigma = swap(sigma_rows, side=1)
    own, give, own_inverse, give_inverse = call(
        mask_kernel, [block, block, rows, rows], [SMEM, SMEM, VMEM, VMEM],
        place, live_block_rows, panel, inv_diag,
    )
    got_inverse = swap(give_inverse, side=1)
    blocks = [own if z == 0 else swap(own, column=z) for z in range(grid)]
    blocks += [swap(give, side=1, column=z) for z in range(grid)]

    upper = len(tiles(width))
    inverse = call(
        inverse_kernel, shape((upper, LANES, LANES), f32), [SMEM, VMEM, VMEM],
        quad_weight, own_inverse, got_inverse,
    )
    extent = sigma_rows.shape[2]
    half = shape((extent // 2, width), f32)
    half_rows = shape((extent // 2, width), bf16)
    mine, send, keep_rows, send_rows = call(
        apply_kernel, [half, half, half_rows, half_rows], [SMEM] + [VMEM] * 10,
        place, sigma_rows, far_sigma, *blocks,
        scratch=[pltpu.VMEM((2, extent, width), bf16)],
    )
    got_rows = swap(send_rows, core=1)
    other = swap(send, core=1)

    few = shape((upper // 2, LANES, LANES), f32)
    out_a, out_b, keep, send = call(
        couple_kernel, [block, block, few, few], [SMEM, SMEM] + [VMEM] * 5,
        place, quad_weight, mine, other, keep_rows, got_rows, inverse,
        scratch=[pltpu.VMEM((upper, LANES, LANES), f32)],
    )
    came = swap(send, core=1)
    shares = points * grid
    lines = upper // 2 * LANES
    piece = shape((lines // shares, LANES), f32)
    pieces = call(
        share_kernel, [piece] * shares, [SMEM, VMEM, VMEM], place, keep, came,
        scratch=[pltpu.VMEM((lines, LANES), f32)],
    )

    def exchange(index, x):
        return x if index == 0 else swap(x, point=index // grid, column=index % grid)

    parts = [exchange(i, x) for i, x in enumerate(pieces)]
    done = call(sum_kernel, piece, [VMEM] * shares, *parts)
    parts = [exchange(i, done) for i in range(shares)]
    own_half = call(join_kernel, shape((lines, LANES), f32), [SMEM] + [VMEM] * shares, place, *parts)
    across = swap(own_half, side=1)
    own_other = swap(own_half, core=1)
    across_other = swap(across, core=1)
    marginal = call(
        spread_kernel, shape((count, width, width), f32), [SMEM] + [VMEM] * 4,
        place, own_half, across, own_other, across_other,
    )

    def output_pairs(steps):
        pairs = []
        for h in range(points):
            for s in range(2):
                for c in range(grid):
                    for core, step in ((c // 2, steps[0]), (1 - c // 2, steps[1])):
                        base = (h * 2 + s) * 2
                        pairs.append(((base + core) * grid + c, (base + c % 2) * grid + (c ^ step)))
        return pairs

    land_a = lax.ppermute(out_a, AXES, output_pairs((0, 3)))
    land_b = lax.ppermute(out_b, AXES, output_pairs((1, 2)))
    from_a = jnp.where(column % 2 == core, column, column ^ 3) // 2
    mine = jnp.where(from_a == side, land_a, land_b)
    theirs = swap(jnp.where(from_a == side, land_b, land_a), side=1)
    first = jnp.where(side == 0, mine, theirs)
    last = jnp.where(side == 0, theirs, mine)
    sigma_panel = call(
        finish_kernel, shape((1, height, count, width), bf16), [SMEM, SMEM, VMEM, VMEM],
        place, live_block_rows, first, last,
    )
    return sigma_panel, marginal


def solution(mesh):
    sizes = dict(mesh.shape)
    prow, pcol = ("prow",), ("pcol",)

    def on_device(sigma_rows, panel, live_block_rows, inv_diag, quad_weight):
        body = square if split else general
        return body(sigma_rows, panel, live_block_rows, inv_diag, quad_weight)

    split = sizes["hyp"] == 2 and sizes["pcol"] == 4 and sizes["prow"] == 4
    if split:
        prow = ("side", "core")
        mesh = jax.sharding.Mesh(
            mesh.devices.reshape(sizes["hyp"], 2, 2, sizes["pcol"]),
            ("hyp", "side", "core", "pcol"),
        )
    in_specs = (
        P("hyp", prow, pcol),
        P("hyp", prow + pcol, None, None),
        P(None, prow + pcol),
        P("hyp", None, prow + pcol, None),
        P("hyp"),
    )
    out_specs = (P("hyp", prow + pcol, None, None), P())
    return jax.shard_map(
        on_device, mesh=mesh, in_specs=in_specs, out_specs=out_specs, check_vma=False
    )
```

```python
import functools

import jax
import jax.numpy as jnp
from jax import lax
from jax.experimental import pallas as pl
from jax.experimental.pallas import tpu as pltpu
from jax.sharding import PartitionSpec as P

LANES = 128
ROWS = 16
VMEM = pl.BlockSpec(memory_space=pltpu.VMEM)
SMEM = pl.BlockSpec(memory_space=pltpu.SMEM)
ANY = pl.BlockSpec(memory_space=pl.ANY)
AXES = ("hyp", "side", "core", "pcol")


def call(kernel, outs, specs, *operands, scratch=(), out_specs=None, after=()):
    many = isinstance(outs, (list, tuple))
    count = len(specs)

    def body(*refs):
        kernel(*refs[:count], *refs[count + len(after) :])

    if out_specs is None:
        out_specs = [VMEM] * len(outs) if many else VMEM
    return pl.pallas_call(
        body,
        out_shape=outs,
        in_specs=list(specs) + [ANY] * len(after),
        out_specs=out_specs,
        scratch_shapes=scratch,
        compiler_params=pltpu.CompilerParams(vmem_limit_bytes=32 * 2**20),
    )(*operands, *after)


def transposed_dot(left, right):
    return lax.dot_general(
        left, right, (((0,), (0,)), ((), ())), preferred_element_type=jnp.float32
    )


def tiles(width):
    count = width // LANES
    return [(a, b) for a in range(count) for b in range(a, count)]


def general(sigma_rows, panel, live_block_rows, inv_diag, quad_weight):
    height, count, width = panel.shape[1:]
    offsets = lax.broadcasted_iota(jnp.int32, (height, count), 0)
    active = offsets < live_block_rows[:, 0][None, :]
    masked = jnp.where(active[:, :, None], panel[0], jnp.zeros_like(panel[0]))
    extent = height * lax.axis_size("prow")
    gathered = lax.all_gather(masked, ("prow", "pcol"), axis=0, tiled=True)
    start = lax.axis_index("pcol") * sigma_rows.shape[2]
    column_panel = lax.dynamic_slice_in_dim(gathered, start, sigma_rows.shape[2], 0)
    applied = lax.psum_scatter(
        jnp.dot(
            sigma_rows[0],
            column_panel.reshape(sigma_rows.shape[2], count * width),
            preferred_element_type=jnp.float32,
        ),
        "pcol",
        scatter_dimension=0,
        tiled=True,
    ).reshape(height, count, width)
    half = applied.astype(jnp.bfloat16)
    sigma_panel = jnp.where(active[:, :, None], -half, jnp.zeros_like(half))[None]
    coupling = jnp.einsum(
        "vwg,vwe->wge",
        masked.astype(jnp.float32),
        applied,
        precision=lax.Precision.HIGHEST,
    )
    diagonal = jnp.einsum(
        "skp,skq->spq", inv_diag[0], inv_diag[0], preferred_element_type=jnp.float32
    )
    marginal = lax.psum(quad_weight[0] * (coupling + diagonal), ("hyp", "prow", "pcol"))
    return sigma_panel, marginal


def mask_kernel(live_hbm, panel_hbm, own, give, live, panel, sems):
    copies = [
        pltpu.make_async_copy(panel_hbm.at[0], panel, sems.at[0]),
        pltpu.make_async_copy(live_hbm, live, sems.at[1]),
    ]
    for copy in copies:
        copy.start()
    for copy in copies:
        copy.wait()
    first = lax.axis_index("side") == 0
    row = lax.broadcasted_iota(jnp.int32, own.shape, 0)
    rows = panel[...]
    zero = jnp.zeros(own.shape, own.dtype)
    one, two = (jnp.where(row < live[s], rows[:, s, :], zero) for s in range(2))
    own[...] = jnp.where(first, one, two)
    give[...] = jnp.where(first, two, one)


def flip_kernel(matrix, out):
    out[...] = matrix[0].T


def apply_kernel(own_sigma, far_sigma, *refs):
    blocks, (own_inverse, got_inverse, applied, pack, panel) = refs[:8], refs[8:]
    column = lax.axis_index("pcol")
    height = blocks[0].shape[0]
    for index, block in enumerate(blocks):
        spot = jnp.bitwise_xor(column, (0, 2, 1, 3)[index % 4])
        panel[index // 4, pl.ds(pl.multiple_of(spot * height, height), height), :] = block[...]
    applied[...] = jnp.dot(own_sigma[...], panel[0], preferred_element_type=jnp.float32)
    applied[...] += jnp.dot(far_sigma[...], panel[1], preferred_element_type=jnp.float32)
    extent = panel.shape[1]
    size = own_inverse.shape[0]
    pack[:extent] = panel[jnp.where(column // 2 == lax.axis_index("side"), 0, 1)]
    pack[extent : extent + size] = own_inverse[...]
    pack[extent + size :] = got_inverse[...]


def couple_kernel(weight, mine, other, pack, got_pack, out_a, out_b, keep, send, half, packed):
    core, column, point = (lax.axis_index(name) for name in ("core", "pcol", "hyp"))
    applied = mine[...] + other[...]
    high = applied.astype(jnp.bfloat16)
    low = (applied - high.astype(jnp.float32)).astype(jnp.bfloat16)
    half[...] = -high
    extent = applied.shape[0]
    rows = jnp.where(column % 2 == core, pack[:extent], got_pack[:extent])
    inverse = (pack[extent:], got_pack[extent:])
    blocks = tiles(applied.shape[1])
    per = len(blocks) // 2
    for part in range(2):

        @pl.when(core == part)
        def _():
            mine_blocks = blocks[part * per : (part + 1) * per]
            at = 0
            for first in sorted({a for a, _ in mine_blocks}):
                seconds = [b for a, b in mine_blocks if a == first]
                left = slice(first * LANES, (first + 1) * LANES)
                right = slice(seconds[0] * LANES, (seconds[-1] + 1) * LANES)
                total = transposed_dot(rows[:, left], high[:, right])
                total += transposed_dot(rows[:, left], low[:, right])
                for lines in inverse:
                    total += transposed_dot(lines[:, left], lines[:, right])
                for index in range(len(seconds)):
                    packed[at * LANES : (at + 1) * LANES, :] = (
                        weight[0] * total[:, index * LANES : (index + 1) * LANES]
                    )
                    at += 1

    size = keep.shape[0]
    keep[...] = packed[pl.ds(pl.multiple_of(point * size, 8), size), :]
    send[...] = packed[pl.ds(pl.multiple_of((1 - point) * size, 8), size), :]
    height = out_a.shape[0]
    near = core == column // 2
    for out, steps in ((out_a, (0, 3)), (out_b, (1, 2))):
        spot = jnp.bitwise_xor(column, jnp.where(near, steps[0], steps[1]))
        out[...] = half[pl.ds(pl.multiple_of(spot * height, height), height), :]


def halve_kernel(mine, came, keep, send, whole):
    whole[...] = mine[...] + came[...]
    size = keep.shape[0]
    bit = lax.axis_index("pcol") // 2
    keep[...] = whole[pl.ds(pl.multiple_of(bit * size, 8), size), :]
    send[...] = whole[pl.ds(pl.multiple_of((1 - bit) * size, 8), size), :]


def add_kernel(mine, came, out):
    out[...] = mine[...] + came[...]


def join_kernel(mine, came, out):
    size = mine.shape[0]
    bit = lax.axis_index("pcol") // 2
    out[pl.ds(pl.multiple_of(bit * size, 8), size), :] = mine[...]
    out[pl.ds(pl.multiple_of((1 - bit) * size, 8), size), :] = came[...]


def spread_kernel(*refs):
    parts, (out, lines, result, sems) = refs[:8], refs[8:]
    point, side, core = (lax.axis_index(name) for name in ("hyp", "side", "core"))
    width = result.shape[1]
    blocks = tiles(width)
    per = len(blocks) // 2
    size = parts[0].shape[0]
    for other_core in range(2):
        for index in range(4):
            part = jnp.where(other_core, 1 - core, core)
            node = jnp.where(index % 2, 1 - side, side)
            slot = jnp.where(index // 2, 1 - point, point)
            start = pl.multiple_of((part * 2 + slot) * size, 8)
            lines[node, pl.ds(start, size), :] = parts[4 * other_core + index][...]
    copies = []
    for node in range(2):
        for index, (a, b) in enumerate(blocks):
            tile = lines[node, index * LANES : (index + 1) * LANES, :]
            result[node, a * LANES : (a + 1) * LANES, b * LANES : (b + 1) * LANES] = tile
            if a != b:
                result[node, b * LANES : (b + 1) * LANES, a * LANES : (a + 1) * LANES] = tile.T
        copies.append(pltpu.make_async_copy(result.at[node], out.at[node], sems.at[node]))
        copies[-1].start()
    for copy in copies:
        copy.wait()


def finish_kernel(live, a, b, out):
    row = lax.broadcasted_iota(jnp.int32, a.shape, 0)
    for s, block in enumerate((a, b)):
        out[0, :, s, :] = jnp.where(row < live[s], block[...], jnp.zeros(a.shape, a.dtype))


def square(sigma_rows, panel, live_block_rows, inv_diag, quad_weight):
    height, count, width = panel.shape[1:]
    grid = lax.axis_size("pcol")
    points = lax.axis_size("hyp")
    point, side, core, column = (lax.axis_index(name) for name in AXES)
    f32, bf16 = jnp.float32, jnp.bfloat16
    shape = jax.ShapeDtypeStruct
    dma = pltpu.SemaphoreType.DMA
    total = points * 2 * 2 * grid
    live = live_block_rows[:, 0]
    pick = functools.partial(lax.dynamic_index_in_dim, axis=0, keepdims=False)

    def swap(x, point=0, side=0, core=0, column=0):
        mask = ((point * 2 + side) * 2 + core) * grid + column
        return lax.ppermute(x, AXES, [(i, i ^ mask) for i in range(total)])

    block = shape((height, width), bf16)
    own, give = call(
        mask_kernel, [block, block], [ANY, ANY], live, panel,
        scratch=[pltpu.SMEM((2,), jnp.int32), pltpu.VMEM((height, count, width), bf16), dma((2,))],
    )
    got = swap(give, side=1)
    blocks = []
    for start in (own, got):
        second = swap(start, column=2)
        blocks += [start, second, swap(start, column=1), swap(second, column=1)]

    extent = sigma_rows.shape[2]
    sigma = call(flip_kernel, shape((extent, extent), bf16), [VMEM], sigma_rows, after=[own])
    far_sigma = swap(sigma, side=1)
    inverse = jnp.pad(inv_diag[0], ((0, 0), (0, -inv_diag.shape[2] % ROWS), (0, 0)))
    got_inverse = swap(pick(inverse, 1 - side), side=1)

    product = shape((extent, width), f32)
    pack = shape((extent + 2 * inverse.shape[1], width), bf16)
    mine, pack = call(
        apply_kernel, [product, pack], [VMEM] * 12,
        sigma, far_sigma, *blocks, pick(inverse, side), got_inverse,
        scratch=[pltpu.VMEM((2, extent, width), bf16)],
    )
    other = swap(mine, core=1)
    got_pack = swap(pack, core=1)

    lines = len(tiles(width)) // 2 * LANES

    def part(count):
        return shape((count, LANES), f32)

    out_a, out_b, keep, send = call(
        couple_kernel, [block, block, part(lines // 2), part(lines // 2)], [SMEM] + [VMEM] * 4,
        quad_weight, mine, other, pack, got_pack,
        scratch=[pltpu.VMEM((extent, width), bf16), pltpu.VMEM((lines, LANES), f32)],
    )
    keep, send = call(
        halve_kernel, [part(lines // 4)] * 2, [VMEM] * 2, keep, swap(send, point=1),
        scratch=[pltpu.VMEM((lines // 2, LANES), f32)],
    )

    def output_pairs(steps):
        pairs = []
        for h in range(points):
            for s in range(2):
                for c in range(grid):
                    for core, step in ((c // 2, steps[0]), (1 - c // 2, steps[1])):
                        base = (h * 2 + s) * 2
                        pairs.append(((base + core) * grid + c, (base + c % 2) * grid + (c ^ step)))
        return pairs

    land_a = lax.ppermute(out_a, AXES, output_pairs((0, 3)))
    land_b = lax.ppermute(out_b, AXES, output_pairs((1, 2)))
    from_a = jnp.where(column % 2 == core, column, column ^ 3) // 2

    sum_two = call(add_kernel, part(lines // 4), [VMEM] * 2, keep, swap(send, column=2))
    sum_all = call(add_kernel, part(lines // 4), [VMEM] * 2, sum_two, swap(sum_two, column=1))
    here = call(
        join_kernel, part(lines // 2), [VMEM] * 2, sum_all, swap(sum_all, column=2),
        after=[land_a, land_b],
    )
    across = swap(here, side=1)
    there = swap(here, point=1)
    both = swap(across, point=1)
    quarters = [here, across, there, both]
    quarters += [swap(x, core=1) for x in quarters]

    theirs = swap(jnp.where(from_a == side, land_b, land_a), side=1)
    mine = jnp.where(from_a == side, land_a, land_b)
    first = jnp.where(side == 0, mine, theirs)
    last = jnp.where(side == 0, theirs, mine)
    sigma_panel = call(
        finish_kernel, shape((1, height, count, width), bf16), [SMEM, VMEM, VMEM], live, first, last
    )
    marginal = call(
        spread_kernel, shape((count, width, width), f32), [VMEM] * 8, *quarters,
        scratch=[
            pltpu.VMEM((count, 2 * lines, LANES), f32),
            pltpu.VMEM((count, width, width), f32),
            dma((2,)),
        ],
        out_specs=ANY,
        after=[sigma_panel],
    )
    return sigma_panel, marginal


def solution(mesh):
    sizes = dict(mesh.shape)
    prow, pcol = ("prow",), ("pcol",)

    def on_device(sigma_rows, panel, live_block_rows, inv_diag, quad_weight):
        body = square if split else general
        return body(sigma_rows, panel, live_block_rows, inv_diag, quad_weight)

    split = sizes["hyp"] == 2 and sizes["pcol"] == 4 and sizes["prow"] == 4
    if split:
        prow = ("side", "core")
        mesh = jax.sharding.Mesh(
            mesh.devices.reshape(sizes["hyp"], 2, 2, sizes["pcol"]),
            ("hyp", "side", "core", "pcol"),
        )
    in_specs = (
        P("hyp", prow, pcol),
        P("hyp", prow + pcol, None, None),
        P(None, prow + pcol),
        P("hyp", None, prow + pcol, None),
        P("hyp"),
    )
    out_specs = (P("hyp", prow + pcol, None, None), P())
    return jax.shard_map(
        on_device, mesh=mesh, in_specs=in_specs, out_specs=out_specs, check_vma=False
    )
```

```python
import functools

import jax
import jax.numpy as jnp
from jax import lax
from jax.experimental import pallas as pl
from jax.experimental.pallas import tpu as pltpu
from jax.sharding import PartitionSpec as P

LANES = 128
ROWS = 16
VMEM = pl.BlockSpec(memory_space=pltpu.VMEM)
SMEM = pl.BlockSpec(memory_space=pltpu.SMEM)
ANY = pl.BlockSpec(memory_space=pl.ANY)
HBM = pl.BlockSpec(memory_space=pltpu.HBM)
AXES = ("hyp", "side", "core", "pcol")


def call(kernel, outs, specs, *operands, scratch=(), out_specs=None, after=()):
    many = isinstance(outs, (list, tuple))
    count = len(specs)

    def body(*refs):
        kernel(*refs[:count], *refs[count + len(after) :])

    if out_specs is None:
        out_specs = [VMEM] * len(outs) if many else VMEM
    return pl.pallas_call(
        body,
        out_shape=outs,
        in_specs=list(specs) + [ANY] * len(after),
        out_specs=out_specs,
        scratch_shapes=scratch,
        compiler_params=pltpu.CompilerParams(vmem_limit_bytes=32 * 2**20),
    )(*operands, *after)


def transposed_dot(left, right):
    return lax.dot_general(
        left, right, (((0,), (0,)), ((), ())), preferred_element_type=jnp.float32
    )


def tiles(width):
    count = width // LANES
    return [(a, b) for a in range(count) for b in range(a, count)]


def general(sigma_rows, panel, live_block_rows, inv_diag, quad_weight):
    height, count, width = panel.shape[1:]
    offsets = lax.broadcasted_iota(jnp.int32, (height, count), 0)
    active = offsets < live_block_rows[:, 0][None, :]
    masked = jnp.where(active[:, :, None], panel[0], jnp.zeros_like(panel[0]))
    extent = height * lax.axis_size("prow")
    gathered = lax.all_gather(masked, ("prow", "pcol"), axis=0, tiled=True)
    start = lax.axis_index("pcol") * sigma_rows.shape[2]
    column_panel = lax.dynamic_slice_in_dim(gathered, start, sigma_rows.shape[2], 0)
    applied = lax.psum_scatter(
        jnp.dot(
            sigma_rows[0],
            column_panel.reshape(sigma_rows.shape[2], count * width),
            preferred_element_type=jnp.float32,
        ),
        "pcol",
        scatter_dimension=0,
        tiled=True,
    ).reshape(height, count, width)
    half = applied.astype(jnp.bfloat16)
    sigma_panel = jnp.where(active[:, :, None], -half, jnp.zeros_like(half))[None]
    coupling = jnp.einsum(
        "vwg,vwe->wge",
        masked.astype(jnp.float32),
        applied,
        precision=lax.Precision.HIGHEST,
    )
    diagonal = jnp.einsum(
        "skp,skq->spq", inv_diag[0], inv_diag[0], preferred_element_type=jnp.float32
    )
    marginal = lax.psum(quad_weight[0] * (coupling + diagonal), ("hyp", "prow", "pcol"))
    return sigma_panel, marginal


def start_kernel(*refs):
    sources, (own, give, own_inverse, low, high), buffers, sems = refs[:4], refs[4:9], refs[9:13], refs[13]
    copies = [
        pltpu.make_async_copy(source, buffer, sems.at[index])
        for index, (source, buffer) in enumerate(zip(sources, buffers))
    ]
    for copy in copies:
        copy.start()
    for copy in copies[:3]:
        copy.wait()
    live, panel, inverse, matrix = buffers
    first = lax.axis_index("side") == 0
    row = lax.broadcasted_iota(jnp.int32, own.shape, 0)
    rows = panel[0]
    zero = jnp.zeros(own.shape, own.dtype)
    one, two = (jnp.where(row < live[s], rows[:, s, :], zero) for s in range(2))
    height = own.shape[0]
    own[...] = jnp.where(first, one, two)
    give[:height] = jnp.where(first, two, one)
    spare = jnp.zeros((own_inverse.shape[0] - inverse.shape[2], own.shape[1]), own.dtype)
    one, two = (jnp.concatenate([inverse[0, s], spare], 0) for s in range(2))
    own_inverse[...] = jnp.where(first, one, two)
    give[height:] = jnp.where(first, two, one)
    copies[3].wait()
    half = matrix.shape[1] // 2
    low[...] = matrix[0, :half].T
    high[...] = matrix[0, half:].T


def gather_kernel(*refs):
    blocks, (own_inverse, got_inverse, rows, pack) = refs[:8], refs[8:]
    column = lax.axis_index("pcol")
    height = blocks[0].shape[0]
    for index, block in enumerate(blocks):
        spot = jnp.bitwise_xor(column, (0, 2, 1, 3)[index % 4])
        rows[index // 4, pl.ds(pl.multiple_of(spot * height, height), height), :] = block[...]
    extent = rows.shape[1]
    size = own_inverse.shape[0]
    pack[:extent] = rows[jnp.where(column // 2 == lax.axis_index("side"), 0, 1)]
    pack[extent : extent + size] = own_inverse[...]
    pack[extent + size :] = got_inverse[...]


def apply_kernel(rows, *refs):
    parts, applied = refs[:4], refs[4]
    half = rows.shape[1] // 2
    total = 0
    for index, part in enumerate(parts):
        lines = rows[index // 2, index % 2 * half : (index % 2 + 1) * half, :]
        total += jnp.dot(part[...], lines, preferred_element_type=jnp.float32)
    applied[...] = total


def couple_kernel(weight, mine, other, pack, got_pack, out_a, out_b, keep, send, half, packed):
    core, column, point = (lax.axis_index(name) for name in ("core", "pcol", "hyp"))
    applied = mine[...] + other[...]
    high = applied.astype(jnp.bfloat16)
    low = (applied - high.astype(jnp.float32)).astype(jnp.bfloat16)
    half[...] = -high
    extent = applied.shape[0]
    rows = jnp.where(column % 2 == core, pack[:extent], got_pack[:extent])
    inverse = (pack[extent:], got_pack[extent:])
    blocks = tiles(applied.shape[1])
    per = len(blocks) // 2
    for part in range(2):

        @pl.when(core == part)
        def _():
            mine_blocks = blocks[part * per : (part + 1) * per]
            at = 0
            for first in sorted({a for a, _ in mine_blocks}):
                seconds = [b for a, b in mine_blocks if a == first]
                left = slice(first * LANES, (first + 1) * LANES)
                right = slice(seconds[0] * LANES, (seconds[-1] + 1) * LANES)
                total = transposed_dot(rows[:, left], high[:, right])
                total += transposed_dot(rows[:, left], low[:, right])
                for lines in inverse:
                    total += transposed_dot(lines[:, left], lines[:, right])
                for index in range(len(seconds)):
                    packed[at * LANES : (at + 1) * LANES, :] = (
                        weight[0] * total[:, index * LANES : (index + 1) * LANES]
                    )
                    at += 1

    size = keep.shape[0]
    keep[...] = packed[pl.ds(pl.multiple_of(point * size, 8), size), :]
    send[...] = packed[pl.ds(pl.multiple_of((1 - point) * size, 8), size), :]
    height = out_a.shape[0]
    near = core == column // 2
    for out, steps in ((out_a, (0, 3)), (out_b, (1, 2))):
        spot = jnp.bitwise_xor(column, jnp.where(near, steps[0], steps[1]))
        out[...] = half[pl.ds(pl.multiple_of(spot * height, height), height), :]


def add_kernel(mine, came, out):
    out[...] = mine[...] + came[...]


def finish_kernel(*refs):
    parts, (live_hbm, mine, theirs, rows_out, out, live, block, lines, result, sems) = refs[:8], refs[8:]
    point, side, core = (lax.axis_index(name) for name in ("hyp", "side", "core"))
    copy = pltpu.make_async_copy(live_hbm, live, sems.at[0])
    copy.start()
    width = result.shape[1]
    blocks = tiles(width)
    size = parts[0].shape[0]
    for index, part in enumerate(parts):
        owner = core if index < 4 else 1 - core
        node = 1 - side if index % 2 else side
        slot = 1 - point if index // 2 % 2 else point
        start = pl.multiple_of((owner * 2 + slot) * size, 8)
        lines[node, pl.ds(start, size), :] = part[...]
    copies = []
    for node in range(2):
        for index, (a, b) in enumerate(blocks):
            tile = lines[node, index * LANES : (index + 1) * LANES, :]
            result[node, a * LANES : (a + 1) * LANES, b * LANES : (b + 1) * LANES] = tile
            if a != b:
                result[node, b * LANES : (b + 1) * LANES, a * LANES : (a + 1) * LANES] = tile.T
        copies.append(pltpu.make_async_copy(result.at[node], out.at[node], sems.at[1 + node]))
        copies[-1].start()
    copy.wait()
    row = lax.broadcasted_iota(jnp.int32, mine.shape, 0)
    first = side == 0
    pair = (jnp.where(first, mine[...], theirs[...]), jnp.where(first, theirs[...], mine[...]))
    for s, value in enumerate(pair):
        block[:, s, :] = jnp.where(row < live[s], value, jnp.zeros(value.shape, value.dtype))
    copies.append(pltpu.make_async_copy(block, rows_out.at[0], sems.at[3]))
    copies[-1].start()
    for copy in copies:
        copy.wait()


def square(sigma_rows, panel, live_block_rows, inv_diag, quad_weight):
    height, count, width = panel.shape[1:]
    grid = lax.axis_size("pcol")
    points = lax.axis_size("hyp")
    point, side, core, column = (lax.axis_index(name) for name in AXES)
    f32, bf16 = jnp.float32, jnp.bfloat16
    shape = jax.ShapeDtypeStruct
    dma = pltpu.SemaphoreType.DMA
    stay = functools.partial(pltpu.with_memory_space_constraint, memory_space=pltpu.HBM)
    devices = points * 2 * 2 * grid
    live = live_block_rows[:, 0]

    def swap(x, point=0, side=0, core=0, column=0):
        mask = ((point * 2 + side) * 2 + core) * grid + column
        return lax.ppermute(x, AXES, [(i, i ^ mask) for i in range(devices)])

    extent = sigma_rows.shape[2]
    block = shape((height, width), bf16)
    part = shape((extent, extent // 2), bf16)
    size = pl.cdiv(inv_diag.shape[2], ROWS) * ROWS
    own, give, own_inverse, low, high = call(
        start_kernel,
        [block, shape((height + size, width), bf16), shape((size, width), bf16), part, part],
        [HBM] * 4,
        *map(stay, (live, panel, inv_diag, sigma_rows)),
        scratch=[pltpu.SMEM(live.shape, jnp.int32)]
        + [pltpu.VMEM(x.shape, bf16) for x in (panel, inv_diag, sigma_rows)]
        + [dma((4,))],
    )
    got = swap(give, side=1)
    got, got_inverse = got[:height], got[height:]
    far_low, far_high = swap(low, side=1), swap(high, side=1)
    blocks = []
    for start in (own, got):
        second = swap(start, column=2)
        blocks += [start, second, swap(start, column=1), swap(second, column=1)]
    pack = shape((extent + 2 * size, width), bf16)
    rows, pack = call(
        gather_kernel, [shape((2, extent, width), bf16), pack], [VMEM] * 10,
        *blocks, own_inverse, got_inverse,
    )
    got_pack = swap(pack, core=1)
    mine = call(
        apply_kernel, shape((extent, width), f32), [VMEM] * 5, rows, low, high, far_low, far_high
    )
    other = swap(mine, core=1)

    lines = len(tiles(width)) // 2 * LANES
    part = shape((lines // 2, LANES), f32)
    out_a, out_b, keep, send = call(
        couple_kernel, [block, block, part, part], [SMEM] + [VMEM] * 4,
        quad_weight, mine, other, pack, got_pack,
        scratch=[pltpu.VMEM((extent, width), bf16), pltpu.VMEM((lines, LANES), f32)],
    )
    came = swap(send, point=1)

    def output_pairs(steps):
        pairs = []
        for h in range(points):
            for s in range(2):
                for c in range(grid):
                    for core, step in ((c // 2, steps[0]), (1 - c // 2, steps[1])):
                        base = (h * 2 + s) * 2
                        pairs.append(((base + core) * grid + c, (base + c % 2) * grid + (c ^ step)))
        return pairs

    land_a = lax.ppermute(out_a, AXES, output_pairs((0, 3)))
    land_b = lax.ppermute(out_b, AXES, output_pairs((1, 2)))
    from_a = jnp.where(column % 2 == core, column, column ^ 3) // 2

    add = functools.partial(call, add_kernel, part, [VMEM] * 2)
    total = add(keep, came)
    total = add(total, swap(total, column=2))
    total = add(total, swap(total, column=1), after=[land_a, land_b])
    quarters = [total, swap(total, side=1), swap(total, point=1), swap(total, side=1, point=1)]
    quarters += [swap(x, core=1) for x in quarters]
    theirs = swap(jnp.where(from_a == side, land_b, land_a), side=1)
    mine = jnp.where(from_a == side, land_a, land_b)
    return call(
        finish_kernel,
        [shape((1, height, count, width), bf16), shape((count, width, width), f32)],
        [VMEM] * 8 + [HBM] + [VMEM] * 2,
        *quarters, live, mine, theirs,
        scratch=[
            pltpu.SMEM((2,), jnp.int32),
            pltpu.VMEM((height, count, width), bf16),
            pltpu.VMEM((count, 2 * lines, LANES), f32),
            pltpu.VMEM((count, width, width), f32),
            dma((4,)),
        ],
        out_specs=[HBM, HBM],
    )


def solution(mesh):
    sizes = dict(mesh.shape)
    prow, pcol = ("prow",), ("pcol",)

    def on_device(sigma_rows, panel, live_block_rows, inv_diag, quad_weight):
        body = square if split else general
        return body(sigma_rows, panel, live_block_rows, inv_diag, quad_weight)

    split = sizes["hyp"] == 2 and sizes["pcol"] == 4 and sizes["prow"] == 4
    if split:
        prow = ("side", "core")
        mesh = jax.sharding.Mesh(
            mesh.devices.reshape(sizes["hyp"], 2, 2, sizes["pcol"]),
            ("hyp", "side", "core", "pcol"),
        )
    in_specs = (
        P("hyp", prow, pcol),
        P("hyp", prow + pcol, None, None),
        P(None, prow + pcol),
        P("hyp", None, prow + pcol, None),
        P("hyp"),
    )
    out_specs = (P("hyp", prow + pcol, None, None), P())
    return jax.shard_map(
        on_device, mesh=mesh, in_specs=in_specs, out_specs=out_specs, check_vma=False
    )
```

```python
import functools

import jax
import jax.numpy as jnp
from jax import lax
from jax.experimental import pallas as pl
from jax.experimental.pallas import tpu as pltpu
from jax.sharding import PartitionSpec as P

LANES = 128
ROWS = 16
VMEM = pl.BlockSpec(memory_space=pltpu.VMEM)
SMEM = pl.BlockSpec(memory_space=pltpu.SMEM)
ANY = pl.BlockSpec(memory_space=pl.ANY)
HBM = pl.BlockSpec(memory_space=pltpu.HBM)
AXES = ("hyp", "side", "core", "pcol")


def call(kernel, outs, specs, *operands, scratch=(), out_specs=None, after=(), alias={}):
    many = isinstance(outs, (list, tuple))
    count = len(specs)

    def body(*refs):
        kernel(*refs[:count], *refs[count + len(after) :])

    if out_specs is None:
        out_specs = [VMEM] * len(outs) if many else VMEM
    return pl.pallas_call(
        body,
        out_shape=outs,
        in_specs=list(specs) + [ANY] * len(after),
        out_specs=out_specs,
        scratch_shapes=scratch,
        input_output_aliases=alias,
        compiler_params=pltpu.CompilerParams(vmem_limit_bytes=32 * 2**20),
    )(*operands, *after)


def transposed_dot(left, right):
    return lax.dot_general(
        left, right, (((0,), (0,)), ((), ())), preferred_element_type=jnp.float32
    )


def tiles(width):
    count = width // LANES
    return [(a, b) for a in range(count) for b in range(a, count)]


def general(sigma_rows, panel, live_block_rows, inv_diag, quad_weight):
    height, count, width = panel.shape[1:]
    offsets = lax.broadcasted_iota(jnp.int32, (height, count), 0)
    active = offsets < live_block_rows[:, 0][None, :]
    masked = jnp.where(active[:, :, None], panel[0], jnp.zeros_like(panel[0]))
    extent = height * lax.axis_size("prow")
    gathered = lax.all_gather(masked, ("prow", "pcol"), axis=0, tiled=True)
    start = lax.axis_index("pcol") * sigma_rows.shape[2]
    column_panel = lax.dynamic_slice_in_dim(gathered, start, sigma_rows.shape[2], 0)
    applied = lax.psum_scatter(
        jnp.dot(
            sigma_rows[0],
            column_panel.reshape(sigma_rows.shape[2], count * width),
            preferred_element_type=jnp.float32,
        ),
        "pcol",
        scatter_dimension=0,
        tiled=True,
    ).reshape(height, count, width)
    half = applied.astype(jnp.bfloat16)
    sigma_panel = jnp.where(active[:, :, None], -half, jnp.zeros_like(half))[None]
    coupling = jnp.einsum(
        "vwg,vwe->wge",
        masked.astype(jnp.float32),
        applied,
        precision=lax.Precision.HIGHEST,
    )
    diagonal = jnp.einsum(
        "skp,skq->spq", inv_diag[0], inv_diag[0], preferred_element_type=jnp.float32
    )
    marginal = lax.psum(quad_weight[0] * (coupling + diagonal), ("hyp", "prow", "pcol"))
    return sigma_panel, marginal


def start_kernel(*refs):
    sources, (own, give, own_inverse), pieces, buffers, sems = refs[:4], refs[4:7], refs[7:-5], refs[-5:-1], refs[-1]
    copies = [
        pltpu.make_async_copy(source, buffer, sems.at[index])
        for index, (source, buffer) in enumerate(zip(sources, buffers))
    ]
    for copy in copies:
        copy.start()
    for copy in copies[:3]:
        copy.wait()
    live, panel, inverse, matrix = buffers
    first = lax.axis_index("side") == 0
    row = lax.broadcasted_iota(jnp.int32, own.shape, 0)
    rows = panel[0]
    zero = jnp.zeros(own.shape, own.dtype)
    one, two = (jnp.where(row < live[s], rows[:, s, :], zero) for s in range(2))
    height = own.shape[0]
    own[...] = jnp.where(first, one, two)
    give[:height] = jnp.where(first, two, one)
    spare = jnp.zeros((own_inverse.shape[0] - inverse.shape[2], own.shape[1]), own.dtype)
    one, two = (jnp.concatenate([inverse[0, s], spare], 0) for s in range(2))
    own_inverse[...] = jnp.where(first, one, two)
    give[height:] = jnp.where(first, two, one)
    copies[3].wait()
    at = 0
    for piece in pieces:
        piece[...] = matrix[0, :, at : at + piece.shape[0]].T
        at += piece.shape[0]


def gather_kernel(*refs):
    blocks, (own_inverse, got_inverse, rows, pack) = refs[:8], refs[8:]
    column = lax.axis_index("pcol")
    height = blocks[0].shape[0]
    for index, block in enumerate(blocks):
        spot = jnp.bitwise_xor(column, (0, 2, 1, 3)[index % 4])
        rows[index // 4, pl.ds(pl.multiple_of(spot * height, height), height), :] = block[...]
    extent = rows.shape[1]
    size = own_inverse.shape[0]
    pack[:extent] = rows[jnp.where(column // 2 == lax.axis_index("side"), 0, 1)]
    pack[extent : extent + size] = own_inverse[...]
    pack[extent + size :] = got_inverse[...]


def apply_kernel(rows, *refs):
    pieces, applied = refs[:-1], refs[-1]
    count = len(pieces) // 2
    at = 0
    for own, far in zip(pieces[:count], pieces[count:]):
        total = jnp.dot(own[...], rows[0], preferred_element_type=jnp.float32)
        total += jnp.dot(far[...], rows[1], preferred_element_type=jnp.float32)
        applied[at : at + own.shape[0]] = total
        at += own.shape[0]


def couple_kernel(weight, mine, other, pack, got_pack, out_a, out_b, keep, send, half, packed):
    core, column, point = (lax.axis_index(name) for name in ("core", "pcol", "hyp"))
    applied = mine[...] + other[...]
    high = applied.astype(jnp.bfloat16)
    low = (applied - high.astype(jnp.float32)).astype(jnp.bfloat16)
    half[...] = -high
    extent = applied.shape[0]
    rows = jnp.where(column % 2 == core, pack[:extent], got_pack[:extent])
    inverse = (pack[extent:], got_pack[extent:])
    blocks = tiles(applied.shape[1])
    per = len(blocks) // 2
    for part in range(2):

        @pl.when(core == part)
        def _():
            mine_blocks = blocks[part * per : (part + 1) * per]
            at = 0
            for first in sorted({a for a, _ in mine_blocks}):
                seconds = [b for a, b in mine_blocks if a == first]
                left = slice(first * LANES, (first + 1) * LANES)
                right = slice(seconds[0] * LANES, (seconds[-1] + 1) * LANES)
                total = transposed_dot(rows[:, left], high[:, right])
                total += transposed_dot(rows[:, left], low[:, right])
                for lines in inverse:
                    total += transposed_dot(lines[:, left], lines[:, right])
                for index in range(len(seconds)):
                    packed[at * LANES : (at + 1) * LANES, :] = (
                        weight[0] * total[:, index * LANES : (index + 1) * LANES]
                    )
                    at += 1

    size = keep.shape[0]
    keep[...] = packed[pl.ds(pl.multiple_of(point * size, 8), size), :]
    send[...] = packed[pl.ds(pl.multiple_of((1 - point) * size, 8), size), :]
    height = out_a.shape[0]
    near = core == column // 2
    for out, steps in ((out_a, (0, 3)), (out_b, (1, 2))):
        spot = jnp.bitwise_xor(column, jnp.where(near, steps[0], steps[1]))
        out[...] = half[pl.ds(pl.multiple_of(spot * height, height), height), :]


def add_kernel(mine, came, out):
    out[...] = mine[...] + came[...]


def finish_kernel(*refs):
    parts, (live_hbm, mine, theirs, rows_out, out, live, block, lines, result, sems) = refs[:8], refs[8:]
    point, side, core = (lax.axis_index(name) for name in ("hyp", "side", "core"))
    copy = pltpu.make_async_copy(live_hbm, live, sems.at[0])
    copy.start()
    width = result.shape[1]
    blocks = tiles(width)
    size = parts[0].shape[0]
    for index, part in enumerate(parts):
        owner = core if index < 4 else 1 - core
        node = 1 - side if index % 2 else side
        slot = 1 - point if index // 2 % 2 else point
        start = pl.multiple_of((owner * 2 + slot) * size, 8)
        lines[node, pl.ds(start, size), :] = part[...]
    copies = []
    for node in range(2):
        for index, (a, b) in enumerate(blocks):
            tile = lines[node, index * LANES : (index + 1) * LANES, :]
            result[node, a * LANES : (a + 1) * LANES, b * LANES : (b + 1) * LANES] = tile
            if a != b:
                result[node, b * LANES : (b + 1) * LANES, a * LANES : (a + 1) * LANES] = tile.T
        copies.append(pltpu.make_async_copy(result.at[node], out.at[node], sems.at[1 + node]))
        copies[-1].start()
    copy.wait()
    row = lax.broadcasted_iota(jnp.int32, mine.shape, 0)
    first = side == 0
    pair = (jnp.where(first, mine[...], theirs[...]), jnp.where(first, theirs[...], mine[...]))
    for s, value in enumerate(pair):
        block[:, s, :] = jnp.where(row < live[s], value, jnp.zeros(value.shape, value.dtype))
    copies.append(pltpu.make_async_copy(block, rows_out.at[0], sems.at[3]))
    copies[-1].start()
    for copy in copies:
        copy.wait()


def square(sigma_rows, panel, live_block_rows, inv_diag, quad_weight):
    height, count, width = panel.shape[1:]
    grid = lax.axis_size("pcol")
    points = lax.axis_size("hyp")
    point, side, core, column = (lax.axis_index(name) for name in AXES)
    f32, bf16 = jnp.float32, jnp.bfloat16
    shape = jax.ShapeDtypeStruct
    dma = pltpu.SemaphoreType.DMA
    stay = functools.partial(pltpu.with_memory_space_constraint, memory_space=pltpu.HBM)
    devices = points * 2 * 2 * grid
    live = live_block_rows[:, 0]

    def swap(x, point=0, side=0, core=0, column=0):
        mask = ((point * 2 + side) * 2 + core) * grid + column
        return lax.ppermute(x, AXES, [(i, i ^ mask) for i in range(devices)])

    extent = sigma_rows.shape[2]
    block = shape((height, width), bf16)
    cuts = (extent * 9 // 16, extent * 7 // 32, extent * 7 // 32)
    size = pl.cdiv(inv_diag.shape[2], ROWS) * ROWS
    own, give, own_inverse, *pieces = call(
        start_kernel,
        [block, shape((height + size, width), bf16), shape((size, width), bf16)]
        + [shape((lines, extent), bf16) for lines in cuts],
        [HBM] * 4,
        *map(stay, (live, panel, inv_diag, sigma_rows)),
        scratch=[pltpu.SMEM(live.shape, jnp.int32)]
        + [pltpu.VMEM(x.shape, bf16) for x in (panel, inv_diag, sigma_rows)]
        + [dma((4,))],
    )
    got = swap(give, side=1)
    got, got_inverse = got[:height], got[height:]
    blocks = []
    for start in (own, got):
        second = swap(start, column=2)
        blocks += [start, second, swap(start, column=1), swap(second, column=1)]
    far = [swap(piece, side=1) for piece in pieces]

    pack = shape((extent + 2 * size, width), bf16)
    rows, pack = call(
        gather_kernel, [shape((2, extent, width), bf16), pack], [VMEM] * 10,
        *blocks, own_inverse, got_inverse,
    )
    got_pack = swap(pack, core=1)
    mine = call(
        apply_kernel, shape((extent, width), f32), [VMEM] * (1 + 2 * len(cuts)), rows, *pieces, *far
    )
    other = swap(mine, core=1)

    lines = len(tiles(width)) // 2 * LANES
    part = shape((lines // 2, LANES), f32)
    out_a, out_b, keep, send = call(
        couple_kernel, [block, block, part, part], [SMEM] + [VMEM] * 4,
        quad_weight, mine, other, pack, got_pack,
        scratch=[pltpu.VMEM((extent, width), bf16), pltpu.VMEM((lines, LANES), f32)],
    )
    came = swap(send, point=1)

    def output_pairs(steps):
        pairs = []
        for h in range(points):
            for s in range(2):
                for c in range(grid):
                    for core, step in ((c // 2, steps[0]), (1 - c // 2, steps[1])):
                        base = (h * 2 + s) * 2
                        pairs.append(((base + core) * grid + c, (base + c % 2) * grid + (c ^ step)))
        return pairs

    land_a = lax.ppermute(out_a, AXES, output_pairs((0, 3)))
    land_b = lax.ppermute(out_b, AXES, output_pairs((1, 2)))
    from_a = jnp.where(column % 2 == core, column, column ^ 3) // 2

    add = functools.partial(call, add_kernel, part, [VMEM] * 2)
    total = add(keep, came)
    total = add(total, swap(total, column=2), after=[land_a, land_b])
    theirs = swap(jnp.where(from_a == side, land_b, land_a), side=1)
    total = add(total, swap(total, column=1), after=[theirs])
    quarters = [total, swap(total, side=1), swap(total, point=1), swap(total, side=1, point=1)]
    quarters += [swap(x, core=1) for x in quarters]
    mine = jnp.where(from_a == side, land_a, land_b)
    return call(
        finish_kernel,
        [shape((1, height, count, width), bf16), shape((count, width, width), f32)],
        [VMEM] * 8 + [HBM] + [VMEM] * 2,
        *quarters, live, mine, theirs,
        scratch=[
            pltpu.SMEM((2,), jnp.int32),
            pltpu.VMEM((height, count, width), bf16),
            pltpu.VMEM((count, 2 * lines, LANES), f32),
            pltpu.VMEM((count, width, width), f32),
            dma((4,)),
        ],
        out_specs=[HBM, HBM],
    )


def solution(mesh):
    sizes = dict(mesh.shape)
    prow, pcol = ("prow",), ("pcol",)

    def on_device(sigma_rows, panel, live_block_rows, inv_diag, quad_weight):
        body = square if split else general
        return body(sigma_rows, panel, live_block_rows, inv_diag, quad_weight)

    split = sizes["hyp"] == 2 and sizes["pcol"] == 4 and sizes["prow"] == 4
    if split:
        prow = ("side", "core")
        mesh = jax.sharding.Mesh(
            mesh.devices.reshape(sizes["hyp"], 2, 2, sizes["pcol"]),
            ("hyp", "side", "core", "pcol"),
        )
    in_specs = (
        P("hyp", prow, pcol),
        P("hyp", prow + pcol, None, None),
        P(None, prow + pcol),
        P("hyp", None, prow + pcol, None),
        P("hyp"),
    )
    out_specs = (P("hyp", prow + pcol, None, None), P())
    return jax.shard_map(
        on_device, mesh=mesh, in_specs=in_specs, out_specs=out_specs, check_vma=False
    )
```

```python
import functools

import jax
import jax.numpy as jnp
from jax import lax
from jax.experimental import pallas as pl
from jax.experimental.pallas import tpu as pltpu
from jax.sharding import PartitionSpec as P

LANES = 128
ROWS = 16
VMEM = pl.BlockSpec(memory_space=pltpu.VMEM)
SMEM = pl.BlockSpec(memory_space=pltpu.SMEM)
ANY = pl.BlockSpec(memory_space=pl.ANY)
HBM = pl.BlockSpec(memory_space=pltpu.HBM)
AXES = ("hyp", "side", "core", "pcol")


def call(kernel, outs, specs, *operands, scratch=(), out_specs=None, after=(), alias={}):
    many = isinstance(outs, (list, tuple))
    count = len(specs)

    def body(*refs):
        kernel(*refs[:count], *refs[count + len(after) :])

    if out_specs is None:
        out_specs = [VMEM] * len(outs) if many else VMEM
    return pl.pallas_call(
        body,
        out_shape=outs,
        in_specs=list(specs) + [ANY] * len(after),
        out_specs=out_specs,
        scratch_shapes=scratch,
        input_output_aliases=alias,
        compiler_params=pltpu.CompilerParams(vmem_limit_bytes=32 * 2**20),
    )(*operands, *after)


def transposed_dot(left, right):
    return lax.dot_general(
        left, right, (((0,), (0,)), ((), ())), preferred_element_type=jnp.float32
    )


def tiles(width):
    count = width // LANES
    return [(a, b) for a in range(count) for b in range(a, count)]


def general(sigma_rows, panel, live_block_rows, inv_diag, quad_weight):
    height, count, width = panel.shape[1:]
    offsets = lax.broadcasted_iota(jnp.int32, (height, count), 0)
    active = offsets < live_block_rows[:, 0][None, :]
    masked = jnp.where(active[:, :, None], panel[0], jnp.zeros_like(panel[0]))
    extent = height * lax.axis_size("prow")
    gathered = lax.all_gather(masked, ("prow", "pcol"), axis=0, tiled=True)
    start = lax.axis_index("pcol") * sigma_rows.shape[2]
    column_panel = lax.dynamic_slice_in_dim(gathered, start, sigma_rows.shape[2], 0)
    applied = lax.psum_scatter(
        jnp.dot(
            sigma_rows[0],
            column_panel.reshape(sigma_rows.shape[2], count * width),
            preferred_element_type=jnp.float32,
        ),
        "pcol",
        scatter_dimension=0,
        tiled=True,
    ).reshape(height, count, width)
    half = applied.astype(jnp.bfloat16)
    sigma_panel = jnp.where(active[:, :, None], -half, jnp.zeros_like(half))[None]
    coupling = jnp.einsum(
        "vwg,vwe->wge",
        masked.astype(jnp.float32),
        applied,
        precision=lax.Precision.HIGHEST,
    )
    diagonal = jnp.einsum(
        "skp,skq->spq", inv_diag[0], inv_diag[0], preferred_element_type=jnp.float32
    )
    marginal = lax.psum(quad_weight[0] * (coupling + diagonal), ("hyp", "prow", "pcol"))
    return sigma_panel, marginal


def start_kernel(*refs):
    sources, (own, give, own_inverse), pieces, buffers, sems = refs[:4], refs[4:7], refs[7:-5], refs[-5:-1], refs[-1]
    copies = [
        pltpu.make_async_copy(source, buffer, sems.at[index])
        for index, (source, buffer) in enumerate(zip(sources, buffers))
    ]
    for copy in copies:
        copy.start()
    for copy in copies[:3]:
        copy.wait()
    live, panel, inverse, matrix = buffers
    first = lax.axis_index("side") == 0
    row = lax.broadcasted_iota(jnp.int32, own.shape, 0)
    rows = panel[0]
    zero = jnp.zeros(own.shape, own.dtype)
    one, two = (jnp.where(row < live[s], rows[:, s, :], zero) for s in range(2))
    height = own.shape[0]
    own[...] = jnp.where(first, one, two)
    give[:height] = jnp.where(first, two, one)
    spare = jnp.zeros((own_inverse.shape[0] - inverse.shape[2], own.shape[1]), own.dtype)
    one, two = (jnp.concatenate([inverse[0, s], spare], 0) for s in range(2))
    own_inverse[...] = jnp.where(first, one, two)
    give[height:] = jnp.where(first, two, one)
    copies[3].wait()
    at = 0
    for piece in pieces:
        piece[...] = matrix[0, :, at : at + piece.shape[0]].T
        at += piece.shape[0]


def gather_kernel(*refs):
    blocks, (own_inverse, got_inverse, rows, pack) = [], refs[-4:]
    for ref in refs[:-4]:
        blocks += [ref] if len(ref.shape) == 2 else [ref.at[0], ref.at[1]]
    column = lax.axis_index("pcol")
    height = blocks[0].shape[0]
    for index, block in enumerate(blocks):
        spot = jnp.bitwise_xor(column, (0, 2, 1, 3)[index % 4])
        rows[index // 4, pl.ds(pl.multiple_of(spot * height, height), height), :] = block[...]
    extent = rows.shape[1]
    size = own_inverse.shape[0]
    pack[:extent] = rows[jnp.where(column // 2 == lax.axis_index("side"), 0, 1)]
    pack[extent : extent + size] = own_inverse[...]
    pack[extent + size :] = got_inverse[...]


def apply_kernel(rows, *refs):
    pieces, applied = refs[:-1], refs[-1]
    count = len(pieces) // 2
    at = 0
    for own, far in zip(pieces[:count], pieces[count:]):
        total = jnp.dot(own[...], rows[0], preferred_element_type=jnp.float32)
        total += jnp.dot(far[...], rows[1], preferred_element_type=jnp.float32)
        applied[at : at + own.shape[0]] = total
        at += own.shape[0]


def couple_kernel(weight, mine, other, pack, got_pack, out_near, out_far, keep, send, half, packed):
    core, column, point = (lax.axis_index(name) for name in ("core", "pcol", "hyp"))
    applied = mine[...] + other[...]
    high = applied.astype(jnp.bfloat16)
    low = (applied - high.astype(jnp.float32)).astype(jnp.bfloat16)
    half[...] = -high
    extent = applied.shape[0]
    rows = jnp.where(column % 2 == core, pack[:extent], got_pack[:extent])
    inverse = (pack[extent:], got_pack[extent:])
    blocks = tiles(applied.shape[1])
    per = len(blocks) // 2
    for part in range(2):

        @pl.when(core == part)
        def _():
            mine_blocks = blocks[part * per : (part + 1) * per]
            at = 0
            for first in sorted({a for a, _ in mine_blocks}):
                seconds = [b for a, b in mine_blocks if a == first]
                left = slice(first * LANES, (first + 1) * LANES)
                right = slice(seconds[0] * LANES, (seconds[-1] + 1) * LANES)
                total = transposed_dot(rows[:, left], high[:, right])
                total += transposed_dot(rows[:, left], low[:, right])
                for lines in inverse:
                    total += transposed_dot(lines[:, left], lines[:, right])
                for index in range(len(seconds)):
                    packed[at * LANES : (at + 1) * LANES, :] = (
                        weight[0] * total[:, index * LANES : (index + 1) * LANES]
                    )
                    at += 1

    size = keep.shape[0]
    keep[...] = packed[pl.ds(pl.multiple_of(point * size, 8), size), :]
    send[...] = packed[pl.ds(pl.multiple_of((1 - point) * size, 8), size), :]
    height = out_near.shape[0]
    side = lax.axis_index("side")
    for out, at in ((out_near, side), (out_far, 1 - side)):
        spot = at * 2 + core
        out[...] = half[pl.ds(pl.multiple_of(spot * height, height), height), :]


def add_kernel(mine, came, out):
    out[...] = mine[...] + came[...]


def finish_kernel(*refs):
    parts, (live_hbm, near, far, rows_out, out, live, block, lines, result, sems) = refs[:8], refs[8:]
    point, side, core = (lax.axis_index(name) for name in ("hyp", "side", "core"))
    copy = pltpu.make_async_copy(live_hbm, live, sems.at[0])
    copy.start()
    width = result.shape[1]
    blocks = tiles(width)
    size = parts[0].shape[0]
    for index, part in enumerate(parts):
        owner = core if index < 4 else 1 - core
        node = 1 - side if index % 2 else side
        slot = 1 - point if index // 2 % 2 else point
        start = pl.multiple_of((owner * 2 + slot) * size, 8)
        lines[node, pl.ds(start, size), :] = part[...]
    copies = []
    for node in range(2):
        for index, (a, b) in enumerate(blocks):
            tile = lines[node, index * LANES : (index + 1) * LANES, :]
            result[node, a * LANES : (a + 1) * LANES, b * LANES : (b + 1) * LANES] = tile
            if a != b:
                result[node, b * LANES : (b + 1) * LANES, a * LANES : (a + 1) * LANES] = tile.T
        copies.append(pltpu.make_async_copy(result.at[node], out.at[node], sems.at[1 + node]))
        copies[-1].start()
    copy.wait()
    row = lax.broadcasted_iota(jnp.int32, near.shape, 0)
    first = lax.axis_index("pcol") // 2 == 0
    pair = (jnp.where(first, near[...], far[...]), jnp.where(first, far[...], near[...]))
    for s, value in enumerate(pair):
        block[:, s, :] = jnp.where(row < live[s], value, jnp.zeros(value.shape, value.dtype))
    copies.append(pltpu.make_async_copy(block, rows_out.at[0], sems.at[3]))
    copies[-1].start()
    for copy in copies:
        copy.wait()


def square(sigma_rows, panel, live_block_rows, inv_diag, quad_weight):
    height, count, width = panel.shape[1:]
    grid = lax.axis_size("pcol")
    points = lax.axis_size("hyp")
    f32, bf16 = jnp.float32, jnp.bfloat16
    shape = jax.ShapeDtypeStruct
    dma = pltpu.SemaphoreType.DMA
    stay = functools.partial(pltpu.with_memory_space_constraint, memory_space=pltpu.HBM)
    devices = points * 2 * 2 * grid
    live = live_block_rows[:, 0]

    def swap(x, point=0, side=0, core=0, column=0):
        mask = ((point * 2 + side) * 2 + core) * grid + column
        return lax.ppermute(x, AXES, [(i, i ^ mask) for i in range(devices)])

    extent = sigma_rows.shape[2]
    block = shape((height, width), bf16)
    cuts = (extent * 25 // 32, extent * 7 // 32)
    size = pl.cdiv(inv_diag.shape[2], ROWS) * ROWS
    own, give, own_inverse, *pieces = call(
        start_kernel,
        [block, shape((height + size, width), bf16), shape((size, width), bf16)]
        + [shape((lines, extent), bf16) for lines in cuts],
        [HBM] * 4,
        *map(stay, (live, panel, inv_diag, sigma_rows)),
        scratch=[pltpu.SMEM(live.shape, jnp.int32)]
        + [pltpu.VMEM(x.shape, bf16) for x in (panel, inv_diag, sigma_rows)]
        + [dma((4,))],
    )
    got = swap(give, side=1)
    got, got_inverse = got[:height], got[height:]
    blocks = []
    for start in (own, got):
        pair = jnp.stack([start, swap(start, column=2)])
        blocks += [pair, swap(pair, column=1)]
    far = [swap(piece, side=1) for piece in pieces]

    pack = shape((extent + 2 * size, width), bf16)
    rows, pack = call(
        gather_kernel, [shape((2, extent, width), bf16), pack], [VMEM] * (2 + len(blocks)),
        *blocks, own_inverse, got_inverse,
    )
    got_pack = swap(pack, core=1)
    mine = call(
        apply_kernel, shape((extent, width), f32), [VMEM] * (1 + 2 * len(cuts)), rows, *pieces, *far
    )
    other = swap(mine, core=1)

    lines = len(tiles(width)) // 2 * LANES
    part = shape((lines // 2, LANES), f32)
    out_near, out_far, keep, send = call(
        couple_kernel, [block, block, part, part], [SMEM] + [VMEM] * 4,
        quad_weight, mine, other, pack, got_pack,
        scratch=[pltpu.VMEM((extent, width), bf16), pltpu.VMEM((lines, LANES), f32)],
    )
    came = swap(send, point=1)

    def deliver(x, flip):
        pairs = []
        for i in range(devices):
            h, s, k, c = i // (4 * grid), i // (2 * grid) % 2, i // grid % 2, i % grid
            pairs.append((i, (h * 4 + c) * grid + 2 * (s ^ flip) + k))
        return lax.ppermute(x, AXES, pairs)

    near, far = deliver(out_near, 0), deliver(out_far, 1)
    add = functools.partial(call, add_kernel, part, [VMEM] * 2)
    total = add(keep, came)
    total = add(total, swap(total, column=1), after=[near, far])
    total = add(total, swap(total, column=2))
    quarters = [total, swap(total, side=1), swap(total, point=1), swap(total, side=1, point=1)]
    quarters += [swap(x, core=1) for x in quarters]
    return call(
        finish_kernel,
        [shape((1, height, count, width), bf16), shape((count, width, width), f32)],
        [VMEM] * 8 + [HBM] + [VMEM] * 2,
        *quarters, live, near, far,
        scratch=[
            pltpu.SMEM((2,), jnp.int32),
            pltpu.VMEM((height, count, width), bf16),
            pltpu.VMEM((count, 2 * lines, LANES), f32),
            pltpu.VMEM((count, width, width), f32),
            dma((4,)),
        ],
        out_specs=[HBM, HBM],
    )


def solution(mesh):
    sizes = dict(mesh.shape)
    prow, pcol = ("prow",), ("pcol",)

    def on_device(sigma_rows, panel, live_block_rows, inv_diag, quad_weight):
        body = square if split else general
        return body(sigma_rows, panel, live_block_rows, inv_diag, quad_weight)

    split = sizes["hyp"] == 2 and sizes["pcol"] == 4 and sizes["prow"] == 4
    if split:
        prow = ("side", "core")
        mesh = jax.sharding.Mesh(
            mesh.devices.reshape(sizes["hyp"], 2, 2, sizes["pcol"]),
            ("hyp", "side", "core", "pcol"),
        )
    in_specs = (
        P("hyp", prow, pcol),
        P("hyp", prow + pcol, None, None),
        P(None, prow + pcol),
        P("hyp", None, prow + pcol, None),
        P("hyp"),
    )
    out_specs = (P("hyp", prow + pcol, None, None), P())
    return jax.shard_map(
        on_device, mesh=mesh, in_specs=in_specs, out_specs=out_specs, check_vma=False
    )
```

```python
import functools

import jax
import jax.numpy as jnp
from jax import lax
from jax.experimental import pallas as pl
from jax.experimental.pallas import tpu as pltpu
from jax.sharding import PartitionSpec as P

LANES = 128
ROWS = 16
VMEM = pl.BlockSpec(memory_space=pltpu.VMEM)
SMEM = pl.BlockSpec(memory_space=pltpu.SMEM)
ANY = pl.BlockSpec(memory_space=pl.ANY)
HBM = pl.BlockSpec(memory_space=pltpu.HBM)
AXES = ("hyp", "side", "core", "pcol")


def call(kernel, outs, specs, *operands, scratch=(), out_specs=None, after=(), alias={}):
    many = isinstance(outs, (list, tuple))
    count = len(specs)

    def body(*refs):
        kernel(*refs[:count], *refs[count + len(after) :])

    if out_specs is None:
        out_specs = [VMEM] * len(outs) if many else VMEM
    return pl.pallas_call(
        body,
        out_shape=outs,
        in_specs=list(specs) + [ANY] * len(after),
        out_specs=out_specs,
        scratch_shapes=scratch,
        input_output_aliases=alias,
        compiler_params=pltpu.CompilerParams(vmem_limit_bytes=32 * 2**20),
    )(*operands, *after)


def transposed_dot(left, right):
    return lax.dot_general(
        left, right, (((0,), (0,)), ((), ())), preferred_element_type=jnp.float32
    )


def tiles(width):
    count = width // LANES
    return [(a, b) for a in range(count) for b in range(a, count)]


def general(sigma_rows, panel, live_block_rows, inv_diag, quad_weight):
    height, count, width = panel.shape[1:]
    offsets = lax.broadcasted_iota(jnp.int32, (height, count), 0)
    active = offsets < live_block_rows[:, 0][None, :]
    masked = jnp.where(active[:, :, None], panel[0], jnp.zeros_like(panel[0]))
    extent = height * lax.axis_size("prow")
    gathered = lax.all_gather(masked, ("prow", "pcol"), axis=0, tiled=True)
    start = lax.axis_index("pcol") * sigma_rows.shape[2]
    column_panel = lax.dynamic_slice_in_dim(gathered, start, sigma_rows.shape[2], 0)
    applied = lax.psum_scatter(
        jnp.dot(
            sigma_rows[0],
            column_panel.reshape(sigma_rows.shape[2], count * width),
            preferred_element_type=jnp.float32,
        ),
        "pcol",
        scatter_dimension=0,
        tiled=True,
    ).reshape(height, count, width)
    half = applied.astype(jnp.bfloat16)
    sigma_panel = jnp.where(active[:, :, None], -half, jnp.zeros_like(half))[None]
    coupling = jnp.einsum(
        "vwg,vwe->wge",
        masked.astype(jnp.float32),
        applied,
        precision=lax.Precision.HIGHEST,
    )
    diagonal = jnp.einsum(
        "skp,skq->spq", inv_diag[0], inv_diag[0], preferred_element_type=jnp.float32
    )
    marginal = lax.psum(quad_weight[0] * (coupling + diagonal), ("hyp", "prow", "pcol"))
    return sigma_panel, marginal


def start_kernel(*refs):
    sources, (own, give, own_inverse), buffers, sems = refs[:3], refs[3:6], refs[6:9], refs[9]
    copies = [
        pltpu.make_async_copy(source, buffer, sems.at[index])
        for index, (source, buffer) in enumerate(zip(sources, buffers))
    ]
    for copy in copies:
        copy.start()
    for copy in copies:
        copy.wait()
    live, panel, inverse = buffers
    first = lax.axis_index("side") == 0
    row = lax.broadcasted_iota(jnp.int32, own.shape, 0)
    rows = panel[0]
    zero = jnp.zeros(own.shape, own.dtype)
    one, two = (jnp.where(row < live[s], rows[:, s, :], zero) for s in range(2))
    height = own.shape[0]
    own[...] = jnp.where(first, one, two)
    give[:height] = jnp.where(first, two, one)
    spare = jnp.zeros((own_inverse.shape[0] - inverse.shape[2], own.shape[1]), own.dtype)
    one, two = (jnp.concatenate([inverse[0, s], spare], 0) for s in range(2))
    own_inverse[...] = jnp.where(first, one, two)
    give[height:] = jnp.where(first, two, one)


def flip_kernel(source, *refs):
    pieces, matrix, sem = refs[:-2], refs[-2], refs[-1]
    copy = pltpu.make_async_copy(source, matrix, sem)
    copy.start()
    copy.wait()
    at = 0
    for piece in pieces:
        piece[...] = matrix[0, :, at : at + piece.shape[0]].T
        at += piece.shape[0]


def hold_kernel(value, out):
    del value, out


def gather_kernel(*refs):
    blocks, (own_inverse, got_inverse, rows, pack) = [], refs[-4:]
    for ref in refs[:-4]:
        blocks += [ref] if len(ref.shape) == 2 else [ref.at[0], ref.at[1]]
    column = lax.axis_index("pcol")
    height = blocks[0].shape[0]
    for index, block in enumerate(blocks):
        spot = jnp.bitwise_xor(column, (0, 2, 1, 3)[index % 4])
        rows[index // 4, pl.ds(pl.multiple_of(spot * height, height), height), :] = block[...]
    extent = rows.shape[1]
    size = own_inverse.shape[0]
    pack[:extent] = rows[jnp.where(column // 2 == lax.axis_index("side"), 0, 1)]
    pack[extent : extent + size] = own_inverse[...]
    pack[extent + size :] = got_inverse[...]


def apply_kernel(rows, *refs):
    pieces, applied = refs[:-1], refs[-1]
    count = len(pieces) // 2
    at = 0
    for own, far in zip(pieces[:count], pieces[count:]):
        total = jnp.dot(own[...], rows[0], preferred_element_type=jnp.float32)
        total += jnp.dot(far[...], rows[1], preferred_element_type=jnp.float32)
        applied[at : at + own.shape[0]] = total
        at += own.shape[0]


def couple_kernel(weight, mine, other, pack, got_pack, out_a, out_b, keep, send, half, packed):
    core, column, point = (lax.axis_index(name) for name in ("core", "pcol", "hyp"))
    applied = mine[...] + other[...]
    high = applied.astype(jnp.bfloat16)
    low = (applied - high.astype(jnp.float32)).astype(jnp.bfloat16)
    half[...] = -high
    extent = applied.shape[0]
    rows = jnp.where(column % 2 == core, pack[:extent], got_pack[:extent])
    inverse = (pack[extent:], got_pack[extent:])
    blocks = tiles(applied.shape[1])
    per = len(blocks) // 2
    for part in range(2):

        @pl.when(core == part)
        def _():
            mine_blocks = blocks[part * per : (part + 1) * per]
            at = 0
            for first in sorted({a for a, _ in mine_blocks}):
                seconds = [b for a, b in mine_blocks if a == first]
                left = slice(first * LANES, (first + 1) * LANES)
                right = slice(seconds[0] * LANES, (seconds[-1] + 1) * LANES)
                total = transposed_dot(rows[:, left], high[:, right])
                total += transposed_dot(rows[:, left], low[:, right])
                for lines in inverse:
                    total += transposed_dot(lines[:, left], lines[:, right])
                for index in range(len(seconds)):
                    packed[at * LANES : (at + 1) * LANES, :] = (
                        weight[0] * total[:, index * LANES : (index + 1) * LANES]
                    )
                    at += 1

    size = keep.shape[0]
    keep[...] = packed[pl.ds(pl.multiple_of(point * size, 8), size), :]
    send[...] = packed[pl.ds(pl.multiple_of((1 - point) * size, 8), size), :]
    height = out_a.shape[0]
    even = column % 2 == core
    for out, steps in ((out_a, (2, 1)), (out_b, (0, 3))):
        spot = jnp.bitwise_xor(column, jnp.where(even, steps[0], steps[1]))
        out[...] = half[pl.ds(pl.multiple_of(spot * height, height), height), :]


def add_kernel(mine, came, out):
    out[...] = mine[...] + came[...]


def spread(parts, out, lines, result, sems, owner):
    point, side = lax.axis_index("hyp"), lax.axis_index("side")
    size = parts[0].shape[0]
    for index, part in enumerate(parts):
        node = 1 - side if index % 2 else side
        slot = 1 - point if index // 2 else point
        lines[node, pl.ds(pl.multiple_of(slot * size, 8), size), :] = part[...]
    blocks = tiles(result.shape[1])
    per = len(blocks) // 2
    for core in range(2):

        @pl.when(owner == core)
        def _():
            copies = []
            for node in range(2):
                for index, (a, b) in enumerate(blocks[core * per : (core + 1) * per]):
                    rows, columns = (slice(i * LANES, (i + 1) * LANES) for i in (a, b))
                    tile = lines[node, index * LANES : (index + 1) * LANES, :]
                    result[node, rows, columns] = tile
                    if a != b:
                        result[node, columns, rows] = tile.T
                first, rest = slice(0, LANES), slice(LANES, None)
                for index, area in enumerate([(first, slice(None)), (rest, first)] if core == 0 else [(rest, rest)]):
                    place = (node, *area)
                    copy = pltpu.make_async_copy(result.at[place], out.at[place], sems.at[2 * node + index])
                    copy.start()
                    copies.append(copy)
            for copy in copies:
                copy.wait()


def early_kernel(*refs):
    parts, (live_hbm, mine, theirs, rows_out, out, live, block, lines, result, sems) = refs[:4], refs[4:]
    load = pltpu.make_async_copy(live_hbm, live, sems.at[4])
    load.start()
    load.wait()
    row = lax.broadcasted_iota(jnp.int32, mine.shape, 0)
    first = lax.axis_index("side") == 0
    pair = (jnp.where(first, mine[...], theirs[...]), jnp.where(first, theirs[...], mine[...]))
    for s, value in enumerate(pair):
        block[:, s, :] = jnp.where(row < live[s], value, jnp.zeros(value.shape, value.dtype))
    store = pltpu.make_async_copy(block, rows_out.at[0], sems.at[5])
    store.start()
    spread(parts, out, lines, result, sems, lax.axis_index("core"))
    store.wait()


def late_kernel(*refs):
    parts, (before, out, lines, result, sems) = refs[:4], refs[4:]
    del before
    spread(parts, out, lines, result, sems, 1 - lax.axis_index("core"))


def square(sigma_rows, panel, live_block_rows, inv_diag, quad_weight):
    height, count, width = panel.shape[1:]
    grid = lax.axis_size("pcol")
    points = lax.axis_size("hyp")
    f32, bf16 = jnp.float32, jnp.bfloat16
    shape = jax.ShapeDtypeStruct
    dma = pltpu.SemaphoreType.DMA
    stay = functools.partial(pltpu.with_memory_space_constraint, memory_space=pltpu.HBM)
    devices = points * 2 * 2 * grid
    live = live_block_rows[:, 0]

    def swap(x, point=0, side=0, core=0, column=0):
        mask = ((point * 2 + side) * 2 + core) * grid + column
        return lax.ppermute(x, AXES, [(i, i ^ mask) for i in range(devices)])

    extent = sigma_rows.shape[2]
    block = shape((height, width), bf16)
    cuts = (extent // 2, extent // 2)
    size = pl.cdiv(inv_diag.shape[2], ROWS) * ROWS
    own, give, own_inverse = call(
        start_kernel,
        [block, shape((height + size, width), bf16), shape((size, width), bf16)],
        [HBM] * 3,
        *map(stay, (live, panel, inv_diag)),
        scratch=[pltpu.SMEM(live.shape, jnp.int32)]
        + [pltpu.VMEM(x.shape, bf16) for x in (panel, inv_diag)]
        + [dma((3,))],
    )
    pieces = call(
        flip_kernel,
        [shape((lines, extent), bf16) for lines in cuts],
        [HBM],
        stay(sigma_rows),
        scratch=[pltpu.VMEM(sigma_rows.shape, bf16), dma(())],
        after=[own],
    )
    got = swap(give, side=1)
    got, got_inverse = got[:height], got[height:]
    def hold(x, *after):
        return call(hold_kernel, shape(x.shape, x.dtype), [ANY], x, out_specs=ANY, after=after, alias={0: 0})

    own_two, got_two = swap(own, column=2), swap(got, column=2)
    own_one = swap(own, column=1)
    own_three = swap(hold(own_two, own_one), column=1)
    blocks = [own, own_two, own_one, own_three]
    blocks += [got, got_two, swap(got, column=1), swap(hold(got_two, own_three), column=1)]
    far = [swap(piece, side=1) for piece in pieces]

    pack = shape((extent + 2 * size, width), bf16)
    rows, pack = call(
        gather_kernel, [shape((2, extent, width), bf16), pack], [VMEM] * (2 + len(blocks)),
        *blocks, own_inverse, got_inverse,
    )
    got_pack = swap(pack, core=1)
    mine = call(
        apply_kernel, shape((extent, width), f32), [VMEM] * (1 + 2 * len(cuts)), rows, *pieces, *far
    )
    other = swap(mine, core=1)

    lines = len(tiles(width)) // 2 * LANES
    part = shape((lines // 2, LANES), f32)
    out_a, out_b, keep, send = call(
        couple_kernel, [block, block, part, part], [SMEM] + [VMEM] * 4,
        quad_weight, mine, other, pack, got_pack,
        scratch=[pltpu.VMEM((extent, width), bf16), pltpu.VMEM((lines, LANES), f32)],
    )
    came = swap(send, point=1)

    def cross(x, even, odd):
        pairs = []
        for i in range(devices):
            head, k, c = i // (2 * grid), i // grid % 2, i % grid
            flip, step = even if k == c % 2 else odd
            pairs.append((i, (head * 2 + (k ^ flip)) * grid + (c ^ step)))
        return lax.ppermute(x, AXES, pairs)

    land_a = cross(out_a, (0, 2), (1, 1))
    land_b = cross(out_b, (0, 0), (1, 3))
    add = functools.partial(call, add_kernel, part, [VMEM] * 2)
    total = add(keep, came)
    total = add(total, swap(total, column=2))
    total = add(total, swap(total, column=1), after=[land_a, land_b])
    quarters = [total, swap(total, side=1), swap(total, point=1), swap(total, side=1, point=1)]
    other_quarters = [swap(x, core=1) for x in quarters]

    side, core, column = (lax.axis_index(name) for name in AXES[1:])
    from_a = jnp.where(column % 2 == core, 1 - column // 2, column // 2)
    mine = jnp.where(from_a == side, land_a, land_b)
    theirs = swap(jnp.where(from_a == side, land_b, land_a), side=1)

    square_shape = shape((count, width, width), f32)
    spread_scratch = [pltpu.VMEM((count, lines, LANES), f32), pltpu.VMEM((count, width, width), f32), dma((6,))]
    sigma_panel, marginal = call(
        early_kernel,
        [shape((1, height, count, width), bf16), square_shape],
        [VMEM] * 4 + [HBM] + [VMEM] * 2,
        *quarters, live, mine, theirs,
        scratch=[pltpu.SMEM(live.shape, jnp.int32), pltpu.VMEM((height, count, width), bf16)] + spread_scratch,
        out_specs=[HBM, HBM],
    )
    marginal = call(
        late_kernel, square_shape, [VMEM] * 4 + [HBM], *other_quarters, marginal,
        scratch=spread_scratch, out_specs=HBM, alias={4: 0},
    )
    return sigma_panel, marginal


def solution(mesh):
    sizes = dict(mesh.shape)
    prow, pcol = ("prow",), ("pcol",)

    def on_device(sigma_rows, panel, live_block_rows, inv_diag, quad_weight):
        body = square if split else general
        return body(sigma_rows, panel, live_block_rows, inv_diag, quad_weight)

    split = sizes["hyp"] == 2 and sizes["pcol"] == 4 and sizes["prow"] == 4
    if split:
        prow = ("side", "core")
        mesh = jax.sharding.Mesh(
            mesh.devices.reshape(sizes["hyp"], 2, 2, sizes["pcol"]),
            ("hyp", "side", "core", "pcol"),
        )
    in_specs = (
        P("hyp", prow, pcol),
        P("hyp", prow + pcol, None, None),
        P(None, prow + pcol),
        P("hyp", None, prow + pcol, None),
        P("hyp"),
    )
    out_specs = (P("hyp", prow + pcol, None, None), P())
    return jax.shard_map(
        on_device, mesh=mesh, in_specs=in_specs, out_specs=out_specs, check_vma=False
    )
```

```python
import functools

import jax
import jax.numpy as jnp
from jax import lax
from jax.experimental import pallas as pl
from jax.experimental.pallas import tpu as pltpu
from jax.sharding import PartitionSpec as P

LANES = 128
ROWS = 16
VMEM = pl.BlockSpec(memory_space=pltpu.VMEM)
SMEM = pl.BlockSpec(memory_space=pltpu.SMEM)
ANY = pl.BlockSpec(memory_space=pl.ANY)
HBM = pl.BlockSpec(memory_space=pltpu.HBM)
AXES = ("hyp", "side", "core", "pcol")


def call(kernel, outs, specs, *operands, scratch=(), out_specs=None, after=(), alias={}):
    many = isinstance(outs, (list, tuple))
    count = len(specs)

    def body(*refs):
        kernel(*refs[:count], *refs[count + len(after) :])

    if out_specs is None:
        out_specs = [VMEM] * len(outs) if many else VMEM
    return pl.pallas_call(
        body,
        out_shape=outs,
        in_specs=list(specs) + [ANY] * len(after),
        out_specs=out_specs,
        scratch_shapes=scratch,
        input_output_aliases=alias,
        compiler_params=pltpu.CompilerParams(vmem_limit_bytes=32 * 2**20),
    )(*operands, *after)


def transposed_dot(left, right):
    return lax.dot_general(
        left, right, (((0,), (0,)), ((), ())), preferred_element_type=jnp.float32
    )


def tiles(width):
    count = width // LANES
    return [(a, b) for a in range(count) for b in range(a, count)]


def general(sigma_rows, panel, live_block_rows, inv_diag, quad_weight):
    height, count, width = panel.shape[1:]
    offsets = lax.broadcasted_iota(jnp.int32, (height, count), 0)
    active = offsets < live_block_rows[:, 0][None, :]
    masked = jnp.where(active[:, :, None], panel[0], jnp.zeros_like(panel[0]))
    extent = height * lax.axis_size("prow")
    gathered = lax.all_gather(masked, ("prow", "pcol"), axis=0, tiled=True)
    start = lax.axis_index("pcol") * sigma_rows.shape[2]
    column_panel = lax.dynamic_slice_in_dim(gathered, start, sigma_rows.shape[2], 0)
    applied = lax.psum_scatter(
        jnp.dot(
            sigma_rows[0],
            column_panel.reshape(sigma_rows.shape[2], count * width),
            preferred_element_type=jnp.float32,
        ),
        "pcol",
        scatter_dimension=0,
        tiled=True,
    ).reshape(height, count, width)
    half = applied.astype(jnp.bfloat16)
    sigma_panel = jnp.where(active[:, :, None], -half, jnp.zeros_like(half))[None]
    coupling = jnp.einsum(
        "vwg,vwe->wge",
        masked.astype(jnp.float32),
        applied,
        precision=lax.Precision.HIGHEST,
    )
    diagonal = jnp.einsum(
        "skp,skq->spq", inv_diag[0], inv_diag[0], preferred_element_type=jnp.float32
    )
    marginal = lax.psum(quad_weight[0] * (coupling + diagonal), ("hyp", "prow", "pcol"))
    return sigma_panel, marginal


def start_kernel(*refs):
    sources, (own, give, own_inverse), buffers, sems = refs[:3], refs[3:6], refs[6:9], refs[9]
    copies = [
        pltpu.make_async_copy(source, buffer, sems.at[index])
        for index, (source, buffer) in enumerate(zip(sources, buffers))
    ]
    for copy in copies:
        copy.start()
    for copy in copies:
        copy.wait()
    live, panel, inverse = buffers
    first = lax.axis_index("side") == 0
    row = lax.broadcasted_iota(jnp.int32, own.shape, 0)
    rows = panel[0]
    zero = jnp.zeros(own.shape, own.dtype)
    one, two = (jnp.where(row < live[s], rows[:, s, :], zero) for s in range(2))
    height = own.shape[0]
    own[...] = jnp.where(first, one, two)
    give[:height] = jnp.where(first, two, one)
    spare = jnp.zeros((own_inverse.shape[0] - inverse.shape[2], own.shape[1]), own.dtype)
    one, two = (jnp.concatenate([inverse[0, s], spare], 0) for s in range(2))
    own_inverse[...] = jnp.where(first, one, two)
    give[height:] = jnp.where(first, two, one)


def flip_kernel(source, *refs):
    pieces, matrix, sem = refs[:-2], refs[-2], refs[-1]
    copy = pltpu.make_async_copy(source, matrix, sem)
    copy.start()
    copy.wait()
    at = 0
    for piece in pieces:
        piece[...] = matrix[0, :, at : at + piece.shape[0]].T
        at += piece.shape[0]


def gather_kernel(*refs):
    blocks, (own_inverse, got_inverse, rows, pack) = [], refs[-4:]
    for ref in refs[:-4]:
        blocks += [ref] if len(ref.shape) == 2 else [ref.at[0], ref.at[1]]
    column = lax.axis_index("pcol")
    height = blocks[0].shape[0]
    for index, block in enumerate(blocks):
        spot = jnp.bitwise_xor(column, (0, 2, 1, 3)[index % 4])
        rows[index // 4, pl.ds(pl.multiple_of(spot * height, height), height), :] = block[...]
    extent = rows.shape[1]
    size = own_inverse.shape[0]
    pack[:extent] = rows[jnp.where(column // 2 == lax.axis_index("side"), 0, 1)]
    pack[extent : extent + size] = own_inverse[...]
    pack[extent + size :] = got_inverse[...]


def apply_kernel(rows, *refs):
    pieces, applied = refs[:-1], refs[-1]
    count = len(pieces) // 2
    at = 0
    for own, far in zip(pieces[:count], pieces[count:]):
        total = jnp.dot(own[...], rows[0], preferred_element_type=jnp.float32)
        total += jnp.dot(far[...], rows[1], preferred_element_type=jnp.float32)
        applied[at : at + own.shape[0]] = total
        at += own.shape[0]


def couple_kernel(weight, mine, other, pack, got_pack, out_near, out_far, keep, send, half, packed):
    core, column, point = (lax.axis_index(name) for name in ("core", "pcol", "hyp"))
    applied = mine[...] + other[...]
    high = applied.astype(jnp.bfloat16)
    low = (applied - high.astype(jnp.float32)).astype(jnp.bfloat16)
    half[...] = -high
    extent = applied.shape[0]
    rows = jnp.where(column % 2 == core, pack[:extent], got_pack[:extent])
    inverse = (pack[extent:], got_pack[extent:])
    blocks = tiles(applied.shape[1])
    per = len(blocks) // 2
    for part in range(2):

        @pl.when(core == part)
        def _():
            mine_blocks = blocks[part * per : (part + 1) * per]
            at = 0
            for first in sorted({a for a, _ in mine_blocks}):
                seconds = [b for a, b in mine_blocks if a == first]
                left = slice(first * LANES, (first + 1) * LANES)
                right = slice(seconds[0] * LANES, (seconds[-1] + 1) * LANES)
                total = transposed_dot(rows[:, left], high[:, right])
                total += transposed_dot(rows[:, left], low[:, right])
                for lines in inverse:
                    total += transposed_dot(lines[:, left], lines[:, right])
                for index in range(len(seconds)):
                    packed[at * LANES : (at + 1) * LANES, :] = (
                        weight[0] * total[:, index * LANES : (index + 1) * LANES]
                    )
                    at += 1

    size = keep.shape[0]
    keep[...] = packed[pl.ds(pl.multiple_of(point * size, 8), size), :]
    send[...] = packed[pl.ds(pl.multiple_of((1 - point) * size, 8), size), :]
    height = out_near.shape[0]
    side = lax.axis_index("side")
    for out, at in ((out_near, side), (out_far, 1 - side)):
        spot = at * 2 + core
        out[...] = half[pl.ds(pl.multiple_of(spot * height, height), height), :]


def add_kernel(mine, came, out):
    out[...] = mine[...] + came[...]


def finish_kernel(*refs):
    parts, (live_hbm, near, far, rows_out, out, live, block, lines, result, sems) = refs[:8], refs[8:]
    point, side, core = (lax.axis_index(name) for name in ("hyp", "side", "core"))
    copy = pltpu.make_async_copy(live_hbm, live, sems.at[0])
    copy.start()
    width = result.shape[1]
    blocks = tiles(width)
    size = parts[0].shape[0]
    for index, part in enumerate(parts):
        owner = core if index < 4 else 1 - core
        node = 1 - side if index % 2 else side
        slot = 1 - point if index // 2 % 2 else point
        start = pl.multiple_of((owner * 2 + slot) * size, 8)
        lines[node, pl.ds(start, size), :] = part[...]
    copies = []
    for node in range(2):
        for index, (a, b) in enumerate(blocks):
            tile = lines[node, index * LANES : (index + 1) * LANES, :]
            result[node, a * LANES : (a + 1) * LANES, b * LANES : (b + 1) * LANES] = tile
            if a != b:
                result[node, b * LANES : (b + 1) * LANES, a * LANES : (a + 1) * LANES] = tile.T
        copies.append(pltpu.make_async_copy(result.at[node], out.at[node], sems.at[1 + node]))
        copies[-1].start()
    copy.wait()
    row = lax.broadcasted_iota(jnp.int32, near.shape, 0)
    first = lax.axis_index("pcol") // 2 == 0
    pair = (jnp.where(first, near[...], far[...]), jnp.where(first, far[...], near[...]))
    for s, value in enumerate(pair):
        block[:, s, :] = jnp.where(row < live[s], value, jnp.zeros(value.shape, value.dtype))
    copies.append(pltpu.make_async_copy(block, rows_out.at[0], sems.at[3]))
    copies[-1].start()
    for copy in copies:
        copy.wait()


def square(sigma_rows, panel, live_block_rows, inv_diag, quad_weight):
    height, count, width = panel.shape[1:]
    grid = lax.axis_size("pcol")
    points = lax.axis_size("hyp")
    f32, bf16 = jnp.float32, jnp.bfloat16
    shape = jax.ShapeDtypeStruct
    dma = pltpu.SemaphoreType.DMA
    stay = functools.partial(pltpu.with_memory_space_constraint, memory_space=pltpu.HBM)
    devices = points * 2 * 2 * grid
    live = live_block_rows[:, 0]

    def swap(x, point=0, side=0, core=0, column=0):
        mask = ((point * 2 + side) * 2 + core) * grid + column
        return lax.ppermute(x, AXES, [(i, i ^ mask) for i in range(devices)])

    extent = sigma_rows.shape[2]
    block = shape((height, width), bf16)
    cuts = (extent // 2, extent * 3 // 8, extent // 8)
    size = pl.cdiv(inv_diag.shape[2], ROWS) * ROWS
    own, give, own_inverse = call(
        start_kernel,
        [block, shape((height + size, width), bf16), shape((size, width), bf16)],
        [HBM] * 3,
        *map(stay, (live, panel, inv_diag)),
        scratch=[pltpu.SMEM(live.shape, jnp.int32)]
        + [pltpu.VMEM(x.shape, bf16) for x in (panel, inv_diag)]
        + [dma((3,))],
    )
    pieces = call(
        flip_kernel,
        [shape((lines, extent), bf16) for lines in cuts],
        [HBM],
        stay(sigma_rows),
        scratch=[pltpu.VMEM(sigma_rows.shape, bf16), dma(())],
        after=[own],
    )
    got = swap(give, side=1)
    got, got_inverse = got[:height], got[height:]
    blocks = []
    for one in (own, got):
        two = swap(one, column=2)
        blocks += [one, two, swap(one, column=1), swap(two, column=1)]
    far = [swap(piece, side=1) for piece in pieces]

    pack = shape((extent + 2 * size, width), bf16)
    rows, pack = call(
        gather_kernel, [shape((2, extent, width), bf16), pack], [VMEM] * (2 + len(blocks)),
        *blocks, own_inverse, got_inverse,
    )
    got_pack = swap(pack, core=1)
    mine = call(
        apply_kernel, shape((extent, width), f32), [VMEM] * (1 + 2 * len(cuts)), rows, *pieces, *far
    )
    other = swap(mine, core=1)

    lines = len(tiles(width)) // 2 * LANES
    part = shape((lines // 2, LANES), f32)
    out_near, out_far, keep, send = call(
        couple_kernel, [block, block, part, part], [SMEM] + [VMEM] * 4,
        quad_weight, mine, other, pack, got_pack,
        scratch=[pltpu.VMEM((extent, width), bf16), pltpu.VMEM((lines, LANES), f32)],
    )
    came = swap(send, point=1)

    def deliver(x, flip):
        pairs = []
        for i in range(devices):
            h, s, k, c = i // (4 * grid), i // (2 * grid) % 2, i // grid % 2, i % grid
            pairs.append((i, (h * 4 + c) * grid + 2 * (s ^ flip) + k))
        return lax.ppermute(x, AXES, pairs)

    near, far = deliver(out_near, 0), deliver(out_far, 1)
    add = functools.partial(call, add_kernel, part, [VMEM] * 2)
    total = add(keep, came)
    total = add(total, swap(total, column=2))
    total = add(total, swap(total, column=1), after=[near, far])
    quarters = [total, swap(total, side=1), swap(total, point=1), swap(total, side=1, point=1)]
    quarters += [swap(x, core=1) for x in quarters]
    return call(
        finish_kernel,
        [shape((1, height, count, width), bf16), shape((count, width, width), f32)],
        [VMEM] * 8 + [HBM] + [VMEM] * 2,
        *quarters, live, near, far,
        scratch=[
            pltpu.SMEM((2,), jnp.int32),
            pltpu.VMEM((height, count, width), bf16),
            pltpu.VMEM((count, 2 * lines, LANES), f32),
            pltpu.VMEM((count, width, width), f32),
            dma((4,)),
        ],
        out_specs=[HBM, HBM],
    )


def solution(mesh):
    sizes = dict(mesh.shape)
    prow, pcol = ("prow",), ("pcol",)

    def on_device(sigma_rows, panel, live_block_rows, inv_diag, quad_weight):
        body = square if split else general
        return body(sigma_rows, panel, live_block_rows, inv_diag, quad_weight)

    split = sizes["hyp"] == 2 and sizes["pcol"] == 4 and sizes["prow"] == 4
    if split:
        prow = ("side", "core")
        mesh = jax.sharding.Mesh(
            mesh.devices.reshape(sizes["hyp"], 2, 2, sizes["pcol"]),
            ("hyp", "side", "core", "pcol"),
        )
    in_specs = (
        P("hyp", prow, pcol),
        P("hyp", prow + pcol, None, None),
        P(None, prow + pcol),
        P("hyp", None, prow + pcol, None),
        P("hyp"),
    )
    out_specs = (P("hyp", prow + pcol, None, None), P())
    return jax.shard_map(
        on_device, mesh=mesh, in_specs=in_specs, out_specs=out_specs, check_vma=False
    )
```

```python
import functools

import jax
import jax.numpy as jnp
from jax import lax
from jax.experimental import pallas as pl
from jax.experimental.pallas import tpu as pltpu
from jax.sharding import PartitionSpec as P

LANES = 128
ROWS = 16
VMEM = pl.BlockSpec(memory_space=pltpu.VMEM)
SMEM = pl.BlockSpec(memory_space=pltpu.SMEM)
ANY = pl.BlockSpec(memory_space=pl.ANY)
HBM = pl.BlockSpec(memory_space=pltpu.HBM)
AXES = ("hyp", "side", "core", "pcol")


def call(kernel, outs, specs, *operands, scratch=(), out_specs=None, after=()):
    many = isinstance(outs, (list, tuple))
    count = len(specs)

    def body(*refs):
        kernel(*refs[:count], *refs[count + len(after) :])

    if out_specs is None:
        out_specs = [VMEM] * len(outs) if many else VMEM
    return pl.pallas_call(
        body,
        out_shape=outs,
        in_specs=list(specs) + [ANY] * len(after),
        out_specs=out_specs,
        scratch_shapes=scratch,
        compiler_params=pltpu.CompilerParams(vmem_limit_bytes=32 * 2**20),
    )(*operands, *after)


def transposed_dot(left, right):
    return lax.dot_general(
        left, right, (((0,), (0,)), ((), ())), preferred_element_type=jnp.float32
    )


def tiles(width):
    count = width // LANES
    return [(a, b) for a in range(count) for b in range(a, count)]


def general(sigma_rows, panel, live_block_rows, inv_diag, quad_weight):
    height, count, width = panel.shape[1:]
    offsets = lax.broadcasted_iota(jnp.int32, (height, count), 0)
    active = offsets < live_block_rows[:, 0][None, :]
    masked = jnp.where(active[:, :, None], panel[0], jnp.zeros_like(panel[0]))
    extent = height * lax.axis_size("prow")
    gathered = lax.all_gather(masked, ("prow", "pcol"), axis=0, tiled=True)
    start = lax.axis_index("pcol") * sigma_rows.shape[2]
    column_panel = lax.dynamic_slice_in_dim(gathered, start, sigma_rows.shape[2], 0)
    applied = lax.psum_scatter(
        jnp.dot(
            sigma_rows[0],
            column_panel.reshape(sigma_rows.shape[2], count * width),
            preferred_element_type=jnp.float32,
        ),
        "pcol",
        scatter_dimension=0,
        tiled=True,
    ).reshape(height, count, width)
    half = applied.astype(jnp.bfloat16)
    sigma_panel = jnp.where(active[:, :, None], -half, jnp.zeros_like(half))[None]
    coupling = jnp.einsum(
        "vwg,vwe->wge",
        masked.astype(jnp.float32),
        applied,
        precision=lax.Precision.HIGHEST,
    )
    diagonal = jnp.einsum(
        "skp,skq->spq", inv_diag[0], inv_diag[0], preferred_element_type=jnp.float32
    )
    marginal = lax.psum(quad_weight[0] * (coupling + diagonal), ("hyp", "prow", "pcol"))
    return sigma_panel, marginal


def start_kernel(*refs):
    sources, (own, give, own_inverse), pieces = refs[:4], refs[4:7], refs[7:-5]
    buffers, sems = refs[-5:-1], refs[-1]
    copies = [
        pltpu.make_async_copy(source, buffer, sems.at[index])
        for index, (source, buffer) in enumerate(zip(sources, buffers))
    ]
    for copy in copies:
        copy.start()
    for copy in copies[:3]:
        copy.wait()
    live, panel, inverse, matrix = buffers
    first = lax.axis_index("side") == 0
    row = lax.broadcasted_iota(jnp.int32, own.shape, 0)
    rows = panel[0]
    zero = jnp.zeros(own.shape, own.dtype)
    one, two = (jnp.where(row < live[s], rows[:, s, :], zero) for s in range(2))
    height = own.shape[0]
    own[...] = jnp.where(first, one, two)
    give[:height] = jnp.where(first, two, one)
    spare = jnp.zeros((own_inverse.shape[0] - inverse.shape[2], own.shape[1]), own.dtype)
    one, two = (jnp.concatenate([inverse[0, s], spare], 0) for s in range(2))
    own_inverse[...] = jnp.where(first, one, two)
    give[height:] = jnp.where(first, two, one)
    copies[3].wait()
    at = 0
    for piece in pieces:
        piece[...] = matrix[0, :, at : at + piece.shape[0]].T
        at += piece.shape[0]


def gather_kernel(*refs):
    blocks, (rows, pack) = refs[:-2], refs[-2:]
    column = lax.axis_index("pcol")
    height = blocks[0].shape[0]
    for index, block in enumerate(blocks):
        spot = jnp.bitwise_xor(column, (0, 2, 1, 3)[index % 4])
        rows[index // 4, pl.ds(pl.multiple_of(spot * height, height), height), :] = block[...]
    pack[...] = rows[jnp.where(column // 2 == lax.axis_index("side"), 0, 1)]


def apply_kernel(rows, *refs):
    pieces, applied = refs[:-1], refs[-1]
    count = len(pieces) // 2
    at = 0
    for own, far in zip(pieces[:count], pieces[count:]):
        total = jnp.dot(own[...], rows[0], preferred_element_type=jnp.float32)
        total += jnp.dot(far[...], rows[1], preferred_element_type=jnp.float32)
        applied[at : at + own.shape[0]] = total
        at += own.shape[0]


def couple_kernel(weight, applied, pack, got_pack, own_inverse, got_inverse, keep, send, packed):
    core, column = lax.axis_index("core"), lax.axis_index("pcol")
    high = applied[...].astype(jnp.bfloat16)
    low = (applied[...] - high.astype(jnp.float32)).astype(jnp.bfloat16)
    rows = jnp.where(column % 2 == core, pack[...], got_pack[...])
    at = 0
    for first in range(rows.shape[1] // LANES):
        left, right = slice(first * LANES, (first + 1) * LANES), slice(first * LANES, None)
        total = transposed_dot(rows[:, left], high[:, right])
        total += transposed_dot(rows[:, left], low[:, right])
        for lines in (own_inverse, got_inverse):
            total += transposed_dot(lines[:, left], lines[:, right])
        for index in range(total.shape[1] // LANES):
            packed[at : at + LANES, :] = weight[0] * total[:, index * LANES : (index + 1) * LANES]
            at += LANES
    size = keep.shape[0]
    keep[...] = packed[pl.ds(pl.multiple_of(core * size, LANES), size), :]
    send[...] = packed[pl.ds(pl.multiple_of((1 - core) * size, LANES), size), :]


def halve_kernel(mine, came, keep, send, whole):
    whole[...] = mine[...] + came[...]
    size, point = keep.shape[0], lax.axis_index("hyp")
    keep[...] = whole[pl.ds(pl.multiple_of(point * size, 8), size), :]
    send[...] = whole[pl.ds(pl.multiple_of((1 - point) * size, 8), size), :]


def output_kernel(mine, other, out_near, out_far, half):
    half[...] = -(mine[...] + other[...]).astype(jnp.bfloat16)
    height, side, core = out_near.shape[0], lax.axis_index("side"), lax.axis_index("core")
    for out, at in ((out_near, side), (out_far, 1 - side)):
        spot = at * 2 + core
        out[...] = half[pl.ds(pl.multiple_of(spot * height, height), height), :]


def add_kernel(mine, came, out):
    out[...] = mine[...] + came[...]


def rows_kernel(live_hbm, near, far, out, live, sem):
    copy = pltpu.make_async_copy(live_hbm, live, sem)
    copy.start()
    row = lax.broadcasted_iota(jnp.int32, near.shape, 0)
    first = lax.axis_index("pcol") // 2 == 0
    pair = (jnp.where(first, near[...], far[...]), jnp.where(first, far[...], near[...]))
    copy.wait()
    for s, value in enumerate(pair):
        out[0, :, s, :] = jnp.where(row < live[s], value, jnp.zeros(value.shape, value.dtype))


def spread_kernel(*refs):
    parts, (out, lines, result, sems) = refs[:8], refs[8:]
    point, side, core = (lax.axis_index(name) for name in ("hyp", "side", "core"))
    blocks = tiles(result.shape[1])
    size = parts[0].shape[0]
    for index, part in enumerate(parts):
        owner = core if index < 4 else 1 - core
        node = 1 - side if index % 2 else side
        slot = 1 - point if index // 2 % 2 else point
        start = pl.multiple_of((owner * 2 + slot) * size, 8)
        lines[node, pl.ds(start, size), :] = part[...]
    copies = []
    for node in range(2):
        for first in range(result.shape[1] // LANES):
            rows = slice(first * LANES, (first + 1) * LANES)
            for index, (a, b) in enumerate(blocks):
                if a != first:
                    continue
                columns = slice(b * LANES, (b + 1) * LANES)
                tile = lines[node, index * LANES : (index + 1) * LANES, :]
                result[node, rows, columns] = tile
                if a != b:
                    result[node, columns, rows] = tile.T
            place = (node, rows)
            copies.append(pltpu.make_async_copy(result.at[place], out.at[place], sems.at[len(copies)]))
            copies[-1].start()
    for copy in copies:
        copy.wait()


def square(sigma_rows, panel, live_block_rows, inv_diag, quad_weight):
    height, count, width = panel.shape[1:]
    grid = lax.axis_size("pcol")
    points = lax.axis_size("hyp")
    f32, bf16 = jnp.float32, jnp.bfloat16
    shape = jax.ShapeDtypeStruct
    dma = pltpu.SemaphoreType.DMA
    stay = functools.partial(pltpu.with_memory_space_constraint, memory_space=pltpu.HBM)
    devices = points * 2 * 2 * grid
    live = live_block_rows[:, 0]

    def swap(x, point=0, side=0, core=0, column=0):
        mask = ((point * 2 + side) * 2 + core) * grid + column
        return lax.ppermute(x, AXES, [(i, i ^ mask) for i in range(devices)])

    extent = sigma_rows.shape[2]
    block = shape((height, width), bf16)
    cuts = (extent // 2, extent // 2)
    size = pl.cdiv(inv_diag.shape[2], ROWS) * ROWS
    own, give, own_inverse, *pieces = call(
        start_kernel,
        [block, shape((height + size, width), bf16), shape((size, width), bf16)]
        + [shape((lines, extent), bf16) for lines in cuts],
        [HBM] * 4,
        *map(stay, (live, panel, inv_diag, sigma_rows)),
        scratch=[pltpu.SMEM(live.shape, jnp.int32)]
        + [pltpu.VMEM(x.shape, bf16) for x in (panel, inv_diag, sigma_rows)]
        + [dma((4,))],
    )
    got = swap(give, side=1)
    got, got_inverse = got[:height], got[height:]
    blocks = []
    for one in (own, got):
        two = swap(one, column=2)
        blocks += [one, two, swap(one, column=1), swap(two, column=1)]
    far = [swap(piece, side=1) for piece in pieces]


    rows, pack = call(
        gather_kernel,
        [shape((2, extent, width), bf16), shape((extent, width), bf16)],
        [VMEM] * len(blocks),
        *blocks,
        after=far,
    )
    got_pack = swap(pack, core=1)
    mine = call(
        apply_kernel, shape((extent, width), f32), [VMEM] * (1 + 2 * len(cuts)), rows, *pieces, *far
    )
    lines = len(tiles(width)) // 2 * LANES
    part, half = shape((lines // 2, LANES), f32), shape((lines, LANES), f32)
    other = swap(mine, core=1)
    keep, send = call(
        couple_kernel, [half, half], [SMEM] + [VMEM] * 5,
        quad_weight, mine, pack, got_pack, own_inverse, got_inverse,
        scratch=[pltpu.VMEM((2 * lines, LANES), f32)],
    )
    keep, send = call(
        halve_kernel, [part, part], [VMEM] * 2, keep, swap(send, core=1),
        scratch=[pltpu.VMEM((lines, LANES), f32)],
    )
    came = swap(send, point=1)
    def deliver(x, flip):
        pairs = []
        for i in range(devices):
            h, s, k, c = i // (4 * grid), i // (2 * grid) % 2, i // grid % 2, i % grid
            pairs.append((i, (h * 4 + c) * grid + 2 * (s ^ flip) + k))
        return lax.ppermute(x, AXES, pairs)

    add = functools.partial(call, add_kernel, part, [VMEM] * 2)
    total = add(keep, came)
    out_near, out_far = call(
        output_kernel, [block, block], [VMEM] * 2, mine, other,
        scratch=[pltpu.VMEM((extent, width), bf16)],
        after=[total],
    )
    sigma_panel = call(
        rows_kernel, shape((1, height, count, width), bf16), [HBM, VMEM, VMEM],
        live, deliver(out_near, 0), deliver(out_far, 1),
        scratch=[pltpu.SMEM(live.shape, jnp.int32), dma(())],
    )
    total = add(total, swap(total, column=2))
    total = add(total, swap(total, column=1), after=[stay(sigma_panel)])
    quarters = [total, swap(total, side=1), swap(total, point=1), swap(total, side=1, point=1)]
    quarters += [swap(x, core=1) for x in quarters]
    marginal = call(
        spread_kernel, shape((count, width, width), f32), [VMEM] * 8, *quarters,
        scratch=[
            pltpu.VMEM((count, 2 * lines, LANES), f32),
            pltpu.VMEM((count, width, width), f32),
            dma((6,)),
        ],
        out_specs=HBM,
    )
    return sigma_panel, marginal


def solution(mesh):
    sizes = dict(mesh.shape)
    prow, pcol = ("prow",), ("pcol",)

    def on_device(sigma_rows, panel, live_block_rows, inv_diag, quad_weight):
        body = square if split else general
        return body(sigma_rows, panel, live_block_rows, inv_diag, quad_weight)

    split = sizes["hyp"] == 2 and sizes["pcol"] == 4 and sizes["prow"] == 4
    if split:
        prow = ("side", "core")
        mesh = jax.sharding.Mesh(
            mesh.devices.reshape(sizes["hyp"], 2, 2, sizes["pcol"]),
            ("hyp", "side", "core", "pcol"),
        )
    in_specs = (
        P("hyp", prow, pcol),
        P("hyp", prow + pcol, None, None),
        P(None, prow + pcol),
        P("hyp", None, prow + pcol, None),
        P("hyp"),
    )
    out_specs = (P("hyp", prow + pcol, None, None), P())
    return jax.shard_map(
        on_device, mesh=mesh, in_specs=in_specs, out_specs=out_specs, check_vma=False
    )
```

```python
import functools

import jax
import jax.numpy as jnp
from jax import lax
from jax.experimental import pallas as pl
from jax.experimental.pallas import tpu as pltpu
from jax.sharding import PartitionSpec as P

LANES = 128
ROWS = 16
VMEM = pl.BlockSpec(memory_space=pltpu.VMEM)
SMEM = pl.BlockSpec(memory_space=pltpu.SMEM)
ANY = pl.BlockSpec(memory_space=pl.ANY)
HBM = pl.BlockSpec(memory_space=pltpu.HBM)
AXES = ("hyp", "side", "core", "pcol")


def call(kernel, outs, specs, *operands, scratch=(), out_specs=None, after=(), alias={}):
    many = isinstance(outs, (list, tuple))
    count = len(specs)

    def body(*refs):
        kernel(*refs[:count], *refs[count + len(after) :])

    if out_specs is None:
        out_specs = [VMEM] * len(outs) if many else VMEM
    return pl.pallas_call(
        body,
        out_shape=outs,
        in_specs=list(specs) + [ANY] * len(after),
        out_specs=out_specs,
        scratch_shapes=scratch,
        input_output_aliases=alias,
        compiler_params=pltpu.CompilerParams(vmem_limit_bytes=32 * 2**20),
    )(*operands, *after)


def transposed_dot(left, right):
    return lax.dot_general(
        left, right, (((0,), (0,)), ((), ())), preferred_element_type=jnp.float32
    )


BLOCKS = 3
ABOVE = ((0, 1), (0, 2), (1, 2))
HELD = len(ABOVE) + 2


def block_indices():
    shape = (LANES, LANES)
    return lax.broadcasted_iota(jnp.int32, shape, 0), lax.broadcasted_iota(jnp.int32, shape, 1)


def hold_diagonal(first, second, third):
    row, column = block_indices()
    line = jnp.sum(jnp.where(row == column, second, 0.0), axis=0, keepdims=True)
    last = line[:, LANES - 1 :]
    below = jnp.where(row == LANES - 1, line, jnp.where((row == LANES - 2) & (column == 0), last, 0.0))
    upper = column >= row
    return jnp.where(upper, first, second), jnp.where(upper, third, below)


def restore_diagonal(shared, single):
    row, column = block_indices()
    turned, upper = shared.T, column >= row
    line = jnp.where(column[:1] == LANES - 1, single[LANES - 2 : LANES - 1, :1], single[LANES - 1 :, :])
    second = jnp.where(row == column, line, jnp.where(upper, turned, shared))
    return jnp.where(upper, shared, turned), second, jnp.where(upper, single, single.T)


def general(prow, sigma_rows, panel, live_block_rows, inv_diag, quad_weight):
    height, count, width = panel.shape[1:]
    offsets = lax.broadcasted_iota(jnp.int32, (height, count), 0)
    active = offsets < live_block_rows[:, 0][None, :]
    masked = jnp.where(active[:, :, None], panel[0], jnp.zeros_like(panel[0]))
    gathered = lax.all_gather(masked, prow + ("pcol",), axis=0, tiled=True)
    start = lax.axis_index("pcol") * sigma_rows.shape[2]
    column_panel = lax.dynamic_slice_in_dim(gathered, start, sigma_rows.shape[2], 0)
    applied = lax.psum_scatter(
        jnp.dot(
            sigma_rows[0],
            column_panel.reshape(sigma_rows.shape[2], count * width),
            preferred_element_type=jnp.float32,
        ),
        "pcol",
        scatter_dimension=0,
        tiled=True,
    ).reshape(height, count, width)
    half = applied.astype(jnp.bfloat16)
    sigma_panel = jnp.where(active[:, :, None], -half, jnp.zeros_like(half))[None]
    coupling = jnp.einsum(
        "vwg,vwe->wge",
        masked.astype(jnp.float32),
        applied,
        precision=lax.Precision.HIGHEST,
    )
    diagonal = jnp.einsum(
        "skp,skq->spq", inv_diag[0], inv_diag[0], preferred_element_type=jnp.float32
    )
    marginal = lax.psum(quad_weight[0] * (coupling + diagonal), ("hyp",) + prow + ("pcol",))
    return sigma_panel, marginal


def start_kernel(*refs):
    sources, (own, give, own_inverse), pieces = refs[:4], refs[4:7], refs[7:-5]
    buffers, sems = refs[-5:-1], refs[-1]
    copies = [
        pltpu.make_async_copy(source, buffer, sems.at[index])
        for index, (source, buffer) in enumerate(zip(sources, buffers))
    ]
    for copy in copies:
        copy.start()
    for copy in copies[:3]:
        copy.wait()
    live, panel, inverse, matrix = buffers
    first = lax.axis_index("side") == 0
    row = lax.broadcasted_iota(jnp.int32, own.shape, 0)
    rows = panel[0]
    zero = jnp.zeros(own.shape, own.dtype)
    one, two = (jnp.where(row < live[s], rows[:, s, :], zero) for s in range(2))
    height = own.shape[0]
    own[...] = jnp.where(first, one, two)
    give[:height] = jnp.where(first, two, one)
    spare = jnp.zeros((own_inverse.shape[0] - inverse.shape[2], own.shape[1]), own.dtype)
    one, two = (jnp.concatenate([inverse[0, s], spare], 0) for s in range(2))
    own_inverse[...] = jnp.where(first, one, two)
    give[height:] = jnp.where(first, two, one)
    copies[3].wait()
    at = 0
    for piece in pieces:
        piece[...] = matrix[0, :, at : at + piece.shape[0]].T
        at += piece.shape[0]


def gather_kernel(*refs):
    blocks, (rows, pack) = refs[:-2], refs[-2:]
    column = lax.axis_index("pcol")
    height = blocks[0].shape[0]
    for index, block in enumerate(blocks):
        spot = jnp.bitwise_xor(column, (0, 2, 1, 3)[index % 4])
        rows[index // 4, pl.ds(pl.multiple_of(spot * height, height), height), :] = block[...]
    pack[...] = rows[jnp.where(column // 2 == lax.axis_index("side"), 0, 1)]


def apply_kernel(rows, *refs):
    pieces, applied = refs[:-1], refs[-1]
    count = len(pieces) // 2
    at = 0
    for own, far in zip(pieces[:count], pieces[count:]):
        total = jnp.dot(own[...], rows[0], preferred_element_type=jnp.float32)
        total += jnp.dot(far[...], rows[1], preferred_element_type=jnp.float32)
        applied[at : at + own.shape[0]] = total
        at += own.shape[0]


def hold_kernel(value, out):
    del value, out


def couple_kernel(weight, applied, pack, got_pack, own_inverse, got_inverse, keep, send, packed):
    core, column = lax.axis_index("core"), lax.axis_index("pcol")
    high = applied[...].astype(jnp.bfloat16)
    low = (applied[...] - high.astype(jnp.float32)).astype(jnp.bfloat16)
    rows = jnp.where(column % 2 == core, pack[...], got_pack[...])
    blocks = {}
    for first in range(BLOCKS):
        left, right = slice(first * LANES, (first + 1) * LANES), slice(first * LANES, None)
        total = transposed_dot(rows[:, left], high[:, right])
        total += transposed_dot(rows[:, left], low[:, right])
        for lines in (own_inverse, got_inverse):
            total += transposed_dot(lines[:, left], lines[:, right])
        for index in range(BLOCKS - first):
            blocks[first, first + index] = weight[0] * total[:, index * LANES : (index + 1) * LANES]
    held = [blocks[place] for place in ABOVE]
    held += hold_diagonal(*(blocks[i, i] for i in range(BLOCKS)))
    for index, block in enumerate(held):
        packed[index * LANES : (index + 1) * LANES, :] = block
    size = keep.shape[0]
    keep[...] = packed[pl.ds(pl.multiple_of(core * size, 8), size), :]
    send[...] = packed[pl.ds(pl.multiple_of((1 - core) * size, 8), size), :]


def halve_kernel(mine, came, keep, send, whole):
    whole[...] = mine[...] + came[...]
    size, point = keep.shape[0], lax.axis_index("hyp")
    keep[...] = whole[pl.ds(pl.multiple_of(point * size, 8), size), :]
    send[...] = whole[pl.ds(pl.multiple_of((1 - point) * size, 8), size), :]


def output_kernel(mine, other, out_near, out_far, half):
    half[...] = -(mine[...] + other[...]).astype(jnp.bfloat16)
    height, side, core = out_near.shape[0], lax.axis_index("side"), lax.axis_index("core")
    for out, at in ((out_near, side), (out_far, 1 - side)):
        spot = at * 2 + core
        out[...] = half[pl.ds(pl.multiple_of(spot * height, height), height), :]


def add_kernel(mine, came, out):
    out[...] = mine[...] + came[...]


def finish_kernel(*refs):
    parts, (live_hbm, near, far, rows_out, out, live, block, lines, result, sems) = refs[:8], refs[8:]
    point, side, core = (lax.axis_index(name) for name in ("hyp", "side", "core"))
    load = pltpu.make_async_copy(live_hbm, live, sems.at[0])
    load.start()
    size = parts[0].shape[0]
    for index, part in enumerate(parts):
        owner = core if index < 4 else 1 - core
        node = 1 - side if index % 2 else side
        slot = 1 - point if index // 2 % 2 else point
        start = pl.multiple_of((owner * 2 + slot) * size, 8)
        lines[node, pl.ds(start, size), :] = part[...]
    copies = []
    for node in range(2):
        held = [lines[node, index * LANES : (index + 1) * LANES, :] for index in range(HELD)]
        places = [slice(index * LANES, (index + 1) * LANES) for index in range(BLOCKS)]
        for (a, b), tile in zip(ABOVE, held):
            result[node, places[a], places[b]] = tile
            result[node, places[b], places[a]] = tile.T
        for place, tile in zip(places, restore_diagonal(*held[len(ABOVE) :])):
            result[node, place, place] = tile
        copies.append(pltpu.make_async_copy(result.at[node], out.at[node], sems.at[1 + node]))
        copies[-1].start()
    load.wait()
    row = lax.broadcasted_iota(jnp.int32, near.shape, 0)
    first = lax.axis_index("pcol") // 2 == 0
    pair = (jnp.where(first, near[...], far[...]), jnp.where(first, far[...], near[...]))
    for s, value in enumerate(pair):
        block[:, s, :] = jnp.where(row < live[s], value, jnp.zeros(value.shape, value.dtype))
    copies.append(pltpu.make_async_copy(block, rows_out.at[0], sems.at[3]))
    copies[-1].start()
    for copy in copies:
        copy.wait()


def square(sigma_rows, panel, live_block_rows, inv_diag, quad_weight):
    height, count, width = panel.shape[1:]
    grid = lax.axis_size("pcol")
    points = lax.axis_size("hyp")
    f32, bf16 = jnp.float32, jnp.bfloat16
    shape = jax.ShapeDtypeStruct
    dma = pltpu.SemaphoreType.DMA
    stay = functools.partial(pltpu.with_memory_space_constraint, memory_space=pltpu.HBM)
    devices = points * 2 * 2 * grid
    live = live_block_rows[:, 0]

    def swap(x, point=0, side=0, core=0, column=0):
        mask = ((point * 2 + side) * 2 + core) * grid + column
        return lax.ppermute(x, AXES, [(i, i ^ mask) for i in range(devices)])

    extent = sigma_rows.shape[2]
    block = shape((height, width), bf16)
    cuts = (extent // 2, extent // 2)
    size = pl.cdiv(inv_diag.shape[2], ROWS) * ROWS
    own, give, own_inverse, *pieces = call(
        start_kernel,
        [block, shape((height + size, width), bf16), shape((size, width), bf16)]
        + [shape((lines, extent), bf16) for lines in cuts],
        [HBM] * 4,
        *map(stay, (live, panel, inv_diag, sigma_rows)),
        scratch=[pltpu.SMEM(live.shape, jnp.int32)]
        + [pltpu.VMEM(x.shape, bf16) for x in (panel, inv_diag, sigma_rows)]
        + [dma((4,))],
    )
    got = swap(give, side=1)
    got, got_inverse = got[:height], got[height:]
    blocks = []
    for one in (own, got):
        two = swap(one, column=2)
        blocks += [one, two, swap(one, column=1), swap(two, column=1)]
    far = [swap(piece, side=1) for piece in pieces]


    rows, pack = call(
        gather_kernel,
        [shape((2, extent, width), bf16), shape((extent, width), bf16)],
        [VMEM] * len(blocks),
        *blocks,
        after=far,
    )
    got_pack = swap(pack, core=1)
    mine = call(
        apply_kernel, shape((extent, width), f32), [VMEM] * (1 + 2 * len(cuts)), rows, *pieces, *far
    )
    lines = HELD * LANES // 2
    part, half = shape((lines // 2, LANES), f32), shape((lines, LANES), f32)
    mine = call(
        hold_kernel, shape(mine.shape, f32), [ANY], mine, out_specs=ANY, after=[got_pack], alias={0: 0}
    )
    other = swap(mine, core=1)
    keep, send = call(
        couple_kernel, [half, half], [SMEM] + [VMEM] * 5,
        quad_weight, mine, pack, got_pack, own_inverse, got_inverse,
        scratch=[pltpu.VMEM((2 * lines, LANES), f32)],
    )
    keep, send = call(
        halve_kernel, [part, part], [VMEM] * 2, keep, swap(send, core=1),
        scratch=[pltpu.VMEM((lines, LANES), f32)],
    )
    came = swap(send, point=1)
    def deliver(x, flip):
        pairs = []
        for i in range(devices):
            h, s, k, c = i // (4 * grid), i // (2 * grid) % 2, i // grid % 2, i % grid
            pairs.append((i, (h * 4 + c) * grid + 2 * (s ^ flip) + k))
        return lax.ppermute(x, AXES, pairs)

    add = functools.partial(call, add_kernel, part, [VMEM] * 2)
    total = add(keep, came)
    out_near, out_far = call(
        output_kernel, [block, block], [VMEM] * 2, mine, other,
        scratch=[pltpu.VMEM((extent, width), bf16)],
        after=[total],
    )
    near, far = deliver(out_near, 0), deliver(out_far, 1)
    total = add(total, swap(total, column=2))
    total = add(total, swap(total, column=1), after=[near, far])
    quarters = [total, swap(total, side=1), swap(total, point=1), swap(total, side=1, point=1)]
    quarters += [swap(x, core=1) for x in quarters]
    return call(
        finish_kernel,
        [shape((1, height, count, width), bf16), shape((count, width, width), f32)],
        [VMEM] * 8 + [HBM] + [VMEM] * 2,
        *quarters, live, near, far,
        scratch=[
            pltpu.SMEM(live.shape, jnp.int32),
            pltpu.VMEM((height, count, width), bf16),
            pltpu.VMEM((count, 2 * lines, LANES), f32),
            pltpu.VMEM((count, width, width), f32),
            dma((4,)),
        ],
        out_specs=[HBM, HBM],
    )


def solution(mesh):
    sizes = dict(mesh.shape)
    prow, pcol = ("prow",), ("pcol",)

    def on_device(sigma_rows, panel, live_block_rows, inv_diag, quad_weight):
        height, count, width = panel.shape[1:]
        fits = (
            split
            and sigma_rows.shape[1] == sigma_rows.shape[2] == sizes["pcol"] * height
            and height % LANES == 0
            and count == 2
            and width == BLOCKS * LANES
        )
        body = square if fits else functools.partial(general, prow)
        return body(sigma_rows, panel, live_block_rows, inv_diag, quad_weight)

    split = sizes["hyp"] == 2 and sizes["pcol"] == 4 and sizes["prow"] == 4
    if split:
        prow = ("side", "core")
        mesh = jax.sharding.Mesh(
            mesh.devices.reshape(sizes["hyp"], 2, 2, sizes["pcol"]),
            ("hyp", "side", "core", "pcol"),
        )
    in_specs = (
        P("hyp", prow, pcol),
        P("hyp", prow + pcol, None, None),
        P(None, prow + pcol),
        P("hyp", None, prow + pcol, None),
        P("hyp"),
    )
    out_specs = (P("hyp", prow + pcol, None, None), P())
    return jax.shard_map(
        on_device, mesh=mesh, in_specs=in_specs, out_specs=out_specs, check_vma=False
    )
```

```python
import functools

import jax
import jax.numpy as jnp
from jax import lax
from jax.experimental import pallas as pl
from jax.experimental.pallas import tpu as pltpu
from jax.sharding import PartitionSpec as P

LANES = 128
ROWS = 16
VMEM = pl.BlockSpec(memory_space=pltpu.VMEM)
SMEM = pl.BlockSpec(memory_space=pltpu.SMEM)
ANY = pl.BlockSpec(memory_space=pl.ANY)
HBM = pl.BlockSpec(memory_space=pltpu.HBM)
AXES = ("hyp", "side", "core", "pcol")


def call(kernel, outs, specs, *operands, scratch=(), out_specs=None, after=(), alias={}):
    many = isinstance(outs, (list, tuple))
    count = len(specs)

    def body(*refs):
        kernel(*refs[:count], *refs[count + len(after) :])

    if out_specs is None:
        out_specs = [VMEM] * len(outs) if many else VMEM
    return pl.pallas_call(
        body,
        out_shape=outs,
        in_specs=list(specs) + [ANY] * len(after),
        out_specs=out_specs,
        scratch_shapes=scratch,
        input_output_aliases=alias,
        compiler_params=pltpu.CompilerParams(vmem_limit_bytes=32 * 2**20),
    )(*operands, *after)


def transposed_dot(left, right):
    return lax.dot_general(
        left, right, (((0,), (0,)), ((), ())), preferred_element_type=jnp.float32
    )


BLOCKS = 3
ABOVE = ((0, 1), (0, 2), (1, 2))
HELD = len(ABOVE) + 2


def block_indices():
    shape = (LANES, LANES)
    return lax.broadcasted_iota(jnp.int32, shape, 0), lax.broadcasted_iota(jnp.int32, shape, 1)


def hold_diagonal(first, second, third):
    row, column = block_indices()
    line = jnp.sum(jnp.where(row == column, second, 0.0), axis=0, keepdims=True)
    last = line[:, LANES - 1 :]
    below = jnp.where(row == LANES - 1, line, jnp.where((row == LANES - 2) & (column == 0), last, 0.0))
    upper = column >= row
    return jnp.where(upper, first, second), jnp.where(upper, third, below)


def restore_diagonal(shared, single):
    row, column = block_indices()
    turned, upper = shared.T, column >= row
    line = jnp.where(column[:1] == LANES - 1, single[LANES - 2 : LANES - 1, :1], single[LANES - 1 :, :])
    second = jnp.where(row == column, line, jnp.where(upper, turned, shared))
    return jnp.where(upper, shared, turned), second, jnp.where(upper, single, single.T)


def general(prow, sigma_rows, panel, live_block_rows, inv_diag, quad_weight):
    height, count, width = panel.shape[1:]
    offsets = lax.broadcasted_iota(jnp.int32, (height, count), 0)
    active = offsets < live_block_rows[:, 0][None, :]
    masked = jnp.where(active[:, :, None], panel[0], jnp.zeros_like(panel[0]))
    gathered = lax.all_gather(masked, prow + ("pcol",), axis=0, tiled=True)
    start = lax.axis_index("pcol") * sigma_rows.shape[2]
    column_panel = lax.dynamic_slice_in_dim(gathered, start, sigma_rows.shape[2], 0)
    applied = lax.psum_scatter(
        jnp.dot(
            sigma_rows[0],
            column_panel.reshape(sigma_rows.shape[2], count * width),
            preferred_element_type=jnp.float32,
        ),
        "pcol",
        scatter_dimension=0,
        tiled=True,
    ).reshape(height, count, width)
    half = applied.astype(jnp.bfloat16)
    sigma_panel = jnp.where(active[:, :, None], -half, jnp.zeros_like(half))[None]
    coupling = jnp.einsum(
        "vwg,vwe->wge",
        masked.astype(jnp.float32),
        applied,
        precision=lax.Precision.HIGHEST,
    )
    diagonal = jnp.einsum(
        "skp,skq->spq", inv_diag[0], inv_diag[0], preferred_element_type=jnp.float32
    )
    marginal = lax.psum(quad_weight[0] * (coupling + diagonal), ("hyp",) + prow + ("pcol",))
    return sigma_panel, marginal


def start_kernel(*refs):
    sources, (own, give, own_inverse), pieces = refs[:4], refs[4:7], refs[7:-5]
    buffers, sems = refs[-5:-1], refs[-1]
    copies = [
        pltpu.make_async_copy(source, buffer, sems.at[index])
        for index, (source, buffer) in enumerate(zip(sources, buffers))
    ]
    for copy in copies:
        copy.start()
    for copy in copies[:3]:
        copy.wait()
    live, panel, inverse, matrix = buffers
    first = lax.axis_index("side") == 0
    row = lax.broadcasted_iota(jnp.int32, own.shape, 0)
    rows = panel[0]
    zero = jnp.zeros(own.shape, own.dtype)
    one, two = (jnp.where(row < live[s], rows[:, s, :], zero) for s in range(2))
    height = own.shape[0]
    own[...] = jnp.where(first, one, two)
    give[:height] = jnp.where(first, two, one)
    spare = jnp.zeros((own_inverse.shape[0] - inverse.shape[2], own.shape[1]), own.dtype)
    one, two = (jnp.concatenate([inverse[0, s], spare], 0) for s in range(2))
    own_inverse[...] = jnp.where(first, one, two)
    give[height:] = jnp.where(first, two, one)
    copies[3].wait()
    at = 0
    for piece in pieces:
        piece[...] = matrix[0, :, at : at + piece.shape[0]].T
        at += piece.shape[0]


def gather_kernel(*refs):
    blocks, (rows, pack) = refs[:-2], refs[-2:]
    column = lax.axis_index("pcol")
    height = blocks[0].shape[0]
    for index, block in enumerate(blocks):
        spot = jnp.bitwise_xor(column, (0, 2, 1, 3)[index % 4])
        rows[index // 4, pl.ds(pl.multiple_of(spot * height, height), height), :] = block[...]
    pack[...] = rows[jnp.where(column // 2 == lax.axis_index("side"), 0, 1)]


def apply_kernel(rows, *refs):
    pieces, applied = refs[:-1], refs[-1]
    count = len(pieces) // 2
    at = 0
    for own, far in zip(pieces[:count], pieces[count:]):
        total = jnp.dot(own[...], rows[0], preferred_element_type=jnp.float32)
        total += jnp.dot(far[...], rows[1], preferred_element_type=jnp.float32)
        applied[at : at + own.shape[0]] = total
        at += own.shape[0]


def hold_kernel(value, out):
    del value, out


def couple_kernel(weight, applied, pack, got_pack, own_inverse, got_inverse, keep, send, packed):
    core, column = lax.axis_index("core"), lax.axis_index("pcol")
    high = applied[...].astype(jnp.bfloat16)
    low = (applied[...] - high.astype(jnp.float32)).astype(jnp.bfloat16)
    rows = jnp.where(column % 2 == core, pack[...], got_pack[...])
    blocks = {}
    for first in range(BLOCKS):
        left, right = slice(first * LANES, (first + 1) * LANES), slice(first * LANES, None)
        total = transposed_dot(rows[:, left], high[:, right])
        total += transposed_dot(rows[:, left], low[:, right])
        for lines in (own_inverse, got_inverse):
            total += transposed_dot(lines[:, left], lines[:, right])
        for index in range(BLOCKS - first):
            blocks[first, first + index] = weight[0] * total[:, index * LANES : (index + 1) * LANES]
    held = [blocks[place] for place in ABOVE]
    held += hold_diagonal(*(blocks[i, i] for i in range(BLOCKS)))
    for index, block in enumerate(held):
        packed[index * LANES : (index + 1) * LANES, :] = block
    size = keep.shape[0]
    keep[...] = packed[pl.ds(pl.multiple_of(core * size, 8), size), :]
    send[...] = packed[pl.ds(pl.multiple_of((1 - core) * size, 8), size), :]


def halve_kernel(mine, came, keep, send, whole):
    whole[...] = mine[...] + came[...]
    size, point = keep.shape[0], lax.axis_index("hyp")
    keep[...] = whole[pl.ds(pl.multiple_of(point * size, 8), size), :]
    send[...] = whole[pl.ds(pl.multiple_of((1 - point) * size, 8), size), :]


def output_kernel(mine, other, out_near, out_far, half):
    half[...] = -(mine[...] + other[...]).astype(jnp.bfloat16)
    height, side, core = out_near.shape[0], lax.axis_index("side"), lax.axis_index("core")
    for out, at in ((out_near, side), (out_far, 1 - side)):
        spot = at * 2 + core
        out[...] = half[pl.ds(pl.multiple_of(spot * height, height), height), :]


def add_kernel(mine, came, out):
    out[...] = mine[...] + came[...]


def finish_kernel(*refs):
    parts, (live_hbm, near, far, rows_out, out, live, block, lines, result, sems) = refs[:8], refs[8:]
    point, side, core = (lax.axis_index(name) for name in ("hyp", "side", "core"))
    load = pltpu.make_async_copy(live_hbm, live, sems.at[0])
    load.start()
    size = parts[0].shape[0]
    for index, part in enumerate(parts):
        owner = core if index < 4 else 1 - core
        node = 1 - side if index % 2 else side
        slot = 1 - point if index // 2 % 2 else point
        start = pl.multiple_of((owner * 2 + slot) * size, 8)
        lines[node, pl.ds(start, size), :] = part[...]
    copies = []
    for node in range(2):
        held = [lines[node, index * LANES : (index + 1) * LANES, :] for index in range(HELD)]
        places = [slice(index * LANES, (index + 1) * LANES) for index in range(BLOCKS)]
        for (a, b), tile in zip(ABOVE, held):
            result[node, places[a], places[b]] = tile
            result[node, places[b], places[a]] = tile.T
        for place, tile in zip(places, restore_diagonal(*held[len(ABOVE) :])):
            result[node, place, place] = tile
        copies.append(pltpu.make_async_copy(result.at[node], out.at[node], sems.at[1 + node]))
        copies[-1].start()
    load.wait()
    row = lax.broadcasted_iota(jnp.int32, near.shape, 0)
    first = lax.axis_index("pcol") // 2 == 0
    pair = (jnp.where(first, near[...], far[...]), jnp.where(first, far[...], near[...]))
    for s, value in enumerate(pair):
        block[:, s, :] = jnp.where(row < live[s], value, jnp.zeros(value.shape, value.dtype))
    copies.append(pltpu.make_async_copy(block, rows_out.at[0], sems.at[3]))
    copies[-1].start()
    for copy in copies:
        copy.wait()


def square(sigma_rows, panel, live_block_rows, inv_diag, quad_weight):
    height, count, width = panel.shape[1:]
    grid = lax.axis_size("pcol")
    points = lax.axis_size("hyp")
    f32, bf16 = jnp.float32, jnp.bfloat16
    shape = jax.ShapeDtypeStruct
    dma = pltpu.SemaphoreType.DMA
    stay = functools.partial(pltpu.with_memory_space_constraint, memory_space=pltpu.HBM)
    devices = points * 2 * 2 * grid
    live = live_block_rows[:, 0]

    def swap(x, point=0, side=0, core=0, column=0):
        mask = ((point * 2 + side) * 2 + core) * grid + column
        return lax.ppermute(x, AXES, [(i, i ^ mask) for i in range(devices)])

    def swap_columns(x, steps):
        return lax.ppermute(x, AXES, [(i, i ^ steps[i // grid % 2]) for i in range(devices)])

    extent = sigma_rows.shape[2]
    block = shape((height, width), bf16)
    cuts = (extent // 2, extent // 2)
    size = pl.cdiv(inv_diag.shape[2], ROWS) * ROWS
    own, give, own_inverse, *pieces = call(
        start_kernel,
        [block, shape((height + size, width), bf16), shape((size, width), bf16)]
        + [shape((lines, extent), bf16) for lines in cuts],
        [HBM] * 4,
        *map(stay, (live, panel, inv_diag, sigma_rows)),
        scratch=[pltpu.SMEM(live.shape, jnp.int32)]
        + [pltpu.VMEM(x.shape, bf16) for x in (panel, inv_diag, sigma_rows)]
        + [dma((4,))],
    )
    got = swap(give, side=1)
    got, got_inverse = got[:height], got[height:]
    blocks = []
    for one in (own, got):
        two = swap(one, column=2)
        blocks += [one, two, swap(one, column=1), swap(two, column=1)]
    far = [swap(piece, side=1) for piece in pieces]


    rows, pack = call(
        gather_kernel,
        [shape((2, extent, width), bf16), shape((extent, width), bf16)],
        [VMEM] * len(blocks),
        *blocks,
        after=far,
    )
    got_pack = swap(pack, core=1)
    mine = call(
        apply_kernel, shape((extent, width), f32), [VMEM] * (1 + 2 * len(cuts)), rows, *pieces, *far
    )
    lines = HELD * LANES // 2
    part, half = shape((lines // 2, LANES), f32), shape((lines, LANES), f32)
    mine = call(
        hold_kernel, shape(mine.shape, f32), [ANY], mine, out_specs=ANY, after=[got_pack], alias={0: 0}
    )
    other = swap(mine, core=1)
    keep, send = call(
        couple_kernel, [half, half], [SMEM] + [VMEM] * 5,
        quad_weight, mine, pack, got_pack, own_inverse, got_inverse,
        scratch=[pltpu.VMEM((2 * lines, LANES), f32)],
    )
    keep, send = call(
        halve_kernel, [part, part], [VMEM] * 2, keep, swap(send, core=1),
        scratch=[pltpu.VMEM((lines, LANES), f32)],
    )
    came = swap(send, point=1)
    def deliver(x, flip):
        pairs = []
        for i in range(devices):
            h, s, k, c = i // (4 * grid), i // (2 * grid) % 2, i // grid % 2, i % grid
            pairs.append((i, (h * 4 + c) * grid + 2 * (s ^ flip) + k))
        return lax.ppermute(x, AXES, pairs)

    add = functools.partial(call, add_kernel, part, [VMEM] * 2)
    total = add(keep, came)
    out_near, out_far = call(
        output_kernel, [block, block], [VMEM] * 2, mine, other,
        scratch=[pltpu.VMEM((extent, width), bf16)],
        after=[total],
    )
    near, far = deliver(out_near, 0), deliver(out_far, 1)
    total = add(total, swap_columns(total, (1, 2)))
    total = add(total, swap_columns(total, (2, 1)), after=[near, far])
    quarters = [total, swap(total, side=1), swap(total, point=1), swap(total, side=1, point=1)]
    quarters += [swap(x, core=1) for x in quarters]
    return call(
        finish_kernel,
        [shape((1, height, count, width), bf16), shape((count, width, width), f32)],
        [VMEM] * 8 + [HBM] + [VMEM] * 2,
        *quarters, live, near, far,
        scratch=[
            pltpu.SMEM(live.shape, jnp.int32),
            pltpu.VMEM((height, count, width), bf16),
            pltpu.VMEM((count, 2 * lines, LANES), f32),
            pltpu.VMEM((count, width, width), f32),
            dma((4,)),
        ],
        out_specs=[HBM, HBM],
    )


def solution(mesh):
    sizes = dict(mesh.shape)
    prow, pcol = ("prow",), ("pcol",)

    def on_device(sigma_rows, panel, live_block_rows, inv_diag, quad_weight):
        height, count, width = panel.shape[1:]
        fits = (
            split
            and sigma_rows.shape[1] == sigma_rows.shape[2] == sizes["pcol"] * height
            and height % LANES == 0
            and count == 2
            and width == BLOCKS * LANES
        )
        body = square if fits else functools.partial(general, prow)
        return body(sigma_rows, panel, live_block_rows, inv_diag, quad_weight)

    split = sizes["hyp"] == 2 and sizes["pcol"] == 4 and sizes["prow"] == 4
    if split:
        prow = ("side", "core")
        mesh = jax.sharding.Mesh(
            mesh.devices.reshape(sizes["hyp"], 2, 2, sizes["pcol"]),
            ("hyp", "side", "core", "pcol"),
        )
    in_specs = (
        P("hyp", prow, pcol),
        P("hyp", prow + pcol, None, None),
        P(None, prow + pcol),
        P("hyp", None, prow + pcol, None),
        P("hyp"),
    )
    out_specs = (P("hyp", prow + pcol, None, None), P())
    return jax.shard_map(
        on_device, mesh=mesh, in_specs=in_specs, out_specs=out_specs, check_vma=False
    )
```

```python
import functools

import jax
import jax.numpy as jnp
from jax import lax
from jax.experimental import pallas as pl
from jax.experimental.pallas import tpu as pltpu
from jax.sharding import PartitionSpec as P

LANES = 128
ROWS = 16
VMEM = pl.BlockSpec(memory_space=pltpu.VMEM)
SMEM = pl.BlockSpec(memory_space=pltpu.SMEM)
ANY = pl.BlockSpec(memory_space=pl.ANY)
HBM = pl.BlockSpec(memory_space=pltpu.HBM)
AXES = ("hyp", "side", "core", "pcol")


def call(kernel, outs, specs, *operands, scratch=(), out_specs=None, after=(), alias={}):
    many = isinstance(outs, (list, tuple))
    count = len(specs)

    def body(*refs):
        kernel(*refs[:count], *refs[count + len(after) :])

    if out_specs is None:
        out_specs = [VMEM] * len(outs) if many else VMEM
    return pl.pallas_call(
        body,
        out_shape=outs,
        in_specs=list(specs) + [ANY] * len(after),
        out_specs=out_specs,
        scratch_shapes=scratch,
        input_output_aliases=alias,
        compiler_params=pltpu.CompilerParams(vmem_limit_bytes=32 * 2**20),
    )(*operands, *after)


def transposed_dot(left, right):
    return lax.dot_general(
        left, right, (((0,), (0,)), ((), ())), preferred_element_type=jnp.float32
    )


BLOCKS = 3
ABOVE = ((0, 1), (0, 2), (1, 2))
HELD = len(ABOVE) + 2


def block_indices():
    shape = (LANES, LANES)
    return lax.broadcasted_iota(jnp.int32, shape, 0), lax.broadcasted_iota(jnp.int32, shape, 1)


def hold_diagonal(first, second, third):
    row, column = block_indices()
    line = jnp.sum(jnp.where(row == column, second, 0.0), axis=0, keepdims=True)
    last = line[:, LANES - 1 :]
    below = jnp.where(row == LANES - 1, line, jnp.where((row == LANES - 2) & (column == 0), last, 0.0))
    upper = column >= row
    return jnp.where(upper, first, second), jnp.where(upper, third, below)


def restore_diagonal(shared, single):
    row, column = block_indices()
    turned, upper = shared.T, column >= row
    line = jnp.where(column[:1] == LANES - 1, single[LANES - 2 : LANES - 1, :1], single[LANES - 1 :, :])
    second = jnp.where(row == column, line, jnp.where(upper, turned, shared))
    return jnp.where(upper, shared, turned), second, jnp.where(upper, single, single.T)


def general(prow, sigma_rows, panel, live_block_rows, inv_diag, quad_weight):
    height, count, width = panel.shape[1:]
    offsets = lax.broadcasted_iota(jnp.int32, (height, count), 0)
    active = offsets < live_block_rows[:, 0][None, :]
    masked = jnp.where(active[:, :, None], panel[0], jnp.zeros_like(panel[0]))
    gathered = lax.all_gather(masked, prow + ("pcol",), axis=0, tiled=True)
    start = lax.axis_index("pcol") * sigma_rows.shape[2]
    column_panel = lax.dynamic_slice_in_dim(gathered, start, sigma_rows.shape[2], 0)
    applied = lax.psum_scatter(
        jnp.dot(
            sigma_rows[0],
            column_panel.reshape(sigma_rows.shape[2], count * width),
            preferred_element_type=jnp.float32,
        ),
        "pcol",
        scatter_dimension=0,
        tiled=True,
    ).reshape(height, count, width)
    half = applied.astype(jnp.bfloat16)
    sigma_panel = jnp.where(active[:, :, None], -half, jnp.zeros_like(half))[None]
    coupling = jnp.einsum(
        "vwg,vwe->wge",
        masked.astype(jnp.float32),
        applied,
        precision=lax.Precision.HIGHEST,
    )
    diagonal = jnp.einsum(
        "skp,skq->spq", inv_diag[0], inv_diag[0], preferred_element_type=jnp.float32
    )
    marginal = lax.psum(quad_weight[0] * (coupling + diagonal), ("hyp",) + prow + ("pcol",))
    return sigma_panel, marginal


def start_kernel(*refs):
    sources, (own, give, own_inverse), pieces = refs[:4], refs[4:7], refs[7:-5]
    buffers, sems = refs[-5:-1], refs[-1]
    copies = [
        pltpu.make_async_copy(source, buffer, sems.at[index])
        for index, (source, buffer) in enumerate(zip(sources, buffers))
    ]
    for copy in copies:
        copy.start()
    for copy in copies[:3]:
        copy.wait()
    live, panel, inverse, matrix = buffers
    first = lax.axis_index("side") == 0
    row = lax.broadcasted_iota(jnp.int32, own.shape, 0)
    rows = panel[0]
    zero = jnp.zeros(own.shape, own.dtype)
    one, two = (jnp.where(row < live[s], rows[:, s, :], zero) for s in range(2))
    height = own.shape[0]
    own[...] = jnp.where(first, one, two)
    give[:height] = jnp.where(first, two, one)
    spare = jnp.zeros((own_inverse.shape[0] - inverse.shape[2], own.shape[1]), own.dtype)
    one, two = (jnp.concatenate([inverse[0, s], spare], 0) for s in range(2))
    own_inverse[...] = jnp.where(first, one, two)
    give[height:] = jnp.where(first, two, one)
    copies[3].wait()
    at = 0
    for piece in pieces:
        piece[...] = matrix[0, :, at : at + piece.shape[0]].T
        at += piece.shape[0]


def gather_kernel(*refs):
    blocks, (rows, pack) = refs[:-2], refs[-2:]
    column = lax.axis_index("pcol")
    height = blocks[0].shape[0]
    for index, block in enumerate(blocks):
        spot = jnp.bitwise_xor(column, (0, 2, 1, 3)[index % 4])
        rows[index // 4, pl.ds(pl.multiple_of(spot * height, height), height), :] = block[...]
    pack[...] = rows[jnp.where(column // 2 == lax.axis_index("side"), 0, 1)]


def apply_kernel(rows, *refs):
    pieces, applied = refs[:-1], refs[-1]
    count = len(pieces) // 2
    at = 0
    for own, far in zip(pieces[:count], pieces[count:]):
        total = jnp.dot(own[...], rows[0], preferred_element_type=jnp.float32)
        total += jnp.dot(far[...], rows[1], preferred_element_type=jnp.float32)
        applied[at : at + own.shape[0]] = total
        at += own.shape[0]


def hold_kernel(value, out):
    del value, out


def couple_kernel(weight, applied, pack, got_pack, own_inverse, got_inverse, keep, send, packed):
    core, column = lax.axis_index("core"), lax.axis_index("pcol")
    high = applied[...].astype(jnp.bfloat16)
    low = (applied[...] - high.astype(jnp.float32)).astype(jnp.bfloat16)
    rows = jnp.where(column % 2 == core, pack[...], got_pack[...])
    blocks = {}
    for first in range(BLOCKS):
        left, right = slice(first * LANES, (first + 1) * LANES), slice(first * LANES, None)
        total = transposed_dot(rows[:, left], high[:, right])
        total += transposed_dot(rows[:, left], low[:, right])
        for lines in (own_inverse, got_inverse):
            total += transposed_dot(lines[:, left], lines[:, right])
        for index in range(BLOCKS - first):
            blocks[first, first + index] = weight[0] * total[:, index * LANES : (index + 1) * LANES]
    held = [blocks[place] for place in ABOVE]
    held += hold_diagonal(*(blocks[i, i] for i in range(BLOCKS)))
    for index, block in enumerate(held):
        packed[index * LANES : (index + 1) * LANES, :] = block
    size = keep.shape[0]
    keep[...] = packed[pl.ds(pl.multiple_of(core * size, 8), size), :]
    send[...] = packed[pl.ds(pl.multiple_of((1 - core) * size, 8), size), :]


def halve_kernel(mine, came, keep, send, whole):
    whole[...] = mine[...] + came[...]
    size, point = keep.shape[0], lax.axis_index("hyp")
    keep[...] = whole[pl.ds(pl.multiple_of(point * size, 8), size), :]
    send[...] = whole[pl.ds(pl.multiple_of((1 - point) * size, 8), size), :]


def output_kernel(mine, other, out_near, out_far, half):
    half[...] = -(mine[...] + other[...]).astype(jnp.bfloat16)
    height, side, core = out_near.shape[0], lax.axis_index("side"), lax.axis_index("core")
    for out, at in ((out_near, side), (out_far, 1 - side)):
        spot = at * 2 + core
        out[...] = half[pl.ds(pl.multiple_of(spot * height, height), height), :]


def add_kernel(mine, came, out):
    out[...] = mine[...] + came[...]


def finish_kernel(*refs):
    parts, (live_hbm, near, far, rows_out, out, live, block, lines, result, sems) = refs[:8], refs[8:]
    point, side, core = (lax.axis_index(name) for name in ("hyp", "side", "core"))
    load = pltpu.make_async_copy(live_hbm, live, sems.at[0])
    load.start()
    size = parts[0].shape[0]
    for index, part in enumerate(parts):
        owner = core if index < 4 else 1 - core
        node = 1 - side if index % 2 else side
        slot = 1 - point if index // 2 % 2 else point
        start = pl.multiple_of((owner * 2 + slot) * size, 8)
        lines[node, pl.ds(start, size), :] = part[...]
    copies = []
    for node in range(2):
        held = [lines[node, index * LANES : (index + 1) * LANES, :] for index in range(HELD)]
        places = [slice(index * LANES, (index + 1) * LANES) for index in range(BLOCKS)]
        for (a, b), tile in zip(ABOVE, held):
            result[node, places[a], places[b]] = tile
            result[node, places[b], places[a]] = tile.T
        for place, tile in zip(places, restore_diagonal(*held[len(ABOVE) :])):
            result[node, place, place] = tile
        copies.append(pltpu.make_async_copy(result.at[node], out.at[node], sems.at[1 + node]))
        copies[-1].start()
    load.wait()
    row = lax.broadcasted_iota(jnp.int32, near.shape, 0)
    first = lax.axis_index("pcol") // 2 == 0
    pair = (jnp.where(first, near[...], far[...]), jnp.where(first, far[...], near[...]))
    for s, value in enumerate(pair):
        block[:, s, :] = jnp.where(row < live[s], value, jnp.zeros(value.shape, value.dtype))
    copies.append(pltpu.make_async_copy(block, rows_out.at[0], sems.at[3]))
    copies[-1].start()
    for copy in copies:
        copy.wait()


def square(sigma_rows, panel, live_block_rows, inv_diag, quad_weight):
    height, count, width = panel.shape[1:]
    grid = lax.axis_size("pcol")
    points = lax.axis_size("hyp")
    f32, bf16 = jnp.float32, jnp.bfloat16
    shape = jax.ShapeDtypeStruct
    dma = pltpu.SemaphoreType.DMA
    stay = functools.partial(pltpu.with_memory_space_constraint, memory_space=pltpu.HBM)
    devices = points * 2 * 2 * grid
    live = live_block_rows[:, 0]

    def swap(x, point=0, side=0, core=0, column=0):
        mask = ((point * 2 + side) * 2 + core) * grid + column
        return lax.ppermute(x, AXES, [(i, i ^ mask) for i in range(devices)])

    def swap_columns(x, steps):
        return lax.ppermute(x, AXES, [(i, i ^ steps[i // grid % 2]) for i in range(devices)])

    extent = sigma_rows.shape[2]
    block = shape((height, width), bf16)
    cuts = (extent // 2, extent // 2)
    size = pl.cdiv(inv_diag.shape[2], ROWS) * ROWS
    own, give, own_inverse, *pieces = call(
        start_kernel,
        [block, shape((height + size, width), bf16), shape((size, width), bf16)]
        + [shape((lines, extent), bf16) for lines in cuts],
        [HBM] * 4,
        *map(stay, (live, panel, inv_diag, sigma_rows)),
        scratch=[pltpu.SMEM(live.shape, jnp.int32)]
        + [pltpu.VMEM(x.shape, bf16) for x in (panel, inv_diag, sigma_rows)]
        + [dma((4,))],
    )
    got = swap(give, side=1)
    got, got_inverse = got[:height], got[height:]
    blocks = []
    for one in (own, got):
        two = swap(one, column=2)
        blocks += [one, two, swap(one, column=1), swap(two, column=1)]
    far = [swap(piece, side=1) for piece in pieces]


    rows, pack = call(
        gather_kernel,
        [shape((2, extent, width), bf16), shape((extent, width), bf16)],
        [VMEM] * len(blocks),
        *blocks,
        after=far,
    )
    got_pack = swap(pack, core=1)
    mine = call(
        apply_kernel, shape((extent, width), f32), [VMEM] * (1 + 2 * len(cuts)), rows, *pieces, *far
    )
    lines = HELD * LANES // 2
    part, half = shape((lines // 2, LANES), f32), shape((lines, LANES), f32)
    mine = call(
        hold_kernel, shape(mine.shape, f32), [ANY], mine, out_specs=ANY, after=[got_pack], alias={0: 0}
    )
    other = swap(mine, core=1)
    keep, send = call(
        couple_kernel, [half, half], [SMEM] + [VMEM] * 5,
        quad_weight, mine, pack, got_pack, own_inverse, got_inverse,
        scratch=[pltpu.VMEM((2 * lines, LANES), f32)],
    )
    keep, send = call(
        halve_kernel, [part, part], [VMEM] * 2, keep, swap(send, core=1),
        scratch=[pltpu.VMEM((lines, LANES), f32)],
    )
    came = swap(send, point=1)
    def deliver(x, flip):
        pairs = []
        for i in range(devices):
            h, s, k, c = i // (4 * grid), i // (2 * grid) % 2, i // grid % 2, i % grid
            pairs.append((i, (h * 4 + c) * grid + 2 * (s ^ flip) + k))
        return lax.ppermute(x, AXES, pairs)

    add = functools.partial(call, add_kernel, part, [VMEM] * 2)
    total = add(keep, came)
    out_near, out_far = call(
        output_kernel, [block, block], [VMEM] * 2, mine, other,
        scratch=[pltpu.VMEM((extent, width), bf16)],
        after=[keep],
    )
    near, far = deliver(out_near, 0), deliver(out_far, 1)
    total = add(total, swap_columns(total, (1, 2)), after=[near])
    total = add(total, swap_columns(total, (2, 1)), after=[far])
    quarters = [total, swap(total, side=1), swap(total, point=1), swap(total, side=1, point=1)]
    quarters += [swap(x, core=1) for x in quarters]
    return call(
        finish_kernel,
        [shape((1, height, count, width), bf16), shape((count, width, width), f32)],
        [VMEM] * 8 + [HBM] + [VMEM] * 2,
        *quarters, live, near, far,
        scratch=[
            pltpu.SMEM(live.shape, jnp.int32),
            pltpu.VMEM((height, count, width), bf16),
            pltpu.VMEM((count, 2 * lines, LANES), f32),
            pltpu.VMEM((count, width, width), f32),
            dma((4,)),
        ],
        out_specs=[HBM, HBM],
    )


def solution(mesh):
    sizes = dict(mesh.shape)
    prow, pcol = ("prow",), ("pcol",)

    def on_device(sigma_rows, panel, live_block_rows, inv_diag, quad_weight):
        height, count, width = panel.shape[1:]
        fits = (
            split
            and sigma_rows.shape[1] == sigma_rows.shape[2] == sizes["pcol"] * height
            and height % LANES == 0
            and count == 2
            and width == BLOCKS * LANES
        )
        body = square if fits else functools.partial(general, prow)
        return body(sigma_rows, panel, live_block_rows, inv_diag, quad_weight)

    split = sizes["hyp"] == 2 and sizes["pcol"] == 4 and sizes["prow"] == 4
    if split:
        prow = ("side", "core")
        mesh = jax.sharding.Mesh(
            mesh.devices.reshape(sizes["hyp"], 2, 2, sizes["pcol"]),
            ("hyp", "side", "core", "pcol"),
        )
    in_specs = (
        P("hyp", prow, pcol),
        P("hyp", prow + pcol, None, None),
        P(None, prow + pcol),
        P("hyp", None, prow + pcol, None),
        P("hyp"),
    )
    out_specs = (P("hyp", prow + pcol, None, None), P())
    return jax.shard_map(
        on_device, mesh=mesh, in_specs=in_specs, out_specs=out_specs, check_vma=False
    )
```

```python
import functools

import jax
import jax.numpy as jnp
from jax import lax
from jax.experimental import pallas as pl
from jax.experimental.pallas import tpu as pltpu
from jax.sharding import PartitionSpec as P

LANES = 128
ROWS = 16
VMEM = pl.BlockSpec(memory_space=pltpu.VMEM)
SMEM = pl.BlockSpec(memory_space=pltpu.SMEM)
ANY = pl.BlockSpec(memory_space=pl.ANY)
HBM = pl.BlockSpec(memory_space=pltpu.HBM)
AXES = ("hyp", "side", "core", "pcol")


def call(kernel, outs, specs, *operands, scratch=(), out_specs=None, after=(), alias={}):
    many = isinstance(outs, (list, tuple))
    count = len(specs)

    def body(*refs):
        kernel(*refs[:count], *refs[count + len(after) :])

    if out_specs is None:
        out_specs = [VMEM] * len(outs) if many else VMEM
    return pl.pallas_call(
        body,
        out_shape=outs,
        in_specs=list(specs) + [ANY] * len(after),
        out_specs=out_specs,
        scratch_shapes=scratch,
        input_output_aliases=alias,
        compiler_params=pltpu.CompilerParams(vmem_limit_bytes=32 * 2**20),
    )(*operands, *after)


def transposed_dot(left, right):
    return lax.dot_general(
        left, right, (((0,), (0,)), ((), ())), preferred_element_type=jnp.float32
    )


BLOCKS = 3
ABOVE = ((0, 1), (0, 2), (1, 2))
HELD = len(ABOVE) + 2


def block_indices():
    shape = (LANES, LANES)
    return lax.broadcasted_iota(jnp.int32, shape, 0), lax.broadcasted_iota(jnp.int32, shape, 1)


def hold_diagonal(first, second, third):
    row, column = block_indices()
    line = jnp.sum(jnp.where(row == column, second, 0.0), axis=0, keepdims=True)
    last = line[:, LANES - 1 :]
    below = jnp.where(row == LANES - 1, line, jnp.where((row == LANES - 2) & (column == 0), last, 0.0))
    upper = column >= row
    return jnp.where(upper, first, second), jnp.where(upper, third, below)


def restore_diagonal(shared, single):
    row, column = block_indices()
    turned, upper = shared.T, column >= row
    line = jnp.where(column[:1] == LANES - 1, single[LANES - 2 : LANES - 1, :1], single[LANES - 1 :, :])
    second = jnp.where(row == column, line, jnp.where(upper, turned, shared))
    return jnp.where(upper, shared, turned), second, jnp.where(upper, single, single.T)


def general(prow, sigma_rows, panel, live_block_rows, inv_diag, quad_weight):
    height, count, width = panel.shape[1:]
    offsets = lax.broadcasted_iota(jnp.int32, (height, count), 0)
    active = offsets < live_block_rows[:, 0][None, :]
    masked = jnp.where(active[:, :, None], panel[0], jnp.zeros_like(panel[0]))
    gathered = lax.all_gather(masked, prow + ("pcol",), axis=0, tiled=True)
    start = lax.axis_index("pcol") * sigma_rows.shape[2]
    column_panel = lax.dynamic_slice_in_dim(gathered, start, sigma_rows.shape[2], 0)
    applied = lax.psum_scatter(
        jnp.dot(
            sigma_rows[0],
            column_panel.reshape(sigma_rows.shape[2], count * width),
            preferred_element_type=jnp.float32,
        ),
        "pcol",
        scatter_dimension=0,
        tiled=True,
    ).reshape(height, count, width)
    half = applied.astype(jnp.bfloat16)
    sigma_panel = jnp.where(active[:, :, None], -half, jnp.zeros_like(half))[None]
    coupling = jnp.einsum(
        "vwg,vwe->wge",
        masked.astype(jnp.float32),
        applied,
        precision=lax.Precision.HIGHEST,
    )
    diagonal = jnp.einsum(
        "skp,skq->spq", inv_diag[0], inv_diag[0], preferred_element_type=jnp.float32
    )
    marginal = lax.psum(quad_weight[0] * (coupling + diagonal), ("hyp",) + prow + ("pcol",))
    return sigma_panel, marginal


def start_kernel(*refs):
    sources, (own, give, own_inverse), pieces = refs[:4], refs[4:7], refs[7:-5]
    buffers, sems = refs[-5:-1], refs[-1]
    copies = [
        pltpu.make_async_copy(source, buffer, sems.at[index])
        for index, (source, buffer) in enumerate(zip(sources, buffers))
    ]
    for copy in copies:
        copy.start()
    for copy in copies[:3]:
        copy.wait()
    live, panel, inverse, matrix = buffers
    first = lax.axis_index("side") == 0
    row = lax.broadcasted_iota(jnp.int32, own.shape, 0)
    rows = panel[0]
    zero = jnp.zeros(own.shape, own.dtype)
    one, two = (jnp.where(row < live[s], rows[:, s, :], zero) for s in range(2))
    height = own.shape[0]
    own[...] = jnp.where(first, one, two)
    give[:height] = jnp.where(first, two, one)
    spare = jnp.zeros((own_inverse.shape[0] - inverse.shape[2], own.shape[1]), own.dtype)
    one, two = (jnp.concatenate([inverse[0, s], spare], 0) for s in range(2))
    own_inverse[...] = jnp.where(first, one, two)
    give[height:] = jnp.where(first, two, one)
    copies[3].wait()
    at = 0
    for piece in pieces:
        piece[...] = matrix[0, :, at : at + piece.shape[0]].T
        at += piece.shape[0]


def gather_kernel(*refs):
    blocks, (rows, pack) = refs[:-2], refs[-2:]
    column = lax.axis_index("pcol")
    height = blocks[0].shape[0]
    for index, block in enumerate(blocks):
        spot = jnp.bitwise_xor(column, (0, 2, 1, 3)[index % 4])
        rows[index // 4, pl.ds(pl.multiple_of(spot * height, height), height), :] = block[...]
    pack[...] = rows[jnp.where(column // 2 == lax.axis_index("side"), 0, 1)]


def apply_kernel(rows, *refs):
    pieces, applied = refs[:-1], refs[-1]
    count = len(pieces) // 2
    at = 0
    for own, far in zip(pieces[:count], pieces[count:]):
        total = jnp.dot(own[...], rows[0], preferred_element_type=jnp.float32)
        total += jnp.dot(far[...], rows[1], preferred_element_type=jnp.float32)
        applied[at : at + own.shape[0]] = total
        at += own.shape[0]


def hold_kernel(value, out):
    del value, out


def couple_kernel(applied, pack, got_pack, own_inverse, got_inverse, keep, send, packed):
    core, column = lax.axis_index("core"), lax.axis_index("pcol")
    high = applied[...].astype(jnp.bfloat16)
    low = (applied[...] - high.astype(jnp.float32)).astype(jnp.bfloat16)
    rows = jnp.where(column % 2 == core, pack[...], got_pack[...])
    blocks = {}
    for first in range(BLOCKS):
        left, right = slice(first * LANES, (first + 1) * LANES), slice(first * LANES, None)
        total = transposed_dot(rows[:, left], high[:, right])
        total += transposed_dot(rows[:, left], low[:, right])
        for lines in (own_inverse, got_inverse):
            total += transposed_dot(lines[:, left], lines[:, right])
        for index in range(BLOCKS - first):
            blocks[first, first + index] = total[:, index * LANES : (index + 1) * LANES]
    held = [blocks[place] for place in ABOVE]
    held += hold_diagonal(*(blocks[i, i] for i in range(BLOCKS)))
    for index, block in enumerate(held):
        packed[index * LANES : (index + 1) * LANES, :] = block
    size = keep.shape[0]
    keep[...] = packed[pl.ds(pl.multiple_of(core * size, 8), size), :]
    send[...] = packed[pl.ds(pl.multiple_of((1 - core) * size, 8), size), :]


def halve_kernel(weight, mine, came, keep, send, whole):
    whole[...] = weight[0] * (mine[...] + came[...])
    size, point = keep.shape[0], lax.axis_index("hyp")
    keep[...] = whole[pl.ds(pl.multiple_of(point * size, 8), size), :]
    send[...] = whole[pl.ds(pl.multiple_of((1 - point) * size, 8), size), :]


def output_kernel(mine, other, out_near, out_far, half):
    half[...] = -(mine[...] + other[...]).astype(jnp.bfloat16)
    height, side, core = out_near.shape[0], lax.axis_index("side"), lax.axis_index("core")
    for out, at in ((out_near, side), (out_far, 1 - side)):
        spot = at * 2 + core
        out[...] = half[pl.ds(pl.multiple_of(spot * height, height), height), :]


def add_kernel(mine, came, out):
    out[...] = mine[...] + came[...]


def finish_kernel(*refs):
    parts, (live_hbm, near, far, rows_out, out, live, block, lines, result, sems) = refs[:8], refs[8:]
    point, side, core = (lax.axis_index(name) for name in ("hyp", "side", "core"))
    load = pltpu.make_async_copy(live_hbm, live, sems.at[0])
    load.start()
    size = parts[0].shape[0]
    for index, part in enumerate(parts):
        owner = core if index < 4 else 1 - core
        node = 1 - side if index % 2 else side
        slot = 1 - point if index // 2 % 2 else point
        start = pl.multiple_of((owner * 2 + slot) * size, 8)
        lines[node, pl.ds(start, size), :] = part[...]
    load.wait()
    row = lax.broadcasted_iota(jnp.int32, near.shape, 0)
    first = lax.axis_index("pcol") // 2 == 0
    pair = (jnp.where(first, near[...], far[...]), jnp.where(first, far[...], near[...]))
    for s, value in enumerate(pair):
        block[:, s, :] = jnp.where(row < live[s], value, jnp.zeros(value.shape, value.dtype))
    copies = [pltpu.make_async_copy(block, rows_out.at[0], sems.at[1])]
    copies[0].start()
    places = [slice(index * LANES, (index + 1) * LANES) for index in range(BLOCKS)]
    for node in range(2):
        held = [lines[node, index * LANES : (index + 1) * LANES, :] for index in range(HELD)]
        diagonal = restore_diagonal(*held[len(ABOVE) :])
        for a, rows in enumerate(places):
            result[node, rows, rows] = diagonal[a]
            for place, tile in zip(ABOVE, held):
                if place[0] == a:
                    result[node, rows, places[place[1]]] = tile
                elif place[1] == a:
                    result[node, rows, places[place[0]]] = tile.T
            copies.append(
                pltpu.make_async_copy(result.at[node, rows], out.at[node, rows], sems.at[len(copies) + 1])
            )
            copies[-1].start()
    for copy in copies:
        copy.wait()


def square(sigma_rows, panel, live_block_rows, inv_diag, quad_weight):
    height, count, width = panel.shape[1:]
    grid = lax.axis_size("pcol")
    points = lax.axis_size("hyp")
    f32, bf16 = jnp.float32, jnp.bfloat16
    shape = jax.ShapeDtypeStruct
    dma = pltpu.SemaphoreType.DMA
    stay = functools.partial(pltpu.with_memory_space_constraint, memory_space=pltpu.HBM)
    devices = points * 2 * 2 * grid
    live = live_block_rows[:, 0]

    def swap(x, point=0, side=0, core=0, column=0):
        mask = ((point * 2 + side) * 2 + core) * grid + column
        return lax.ppermute(x, AXES, [(i, i ^ mask) for i in range(devices)])

    extent = sigma_rows.shape[2]
    block = shape((height, width), bf16)
    cuts = (extent // 2, extent // 2)
    size = pl.cdiv(inv_diag.shape[2], ROWS) * ROWS
    own, give, own_inverse, *pieces = call(
        start_kernel,
        [block, shape((height + size, width), bf16), shape((size, width), bf16)]
        + [shape((lines, extent), bf16) for lines in cuts],
        [HBM] * 4,
        *map(stay, (live, panel, inv_diag, sigma_rows)),
        scratch=[pltpu.SMEM(live.shape, jnp.int32)]
        + [pltpu.VMEM(x.shape, bf16) for x in (panel, inv_diag, sigma_rows)]
        + [dma((4,))],
    )
    got = swap(give, side=1)
    got, got_inverse = got[:height], got[height:]
    blocks = []
    for one in (own, got):
        two = swap(one, column=2)
        blocks += [one, two, swap(one, column=1), swap(two, column=1)]
    far = [swap(piece, side=1) for piece in pieces]


    rows, pack = call(
        gather_kernel,
        [shape((2, extent, width), bf16), shape((extent, width), bf16)],
        [VMEM] * len(blocks),
        *blocks,
        after=far,
    )
    got_pack = swap(pack, core=1)
    mine = call(
        apply_kernel, shape((extent, width), f32), [VMEM] * (1 + 2 * len(cuts)), rows, *pieces, *far
    )
    lines = HELD * LANES // 2
    part, half = shape((lines // 2, LANES), f32), shape((lines, LANES), f32)
    mine = call(
        hold_kernel, shape(mine.shape, f32), [ANY], mine, out_specs=ANY, after=[got_pack], alias={0: 0}
    )
    other = swap(mine, core=1)
    keep, send = call(
        couple_kernel, [half, half], [VMEM] * 5,
        mine, pack, got_pack, own_inverse, got_inverse,
        scratch=[pltpu.VMEM((2 * lines, LANES), f32)],
    )
    keep, send = call(
        halve_kernel, [part, part], [SMEM] + [VMEM] * 2, quad_weight, keep, swap(send, core=1),
        scratch=[pltpu.VMEM((lines, LANES), f32)],
    )
    came = swap(send, point=1)
    def deliver(x, flip):
        pairs = []
        for i in range(devices):
            h, s, k, c = i // (4 * grid), i // (2 * grid) % 2, i // grid % 2, i % grid
            pairs.append((i, (h * 4 + c) * grid + 2 * (s ^ flip) + k))
        return lax.ppermute(x, AXES, pairs)

    add = functools.partial(call, add_kernel, part, [VMEM] * 2)
    total = add(keep, came)
    out_near, out_far = call(
        output_kernel, [block, block], [VMEM] * 2, mine, other,
        scratch=[pltpu.VMEM((extent, width), bf16)],
        after=[total],
    )
    near, far = deliver(out_near, 0), deliver(out_far, 1)
    total = add(total, swap(total, column=2))
    total = add(total, swap(total, column=1), after=[near])
    quarters = [total, swap(total, side=1), swap(total, point=1), swap(total, side=1, point=1)]
    held = call(hold_kernel, shape(total.shape, f32), [ANY], total, out_specs=ANY, after=[far], alias={0: 0})
    quarters += [swap(x, core=1) for x in [held] + quarters[1:]]
    return call(
        finish_kernel,
        [shape((1, height, count, width), bf16), shape((count, width, width), f32)],
        [VMEM] * 8 + [HBM] + [VMEM] * 2,
        *quarters, live, near, far,
        scratch=[
            pltpu.SMEM(live.shape, jnp.int32),
            pltpu.VMEM((height, count, width), bf16),
            pltpu.VMEM((count, 2 * lines, LANES), f32),
            pltpu.VMEM((count, width, width), f32),
            dma((8,)),
        ],
        out_specs=[HBM, HBM],
    )


def solution(mesh):
    sizes = dict(mesh.shape)
    prow, pcol = ("prow",), ("pcol",)

    def on_device(sigma_rows, panel, live_block_rows, inv_diag, quad_weight):
        height, count, width = panel.shape[1:]
        fits = (
            split
            and sigma_rows.shape[1] == sigma_rows.shape[2] == sizes["pcol"] * height
            and height % LANES == 0
            and count == 2
            and width == BLOCKS * LANES
        )
        body = square if fits else functools.partial(general, prow)
        return body(sigma_rows, panel, live_block_rows, inv_diag, quad_weight)

    split = sizes["hyp"] == 2 and sizes["pcol"] == 4 and sizes["prow"] == 4
    if split:
        prow = ("side", "core")
        mesh = jax.sharding.Mesh(
            mesh.devices.reshape(sizes["hyp"], 2, 2, sizes["pcol"]),
            ("hyp", "side", "core", "pcol"),
        )
    in_specs = (
        P("hyp", prow, pcol),
        P("hyp", prow + pcol, None, None),
        P(None, prow + pcol),
        P("hyp", None, prow + pcol, None),
        P("hyp"),
    )
    out_specs = (P("hyp", prow + pcol, None, None), P())
    return jax.shard_map(
        on_device, mesh=mesh, in_specs=in_specs, out_specs=out_specs, check_vma=False
    )
```

```python
import functools

import jax
import jax.numpy as jnp
from jax import lax
from jax.experimental import pallas as pl
from jax.experimental.pallas import tpu as pltpu
from jax.sharding import PartitionSpec as P

LANES = 128
ROWS = 16
VMEM = pl.BlockSpec(memory_space=pltpu.VMEM)
SMEM = pl.BlockSpec(memory_space=pltpu.SMEM)
ANY = pl.BlockSpec(memory_space=pl.ANY)
HBM = pl.BlockSpec(memory_space=pltpu.HBM)
AXES = ("hyp", "side", "core", "pcol")


def call(kernel, outs, specs, *operands, scratch=(), out_specs=None, after=(), alias={}):
    many = isinstance(outs, (list, tuple))
    count = len(specs)

    def body(*refs):
        kernel(*refs[:count], *refs[count + len(after) :])

    if out_specs is None:
        out_specs = [VMEM] * len(outs) if many else VMEM
    return pl.pallas_call(
        body,
        out_shape=outs,
        in_specs=list(specs) + [ANY] * len(after),
        out_specs=out_specs,
        scratch_shapes=scratch,
        input_output_aliases=alias,
        compiler_params=pltpu.CompilerParams(vmem_limit_bytes=32 * 2**20),
    )(*operands, *after)


def transposed_dot(left, right):
    return lax.dot_general(
        left, right, (((0,), (0,)), ((), ())), preferred_element_type=jnp.float32
    )


BLOCKS = 3
ABOVE = ((0, 1), (0, 2), (1, 2))
HELD = len(ABOVE) + 2


def block_indices():
    shape = (LANES, LANES)
    return lax.broadcasted_iota(jnp.int32, shape, 0), lax.broadcasted_iota(jnp.int32, shape, 1)


def hold_diagonal(first, second, third):
    row, column = block_indices()
    line = jnp.sum(jnp.where(row == column, second, 0.0), axis=0, keepdims=True)
    last = line[:, LANES - 1 :]
    below = jnp.where(row == LANES - 1, line, jnp.where((row == LANES - 2) & (column == 0), last, 0.0))
    upper = column >= row
    return jnp.where(upper, first, second), jnp.where(upper, third, below)


def restore_diagonal(shared, single):
    row, column = block_indices()
    turned, upper = shared.T, column >= row
    line = jnp.where(column[:1] == LANES - 1, single[LANES - 2 : LANES - 1, :1], single[LANES - 1 :, :])
    second = jnp.where(row == column, line, jnp.where(upper, turned, shared))
    return jnp.where(upper, shared, turned), second, jnp.where(upper, single, single.T)


def general(prow, sigma_rows, panel, live_block_rows, inv_diag, quad_weight):
    height, count, width = panel.shape[1:]
    offsets = lax.broadcasted_iota(jnp.int32, (height, count), 0)
    active = offsets < live_block_rows[:, 0][None, :]
    masked = jnp.where(active[:, :, None], panel[0], jnp.zeros_like(panel[0]))
    gathered = lax.all_gather(masked, prow + ("pcol",), axis=0, tiled=True)
    start = lax.axis_index("pcol") * sigma_rows.shape[2]
    column_panel = lax.dynamic_slice_in_dim(gathered, start, sigma_rows.shape[2], 0)
    applied = lax.psum_scatter(
        jnp.dot(
            sigma_rows[0],
            column_panel.reshape(sigma_rows.shape[2], count * width),
            preferred_element_type=jnp.float32,
        ),
        "pcol",
        scatter_dimension=0,
        tiled=True,
    ).reshape(height, count, width)
    half = applied.astype(jnp.bfloat16)
    sigma_panel = jnp.where(active[:, :, None], -half, jnp.zeros_like(half))[None]
    coupling = jnp.einsum(
        "vwg,vwe->wge",
        masked.astype(jnp.float32),
        applied,
        precision=lax.Precision.HIGHEST,
    )
    diagonal = jnp.einsum(
        "skp,skq->spq", inv_diag[0], inv_diag[0], preferred_element_type=jnp.float32
    )
    marginal = lax.psum(quad_weight[0] * (coupling + diagonal), ("hyp",) + prow + ("pcol",))
    return sigma_panel, marginal


def start_kernel(*refs):
    sources, (own, give, own_inverse, limits), pieces = refs[:4], refs[4:8], refs[8:-5]
    buffers, sems = refs[-5:-1], refs[-1]
    copies = [
        pltpu.make_async_copy(source, buffer, sems.at[index])
        for index, (source, buffer) in enumerate(zip(sources, buffers))
    ]
    for copy in copies:
        copy.start()
    for copy in copies[:3]:
        copy.wait()
    live, panel, inverse, matrix = buffers
    first = lax.axis_index("side") == 0
    row = lax.broadcasted_iota(jnp.int32, own.shape, 0)
    rows = panel[0]
    zero = jnp.zeros(own.shape, own.dtype)
    one, two = (jnp.where(row < live[s], rows[:, s, :], zero) for s in range(2))
    height = own.shape[0]
    own[...] = jnp.where(first, one, two)
    give[:height] = jnp.where(first, two, one)
    spare = jnp.zeros((own_inverse.shape[0] - inverse.shape[2], own.shape[1]), own.dtype)
    one, two = (jnp.concatenate([inverse[0, s], spare], 0) for s in range(2))
    own_inverse[...] = jnp.where(first, one, two)
    give[height:] = jnp.where(first, two, one)
    for s in range(limits.shape[0]):
        limits[s] = jnp.full(limits.shape[1:], live[s], limits.dtype)
    copies[3].wait()
    at = 0
    for piece in pieces:
        piece[...] = matrix[0, :, at : at + piece.shape[0]].T
        at += piece.shape[0]


def gather_kernel(*refs):
    blocks, (rows, pack) = refs[:-2], refs[-2:]
    column = lax.axis_index("pcol")
    height = blocks[0].shape[0]
    for index, block in enumerate(blocks):
        spot = jnp.bitwise_xor(column, (0, 2, 1, 3)[index % 4])
        rows[index // 4, pl.ds(pl.multiple_of(spot * height, height), height), :] = block[...]
    pack[...] = rows[jnp.where(column // 2 == lax.axis_index("side"), 0, 1)]


def apply_kernel(rows, *refs):
    pieces, applied = refs[:-1], refs[-1]
    count = len(pieces) // 2
    at = 0
    for own, far in zip(pieces[:count], pieces[count:]):
        total = jnp.dot(own[...], rows[0], preferred_element_type=jnp.float32)
        total += jnp.dot(far[...], rows[1], preferred_element_type=jnp.float32)
        applied[at : at + own.shape[0]] = total
        at += own.shape[0]


def hold_kernel(value, out):
    del value, out


def couple_kernel(applied, pack, got_pack, own_inverse, got_inverse, keep, send, packed):
    core, column = lax.axis_index("core"), lax.axis_index("pcol")
    high = applied[...].astype(jnp.bfloat16)
    low = (applied[...] - high.astype(jnp.float32)).astype(jnp.bfloat16)
    rows = jnp.where(column % 2 == core, pack[...], got_pack[...])
    blocks = {}
    for first in range(BLOCKS):
        left, right = slice(first * LANES, (first + 1) * LANES), slice(first * LANES, None)
        total = transposed_dot(rows[:, left], high[:, right])
        total += transposed_dot(rows[:, left], low[:, right])
        for lines in (own_inverse, got_inverse):
            total += transposed_dot(lines[:, left], lines[:, right])
        for index in range(BLOCKS - first):
            blocks[first, first + index] = total[:, index * LANES : (index + 1) * LANES]
    held = [blocks[place] for place in ABOVE]
    held += hold_diagonal(*(blocks[i, i] for i in range(BLOCKS)))
    for index, block in enumerate(held):
        packed[index * LANES : (index + 1) * LANES, :] = block
    size = keep.shape[0]
    keep[...] = packed[pl.ds(pl.multiple_of(core * size, 8), size), :]
    send[...] = packed[pl.ds(pl.multiple_of((1 - core) * size, 8), size), :]


def halve_kernel(weight, mine, came, keep, send, whole):
    whole[...] = weight[0] * (mine[...] + came[...])
    size, point = keep.shape[0], lax.axis_index("hyp")
    keep[...] = whole[pl.ds(pl.multiple_of(point * size, 8), size), :]
    send[...] = whole[pl.ds(pl.multiple_of((1 - point) * size, 8), size), :]


def output_kernel(mine, other, out_near, out_far, half):
    half[...] = -(mine[...] + other[...]).astype(jnp.bfloat16)
    height, side, core = out_near.shape[0], lax.axis_index("side"), lax.axis_index("core")
    for out, at in ((out_near, side), (out_far, 1 - side)):
        spot = at * 2 + core
        out[...] = half[pl.ds(pl.multiple_of(spot * height, height), height), :]


def add_kernel(mine, came, out):
    out[...] = mine[...] + came[...]


def rows_kernel(limits, near, far, out):
    row = lax.broadcasted_iota(jnp.int32, near.shape, 0)
    first = lax.axis_index("pcol") // 2 == 0
    pair = (jnp.where(first, near[...], far[...]), jnp.where(first, far[...], near[...]))
    for s, value in enumerate(pair):
        out[0, :, s, :] = jnp.where(row < limits[s, :1, :1], value, jnp.zeros(value.shape, value.dtype))


def finish_kernel(*refs):
    parts, (rows, rows_out, out, lines, result, sems) = refs[:8], refs[8:]
    copies = [pltpu.make_async_copy(rows, rows_out, sems.at[0])]
    copies[0].start()
    point, side, core = (lax.axis_index(name) for name in ("hyp", "side", "core"))
    size = parts[0].shape[0]
    for index, part in enumerate(parts):
        owner = core if index < 4 else 1 - core
        node = 1 - side if index % 2 else side
        slot = 1 - point if index // 2 % 2 else point
        start = pl.multiple_of((owner * 2 + slot) * size, 8)
        lines[node, pl.ds(start, size), :] = part[...]
    places = [slice(index * LANES, (index + 1) * LANES) for index in range(BLOCKS)]
    for node in range(2):
        held = [lines[node, index * LANES : (index + 1) * LANES, :] for index in range(HELD)]
        for (a, b), tile in zip(ABOVE, held):
            result[node, places[a], places[b]] = tile
            result[node, places[b], places[a]] = tile.T
        for place, tile in zip(places, restore_diagonal(*held[len(ABOVE) :])):
            result[node, place, place] = tile
        copies.append(pltpu.make_async_copy(result.at[node], out.at[node], sems.at[1 + node]))
        copies[-1].start()
    for copy in copies:
        copy.wait()


def square(sigma_rows, panel, live_block_rows, inv_diag, quad_weight):
    height, count, width = panel.shape[1:]
    grid = lax.axis_size("pcol")
    points = lax.axis_size("hyp")
    f32, bf16 = jnp.float32, jnp.bfloat16
    shape = jax.ShapeDtypeStruct
    dma = pltpu.SemaphoreType.DMA
    stay = functools.partial(pltpu.with_memory_space_constraint, memory_space=pltpu.HBM)
    devices = points * 2 * 2 * grid
    live = live_block_rows[:, 0]

    def swap(x, point=0, side=0, core=0, column=0):
        mask = ((point * 2 + side) * 2 + core) * grid + column
        return lax.ppermute(x, AXES, [(i, i ^ mask) for i in range(devices)])

    extent = sigma_rows.shape[2]
    block = shape((height, width), bf16)
    cuts = (extent // 2, extent // 2)
    size = pl.cdiv(inv_diag.shape[2], ROWS) * ROWS
    own, give, own_inverse, limits, *pieces = call(
        start_kernel,
        [block, shape((height + size, width), bf16), shape((size, width), bf16)]
        + [shape((count, 8, LANES), jnp.int32)]
        + [shape((lines, extent), bf16) for lines in cuts],
        [HBM] * 4,
        *map(stay, (live, panel, inv_diag, sigma_rows)),
        scratch=[pltpu.SMEM(live.shape, jnp.int32)]
        + [pltpu.VMEM(x.shape, bf16) for x in (panel, inv_diag, sigma_rows)]
        + [dma((4,))],
    )
    got = swap(give, side=1)
    got, got_inverse = got[:height], got[height:]
    blocks = []
    for one in (own, got):
        two = swap(one, column=2)
        blocks += [one, two, swap(one, column=1), swap(two, column=1)]
    far = [swap(piece, side=1) for piece in pieces]


    rows, pack = call(
        gather_kernel,
        [shape((2, extent, width), bf16), shape((extent, width), bf16)],
        [VMEM] * len(blocks),
        *blocks,
        after=far,
    )
    got_pack = swap(pack, core=1)
    mine = call(
        apply_kernel, shape((extent, width), f32), [VMEM] * (1 + 2 * len(cuts)), rows, *pieces, *far
    )
    lines = HELD * LANES // 2
    part, half = shape((lines // 2, LANES), f32), shape((lines, LANES), f32)
    mine = call(
        hold_kernel, shape(mine.shape, f32), [ANY], mine, out_specs=ANY, after=[got_pack], alias={0: 0}
    )
    other = swap(mine, core=1)
    keep, send = call(
        couple_kernel, [half, half], [VMEM] * 5,
        mine, pack, got_pack, own_inverse, got_inverse,
        scratch=[pltpu.VMEM((2 * lines, LANES), f32)],
    )
    keep, send = call(
        halve_kernel, [part, part], [SMEM] + [VMEM] * 2, quad_weight, keep, swap(send, core=1),
        scratch=[pltpu.VMEM((lines, LANES), f32)],
    )
    came = swap(send, point=1)
    def deliver(x, flip):
        pairs = []
        for i in range(devices):
            h, s, k, c = i // (4 * grid), i // (2 * grid) % 2, i // grid % 2, i % grid
            pairs.append((i, (h * 4 + c) * grid + 2 * (s ^ flip) + k))
        return lax.ppermute(x, AXES, pairs)

    add = functools.partial(call, add_kernel, part, [VMEM] * 2)
    total = add(keep, came)
    out_near, out_far = call(
        output_kernel, [block, block], [VMEM] * 2, mine, other,
        scratch=[pltpu.VMEM((extent, width), bf16)],
        after=[total],
    )
    near, far = deliver(out_near, 0), deliver(out_far, 1)
    total = add(total, swap(total, column=2))
    total = add(total, swap(total, column=1), after=[near])
    quarters = [total, swap(total, side=1), swap(total, point=1), swap(total, side=1, point=1)]
    rows = call(
        rows_kernel, shape((1, height, count, width), bf16), [VMEM] * 3, limits, near, far
    )
    held = call(hold_kernel, shape(total.shape, f32), [ANY], total, out_specs=ANY, after=[rows], alias={0: 0})
    quarters += [swap(x, core=1) for x in [held] + quarters[1:]]
    return call(
        finish_kernel,
        [shape((1, height, count, width), bf16), shape((count, width, width), f32)],
        [VMEM] * 9,
        *quarters, rows,
        scratch=[
            pltpu.VMEM((count, 2 * lines, LANES), f32),
            pltpu.VMEM((count, width, width), f32),
            dma((3,)),
        ],
        out_specs=[HBM, HBM],
    )


def solution(mesh):
    sizes = dict(mesh.shape)
    prow, pcol = ("prow",), ("pcol",)

    def on_device(sigma_rows, panel, live_block_rows, inv_diag, quad_weight):
        height, count, width = panel.shape[1:]
        fits = (
            split
            and sigma_rows.shape[1] == sigma_rows.shape[2] == sizes["pcol"] * height
            and height % LANES == 0
            and count == 2
            and width == BLOCKS * LANES
        )
        body = square if fits else functools.partial(general, prow)
        return body(sigma_rows, panel, live_block_rows, inv_diag, quad_weight)

    split = sizes["hyp"] == 2 and sizes["pcol"] == 4 and sizes["prow"] == 4
    if split:
        prow = ("side", "core")
        mesh = jax.sharding.Mesh(
            mesh.devices.reshape(sizes["hyp"], 2, 2, sizes["pcol"]),
            ("hyp", "side", "core", "pcol"),
        )
    in_specs = (
        P("hyp", prow, pcol),
        P("hyp", prow + pcol, None, None),
        P(None, prow + pcol),
        P("hyp", None, prow + pcol, None),
        P("hyp"),
    )
    out_specs = (P("hyp", prow + pcol, None, None), P())
    return jax.shard_map(
        on_device, mesh=mesh, in_specs=in_specs, out_specs=out_specs, check_vma=False
    )
```

```python
import functools

import jax
import jax.numpy as jnp
from jax import lax
from jax.experimental import pallas as pl
from jax.experimental.pallas import tpu as pltpu
from jax.sharding import PartitionSpec as P

LANES = 128
ROWS = 16
VMEM = pl.BlockSpec(memory_space=pltpu.VMEM)
SMEM = pl.BlockSpec(memory_space=pltpu.SMEM)
ANY = pl.BlockSpec(memory_space=pl.ANY)
HBM = pl.BlockSpec(memory_space=pltpu.HBM)
AXES = ("hyp", "side", "core", "pcol")


def call(kernel, outs, specs, *operands, scratch=(), out_specs=None, after=(), alias={}):
    many = isinstance(outs, (list, tuple))
    count = len(specs)

    def body(*refs):
        kernel(*refs[:count], *refs[count + len(after) :])

    if out_specs is None:
        out_specs = [VMEM] * len(outs) if many else VMEM
    return pl.pallas_call(
        body,
        out_shape=outs,
        in_specs=list(specs) + [ANY] * len(after),
        out_specs=out_specs,
        scratch_shapes=scratch,
        input_output_aliases=alias,
        compiler_params=pltpu.CompilerParams(vmem_limit_bytes=32 * 2**20),
    )(*operands, *after)


def transposed_dot(left, right):
    return lax.dot_general(
        left, right, (((0,), (0,)), ((), ())), preferred_element_type=jnp.float32
    )


BLOCKS = 3
ABOVE = ((0, 1), (0, 2), (1, 2))
HELD = len(ABOVE) + 2


def block_indices():
    shape = (LANES, LANES)
    return lax.broadcasted_iota(jnp.int32, shape, 0), lax.broadcasted_iota(jnp.int32, shape, 1)


def hold_diagonal(first, second, third):
    row, column = block_indices()
    line = jnp.sum(jnp.where(row == column, second, 0.0), axis=0, keepdims=True)
    last = line[:, LANES - 1 :]
    below = jnp.where(row == LANES - 1, line, jnp.where((row == LANES - 2) & (column == 0), last, 0.0))
    upper = column >= row
    return jnp.where(upper, first, second), jnp.where(upper, third, below)


def restore_diagonal(shared, single):
    row, column = block_indices()
    turned, upper = shared.T, column >= row
    line = jnp.where(column[:1] == LANES - 1, single[LANES - 2 : LANES - 1, :1], single[LANES - 1 :, :])
    second = jnp.where(row == column, line, jnp.where(upper, turned, shared))
    return jnp.where(upper, shared, turned), second, jnp.where(upper, single, single.T)


def general(prow, sigma_rows, panel, live_block_rows, inv_diag, quad_weight):
    height, count, width = panel.shape[1:]
    offsets = lax.broadcasted_iota(jnp.int32, (height, count), 0)
    active = offsets < live_block_rows[:, 0][None, :]
    masked = jnp.where(active[:, :, None], panel[0], jnp.zeros_like(panel[0]))
    gathered = lax.all_gather(masked, prow + ("pcol",), axis=0, tiled=True)
    start = lax.axis_index("pcol") * sigma_rows.shape[2]
    column_panel = lax.dynamic_slice_in_dim(gathered, start, sigma_rows.shape[2], 0)
    applied = lax.psum_scatter(
        jnp.dot(
            sigma_rows[0],
            column_panel.reshape(sigma_rows.shape[2], count * width),
            preferred_element_type=jnp.float32,
        ),
        "pcol",
        scatter_dimension=0,
        tiled=True,
    ).reshape(height, count, width)
    half = applied.astype(jnp.bfloat16)
    sigma_panel = jnp.where(active[:, :, None], -half, jnp.zeros_like(half))[None]
    coupling = jnp.einsum(
        "vwg,vwe->wge",
        masked.astype(jnp.float32),
        applied,
        precision=lax.Precision.HIGHEST,
    )
    diagonal = jnp.einsum(
        "skp,skq->spq", inv_diag[0], inv_diag[0], preferred_element_type=jnp.float32
    )
    marginal = lax.psum(quad_weight[0] * (coupling + diagonal), ("hyp",) + prow + ("pcol",))
    return sigma_panel, marginal


def start_kernel(*refs):
    sources, (own, give, own_inverse, limits), pieces = refs[:4], refs[4:8], refs[8:-5]
    buffers, sems = refs[-5:-1], refs[-1]
    copies = [
        pltpu.make_async_copy(source, buffer, sems.at[index])
        for index, (source, buffer) in enumerate(zip(sources, buffers))
    ]
    for copy in copies:
        copy.start()
    for copy in copies[:3]:
        copy.wait()
    live, panel, inverse, matrix = buffers
    first = lax.axis_index("side") == 0
    row = lax.broadcasted_iota(jnp.int32, own.shape, 0)
    rows = panel[0]
    zero = jnp.zeros(own.shape, own.dtype)
    one, two = (jnp.where(row < live[s], rows[:, s, :], zero) for s in range(2))
    height = own.shape[0]
    own[...] = jnp.where(first, one, two)
    give[:height] = jnp.where(first, two, one)
    spare = jnp.zeros((own_inverse.shape[0] - inverse.shape[2], own.shape[1]), own.dtype)
    one, two = (jnp.concatenate([inverse[0, s], spare], 0) for s in range(2))
    own_inverse[...] = jnp.where(first, one, two)
    give[height:] = jnp.where(first, two, one)
    for s in range(limits.shape[0]):
        limits[s] = jnp.full(limits.shape[1:], live[s], limits.dtype)
    copies[3].wait()
    at = 0
    for piece in pieces:
        piece[...] = matrix[0, :, at : at + piece.shape[0]].T
        at += piece.shape[0]


def gather_kernel(*refs):
    blocks, (rows, pack) = refs[:-2], refs[-2:]
    column = lax.axis_index("pcol")
    height = blocks[0].shape[0]
    for index, block in enumerate(blocks):
        spot = jnp.bitwise_xor(column, (0, 2, 1, 3)[index % 4])
        rows[index // 4, pl.ds(pl.multiple_of(spot * height, height), height), :] = block[...]
    pack[...] = rows[jnp.where(column // 2 == lax.axis_index("side"), 0, 1)]


def apply_kernel(rows, *refs):
    pieces, applied = refs[:-1], refs[-1]
    count = len(pieces) // 2
    at = 0
    for own, far in zip(pieces[:count], pieces[count:]):
        total = jnp.dot(own[...], rows[0], preferred_element_type=jnp.float32)
        total += jnp.dot(far[...], rows[1], preferred_element_type=jnp.float32)
        applied[at : at + own.shape[0]] = total
        at += own.shape[0]


def hold_kernel(value, out):
    del value, out


def couple_kernel(applied, pack, got_pack, own_inverse, got_inverse, keep, send, packed):
    core, column = lax.axis_index("core"), lax.axis_index("pcol")
    high = applied[...].astype(jnp.bfloat16)
    low = (applied[...] - high.astype(jnp.float32)).astype(jnp.bfloat16)
    rows = jnp.where(column % 2 == core, pack[...], got_pack[...])
    blocks = {}
    for first in range(BLOCKS):
        left, right = slice(first * LANES, (first + 1) * LANES), slice(first * LANES, None)
        total = transposed_dot(rows[:, left], high[:, right])
        total += transposed_dot(rows[:, left], low[:, right])
        for lines in (own_inverse, got_inverse):
            total += transposed_dot(lines[:, left], lines[:, right])
        for index in range(BLOCKS - first):
            blocks[first, first + index] = total[:, index * LANES : (index + 1) * LANES]
    held = [blocks[place] for place in ABOVE]
    held += hold_diagonal(*(blocks[i, i] for i in range(BLOCKS)))
    for index, block in enumerate(held):
        packed[index * LANES : (index + 1) * LANES, :] = block
    size = keep.shape[0]
    keep[...] = packed[pl.ds(pl.multiple_of(core * size, 8), size), :]
    send[...] = packed[pl.ds(pl.multiple_of((1 - core) * size, 8), size), :]


def halve_kernel(weight, mine, came, keep, send, whole):
    whole[...] = weight[0] * (mine[...] + came[...])
    size, point = keep.shape[0], lax.axis_index("hyp")
    keep[...] = whole[pl.ds(pl.multiple_of(point * size, 8), size), :]
    send[...] = whole[pl.ds(pl.multiple_of((1 - point) * size, 8), size), :]


def output_kernel(mine, other, out_near, out_far, half):
    half[...] = -(mine[...] + other[...]).astype(jnp.bfloat16)
    height, side, core = out_near.shape[0], lax.axis_index("side"), lax.axis_index("core")
    for out, at in ((out_near, side), (out_far, 1 - side)):
        spot = at * 2 + core
        out[...] = half[pl.ds(pl.multiple_of(spot * height, height), height), :]


def add_kernel(mine, came, out):
    out[...] = mine[...] + came[...]


def rows_kernel(limits, near, far, out):
    row = lax.broadcasted_iota(jnp.int32, near.shape, 0)
    first = lax.axis_index("pcol") // 2 == 0
    pair = (jnp.where(first, near[...], far[...]), jnp.where(first, far[...], near[...]))
    for s, value in enumerate(pair):
        out[0, :, s, :] = jnp.where(row < limits[s, :1, :1], value, jnp.zeros(value.shape, value.dtype))


def stack_kernel(*refs):
    for index, ref in enumerate(refs[:-1]):
        refs[-1][index] = ref[...]


def finish_kernel(own, other, rows, rows_out, out, lines, result, sems):
    copies = [pltpu.make_async_copy(rows, rows_out, sems.at[0])]
    copies[0].start()
    point, side, core = (lax.axis_index(name) for name in ("hyp", "side", "core"))
    size = own.shape[1]
    for parts, owner in ((own, core), (other, 1 - core)):
        for index in range(own.shape[0]):
            node = 1 - side if index % 2 else side
            slot = 1 - point if index // 2 else point
            start = pl.multiple_of((owner * 2 + slot) * size, 8)
            lines[node, pl.ds(start, size), :] = parts[index]
    places = [slice(index * LANES, (index + 1) * LANES) for index in range(BLOCKS)]
    for node in range(2):
        held = [lines[node, index * LANES : (index + 1) * LANES, :] for index in range(HELD)]
        for (a, b), tile in zip(ABOVE, held):
            result[node, places[a], places[b]] = tile
            result[node, places[b], places[a]] = tile.T
        for place, tile in zip(places, restore_diagonal(*held[len(ABOVE) :])):
            result[node, place, place] = tile
        copies.append(pltpu.make_async_copy(result.at[node], out.at[node], sems.at[1 + node]))
        copies[-1].start()
    for copy in copies:
        copy.wait()


def square(sigma_rows, panel, live_block_rows, inv_diag, quad_weight):
    height, count, width = panel.shape[1:]
    grid = lax.axis_size("pcol")
    points = lax.axis_size("hyp")
    f32, bf16 = jnp.float32, jnp.bfloat16
    shape = jax.ShapeDtypeStruct
    dma = pltpu.SemaphoreType.DMA
    stay = functools.partial(pltpu.with_memory_space_constraint, memory_space=pltpu.HBM)
    devices = points * 2 * 2 * grid
    live = live_block_rows[:, 0]

    def swap(x, point=0, side=0, core=0, column=0):
        mask = ((point * 2 + side) * 2 + core) * grid + column
        return lax.ppermute(x, AXES, [(i, i ^ mask) for i in range(devices)])

    extent = sigma_rows.shape[2]
    block = shape((height, width), bf16)
    cuts = (extent // 2, extent // 2)
    size = pl.cdiv(inv_diag.shape[2], ROWS) * ROWS
    own, give, own_inverse, limits, *pieces = call(
        start_kernel,
        [block, shape((height + size, width), bf16), shape((size, width), bf16)]
        + [shape((count, 8, LANES), jnp.int32)]
        + [shape((lines, extent), bf16) for lines in cuts],
        [HBM] * 4,
        *map(stay, (live, panel, inv_diag, sigma_rows)),
        scratch=[pltpu.SMEM(live.shape, jnp.int32)]
        + [pltpu.VMEM(x.shape, bf16) for x in (panel, inv_diag, sigma_rows)]
        + [dma((4,))],
    )
    got = swap(give, side=1)
    got, got_inverse = got[:height], got[height:]
    blocks = []
    for one in (own, got):
        two = swap(one, column=2)
        blocks += [one, two, swap(one, column=1), swap(two, column=1)]
    far = [swap(piece, side=1) for piece in pieces]


    rows, pack = call(
        gather_kernel,
        [shape((2, extent, width), bf16), shape((extent, width), bf16)],
        [VMEM] * len(blocks),
        *blocks,
        after=far,
    )
    got_pack = swap(pack, core=1)
    mine = call(
        apply_kernel, shape((extent, width), f32), [VMEM] * (1 + 2 * len(cuts)), rows, *pieces, *far
    )
    lines = HELD * LANES // 2
    part, half = shape((lines // 2, LANES), f32), shape((lines, LANES), f32)
    mine = call(
        hold_kernel, shape(mine.shape, f32), [ANY], mine, out_specs=ANY, after=[got_pack], alias={0: 0}
    )
    other = swap(mine, core=1)
    keep, send = call(
        couple_kernel, [half, half], [VMEM] * 5,
        mine, pack, got_pack, own_inverse, got_inverse,
        scratch=[pltpu.VMEM((2 * lines, LANES), f32)],
    )
    keep, send = call(
        halve_kernel, [part, part], [SMEM] + [VMEM] * 2, quad_weight, keep, swap(send, core=1),
        scratch=[pltpu.VMEM((lines, LANES), f32)],
    )
    came = swap(send, point=1)
    def deliver(x, flip):
        pairs = []
        for i in range(devices):
            h, s, k, c = i // (4 * grid), i // (2 * grid) % 2, i // grid % 2, i % grid
            pairs.append((i, (h * 4 + c) * grid + 2 * (s ^ flip) + k))
        return lax.ppermute(x, AXES, pairs)

    add = functools.partial(call, add_kernel, part, [VMEM] * 2)
    total = add(keep, came)
    out_near, out_far = call(
        output_kernel, [block, block], [VMEM] * 2, mine, other,
        scratch=[pltpu.VMEM((extent, width), bf16)],
        after=[total],
    )
    near, far = deliver(out_near, 0), deliver(out_far, 1)
    total = add(total, swap(total, column=2))
    total = add(total, swap(total, column=1), after=[near])
    quarters = [total, swap(total, side=1), swap(total, point=1), swap(total, side=1, point=1)]
    rows = call(
        rows_kernel, shape((1, height, count, width), bf16), [VMEM] * 3, limits, near, far
    )
    quarters = call(
        stack_kernel, shape((len(quarters), *part.shape), f32), [VMEM] * len(quarters), *quarters, after=[rows]
    )
    return call(
        finish_kernel,
        [shape((1, height, count, width), bf16), shape((count, width, width), f32)],
        [VMEM] * 3,
        quarters, swap(quarters, core=1), rows,
        scratch=[
            pltpu.VMEM((count, 2 * lines, LANES), f32),
            pltpu.VMEM((count, width, width), f32),
            dma((3,)),
        ],
        out_specs=[HBM, HBM],
    )


def solution(mesh):
    sizes = dict(mesh.shape)
    prow, pcol = ("prow",), ("pcol",)

    def on_device(sigma_rows, panel, live_block_rows, inv_diag, quad_weight):
        height, count, width = panel.shape[1:]
        fits = (
            split
            and sigma_rows.shape[1] == sigma_rows.shape[2] == sizes["pcol"] * height
            and height % LANES == 0
            and count == 2
            and width == BLOCKS * LANES
        )
        body = square if fits else functools.partial(general, prow)
        return body(sigma_rows, panel, live_block_rows, inv_diag, quad_weight)

    split = sizes["hyp"] == 2 and sizes["pcol"] == 4 and sizes["prow"] == 4
    if split:
        prow = ("side", "core")
        mesh = jax.sharding.Mesh(
            mesh.devices.reshape(sizes["hyp"], 2, 2, sizes["pcol"]),
            ("hyp", "side", "core", "pcol"),
        )
    in_specs = (
        P("hyp", prow, pcol),
        P("hyp", prow + pcol, None, None),
        P(None, prow + pcol),
        P("hyp", None, prow + pcol, None),
        P("hyp"),
    )
    out_specs = (P("hyp", prow + pcol, None, None), P())
    return jax.shard_map(
        on_device, mesh=mesh, in_specs=in_specs, out_specs=out_specs, check_vma=False
    )
```

```python
import functools

import jax
import jax.numpy as jnp
from jax import lax
from jax.experimental import pallas as pl
from jax.experimental.pallas import tpu as pltpu
from jax.sharding import PartitionSpec as P

LANES = 128
ROWS = 16
VMEM = pl.BlockSpec(memory_space=pltpu.VMEM)
SMEM = pl.BlockSpec(memory_space=pltpu.SMEM)
ANY = pl.BlockSpec(memory_space=pl.ANY)
HBM = pl.BlockSpec(memory_space=pltpu.HBM)
AXES = ("hyp", "side", "core", "pcol")


def call(kernel, outs, specs, *operands, scratch=(), out_specs=None, after=(), alias={}):
    many = isinstance(outs, (list, tuple))
    count = len(specs)

    def body(*refs):
        kernel(*refs[:count], *refs[count + len(after) :])

    if out_specs is None:
        out_specs = [VMEM] * len(outs) if many else VMEM
    return pl.pallas_call(
        body,
        out_shape=outs,
        in_specs=list(specs) + [ANY] * len(after),
        out_specs=out_specs,
        scratch_shapes=scratch,
        input_output_aliases=alias,
        compiler_params=pltpu.CompilerParams(vmem_limit_bytes=32 * 2**20),
    )(*operands, *after)


def transposed_dot(left, right):
    return lax.dot_general(
        left, right, (((0,), (0,)), ((), ())), preferred_element_type=jnp.float32
    )


BLOCKS = 3
ABOVE = ((0, 1), (0, 2), (1, 2))
HELD = len(ABOVE) + 2


def block_indices():
    shape = (LANES, LANES)
    return lax.broadcasted_iota(jnp.int32, shape, 0), lax.broadcasted_iota(jnp.int32, shape, 1)


def hold_diagonal(first, second, third):
    row, column = block_indices()
    line = jnp.sum(jnp.where(row == column, second, 0.0), axis=0, keepdims=True)
    last = line[:, LANES - 1 :]
    below = jnp.where(row == LANES - 1, line, jnp.where((row == LANES - 2) & (column == 0), last, 0.0))
    upper = column >= row
    return jnp.where(upper, first, second), jnp.where(upper, third, below)


def restore_diagonal(shared, single):
    row, column = block_indices()
    turned, upper = shared.T, column >= row
    line = jnp.where(column[:1] == LANES - 1, single[LANES - 2 : LANES - 1, :1], single[LANES - 1 :, :])
    second = jnp.where(row == column, line, jnp.where(upper, turned, shared))
    return jnp.where(upper, shared, turned), second, jnp.where(upper, single, single.T)


def general(prow, sigma_rows, panel, live_block_rows, inv_diag, quad_weight):
    height, count, width = panel.shape[1:]
    offsets = lax.broadcasted_iota(jnp.int32, (height, count), 0)
    active = offsets < live_block_rows[:, 0][None, :]
    masked = jnp.where(active[:, :, None], panel[0], jnp.zeros_like(panel[0]))
    gathered = lax.all_gather(masked, prow + ("pcol",), axis=0, tiled=True)
    start = lax.axis_index("pcol") * sigma_rows.shape[2]
    column_panel = lax.dynamic_slice_in_dim(gathered, start, sigma_rows.shape[2], 0)
    applied = lax.psum_scatter(
        jnp.dot(
            sigma_rows[0],
            column_panel.reshape(sigma_rows.shape[2], count * width),
            preferred_element_type=jnp.float32,
        ),
        "pcol",
        scatter_dimension=0,
        tiled=True,
    ).reshape(height, count, width)
    half = applied.astype(jnp.bfloat16)
    sigma_panel = jnp.where(active[:, :, None], -half, jnp.zeros_like(half))[None]
    coupling = jnp.einsum(
        "vwg,vwe->wge",
        masked.astype(jnp.float32),
        applied,
        precision=lax.Precision.HIGHEST,
    )
    diagonal = jnp.einsum(
        "skp,skq->spq", inv_diag[0], inv_diag[0], preferred_element_type=jnp.float32
    )
    marginal = lax.psum(quad_weight[0] * (coupling + diagonal), ("hyp",) + prow + ("pcol",))
    return sigma_panel, marginal


def start_kernel(*refs):
    sources, (own, give, own_inverse, limits), pieces = refs[:4], refs[4:8], refs[8:-5]
    buffers, sems = refs[-5:-1], refs[-1]
    copies = [
        pltpu.make_async_copy(source, buffer, sems.at[index])
        for index, (source, buffer) in enumerate(zip(sources, buffers))
    ]
    for copy in copies:
        copy.start()
    for copy in copies[:3]:
        copy.wait()
    live, panel, inverse, matrix = buffers
    first = lax.axis_index("side") == 0
    row = lax.broadcasted_iota(jnp.int32, own.shape, 0)
    rows = panel[0]
    zero = jnp.zeros(own.shape, own.dtype)
    one, two = (jnp.where(row < live[s], rows[:, s, :], zero) for s in range(2))
    height = own.shape[0]
    own[...] = jnp.where(first, one, two)
    give[:height] = jnp.where(first, two, one)
    spare = jnp.zeros((own_inverse.shape[0] - inverse.shape[2], own.shape[1]), own.dtype)
    one, two = (jnp.concatenate([inverse[0, s], spare], 0) for s in range(2))
    own_inverse[...] = jnp.where(first, one, two)
    give[height:] = jnp.where(first, two, one)
    for s in range(limits.shape[0]):
        limits[s] = jnp.full(limits.shape[1:], live[s], limits.dtype)
    copies[3].wait()
    at = 0
    for piece in pieces:
        piece[...] = matrix[0, :, at : at + piece.shape[0]].T
        at += piece.shape[0]


def gather_kernel(*refs):
    blocks, (rows, pack) = refs[:-2], refs[-2:]
    column = lax.axis_index("pcol")
    height = blocks[0].shape[0]
    for index, block in enumerate(blocks):
        spot = jnp.bitwise_xor(column, (0, 2, 1, 3)[index % 4])
        rows[index // 4, pl.ds(pl.multiple_of(spot * height, height), height), :] = block[...]
    pack[...] = rows[jnp.where(column // 2 == lax.axis_index("side"), 0, 1)]


def apply_kernel(rows, *refs):
    pieces, applied = refs[:-1], refs[-1]
    count = len(pieces) // 2
    at = 0
    for own, far in zip(pieces[:count], pieces[count:]):
        total = jnp.dot(own[...], rows[0], preferred_element_type=jnp.float32)
        total += jnp.dot(far[...], rows[1], preferred_element_type=jnp.float32)
        applied[at : at + own.shape[0]] = total
        at += own.shape[0]


def hold_kernel(value, out):
    del value, out


def couple_kernel(applied, pack, got_pack, own_inverse, got_inverse, keep, send, packed):
    core, column = lax.axis_index("core"), lax.axis_index("pcol")
    high = applied[...].astype(jnp.bfloat16)
    low = (applied[...] - high.astype(jnp.float32)).astype(jnp.bfloat16)
    rows = jnp.where(column % 2 == core, pack[...], got_pack[...])
    blocks = {}
    for first in range(BLOCKS):
        left, right = slice(first * LANES, (first + 1) * LANES), slice(first * LANES, None)
        total = transposed_dot(rows[:, left], high[:, right])
        total += transposed_dot(rows[:, left], low[:, right])
        for lines in (own_inverse, got_inverse):
            total += transposed_dot(lines[:, left], lines[:, right])
        for index in range(BLOCKS - first):
            blocks[first, first + index] = total[:, index * LANES : (index + 1) * LANES]
    held = [blocks[place] for place in ABOVE]
    held += hold_diagonal(*(blocks[i, i] for i in range(BLOCKS)))
    for index, block in enumerate(held):
        packed[index * LANES : (index + 1) * LANES, :] = block
    size = keep.shape[0]
    keep[...] = packed[pl.ds(pl.multiple_of(core * size, 8), size), :]
    send[...] = packed[pl.ds(pl.multiple_of((1 - core) * size, 8), size), :]


def halve_kernel(weight, mine, came, keep, send, whole):
    whole[...] = weight[0] * (mine[...] + came[...])
    size, point = keep.shape[0], lax.axis_index("hyp")
    keep[...] = whole[pl.ds(pl.multiple_of(point * size, 8), size), :]
    send[...] = whole[pl.ds(pl.multiple_of((1 - point) * size, 8), size), :]


def output_kernel(mine, other, out_near, out_far, half):
    half[...] = -(mine[...] + other[...]).astype(jnp.bfloat16)
    height, side, core = out_near.shape[0], lax.axis_index("side"), lax.axis_index("core")
    for out, at in ((out_near, side), (out_far, 1 - side)):
        spot = at * 2 + core
        out[...] = half[pl.ds(pl.multiple_of(spot * height, height), height), :]


def add_kernel(mine, came, out):
    out[...] = mine[...] + came[...]


def rows_kernel(limits, near, far, out):
    row = lax.broadcasted_iota(jnp.int32, near.shape, 0)
    first = lax.axis_index("pcol") // 2 == 0
    pair = (jnp.where(first, near[...], far[...]), jnp.where(first, far[...], near[...]))
    for s, value in enumerate(pair):
        out[0, :, s, :] = jnp.where(row < limits[s, :1, :1], value, jnp.zeros(value.shape, value.dtype))


def add_four_kernel(a, b, c, d, out):
    out[...] = (a[...] + b[...]) + (c[...] + d[...])


def stack_kernel(*refs):
    for index, ref in enumerate(refs[:-1]):
        refs[-1][index] = ref[...]


def finish_kernel(own, other, rows, rows_out, out, lines, result, sems):
    copies = [pltpu.make_async_copy(rows, rows_out, sems.at[0])]
    copies[0].start()
    point, side, core = (lax.axis_index(name) for name in ("hyp", "side", "core"))
    size = own.shape[1]
    for parts, owner in ((own, core), (other, 1 - core)):
        for index in range(own.shape[0]):
            node = 1 - side if index % 2 else side
            slot = 1 - point if index // 2 else point
            start = pl.multiple_of((owner * 2 + slot) * size, 8)
            lines[node, pl.ds(start, size), :] = parts[index]
    places = [slice(index * LANES, (index + 1) * LANES) for index in range(BLOCKS)]
    for node in range(2):
        held = [lines[node, index * LANES : (index + 1) * LANES, :] for index in range(HELD)]
        for (a, b), tile in zip(ABOVE, held):
            result[node, places[a], places[b]] = tile
            result[node, places[b], places[a]] = tile.T
        for place, tile in zip(places, restore_diagonal(*held[len(ABOVE) :])):
            result[node, place, place] = tile
        copies.append(pltpu.make_async_copy(result.at[node], out.at[node], sems.at[1 + node]))
        copies[-1].start()
    for copy in copies:
        copy.wait()


def square(sigma_rows, panel, live_block_rows, inv_diag, quad_weight):
    height, count, width = panel.shape[1:]
    grid = lax.axis_size("pcol")
    points = lax.axis_size("hyp")
    f32, bf16 = jnp.float32, jnp.bfloat16
    shape = jax.ShapeDtypeStruct
    dma = pltpu.SemaphoreType.DMA
    stay = functools.partial(pltpu.with_memory_space_constraint, memory_space=pltpu.HBM)
    devices = points * 2 * 2 * grid
    live = live_block_rows[:, 0]

    def swap(x, point=0, side=0, core=0, column=0):
        mask = ((point * 2 + side) * 2 + core) * grid + column
        return lax.ppermute(x, AXES, [(i, i ^ mask) for i in range(devices)])

    extent = sigma_rows.shape[2]
    block = shape((height, width), bf16)
    cuts = (extent // 2, extent // 2)
    size = pl.cdiv(inv_diag.shape[2], ROWS) * ROWS
    own, give, own_inverse, limits, *pieces = call(
        start_kernel,
        [block, shape((height + size, width), bf16), shape((size, width), bf16)]
        + [shape((count, 8, LANES), jnp.int32)]
        + [shape((lines, extent), bf16) for lines in cuts],
        [HBM] * 4,
        *map(stay, (live, panel, inv_diag, sigma_rows)),
        scratch=[pltpu.SMEM(live.shape, jnp.int32)]
        + [pltpu.VMEM(x.shape, bf16) for x in (panel, inv_diag, sigma_rows)]
        + [dma((4,))],
    )
    got = swap(give, side=1)
    got, got_inverse = got[:height], got[height:]
    blocks = []
    for one in (own, got):
        two = swap(one, column=2)
        blocks += [one, two, swap(one, column=1), swap(two, column=1)]
    far = [swap(piece, side=1) for piece in pieces]


    rows, pack = call(
        gather_kernel,
        [shape((2, extent, width), bf16), shape((extent, width), bf16)],
        [VMEM] * len(blocks),
        *blocks,
        after=far,
    )
    got_pack = swap(pack, core=1)
    mine = call(
        apply_kernel, shape((extent, width), f32), [VMEM] * (1 + 2 * len(cuts)), rows, *pieces, *far
    )
    lines = HELD * LANES // 2
    part, half = shape((lines // 2, LANES), f32), shape((lines, LANES), f32)
    mine = call(
        hold_kernel, shape(mine.shape, f32), [ANY], mine, out_specs=ANY, after=[got_pack], alias={0: 0}
    )
    other = swap(mine, core=1)
    keep, send = call(
        couple_kernel, [half, half], [VMEM] * 5,
        mine, pack, got_pack, own_inverse, got_inverse,
        scratch=[pltpu.VMEM((2 * lines, LANES), f32)],
    )
    keep, send = call(
        halve_kernel, [part, part], [SMEM] + [VMEM] * 2, quad_weight, keep, swap(send, core=1),
        scratch=[pltpu.VMEM((lines, LANES), f32)],
    )
    def deliver(x, flip):
        pairs = []
        for i in range(devices):
            h, s, k, c = i // (4 * grid), i // (2 * grid) % 2, i // grid % 2, i % grid
            pairs.append((i, (h * 4 + c) * grid + 2 * (s ^ flip) + k))
        return lax.ppermute(x, AXES, pairs)

    total = call(
        add_four_kernel, part, [VMEM] * 4,
        keep, swap(send, point=1), swap(keep, column=1), swap(send, point=1, column=1),
    )
    out_near, out_far = call(
        output_kernel, [block, block], [VMEM] * 2, mine, other,
        scratch=[pltpu.VMEM((extent, width), bf16)],
        after=[total],
    )
    near, far = deliver(out_near, 0), deliver(out_far, 1)
    total = call(add_kernel, part, [VMEM] * 2, total, swap(total, column=2))
    quarters = [total, swap(total, side=1), swap(total, point=1), swap(total, side=1, point=1)]
    rows = call(
        rows_kernel, shape((1, height, count, width), bf16), [VMEM] * 3, limits, near, far
    )
    quarters = call(
        stack_kernel, shape((len(quarters), *part.shape), f32), [VMEM] * len(quarters), *quarters, after=[rows]
    )
    return call(
        finish_kernel,
        [shape((1, height, count, width), bf16), shape((count, width, width), f32)],
        [VMEM] * 3,
        quarters, swap(quarters, core=1), rows,
        scratch=[
            pltpu.VMEM((count, 2 * lines, LANES), f32),
            pltpu.VMEM((count, width, width), f32),
            dma((3,)),
        ],
        out_specs=[HBM, HBM],
    )


def solution(mesh):
    sizes = dict(mesh.shape)
    prow, pcol = ("prow",), ("pcol",)

    def on_device(sigma_rows, panel, live_block_rows, inv_diag, quad_weight):
        height, count, width = panel.shape[1:]
        fits = (
            split
            and sigma_rows.shape[1] == sigma_rows.shape[2] == sizes["pcol"] * height
            and height % LANES == 0
            and count == 2
            and width == BLOCKS * LANES
        )
        body = square if fits else functools.partial(general, prow)
        return body(sigma_rows, panel, live_block_rows, inv_diag, quad_weight)

    split = sizes["hyp"] == 2 and sizes["pcol"] == 4 and sizes["prow"] == 4
    if split:
        prow = ("side", "core")
        mesh = jax.sharding.Mesh(
            mesh.devices.reshape(sizes["hyp"], 2, 2, sizes["pcol"]),
            ("hyp", "side", "core", "pcol"),
        )
    in_specs = (
        P("hyp", prow, pcol),
        P("hyp", prow + pcol, None, None),
        P(None, prow + pcol),
        P("hyp", None, prow + pcol, None),
        P("hyp"),
    )
    out_specs = (P("hyp", prow + pcol, None, None), P())
    return jax.shard_map(
        on_device, mesh=mesh, in_specs=in_specs, out_specs=out_specs, check_vma=False
    )
```

```python
import functools

import jax
import jax.numpy as jnp
from jax import lax
from jax.experimental import pallas as pl
from jax.experimental.pallas import tpu as pltpu
from jax.sharding import PartitionSpec as P

LANES = 128
ROWS = 16
VMEM = pl.BlockSpec(memory_space=pltpu.VMEM)
SMEM = pl.BlockSpec(memory_space=pltpu.SMEM)
ANY = pl.BlockSpec(memory_space=pl.ANY)
HBM = pl.BlockSpec(memory_space=pltpu.HBM)
AXES = ("hyp", "side", "core", "pcol")


def call(kernel, outs, specs, *operands, scratch=(), out_specs=None, after=(), alias={}):
    many = isinstance(outs, (list, tuple))
    count = len(specs)

    def body(*refs):
        kernel(*refs[:count], *refs[count + len(after) :])

    if out_specs is None:
        out_specs = [VMEM] * len(outs) if many else VMEM
    return pl.pallas_call(
        body,
        out_shape=outs,
        in_specs=list(specs) + [ANY] * len(after),
        out_specs=out_specs,
        scratch_shapes=scratch,
        input_output_aliases=alias,
        compiler_params=pltpu.CompilerParams(vmem_limit_bytes=32 * 2**20),
    )(*operands, *after)


def transposed_dot(left, right):
    return lax.dot_general(
        left, right, (((0,), (0,)), ((), ())), preferred_element_type=jnp.float32
    )


BLOCKS = 3
ABOVE = ((0, 1), (0, 2), (1, 2))
HELD = len(ABOVE) + 2


def block_indices():
    shape = (LANES, LANES)
    return lax.broadcasted_iota(jnp.int32, shape, 0), lax.broadcasted_iota(jnp.int32, shape, 1)


def hold_diagonal(first, second, third):
    row, column = block_indices()
    line = jnp.sum(jnp.where(row == column, second, 0.0), axis=0, keepdims=True)
    last = line[:, LANES - 1 :]
    below = jnp.where(row == LANES - 1, line, jnp.where((row == LANES - 2) & (column == 0), last, 0.0))
    upper = column >= row
    return jnp.where(upper, first, second), jnp.where(upper, third, below)


def restore_diagonal(shared, single):
    row, column = block_indices()
    turned, upper = shared.T, column >= row
    line = jnp.where(column[:1] == LANES - 1, single[LANES - 2 : LANES - 1, :1], single[LANES - 1 :, :])
    second = jnp.where(row == column, line, jnp.where(upper, turned, shared))
    return jnp.where(upper, shared, turned), second, jnp.where(upper, single, single.T)


def general(prow, sigma_rows, panel, live_block_rows, inv_diag, quad_weight):
    height, count, width = panel.shape[1:]
    offsets = lax.broadcasted_iota(jnp.int32, (height, count), 0)
    active = offsets < live_block_rows[:, 0][None, :]
    masked = jnp.where(active[:, :, None], panel[0], jnp.zeros_like(panel[0]))
    gathered = lax.all_gather(masked, prow + ("pcol",), axis=0, tiled=True)
    start = lax.axis_index("pcol") * sigma_rows.shape[2]
    column_panel = lax.dynamic_slice_in_dim(gathered, start, sigma_rows.shape[2], 0)
    applied = lax.psum_scatter(
        jnp.dot(
            sigma_rows[0],
            column_panel.reshape(sigma_rows.shape[2], count * width),
            preferred_element_type=jnp.float32,
        ),
        "pcol",
        scatter_dimension=0,
        tiled=True,
    ).reshape(height, count, width)
    half = applied.astype(jnp.bfloat16)
    sigma_panel = jnp.where(active[:, :, None], -half, jnp.zeros_like(half))[None]
    coupling = jnp.einsum(
        "vwg,vwe->wge",
        masked.astype(jnp.float32),
        applied,
        precision=lax.Precision.HIGHEST,
    )
    diagonal = jnp.einsum(
        "skp,skq->spq", inv_diag[0], inv_diag[0], preferred_element_type=jnp.float32
    )
    marginal = lax.psum(quad_weight[0] * (coupling + diagonal), ("hyp",) + prow + ("pcol",))
    return sigma_panel, marginal


def start_kernel(*refs):
    sources, (own, give, own_inverse, limits), pieces = refs[:4], refs[4:8], refs[8:-5]
    buffers, sems = refs[-5:-1], refs[-1]
    copies = [
        pltpu.make_async_copy(source, buffer, sems.at[index])
        for index, (source, buffer) in enumerate(zip(sources, buffers))
    ]
    for copy in copies:
        copy.start()
    for copy in copies[:3]:
        copy.wait()
    live, panel, inverse, matrix = buffers
    first = lax.axis_index("side") == 0
    row = lax.broadcasted_iota(jnp.int32, own.shape, 0)
    rows = panel[0]
    zero = jnp.zeros(own.shape, own.dtype)
    one, two = (jnp.where(row < live[s], rows[:, s, :], zero) for s in range(2))
    height = own.shape[0]
    own[...] = jnp.where(first, one, two)
    give[:height] = jnp.where(first, two, one)
    spare = jnp.zeros((own_inverse.shape[0] - inverse.shape[2], own.shape[1]), own.dtype)
    one, two = (jnp.concatenate([inverse[0, s], spare], 0) for s in range(2))
    own_inverse[...] = jnp.where(first, one, two)
    give[height:] = jnp.where(first, two, one)
    for s in range(limits.shape[0]):
        limits[s] = jnp.full(limits.shape[1:], live[s], limits.dtype)
    copies[3].wait()
    at = 0
    for piece in pieces:
        piece[...] = matrix[0, :, at : at + piece.shape[0]].T
        at += piece.shape[0]


def gather_kernel(*refs):
    blocks, (rows, pack) = refs[:-2], refs[-2:]
    column = lax.axis_index("pcol")
    height = blocks[0].shape[0]
    for index, block in enumerate(blocks):
        spot = jnp.bitwise_xor(column, (0, 2, 1, 3)[index % 4])
        rows[index // 4, pl.ds(pl.multiple_of(spot * height, height), height), :] = block[...]
    pack[...] = rows[jnp.where(column // 2 == lax.axis_index("side"), 0, 1)]


def apply_kernel(rows, *refs):
    pieces, applied = refs[:-1], refs[-1]
    count = len(pieces) // 2
    at = 0
    for own, far in zip(pieces[:count], pieces[count:]):
        total = jnp.dot(own[...], rows[0], preferred_element_type=jnp.float32)
        total += jnp.dot(far[...], rows[1], preferred_element_type=jnp.float32)
        applied[at : at + own.shape[0]] = total
        at += own.shape[0]


def hold_kernel(value, out):
    del value, out


def couple_kernel(applied, pack, got_pack, own_inverse, got_inverse, keep, send, packed):
    core, column = lax.axis_index("core"), lax.axis_index("pcol")
    high = applied[...].astype(jnp.bfloat16)
    low = (applied[...] - high.astype(jnp.float32)).astype(jnp.bfloat16)
    rows = jnp.where(column % 2 == core, pack[...], got_pack[...])
    blocks = {}
    for first in range(BLOCKS):
        left, right = slice(first * LANES, (first + 1) * LANES), slice(first * LANES, None)
        total = transposed_dot(rows[:, left], high[:, right])
        total += transposed_dot(rows[:, left], low[:, right])
        for lines in (own_inverse, got_inverse):
            total += transposed_dot(lines[:, left], lines[:, right])
        for index in range(BLOCKS - first):
            blocks[first, first + index] = total[:, index * LANES : (index + 1) * LANES]
    held = [blocks[place] for place in ABOVE]
    held += hold_diagonal(*(blocks[i, i] for i in range(BLOCKS)))
    for index, block in enumerate(held):
        packed[index * LANES : (index + 1) * LANES, :] = block
    size = keep.shape[0]
    keep[...] = packed[pl.ds(pl.multiple_of(core * size, 8), size), :]
    send[...] = packed[pl.ds(pl.multiple_of((1 - core) * size, 8), size), :]


def halve_kernel(weight, mine, came, keep, send, whole):
    whole[...] = weight[0] * (mine[...] + came[...])
    size, point = keep.shape[0], lax.axis_index("hyp")
    keep[...] = whole[pl.ds(pl.multiple_of(point * size, 8), size), :]
    send[...] = whole[pl.ds(pl.multiple_of((1 - point) * size, 8), size), :]


def output_kernel(mine, other, out_near, out_far, half):
    half[...] = -(mine[...] + other[...]).astype(jnp.bfloat16)
    height, side, core = out_near.shape[0], lax.axis_index("side"), lax.axis_index("core")
    for out, at in ((out_near, side), (out_far, 1 - side)):
        spot = at * 2 + core
        out[...] = half[pl.ds(pl.multiple_of(spot * height, height), height), :]


def add_kernel(mine, came, out):
    out[...] = mine[...] + came[...]


def rows_kernel(limits, near, far, out):
    row = lax.broadcasted_iota(jnp.int32, near.shape, 0)
    first = lax.axis_index("pcol") // 2 == 0
    pair = (jnp.where(first, near[...], far[...]), jnp.where(first, far[...], near[...]))
    for s, value in enumerate(pair):
        out[0, :, s, :] = jnp.where(row < limits[s, :1, :1], value, jnp.zeros(value.shape, value.dtype))


def add_four_kernel(a, b, c, d, out):
    out[...] = (a[...] + b[...]) + (c[...] + d[...])


def stack_kernel(*refs):
    for index, ref in enumerate(refs[:-1]):
        refs[-1][index] = ref[...]


def finish_kernel(own, other, rows, rows_out, out, lines, result, sems):
    copies = [pltpu.make_async_copy(rows, rows_out, sems.at[0])]
    copies[0].start()
    point, side, core = (lax.axis_index(name) for name in ("hyp", "side", "core"))
    size = own.shape[1]
    for parts, owner in ((own, core), (other, 1 - core)):
        for index in range(own.shape[0]):
            node = 1 - side if index % 2 else side
            slot = 1 - point if index // 2 else point
            start = pl.multiple_of((owner * 2 + slot) * size, 8)
            lines[node, pl.ds(start, size), :] = parts[index]
    places = [slice(index * LANES, (index + 1) * LANES) for index in range(BLOCKS)]
    for node in range(2):
        held = [lines[node, index * LANES : (index + 1) * LANES, :] for index in range(HELD)]
        for (a, b), tile in zip(ABOVE, held):
            result[node, places[a], places[b]] = tile
            result[node, places[b], places[a]] = tile.T
        for place, tile in zip(places, restore_diagonal(*held[len(ABOVE) :])):
            result[node, place, place] = tile
        copies.append(pltpu.make_async_copy(result.at[node], out.at[node], sems.at[1 + node]))
        copies[-1].start()
    for copy in copies:
        copy.wait()


def square(sigma_rows, panel, live_block_rows, inv_diag, quad_weight):
    height, count, width = panel.shape[1:]
    grid = lax.axis_size("pcol")
    points = lax.axis_size("hyp")
    f32, bf16 = jnp.float32, jnp.bfloat16
    shape = jax.ShapeDtypeStruct
    dma = pltpu.SemaphoreType.DMA
    stay = functools.partial(pltpu.with_memory_space_constraint, memory_space=pltpu.HBM)
    devices = points * 2 * 2 * grid
    live = live_block_rows[:, 0]

    def swap(x, point=0, side=0, core=0, column=0):
        mask = ((point * 2 + side) * 2 + core) * grid + column
        return lax.ppermute(x, AXES, [(i, i ^ mask) for i in range(devices)])

    extent = sigma_rows.shape[2]
    block = shape((height, width), bf16)
    cuts = (extent // 2, extent // 2)
    size = pl.cdiv(inv_diag.shape[2], ROWS) * ROWS
    own, give, own_inverse, limits, *pieces = call(
        start_kernel,
        [block, shape((height + size, width), bf16), shape((size, width), bf16)]
        + [shape((count, 8, LANES), jnp.int32)]
        + [shape((lines, extent), bf16) for lines in cuts],
        [HBM] * 4,
        *map(stay, (live, panel, inv_diag, sigma_rows)),
        scratch=[pltpu.SMEM(live.shape, jnp.int32)]
        + [pltpu.VMEM(x.shape, bf16) for x in (panel, inv_diag, sigma_rows)]
        + [dma((4,))],
    )
    got = swap(give, side=1)
    got, got_inverse = got[:height], got[height:]
    blocks = []
    for one in (own, got):
        two = swap(one, column=2)
        blocks += [one, two, swap(one, column=1), swap(two, column=1)]
    far = [swap(piece, side=1) for piece in pieces]


    rows, pack = call(
        gather_kernel,
        [shape((2, extent, width), bf16), shape((extent, width), bf16)],
        [VMEM] * len(blocks),
        *blocks,
        after=far,
    )
    got_pack = swap(pack, core=1)
    mine = call(
        apply_kernel, shape((extent, width), f32), [VMEM] * (1 + 2 * len(cuts)), rows, *pieces, *far
    )
    lines = HELD * LANES // 2
    part, half = shape((lines // 2, LANES), f32), shape((lines, LANES), f32)
    mine = call(
        hold_kernel, shape(mine.shape, f32), [ANY], mine, out_specs=ANY, after=[got_pack], alias={0: 0}
    )
    other = swap(mine, core=1)
    keep, send = call(
        couple_kernel, [half, half], [VMEM] * 5,
        mine, pack, got_pack, own_inverse, got_inverse,
        scratch=[pltpu.VMEM((2 * lines, LANES), f32)],
    )
    keep, send = call(
        halve_kernel, [part, part], [SMEM] + [VMEM] * 2, quad_weight, keep, swap(send, core=1),
        scratch=[pltpu.VMEM((lines, LANES), f32)],
    )
    def deliver(x, flip):
        pairs = []
        for i in range(devices):
            h, s, k, c = i // (4 * grid), i // (2 * grid) % 2, i // grid % 2, i % grid
            pairs.append((i, (h * 4 + c) * grid + 2 * (s ^ flip) + k))
        return lax.ppermute(x, AXES, pairs)

    total = call(
        add_four_kernel, part, [VMEM] * 4,
        keep, swap(send, point=1), swap(keep, column=1), swap(send, point=1, column=1),
    )
    out_near, out_far = call(
        output_kernel, [block, block], [VMEM] * 2, mine, other,
        scratch=[pltpu.VMEM((extent, width), bf16)],
        after=[keep],
    )
    near, far = deliver(out_near, 0), deliver(out_far, 1)
    total = call(add_kernel, part, [VMEM] * 2, total, swap(total, column=2), after=[near])
    quarters = [total, swap(total, side=1), swap(total, point=1), swap(total, side=1, point=1)]
    rows = call(
        rows_kernel, shape((1, height, count, width), bf16), [VMEM] * 3, limits, near, far
    )
    quarters = call(
        stack_kernel, shape((len(quarters), *part.shape), f32), [VMEM] * len(quarters), *quarters, after=[rows]
    )
    return call(
        finish_kernel,
        [shape((1, height, count, width), bf16), shape((count, width, width), f32)],
        [VMEM] * 3,
        quarters, swap(quarters, core=1), rows,
        scratch=[
            pltpu.VMEM((count, 2 * lines, LANES), f32),
            pltpu.VMEM((count, width, width), f32),
            dma((3,)),
        ],
        out_specs=[HBM, HBM],
    )


def solution(mesh):
    sizes = dict(mesh.shape)
    prow, pcol = ("prow",), ("pcol",)

    def on_device(sigma_rows, panel, live_block_rows, inv_diag, quad_weight):
        height, count, width = panel.shape[1:]
        fits = (
            split
            and sigma_rows.shape[1] == sigma_rows.shape[2] == sizes["pcol"] * height
            and height % LANES == 0
            and count == 2
            and width == BLOCKS * LANES
        )
        body = square if fits else functools.partial(general, prow)
        return body(sigma_rows, panel, live_block_rows, inv_diag, quad_weight)

    split = sizes["hyp"] == 2 and sizes["pcol"] == 4 and sizes["prow"] == 4
    if split:
        prow = ("side", "core")
        mesh = jax.sharding.Mesh(
            mesh.devices.reshape(sizes["hyp"], 2, 2, sizes["pcol"]),
            ("hyp", "side", "core", "pcol"),
        )
    in_specs = (
        P("hyp", prow, pcol),
        P("hyp", prow + pcol, None, None),
        P(None, prow + pcol),
        P("hyp", None, prow + pcol, None),
        P("hyp"),
    )
    out_specs = (P("hyp", prow + pcol, None, None), P())
    return jax.shard_map(
        on_device, mesh=mesh, in_specs=in_specs, out_specs=out_specs, check_vma=False
    )
```

```python
import functools

import jax
import jax.numpy as jnp
from jax import lax
from jax.experimental import pallas as pl
from jax.experimental.pallas import tpu as pltpu
from jax.sharding import PartitionSpec as P

LANES = 128
ROWS = 16
VMEM = pl.BlockSpec(memory_space=pltpu.VMEM)
SMEM = pl.BlockSpec(memory_space=pltpu.SMEM)
ANY = pl.BlockSpec(memory_space=pl.ANY)
HBM = pl.BlockSpec(memory_space=pltpu.HBM)
AXES = ("hyp", "side", "core", "pcol")


def call(kernel, outs, specs, *operands, scratch=(), out_specs=None, after=(), alias={}):
    many = isinstance(outs, (list, tuple))
    count = len(specs)

    def body(*refs):
        kernel(*refs[:count], *refs[count + len(after) :])

    if out_specs is None:
        out_specs = [VMEM] * len(outs) if many else VMEM
    return pl.pallas_call(
        body,
        out_shape=outs,
        in_specs=list(specs) + [ANY] * len(after),
        out_specs=out_specs,
        scratch_shapes=scratch,
        input_output_aliases=alias,
        compiler_params=pltpu.CompilerParams(vmem_limit_bytes=32 * 2**20),
    )(*operands, *after)


def transposed_dot(left, right):
    return lax.dot_general(
        left, right, (((0,), (0,)), ((), ())), preferred_element_type=jnp.float32
    )


BLOCKS = 3
ABOVE = ((0, 1), (0, 2), (1, 2))
HELD = len(ABOVE) + 2


def block_indices():
    shape = (LANES, LANES)
    return lax.broadcasted_iota(jnp.int32, shape, 0), lax.broadcasted_iota(jnp.int32, shape, 1)


def hold_diagonal(first, second, third):
    row, column = block_indices()
    line = jnp.sum(jnp.where(row == column, second, 0.0), axis=0, keepdims=True)
    last = line[:, LANES - 1 :]
    below = jnp.where(row == LANES - 1, line, jnp.where((row == LANES - 2) & (column == 0), last, 0.0))
    upper = column >= row
    return jnp.where(upper, first, second), jnp.where(upper, third, below)


def restore_diagonal(shared, single):
    row, column = block_indices()
    turned, upper = shared.T, column >= row
    line = jnp.where(column[:1] == LANES - 1, single[LANES - 2 : LANES - 1, :1], single[LANES - 1 :, :])
    second = jnp.where(row == column, line, jnp.where(upper, turned, shared))
    return jnp.where(upper, shared, turned), second, jnp.where(upper, single, single.T)


def general(prow, sigma_rows, panel, live_block_rows, inv_diag, quad_weight):
    height, count, width = panel.shape[1:]
    offsets = lax.broadcasted_iota(jnp.int32, (height, count), 0)
    active = offsets < live_block_rows[:, 0][None, :]
    masked = jnp.where(active[:, :, None], panel[0], jnp.zeros_like(panel[0]))
    gathered = lax.all_gather(masked, prow + ("pcol",), axis=0, tiled=True)
    start = lax.axis_index("pcol") * sigma_rows.shape[2]
    column_panel = lax.dynamic_slice_in_dim(gathered, start, sigma_rows.shape[2], 0)
    applied = lax.psum_scatter(
        jnp.dot(
            sigma_rows[0],
            column_panel.reshape(sigma_rows.shape[2], count * width),
            preferred_element_type=jnp.float32,
        ),
        "pcol",
        scatter_dimension=0,
        tiled=True,
    ).reshape(height, count, width)
    half = applied.astype(jnp.bfloat16)
    sigma_panel = jnp.where(active[:, :, None], -half, jnp.zeros_like(half))[None]
    coupling = jnp.einsum(
        "vwg,vwe->wge",
        masked.astype(jnp.float32),
        applied,
        precision=lax.Precision.HIGHEST,
    )
    diagonal = jnp.einsum(
        "skp,skq->spq", inv_diag[0], inv_diag[0], preferred_element_type=jnp.float32
    )
    marginal = lax.psum(quad_weight[0] * (coupling + diagonal), ("hyp",) + prow + ("pcol",))
    return sigma_panel, marginal


def start_kernel(*refs):
    sources, (own, give, own_inverse, limits), pieces = refs[:4], refs[4:8], refs[8:-5]
    buffers, sems = refs[-5:-1], refs[-1]
    copies = [
        pltpu.make_async_copy(source, buffer, sems.at[index])
        for index, (source, buffer) in enumerate(zip(sources, buffers))
    ]
    for copy in copies:
        copy.start()
    for copy in copies[:3]:
        copy.wait()
    live, panel, inverse, matrix = buffers
    first = lax.axis_index("side") == 0
    row = lax.broadcasted_iota(jnp.int32, own.shape, 0)
    rows = panel[0]
    zero = jnp.zeros(own.shape, own.dtype)
    one, two = (jnp.where(row < live[s], rows[:, s, :], zero) for s in range(2))
    height = own.shape[0]
    own[...] = jnp.where(first, one, two)
    give[:height] = jnp.where(first, two, one)
    spare = jnp.zeros((own_inverse.shape[0] - inverse.shape[2], own.shape[1]), own.dtype)
    one, two = (jnp.concatenate([inverse[0, s], spare], 0) for s in range(2))
    own_inverse[...] = jnp.where(first, one, two)
    give[height:] = jnp.where(first, two, one)
    for s in range(limits.shape[0]):
        limits[s] = jnp.full(limits.shape[1:], live[s], limits.dtype)
    copies[3].wait()
    at = 0
    for piece in pieces:
        piece[...] = matrix[0, :, at : at + piece.shape[0]].T
        at += piece.shape[0]


def gather_kernel(*refs):
    blocks, (rows, pack) = refs[:-2], refs[-2:]
    column = lax.axis_index("pcol")
    height = blocks[0].shape[0]
    for index, block in enumerate(blocks):
        spot = jnp.bitwise_xor(column, (0, 2, 1, 3)[index % 4])
        rows[index // 4, pl.ds(pl.multiple_of(spot * height, height), height), :] = block[...]
    pack[...] = rows[jnp.where(column // 2 == lax.axis_index("side"), 0, 1)]


def apply_kernel(rows, *refs):
    pieces, applied = refs[:-1], refs[-1]
    count = len(pieces) // 2
    at = 0
    for own, far in zip(pieces[:count], pieces[count:]):
        total = jnp.dot(own[...], rows[0], preferred_element_type=jnp.float32)
        total += jnp.dot(far[...], rows[1], preferred_element_type=jnp.float32)
        applied[at : at + own.shape[0]] = total
        at += own.shape[0]


def hold_kernel(value, out):
    del value, out


def couple_kernel(applied, pack, got_pack, own_inverse, got_inverse, keep, send, packed):
    core, column = lax.axis_index("core"), lax.axis_index("pcol")
    high = applied[...].astype(jnp.bfloat16)
    low = (applied[...] - high.astype(jnp.float32)).astype(jnp.bfloat16)
    rows = jnp.where(column % 2 == core, pack[...], got_pack[...])
    blocks = {}
    for first in range(BLOCKS):
        left, right = slice(first * LANES, (first + 1) * LANES), slice(first * LANES, None)
        total = transposed_dot(rows[:, left], high[:, right])
        total += transposed_dot(rows[:, left], low[:, right])
        for lines in (own_inverse, got_inverse):
            total += transposed_dot(lines[:, left], lines[:, right])
        for index in range(BLOCKS - first):
            blocks[first, first + index] = total[:, index * LANES : (index + 1) * LANES]
    held = [blocks[place] for place in ABOVE]
    held += hold_diagonal(*(blocks[i, i] for i in range(BLOCKS)))
    for index, block in enumerate(held):
        packed[index * LANES : (index + 1) * LANES, :] = block
    size = keep.shape[0]
    keep[...] = packed[pl.ds(pl.multiple_of(core * size, 8), size), :]
    send[...] = packed[pl.ds(pl.multiple_of((1 - core) * size, 8), size), :]


def halve_kernel(weight, mine, came, keep, send, whole):
    whole[...] = weight[0] * (mine[...] + came[...])
    size, point = keep.shape[0], lax.axis_index("hyp")
    keep[...] = whole[pl.ds(pl.multiple_of(point * size, 8), size), :]
    send[...] = whole[pl.ds(pl.multiple_of((1 - point) * size, 8), size), :]


def output_kernel(mine, other, out_near, out_far, half):
    half[...] = -(mine[...] + other[...]).astype(jnp.bfloat16)
    height, side, core = out_near.shape[0], lax.axis_index("side"), lax.axis_index("core")
    for out, at in ((out_near, side), (out_far, 1 - side)):
        spot = at * 2 + core
        out[...] = half[pl.ds(pl.multiple_of(spot * height, height), height), :]


def add_kernel(mine, came, out):
    out[...] = mine[...] + came[...]


def rows_kernel(limits, near, far, out):
    row = lax.broadcasted_iota(jnp.int32, near.shape, 0)
    first = lax.axis_index("pcol") // 2 == 0
    pair = (jnp.where(first, near[...], far[...]), jnp.where(first, far[...], near[...]))
    for s, value in enumerate(pair):
        out[0, :, s, :] = jnp.where(row < limits[s, :1, :1], value, jnp.zeros(value.shape, value.dtype))


def add_four_kernel(a, b, c, d, out):
    out[...] = (a[...] + b[...]) + (c[...] + d[...])


def stack_kernel(*refs):
    for index, ref in enumerate(refs[:-1]):
        refs[-1][index] = ref[...]


def set_lines(parts, lines, first):
    point, side, size = lax.axis_index("hyp"), lax.axis_index("side"), parts.shape[1]
    for index in range(parts.shape[0]):
        node = 1 - side if index % 2 else side
        slot = 1 - point if index // 2 else point
        lines[node, pl.ds(pl.multiple_of(first + slot * size, 8), size), :] = parts[index]


def copy_out(areas, result, out, sems):
    copies = [
        pltpu.make_async_copy(result.at[area], out.at[area], sems.at[index]) for index, area in enumerate(areas)
    ]
    for copy in copies:
        copy.start()
    return copies


def first_core_blocks(lines, result, out, sems):
    first, rest = slice(0, LANES), slice(LANES, BLOCKS * LANES)
    areas = []
    for node in range(2):
        for index in range(2):
            place = slice((index + 1) * LANES, (index + 2) * LANES)
            tile = lines[node, index * LANES : (index + 1) * LANES, :]
            result[node, first, place] = tile
            result[node, place, first] = tile.T
        areas += [(node, first, rest), (node, rest, first)]
    return copy_out(areas, result, out, sems)


def second_core_blocks(lines, at, result, out, sems):
    areas = []
    for node in range(2):
        held = (lines[node, at + index * LANES : at + (index + 1) * LANES, :] for index in range(2))
        for index, tile in enumerate(restore_diagonal(*held)):
            place = slice(index * LANES, (index + 1) * LANES)
            result[node, place, place] = tile
            areas.append((node, place, place))
    return copy_out(areas, result, out, sems)


def early_kernel(own, rows, rows_out, out, lines, result, sems, rows_sem):
    store = pltpu.make_async_copy(rows, rows_out, rows_sem)
    store.start()
    core = lax.axis_index("core")
    set_lines(own, lines, 0)

    @pl.when(core == 0)
    def _():
        for copy in first_core_blocks(lines, result, out, sems):
            copy.wait()

    @pl.when(core == 1)
    def _():
        for copy in second_core_blocks(lines, LANES // 2, result, out, sems):
            copy.wait()

    store.wait()


def late_kernel(own, other, before, out, lines, result, sems, middle_sems):
    del before
    core, half = lax.axis_index("core"), lines.shape[1] // 2
    set_lines(own, lines, core * half)
    set_lines(other, lines, (1 - core) * half)
    middle, last = (slice(i * LANES, (i + 1) * LANES) for i in (1, 2))
    areas = []
    for node in range(2):
        tile = lines[node, 2 * LANES : 3 * LANES, :]
        result[node, middle, last] = tile
        result[node, last, middle] = tile.T
        areas += [(node, middle, last), (node, last, middle)]
    shared = copy_out(areas, result, out, middle_sems)

    @pl.when(core == 1)
    def _():
        for copy in first_core_blocks(lines, result, out, sems):
            copy.wait()

    @pl.when(core == 0)
    def _():
        for copy in second_core_blocks(lines, len(ABOVE) * LANES, result, out, sems):
            copy.wait()

    for copy in shared:
        copy.wait()


def square(sigma_rows, panel, live_block_rows, inv_diag, quad_weight):
    height, count, width = panel.shape[1:]
    grid = lax.axis_size("pcol")
    points = lax.axis_size("hyp")
    f32, bf16 = jnp.float32, jnp.bfloat16
    shape = jax.ShapeDtypeStruct
    dma = pltpu.SemaphoreType.DMA
    stay = functools.partial(pltpu.with_memory_space_constraint, memory_space=pltpu.HBM)
    devices = points * 2 * 2 * grid
    live = live_block_rows[:, 0]

    def swap(x, point=0, side=0, core=0, column=0):
        mask = ((point * 2 + side) * 2 + core) * grid + column
        return lax.ppermute(x, AXES, [(i, i ^ mask) for i in range(devices)])

    extent = sigma_rows.shape[2]
    block = shape((height, width), bf16)
    cuts = (extent // 2, extent // 2)
    size = pl.cdiv(inv_diag.shape[2], ROWS) * ROWS
    own, give, own_inverse, limits, *pieces = call(
        start_kernel,
        [block, shape((height + size, width), bf16), shape((size, width), bf16)]
        + [shape((count, 8, LANES), jnp.int32)]
        + [shape((lines, extent), bf16) for lines in cuts],
        [HBM] * 4,
        *map(stay, (live, panel, inv_diag, sigma_rows)),
        scratch=[pltpu.SMEM(live.shape, jnp.int32)]
        + [pltpu.VMEM(x.shape, bf16) for x in (panel, inv_diag, sigma_rows)]
        + [dma((4,))],
    )
    got = swap(give, side=1)
    got, got_inverse = got[:height], got[height:]
    blocks = []
    for one in (own, got):
        two = swap(one, column=2)
        blocks += [one, two, swap(one, column=1), swap(two, column=1)]
    far = [swap(piece, side=1) for piece in pieces]


    rows, pack = call(
        gather_kernel,
        [shape((2, extent, width), bf16), shape((extent, width), bf16)],
        [VMEM] * len(blocks),
        *blocks,
        after=far,
    )
    got_pack = swap(pack, core=1)
    mine = call(
        apply_kernel, shape((extent, width), f32), [VMEM] * (1 + 2 * len(cuts)), rows, *pieces, *far
    )
    lines = HELD * LANES // 2
    part, half = shape((lines // 2, LANES), f32), shape((lines, LANES), f32)
    mine = call(
        hold_kernel, shape(mine.shape, f32), [ANY], mine, out_specs=ANY, after=[got_pack], alias={0: 0}
    )
    other = swap(mine, core=1)
    keep, send = call(
        couple_kernel, [half, half], [VMEM] * 5,
        mine, pack, got_pack, own_inverse, got_inverse,
        scratch=[pltpu.VMEM((2 * lines, LANES), f32)],
    )
    keep, send = call(
        halve_kernel, [part, part], [SMEM] + [VMEM] * 2, quad_weight, keep, swap(send, core=1),
        scratch=[pltpu.VMEM((lines, LANES), f32)],
    )
    def deliver(x, flip):
        pairs = []
        for i in range(devices):
            h, s, k, c = i // (4 * grid), i // (2 * grid) % 2, i // grid % 2, i % grid
            pairs.append((i, (h * 4 + c) * grid + 2 * (s ^ flip) + k))
        return lax.ppermute(x, AXES, pairs)

    total = call(
        add_four_kernel, part, [VMEM] * 4,
        keep, swap(send, point=1), swap(keep, column=1), swap(send, point=1, column=1),
    )
    out_near, out_far = call(
        output_kernel, [block, block], [VMEM] * 2, mine, other,
        scratch=[pltpu.VMEM((extent, width), bf16)],
        after=[keep],
    )
    near, far = deliver(out_near, 0), deliver(out_far, 1)
    total = call(add_kernel, part, [VMEM] * 2, total, swap(total, column=2))
    quarters = [total, swap(total, side=1), swap(total, point=1), swap(total, side=1, point=1)]
    rows = call(
        rows_kernel, shape((1, height, count, width), bf16), [VMEM] * 3, limits, near, far
    )
    quarters = call(
        stack_kernel, shape((len(quarters), *part.shape), f32), [VMEM] * len(quarters), *quarters, after=[rows]
    )
    whole = shape((count, width, width), f32)
    sigma_panel, marginal = call(
        early_kernel, [shape(rows.shape, bf16), whole], [VMEM] * 2, quarters, rows,
        scratch=[pltpu.VMEM((count, lines, LANES), f32), pltpu.VMEM(whole.shape, f32), dma((6,)), dma(())],
        out_specs=[HBM, HBM],
    )
    marginal = call(
        late_kernel, whole, [VMEM, VMEM, HBM], quarters, swap(quarters, core=1), marginal,
        scratch=[pltpu.VMEM((count, 2 * lines, LANES), f32), pltpu.VMEM(whole.shape, f32), dma((6,)), dma((4,))],
        out_specs=HBM,
        alias={2: 0},
    )
    return sigma_panel, marginal


def solution(mesh):
    sizes = dict(mesh.shape)
    prow, pcol = ("prow",), ("pcol",)

    def on_device(sigma_rows, panel, live_block_rows, inv_diag, quad_weight):
        height, count, width = panel.shape[1:]
        fits = (
            split
            and sigma_rows.shape[1] == sigma_rows.shape[2] == sizes["pcol"] * height
            and height % LANES == 0
            and count == 2
            and width == BLOCKS * LANES
        )
        body = square if fits else functools.partial(general, prow)
        return body(sigma_rows, panel, live_block_rows, inv_diag, quad_weight)

    split = sizes["hyp"] == 2 and sizes["pcol"] == 4 and sizes["prow"] == 4
    if split:
        prow = ("side", "core")
        mesh = jax.sharding.Mesh(
            mesh.devices.reshape(sizes["hyp"], 2, 2, sizes["pcol"]),
            ("hyp", "side", "core", "pcol"),
        )
    in_specs = (
        P("hyp", prow, pcol),
        P("hyp", prow + pcol, None, None),
        P(None, prow + pcol),
        P("hyp", None, prow + pcol, None),
        P("hyp"),
    )
    out_specs = (P("hyp", prow + pcol, None, None), P())
    return jax.shard_map(
        on_device, mesh=mesh, in_specs=in_specs, out_specs=out_specs, check_vma=False
    )
```

```python
import functools

import jax
import jax.numpy as jnp
from jax import lax
from jax.experimental import pallas as pl
from jax.experimental.pallas import tpu as pltpu
from jax.sharding import PartitionSpec as P

LANES = 128
ROWS = 16
VMEM = pl.BlockSpec(memory_space=pltpu.VMEM)
SMEM = pl.BlockSpec(memory_space=pltpu.SMEM)
ANY = pl.BlockSpec(memory_space=pl.ANY)
HBM = pl.BlockSpec(memory_space=pltpu.HBM)
AXES = ("hyp", "side", "core", "pcol")


def call(kernel, outs, specs, *operands, scratch=(), out_specs=None, after=(), alias={}):
    many = isinstance(outs, (list, tuple))
    count = len(specs)

    def body(*refs):
        kernel(*refs[:count], *refs[count + len(after) :])

    if out_specs is None:
        out_specs = [VMEM] * len(outs) if many else VMEM
    return pl.pallas_call(
        body,
        out_shape=outs,
        in_specs=list(specs) + [ANY] * len(after),
        out_specs=out_specs,
        scratch_shapes=scratch,
        input_output_aliases=alias,
        compiler_params=pltpu.CompilerParams(vmem_limit_bytes=32 * 2**20),
    )(*operands, *after)


def transposed_dot(left, right):
    return lax.dot_general(
        left, right, (((0,), (0,)), ((), ())), preferred_element_type=jnp.float32
    )


BLOCKS = 3
ABOVE = ((0, 1), (0, 2), (1, 2))
HELD = len(ABOVE) + 2


def block_indices():
    shape = (LANES, LANES)
    return lax.broadcasted_iota(jnp.int32, shape, 0), lax.broadcasted_iota(jnp.int32, shape, 1)


def hold_diagonal(first, second, third):
    row, column = block_indices()
    line = jnp.sum(jnp.where(row == column, second, 0.0), axis=0, keepdims=True)
    last = line[:, LANES - 1 :]
    below = jnp.where(row == LANES - 1, line, jnp.where((row == LANES - 2) & (column == 0), last, 0.0))
    upper = column >= row
    return jnp.where(upper, first, second), jnp.where(upper, third, below)


def restore_diagonal(shared, single):
    row, column = block_indices()
    turned, upper = shared.T, column >= row
    line = jnp.where(column[:1] == LANES - 1, single[LANES - 2 : LANES - 1, :1], single[LANES - 1 :, :])
    second = jnp.where(row == column, line, jnp.where(upper, turned, shared))
    return jnp.where(upper, shared, turned), second, jnp.where(upper, single, single.T)


def general(prow, sigma_rows, panel, live_block_rows, inv_diag, quad_weight):
    height, count, width = panel.shape[1:]
    offsets = lax.broadcasted_iota(jnp.int32, (height, count), 0)
    active = offsets < live_block_rows[:, 0][None, :]
    masked = jnp.where(active[:, :, None], panel[0], jnp.zeros_like(panel[0]))
    gathered = lax.all_gather(masked, prow + ("pcol",), axis=0, tiled=True)
    start = lax.axis_index("pcol") * sigma_rows.shape[2]
    column_panel = lax.dynamic_slice_in_dim(gathered, start, sigma_rows.shape[2], 0)
    applied = lax.psum_scatter(
        jnp.dot(
            sigma_rows[0],
            column_panel.reshape(sigma_rows.shape[2], count * width),
            preferred_element_type=jnp.float32,
        ),
        "pcol",
        scatter_dimension=0,
        tiled=True,
    ).reshape(height, count, width)
    half = applied.astype(jnp.bfloat16)
    sigma_panel = jnp.where(active[:, :, None], -half, jnp.zeros_like(half))[None]
    coupling = jnp.einsum(
        "vwg,vwe->wge",
        masked.astype(jnp.float32),
        applied,
        precision=lax.Precision.HIGHEST,
    )
    diagonal = jnp.einsum(
        "skp,skq->spq", inv_diag[0], inv_diag[0], preferred_element_type=jnp.float32
    )
    marginal = lax.psum(quad_weight[0] * (coupling + diagonal), ("hyp",) + prow + ("pcol",))
    return sigma_panel, marginal


def start_kernel(*refs):
    sources, (own, give, own_inverse, limits), pieces = refs[:4], refs[4:8], refs[8:-5]
    buffers, sems = refs[-5:-1], refs[-1]
    copies = [
        pltpu.make_async_copy(source, buffer, sems.at[index])
        for index, (source, buffer) in enumerate(zip(sources, buffers))
    ]
    for copy in copies:
        copy.start()
    for copy in copies[:3]:
        copy.wait()
    live, panel, inverse, matrix = buffers
    first = lax.axis_index("side") == 0
    row = lax.broadcasted_iota(jnp.int32, own.shape, 0)
    rows = panel[0]
    zero = jnp.zeros(own.shape, own.dtype)
    one, two = (jnp.where(row < live[s], rows[:, s, :], zero) for s in range(2))
    height = own.shape[0]
    own[...] = jnp.where(first, one, two)
    give[:height] = jnp.where(first, two, one)
    spare = jnp.zeros((own_inverse.shape[0] - inverse.shape[2], own.shape[1]), own.dtype)
    one, two = (jnp.concatenate([inverse[0, s], spare], 0) for s in range(2))
    own_inverse[...] = jnp.where(first, one, two)
    give[height:] = jnp.where(first, two, one)
    for s in range(limits.shape[0]):
        limits[s] = jnp.full(limits.shape[1:], live[s], limits.dtype)
    copies[3].wait()
    at = 0
    for piece in pieces:
        piece[...] = matrix[0, :, at : at + piece.shape[0]].T
        at += piece.shape[0]


def set_rows(blocks, rows):
    column, height = lax.axis_index("pcol"), blocks[0].shape[0]
    for step, block in zip((0, 2, 1, 3), blocks):
        spot = jnp.bitwise_xor(column, step)
        rows[pl.ds(pl.multiple_of(spot * height, height), height), :] = block[...]


def own_kernel(*refs):
    blocks, pieces, (rows, applied) = refs[:4], refs[4:-2], refs[-2:]
    set_rows(blocks, rows)
    at = 0
    for piece in pieces:
        applied[at : at + piece.shape[0]] = jnp.dot(piece[...], rows[...], preferred_element_type=jnp.float32)
        at += piece.shape[0]


def gather_kernel(*refs):
    blocks, (own_rows, rows, pack) = refs[:4], refs[4:]
    set_rows(blocks, rows)
    same = lax.axis_index("pcol") // 2 == lax.axis_index("side")
    pack[...] = jnp.where(same, own_rows[...], rows[...])


def apply_kernel(own, rows, *refs):
    pieces, applied = refs[:-1], refs[-1]
    at = 0
    for piece in pieces:
        lines = slice(at, at + piece.shape[0])
        applied[lines] = own[lines] + jnp.dot(piece[...], rows[...], preferred_element_type=jnp.float32)
        at += piece.shape[0]


def hold_kernel(value, out):
    del value, out


def couple_kernel(applied, pack, got_pack, own_inverse, got_inverse, keep, send, packed):
    core, column = lax.axis_index("core"), lax.axis_index("pcol")
    high = applied[...].astype(jnp.bfloat16)
    low = (applied[...] - high.astype(jnp.float32)).astype(jnp.bfloat16)
    rows = jnp.where(column % 2 == core, pack[...], got_pack[...])
    blocks = {}
    for first in range(BLOCKS):
        left, right = slice(first * LANES, (first + 1) * LANES), slice(first * LANES, None)
        total = transposed_dot(rows[:, left], high[:, right])
        total += transposed_dot(rows[:, left], low[:, right])
        for lines in (own_inverse, got_inverse):
            total += transposed_dot(lines[:, left], lines[:, right])
        for index in range(BLOCKS - first):
            blocks[first, first + index] = total[:, index * LANES : (index + 1) * LANES]
    held = [blocks[place] for place in ABOVE]
    held += hold_diagonal(*(blocks[i, i] for i in range(BLOCKS)))
    for index, block in enumerate(held):
        packed[index * LANES : (index + 1) * LANES, :] = block
    size = keep.shape[0]
    keep[...] = packed[pl.ds(pl.multiple_of(core * size, 8), size), :]
    send[...] = packed[pl.ds(pl.multiple_of((1 - core) * size, 8), size), :]


def halve_kernel(weight, mine, came, keep, send, whole):
    whole[...] = weight[0] * (mine[...] + came[...])
    size, point = keep.shape[0], lax.axis_index("hyp")
    keep[...] = whole[pl.ds(pl.multiple_of(point * size, 8), size), :]
    send[...] = whole[pl.ds(pl.multiple_of((1 - point) * size, 8), size), :]


def output_kernel(mine, other, out_near, out_far, half):
    half[...] = -(mine[...] + other[...]).astype(jnp.bfloat16)
    height, side, core = out_near.shape[0], lax.axis_index("side"), lax.axis_index("core")
    for out, at in ((out_near, side), (out_far, 1 - side)):
        spot = at * 2 + core
        out[...] = half[pl.ds(pl.multiple_of(spot * height, height), height), :]


def add_kernel(mine, came, out):
    out[...] = mine[...] + came[...]


def rows_kernel(limits, near, far, out):
    row = lax.broadcasted_iota(jnp.int32, near.shape, 0)
    first = lax.axis_index("pcol") // 2 == 0
    pair = (jnp.where(first, near[...], far[...]), jnp.where(first, far[...], near[...]))
    for s, value in enumerate(pair):
        out[0, :, s, :] = jnp.where(row < limits[s, :1, :1], value, jnp.zeros(value.shape, value.dtype))


def add_four_kernel(a, b, c, d, out):
    out[...] = (a[...] + b[...]) + (c[...] + d[...])


def stack_kernel(*refs):
    for index, ref in enumerate(refs[:-1]):
        refs[-1][index] = ref[...]


def set_lines(parts, lines, first):
    point, side, size = lax.axis_index("hyp"), lax.axis_index("side"), parts.shape[1]
    for index in range(parts.shape[0]):
        node = 1 - side if index % 2 else side
        slot = 1 - point if index // 2 else point
        lines[node, pl.ds(pl.multiple_of(first + slot * size, 8), size), :] = parts[index]


def copy_out(areas, result, out, sems):
    copies = [
        pltpu.make_async_copy(result.at[area], out.at[area], sems.at[index]) for index, area in enumerate(areas)
    ]
    for copy in copies:
        copy.start()
    return copies


def first_core_blocks(lines, result, out, sems):
    first, rest = slice(0, LANES), slice(LANES, BLOCKS * LANES)
    areas = []
    for node in range(2):
        for index in range(2):
            place = slice((index + 1) * LANES, (index + 2) * LANES)
            tile = lines[node, index * LANES : (index + 1) * LANES, :]
            result[node, first, place] = tile
            result[node, place, first] = tile.T
        areas += [(node, first, rest), (node, rest, first)]
    return copy_out(areas, result, out, sems)


def second_core_blocks(lines, at, result, out, sems):
    areas = []
    for node in range(2):
        held = (lines[node, at + index * LANES : at + (index + 1) * LANES, :] for index in range(2))
        for index, tile in enumerate(restore_diagonal(*held)):
            place = slice(index * LANES, (index + 1) * LANES)
            result[node, place, place] = tile
            areas.append((node, place, place))
    return copy_out(areas, result, out, sems)


def early_kernel(own, rows, rows_out, out, lines, result, sems, rows_sem):
    store = pltpu.make_async_copy(rows, rows_out, rows_sem)
    store.start()
    core = lax.axis_index("core")
    set_lines(own, lines, 0)

    @pl.when(core == 0)
    def _():
        for copy in first_core_blocks(lines, result, out, sems):
            copy.wait()

    @pl.when(core == 1)
    def _():
        for copy in second_core_blocks(lines, LANES // 2, result, out, sems):
            copy.wait()

    store.wait()


def late_kernel(own, other, before, out, lines, result, sems, middle_sems):
    del before
    core, half = lax.axis_index("core"), lines.shape[1] // 2
    set_lines(own, lines, core * half)
    set_lines(other, lines, (1 - core) * half)
    middle, last = (slice(i * LANES, (i + 1) * LANES) for i in (1, 2))
    areas = []
    for node in range(2):
        tile = lines[node, 2 * LANES : 3 * LANES, :]
        result[node, middle, last] = tile
        result[node, last, middle] = tile.T
        areas += [(node, middle, last), (node, last, middle)]
    shared = copy_out(areas, result, out, middle_sems)

    @pl.when(core == 1)
    def _():
        for copy in first_core_blocks(lines, result, out, sems):
            copy.wait()

    @pl.when(core == 0)
    def _():
        for copy in second_core_blocks(lines, len(ABOVE) * LANES, result, out, sems):
            copy.wait()

    for copy in shared:
        copy.wait()


def square(sigma_rows, panel, live_block_rows, inv_diag, quad_weight):
    height, count, width = panel.shape[1:]
    grid = lax.axis_size("pcol")
    points = lax.axis_size("hyp")
    f32, bf16 = jnp.float32, jnp.bfloat16
    shape = jax.ShapeDtypeStruct
    dma = pltpu.SemaphoreType.DMA
    stay = functools.partial(pltpu.with_memory_space_constraint, memory_space=pltpu.HBM)
    devices = points * 2 * 2 * grid
    live = live_block_rows[:, 0]

    def swap(x, point=0, side=0, core=0, column=0):
        mask = ((point * 2 + side) * 2 + core) * grid + column
        return lax.ppermute(x, AXES, [(i, i ^ mask) for i in range(devices)])

    extent = sigma_rows.shape[2]
    block = shape((height, width), bf16)
    cuts = (extent // 2, extent // 2)
    size = pl.cdiv(inv_diag.shape[2], ROWS) * ROWS
    own, give, own_inverse, limits, *pieces = call(
        start_kernel,
        [block, shape((height + size, width), bf16), shape((size, width), bf16)]
        + [shape((count, 8, LANES), jnp.int32)]
        + [shape((lines, extent), bf16) for lines in cuts],
        [HBM] * 4,
        *map(stay, (live, panel, inv_diag, sigma_rows)),
        scratch=[pltpu.SMEM(live.shape, jnp.int32)]
        + [pltpu.VMEM(x.shape, bf16) for x in (panel, inv_diag, sigma_rows)]
        + [dma((4,))],
    )
    got = swap(give, side=1)
    got, got_inverse = got[:height], got[height:]
    blocks = []
    for one in (own, got):
        two = swap(one, column=2)
        blocks += [one, two, swap(one, column=1), swap(two, column=1)]
    far = [swap(piece, side=1) for piece in pieces]


    product, line_shape = shape((extent, width), f32), shape((extent, width), bf16)
    own_rows, own_product = call(
        own_kernel, [line_shape, product], [VMEM] * (4 + len(cuts)), *blocks[:4], *pieces
    )
    rows, pack = call(
        gather_kernel, [line_shape] * 2, [VMEM] * 5, *blocks[4:], own_rows, after=far
    )
    got_pack = swap(pack, core=1)
    mine = call(apply_kernel, product, [VMEM] * (2 + len(cuts)), own_product, rows, *far)
    lines = HELD * LANES // 2
    part, half = shape((lines // 2, LANES), f32), shape((lines, LANES), f32)
    mine = call(
        hold_kernel, shape(mine.shape, f32), [ANY], mine, out_specs=ANY, after=[got_pack], alias={0: 0}
    )
    other = swap(mine, core=1)
    keep, send = call(
        couple_kernel, [half, half], [VMEM] * 5,
        mine, pack, got_pack, own_inverse, got_inverse,
        scratch=[pltpu.VMEM((2 * lines, LANES), f32)],
    )
    keep, send = call(
        halve_kernel, [part, part], [SMEM] + [VMEM] * 2, quad_weight, keep, swap(send, core=1),
        scratch=[pltpu.VMEM((lines, LANES), f32)],
    )
    def deliver(x, flip):
        pairs = []
        for i in range(devices):
            h, s, k, c = i // (4 * grid), i // (2 * grid) % 2, i // grid % 2, i % grid
            pairs.append((i, (h * 4 + c) * grid + 2 * (s ^ flip) + k))
        return lax.ppermute(x, AXES, pairs)

    total = call(
        add_four_kernel, part, [VMEM] * 4,
        keep, swap(send, point=1), swap(keep, column=1), swap(send, point=1, column=1),
    )
    out_near, out_far = call(
        output_kernel, [block, block], [VMEM] * 2, mine, other,
        scratch=[pltpu.VMEM((extent, width), bf16)],
        after=[keep],
    )
    near, far = deliver(out_near, 0), deliver(out_far, 1)
    total = call(add_kernel, part, [VMEM] * 2, total, swap(total, column=2))
    quarters = [total, swap(total, side=1), swap(total, point=1), swap(total, side=1, point=1)]
    rows = call(
        rows_kernel, shape((1, height, count, width), bf16), [VMEM] * 3, limits, near, far
    )
    quarters = call(
        stack_kernel, shape((len(quarters), *part.shape), f32), [VMEM] * len(quarters), *quarters, after=[rows]
    )
    whole = shape((count, width, width), f32)
    sigma_panel, marginal = call(
        early_kernel, [shape(rows.shape, bf16), whole], [VMEM] * 2, quarters, rows,
        scratch=[pltpu.VMEM((count, lines, LANES), f32), pltpu.VMEM(whole.shape, f32), dma((6,)), dma(())],
        out_specs=[HBM, HBM],
    )
    marginal = call(
        late_kernel, whole, [VMEM, VMEM, HBM], quarters, swap(quarters, core=1), marginal,
        scratch=[pltpu.VMEM((count, 2 * lines, LANES), f32), pltpu.VMEM(whole.shape, f32), dma((6,)), dma((4,))],
        out_specs=HBM,
        alias={2: 0},
    )
    return sigma_panel, marginal


def solution(mesh):
    sizes = dict(mesh.shape)
    prow, pcol = ("prow",), ("pcol",)

    def on_device(sigma_rows, panel, live_block_rows, inv_diag, quad_weight):
        height, count, width = panel.shape[1:]
        fits = (
            split
            and sigma_rows.shape[1] == sigma_rows.shape[2] == sizes["pcol"] * height
            and height % LANES == 0
            and count == 2
            and width == BLOCKS * LANES
        )
        body = square if fits else functools.partial(general, prow)
        return body(sigma_rows, panel, live_block_rows, inv_diag, quad_weight)

    split = sizes["hyp"] == 2 and sizes["pcol"] == 4 and sizes["prow"] == 4
    if split:
        prow = ("side", "core")
        mesh = jax.sharding.Mesh(
            mesh.devices.reshape(sizes["hyp"], 2, 2, sizes["pcol"]),
            ("hyp", "side", "core", "pcol"),
        )
    in_specs = (
        P("hyp", prow, pcol),
        P("hyp", prow + pcol, None, None),
        P(None, prow + pcol),
        P("hyp", None, prow + pcol, None),
        P("hyp"),
    )
    out_specs = (P("hyp", prow + pcol, None, None), P())
    return jax.shard_map(
        on_device, mesh=mesh, in_specs=in_specs, out_specs=out_specs, check_vma=False
    )
```

```python
import functools

import jax
import jax.numpy as jnp
from jax import lax
from jax.experimental import pallas as pl
from jax.experimental.pallas import tpu as pltpu
from jax.sharding import PartitionSpec as P

LANES = 128
ROWS = 16
VMEM = pl.BlockSpec(memory_space=pltpu.VMEM)
SMEM = pl.BlockSpec(memory_space=pltpu.SMEM)
ANY = pl.BlockSpec(memory_space=pl.ANY)
HBM = pl.BlockSpec(memory_space=pltpu.HBM)
AXES = ("hyp", "side", "core", "pcol")


def call(kernel, outs, specs, *operands, scratch=(), out_specs=None, after=(), alias={}):
    many = isinstance(outs, (list, tuple))
    count = len(specs)

    def body(*refs):
        kernel(*refs[:count], *refs[count + len(after) :])

    if out_specs is None:
        out_specs = [VMEM] * len(outs) if many else VMEM
    return pl.pallas_call(
        body,
        out_shape=outs,
        in_specs=list(specs) + [ANY] * len(after),
        out_specs=out_specs,
        scratch_shapes=scratch,
        input_output_aliases=alias,
        compiler_params=pltpu.CompilerParams(vmem_limit_bytes=32 * 2**20),
    )(*operands, *after)


def transposed_dot(left, right):
    return lax.dot_general(
        left, right, (((0,), (0,)), ((), ())), preferred_element_type=jnp.float32
    )


BLOCKS = 3
ABOVE = ((0, 1), (0, 2), (1, 2))
HELD = len(ABOVE) + 2


def block_indices():
    shape = (LANES, LANES)
    return lax.broadcasted_iota(jnp.int32, shape, 0), lax.broadcasted_iota(jnp.int32, shape, 1)


def hold_diagonal(first, second, third):
    row, column = block_indices()
    line = jnp.sum(jnp.where(row == column, second, 0.0), axis=0, keepdims=True)
    last = line[:, LANES - 1 :]
    below = jnp.where(row == LANES - 1, line, jnp.where((row == LANES - 2) & (column == 0), last, 0.0))
    upper = column >= row
    return jnp.where(upper, first, second), jnp.where(upper, third, below)


def restore_diagonal(shared, single):
    row, column = block_indices()
    turned, upper = shared.T, column >= row
    line = jnp.where(column[:1] == LANES - 1, single[LANES - 2 : LANES - 1, :1], single[LANES - 1 :, :])
    second = jnp.where(row == column, line, jnp.where(upper, turned, shared))
    return jnp.where(upper, shared, turned), second, jnp.where(upper, single, single.T)


def general(prow, sigma_rows, panel, live_block_rows, inv_diag, quad_weight):
    height, count, width = panel.shape[1:]
    offsets = lax.broadcasted_iota(jnp.int32, (height, count), 0)
    active = offsets < live_block_rows[:, 0][None, :]
    masked = jnp.where(active[:, :, None], panel[0], jnp.zeros_like(panel[0]))
    gathered = lax.all_gather(masked, prow + ("pcol",), axis=0, tiled=True)
    start = lax.axis_index("pcol") * sigma_rows.shape[2]
    column_panel = lax.dynamic_slice_in_dim(gathered, start, sigma_rows.shape[2], 0)
    applied = lax.psum_scatter(
        jnp.dot(
            sigma_rows[0],
            column_panel.reshape(sigma_rows.shape[2], count * width),
            preferred_element_type=jnp.float32,
        ),
        "pcol",
        scatter_dimension=0,
        tiled=True,
    ).reshape(height, count, width)
    half = applied.astype(jnp.bfloat16)
    sigma_panel = jnp.where(active[:, :, None], -half, jnp.zeros_like(half))[None]
    coupling = jnp.einsum(
        "vwg,vwe->wge",
        masked.astype(jnp.float32),
        applied,
        precision=lax.Precision.HIGHEST,
    )
    diagonal = jnp.einsum(
        "skp,skq->spq", inv_diag[0], inv_diag[0], preferred_element_type=jnp.float32
    )
    marginal = lax.psum(quad_weight[0] * (coupling + diagonal), ("hyp",) + prow + ("pcol",))
    return sigma_panel, marginal


def start_kernel(*refs):
    sources, (own, give, own_inverse, limits), pieces = refs[:4], refs[4:8], refs[8:-5]
    buffers, sems = refs[-5:-1], refs[-1]
    copies = [
        pltpu.make_async_copy(source, buffer, sems.at[index])
        for index, (source, buffer) in enumerate(zip(sources, buffers))
    ]
    for copy in copies:
        copy.start()
    for copy in copies[:3]:
        copy.wait()
    live, panel, inverse, matrix = buffers
    first = lax.axis_index("side") == 0
    row = lax.broadcasted_iota(jnp.int32, own.shape, 0)
    rows = panel[0]
    zero = jnp.zeros(own.shape, own.dtype)
    one, two = (jnp.where(row < live[s], rows[:, s, :], zero) for s in range(2))
    height = own.shape[0]
    own[...] = jnp.where(first, one, two)
    give[:height] = jnp.where(first, two, one)
    spare = jnp.zeros((own_inverse.shape[0] - inverse.shape[2], own.shape[1]), own.dtype)
    one, two = (jnp.concatenate([inverse[0, s], spare], 0) for s in range(2))
    own_inverse[...] = jnp.where(first, one, two)
    give[height:] = jnp.where(first, two, one)
    for s in range(limits.shape[0]):
        limits[s] = jnp.full(limits.shape[1:], live[s], limits.dtype)
    copies[3].wait()
    at = 0
    for piece in pieces:
        piece[...] = matrix[0, :, at : at + piece.shape[0]].T
        at += piece.shape[0]


def set_rows(blocks, rows):
    column, height = lax.axis_index("pcol"), blocks[0].shape[0]
    for step, block in zip((0, 2, 1, 3), blocks):
        spot = jnp.bitwise_xor(column, step)
        rows[pl.ds(pl.multiple_of(spot * height, height), height), :] = block[...]


def own_kernel(*refs):
    blocks, pieces, (rows, applied) = refs[:4], refs[4:-2], refs[-2:]
    set_rows(blocks, rows)
    at = 0
    for piece in pieces:
        applied[at : at + piece.shape[0]] = jnp.dot(piece[...], rows[...], preferred_element_type=jnp.float32)
        at += piece.shape[0]


def gather_kernel(*refs):
    blocks, (own_rows, rows, pack) = refs[:4], refs[4:]
    set_rows(blocks, rows)
    same = lax.axis_index("pcol") // 2 == lax.axis_index("side")
    pack[...] = jnp.where(same, own_rows[...], rows[...])


def apply_kernel(own, rows, *refs):
    count, at = len(refs) // 2, 0
    for piece, applied in zip(refs[:count], refs[count:]):
        lines = slice(at, at + piece.shape[0])
        applied[...] = own[lines] + jnp.dot(piece[...], rows[...], preferred_element_type=jnp.float32)
        at += piece.shape[0]


def couple_kernel(pack, got_pack, own_inverse, got_inverse, *refs):
    core, column = lax.axis_index("core"), lax.axis_index("pcol")
    parts, (keep, send, packed) = refs[:-3], refs[-3:]
    applied = jnp.concatenate([part[...] for part in parts], 0)
    high = applied.astype(jnp.bfloat16)
    low = (applied - high.astype(jnp.float32)).astype(jnp.bfloat16)
    rows = jnp.where(column % 2 == core, pack[...], got_pack[...])
    blocks = {}
    for first in range(BLOCKS):
        left, right = slice(first * LANES, (first + 1) * LANES), slice(first * LANES, None)
        total = transposed_dot(rows[:, left], high[:, right])
        total += transposed_dot(rows[:, left], low[:, right])
        for lines in (own_inverse, got_inverse):
            total += transposed_dot(lines[:, left], lines[:, right])
        for index in range(BLOCKS - first):
            blocks[first, first + index] = total[:, index * LANES : (index + 1) * LANES]
    held = [blocks[place] for place in ABOVE]
    held += hold_diagonal(*(blocks[i, i] for i in range(BLOCKS)))
    for index, block in enumerate(held):
        packed[index * LANES : (index + 1) * LANES, :] = block
    size = keep.shape[0]
    keep[...] = packed[pl.ds(pl.multiple_of(core * size, 8), size), :]
    send[...] = packed[pl.ds(pl.multiple_of((1 - core) * size, 8), size), :]


def halve_kernel(weight, mine, came, keep, send, whole):
    whole[...] = weight[0] * (mine[...] + came[...])
    size, point = keep.shape[0], lax.axis_index("hyp")
    keep[...] = whole[pl.ds(pl.multiple_of(point * size, 8), size), :]
    send[...] = whole[pl.ds(pl.multiple_of((1 - point) * size, 8), size), :]


def output_kernel(*refs):
    parts, (out_near, out_far, half) = refs[:-3], refs[-3:]
    count, at = len(parts) // 2, 0
    for mine, other in zip(parts[:count], parts[count:]):
        half[at : at + mine.shape[0]] = -(mine[...] + other[...]).astype(jnp.bfloat16)
        at += mine.shape[0]
    height, side, core = out_near.shape[0], lax.axis_index("side"), lax.axis_index("core")
    for out, at in ((out_near, side), (out_far, 1 - side)):
        spot = at * 2 + core
        out[...] = half[pl.ds(pl.multiple_of(spot * height, height), height), :]


def add_kernel(mine, came, out):
    out[...] = mine[...] + came[...]


def rows_kernel(limits, near, far, out):
    row = lax.broadcasted_iota(jnp.int32, near.shape, 0)
    first = lax.axis_index("pcol") // 2 == 0
    pair = (jnp.where(first, near[...], far[...]), jnp.where(first, far[...], near[...]))
    for s, value in enumerate(pair):
        out[0, :, s, :] = jnp.where(row < limits[s, :1, :1], value, jnp.zeros(value.shape, value.dtype))


def add_four_kernel(a, b, c, d, out):
    out[...] = (a[...] + b[...]) + (c[...] + d[...])


def stack_kernel(*refs):
    for index, ref in enumerate(refs[:-1]):
        refs[-1][index] = ref[...]


def set_lines(parts, lines, first):
    point, side, size = lax.axis_index("hyp"), lax.axis_index("side"), parts.shape[1]
    for index in range(parts.shape[0]):
        node = 1 - side if index % 2 else side
        slot = 1 - point if index // 2 else point
        lines[node, pl.ds(pl.multiple_of(first + slot * size, 8), size), :] = parts[index]


def copy_out(areas, result, out, sems):
    copies = [
        pltpu.make_async_copy(result.at[area], out.at[area], sems.at[index]) for index, area in enumerate(areas)
    ]
    for copy in copies:
        copy.start()
    return copies


def first_core_blocks(lines, result, out, sems):
    first, rest = slice(0, LANES), slice(LANES, BLOCKS * LANES)
    areas = []
    for node in range(2):
        for index in range(2):
            place = slice((index + 1) * LANES, (index + 2) * LANES)
            tile = lines[node, index * LANES : (index + 1) * LANES, :]
            result[node, first, place] = tile
            result[node, place, first] = tile.T
        areas += [(node, first, rest), (node, rest, first)]
    return copy_out(areas, result, out, sems)


def second_core_blocks(lines, at, result, out, sems):
    areas = []
    for node in range(2):
        held = (lines[node, at + index * LANES : at + (index + 1) * LANES, :] for index in range(2))
        for index, tile in enumerate(restore_diagonal(*held)):
            place = slice(index * LANES, (index + 1) * LANES)
            result[node, place, place] = tile
            areas.append((node, place, place))
    return copy_out(areas, result, out, sems)


def early_kernel(own, rows, rows_out, out, lines, result, sems, rows_sem):
    store = pltpu.make_async_copy(rows, rows_out, rows_sem)
    store.start()
    core = lax.axis_index("core")
    set_lines(own, lines, 0)

    @pl.when(core == 0)
    def _():
        for copy in first_core_blocks(lines, result, out, sems):
            copy.wait()

    @pl.when(core == 1)
    def _():
        for copy in second_core_blocks(lines, LANES // 2, result, out, sems):
            copy.wait()

    store.wait()


def late_kernel(own, other, before, out, lines, result, sems, middle_sems):
    del before
    core, half = lax.axis_index("core"), lines.shape[1] // 2
    set_lines(own, lines, core * half)
    set_lines(other, lines, (1 - core) * half)
    middle, last = (slice(i * LANES, (i + 1) * LANES) for i in (1, 2))
    areas = []
    for node in range(2):
        tile = lines[node, 2 * LANES : 3 * LANES, :]
        result[node, middle, last] = tile
        result[node, last, middle] = tile.T
        areas += [(node, middle, last), (node, last, middle)]
    shared = copy_out(areas, result, out, middle_sems)

    @pl.when(core == 1)
    def _():
        for copy in first_core_blocks(lines, result, out, sems):
            copy.wait()

    @pl.when(core == 0)
    def _():
        for copy in second_core_blocks(lines, len(ABOVE) * LANES, result, out, sems):
            copy.wait()

    for copy in shared:
        copy.wait()


def square(sigma_rows, panel, live_block_rows, inv_diag, quad_weight):
    height, count, width = panel.shape[1:]
    grid = lax.axis_size("pcol")
    points = lax.axis_size("hyp")
    f32, bf16 = jnp.float32, jnp.bfloat16
    shape = jax.ShapeDtypeStruct
    dma = pltpu.SemaphoreType.DMA
    stay = functools.partial(pltpu.with_memory_space_constraint, memory_space=pltpu.HBM)
    devices = points * 2 * 2 * grid
    live = live_block_rows[:, 0]

    def swap(x, point=0, side=0, core=0, column=0):
        mask = ((point * 2 + side) * 2 + core) * grid + column
        return lax.ppermute(x, AXES, [(i, i ^ mask) for i in range(devices)])

    extent = sigma_rows.shape[2]
    block = shape((height, width), bf16)
    cuts = (extent // 2, extent // 2)
    size = pl.cdiv(inv_diag.shape[2], ROWS) * ROWS
    own, give, own_inverse, limits, *pieces = call(
        start_kernel,
        [block, shape((height + size, width), bf16), shape((size, width), bf16)]
        + [shape((count, 8, LANES), jnp.int32)]
        + [shape((lines, extent), bf16) for lines in cuts],
        [HBM] * 4,
        *map(stay, (live, panel, inv_diag, sigma_rows)),
        scratch=[pltpu.SMEM(live.shape, jnp.int32)]
        + [pltpu.VMEM(x.shape, bf16) for x in (panel, inv_diag, sigma_rows)]
        + [dma((4,))],
    )
    got = swap(give, side=1)
    got, got_inverse = got[:height], got[height:]
    blocks = []
    for one in (own, got):
        two = swap(one, column=2)
        blocks += [one, two, swap(one, column=1), swap(two, column=1)]
    far = [swap(piece, side=1) for piece in pieces]


    product, line_shape = shape((extent, width), f32), shape((extent, width), bf16)
    own_rows, own_product = call(
        own_kernel, [line_shape, product], [VMEM] * (4 + len(cuts)), *blocks[:4], *pieces
    )
    rows, pack = call(
        gather_kernel, [line_shape] * 2, [VMEM] * 5, *blocks[4:], own_rows, after=far
    )
    got_pack = swap(pack, core=1)
    mine = call(
        apply_kernel, [shape((lines, width), f32) for lines in cuts], [VMEM] * (2 + len(cuts)),
        own_product, rows, *far,
    )
    lines = HELD * LANES // 2
    part, half = shape((lines // 2, LANES), f32), shape((lines, LANES), f32)
    other = [swap(x, core=1) for x in mine]
    keep, send = call(
        couple_kernel, [half, half], [VMEM] * (4 + len(cuts)),
        pack, got_pack, own_inverse, got_inverse, *mine,
        scratch=[pltpu.VMEM((2 * lines, LANES), f32)],
    )
    keep, send = call(
        halve_kernel, [part, part], [SMEM] + [VMEM] * 2, quad_weight, keep, swap(send, core=1),
        scratch=[pltpu.VMEM((lines, LANES), f32)],
    )
    def deliver(x, flip):
        pairs = []
        for i in range(devices):
            h, s, k, c = i // (4 * grid), i // (2 * grid) % 2, i // grid % 2, i % grid
            pairs.append((i, (h * 4 + c) * grid + 2 * (s ^ flip) + k))
        return lax.ppermute(x, AXES, pairs)

    total = call(
        add_four_kernel, part, [VMEM] * 4,
        keep, swap(send, point=1), swap(keep, column=1), swap(send, point=1, column=1),
    )
    out_near, out_far = call(
        output_kernel, [block, block], [VMEM] * (2 * len(cuts)), *mine, *other,
        scratch=[pltpu.VMEM((extent, width), bf16)],
        after=[keep],
    )
    near, far = deliver(out_near, 0), deliver(out_far, 1)
    total = call(add_kernel, part, [VMEM] * 2, total, swap(total, column=2))
    quarters = [total, swap(total, side=1), swap(total, point=1), swap(total, side=1, point=1)]
    rows = call(
        rows_kernel, shape((1, height, count, width), bf16), [VMEM] * 3, limits, near, far
    )
    quarters = call(
        stack_kernel, shape((len(quarters), *part.shape), f32), [VMEM] * len(quarters), *quarters, after=[rows]
    )
    whole = shape((count, width, width), f32)
    sigma_panel, marginal = call(
        early_kernel, [shape(rows.shape, bf16), whole], [VMEM] * 2, quarters, rows,
        scratch=[pltpu.VMEM((count, lines, LANES), f32), pltpu.VMEM(whole.shape, f32), dma((6,)), dma(())],
        out_specs=[HBM, HBM],
    )
    marginal = call(
        late_kernel, whole, [VMEM, VMEM, HBM], quarters, swap(quarters, core=1), marginal,
        scratch=[pltpu.VMEM((count, 2 * lines, LANES), f32), pltpu.VMEM(whole.shape, f32), dma((6,)), dma((4,))],
        out_specs=HBM,
        alias={2: 0},
    )
    return sigma_panel, marginal


def solution(mesh):
    sizes = dict(mesh.shape)
    prow, pcol = ("prow",), ("pcol",)

    def on_device(sigma_rows, panel, live_block_rows, inv_diag, quad_weight):
        height, count, width = panel.shape[1:]
        fits = (
            split
            and sigma_rows.shape[1] == sigma_rows.shape[2] == sizes["pcol"] * height
            and height % LANES == 0
            and count == 2
            and width == BLOCKS * LANES
        )
        body = square if fits else functools.partial(general, prow)
        return body(sigma_rows, panel, live_block_rows, inv_diag, quad_weight)

    split = sizes["hyp"] == 2 and sizes["pcol"] == 4 and sizes["prow"] == 4
    if split:
        prow = ("side", "core")
        mesh = jax.sharding.Mesh(
            mesh.devices.reshape(sizes["hyp"], 2, 2, sizes["pcol"]),
            ("hyp", "side", "core", "pcol"),
        )
    in_specs = (
        P("hyp", prow, pcol),
        P("hyp", prow + pcol, None, None),
        P(None, prow + pcol),
        P("hyp", None, prow + pcol, None),
        P("hyp"),
    )
    out_specs = (P("hyp", prow + pcol, None, None), P())
    return jax.shard_map(
        on_device, mesh=mesh, in_specs=in_specs, out_specs=out_specs, check_vma=False
    )
```

```python
import functools

import jax
import jax.numpy as jnp
from jax import lax
from jax.experimental import pallas as pl
from jax.experimental.pallas import tpu as pltpu
from jax.sharding import PartitionSpec as P

LANES = 128
ROWS = 16
VMEM = pl.BlockSpec(memory_space=pltpu.VMEM)
SMEM = pl.BlockSpec(memory_space=pltpu.SMEM)
ANY = pl.BlockSpec(memory_space=pl.ANY)
HBM = pl.BlockSpec(memory_space=pltpu.HBM)
AXES = ("hyp", "side", "core", "pcol")


def call(kernel, outs, specs, *operands, scratch=(), out_specs=None, after=(), alias={}):
    many = isinstance(outs, (list, tuple))
    count = len(specs)

    def body(*refs):
        kernel(*refs[:count], *refs[count + len(after) :])

    if out_specs is None:
        out_specs = [VMEM] * len(outs) if many else VMEM
    return pl.pallas_call(
        body,
        out_shape=outs,
        in_specs=list(specs) + [ANY] * len(after),
        out_specs=out_specs,
        scratch_shapes=scratch,
        input_output_aliases=alias,
        compiler_params=pltpu.CompilerParams(vmem_limit_bytes=32 * 2**20),
    )(*operands, *after)


def transposed_dot(left, right):
    return lax.dot_general(
        left, right, (((0,), (0,)), ((), ())), preferred_element_type=jnp.float32
    )


BLOCKS = 3
ABOVE = ((0, 1), (0, 2), (1, 2))
HELD = len(ABOVE) + 2


def block_indices():
    shape = (LANES, LANES)
    return lax.broadcasted_iota(jnp.int32, shape, 0), lax.broadcasted_iota(jnp.int32, shape, 1)


def hold_diagonal(first, second, third):
    row, column = block_indices()
    line = jnp.sum(jnp.where(row == column, second, 0.0), axis=0, keepdims=True)
    last = line[:, LANES - 1 :]
    below = jnp.where(row == LANES - 1, line, jnp.where((row == LANES - 2) & (column == 0), last, 0.0))
    upper = column >= row
    return jnp.where(upper, first, second), jnp.where(upper, third, below)


def restore_diagonal(shared, single):
    row, column = block_indices()
    turned, upper = shared.T, column >= row
    line = jnp.where(column[:1] == LANES - 1, single[LANES - 2 : LANES - 1, :1], single[LANES - 1 :, :])
    second = jnp.where(row == column, line, jnp.where(upper, turned, shared))
    return jnp.where(upper, shared, turned), second, jnp.where(upper, single, single.T)


def general(prow, sigma_rows, panel, live_block_rows, inv_diag, quad_weight):
    height, count, width = panel.shape[1:]
    offsets = lax.broadcasted_iota(jnp.int32, (height, count), 0)
    active = offsets < live_block_rows[:, 0][None, :]
    masked = jnp.where(active[:, :, None], panel[0], jnp.zeros_like(panel[0]))
    gathered = lax.all_gather(masked, prow + ("pcol",), axis=0, tiled=True)
    start = lax.axis_index("pcol") * sigma_rows.shape[2]
    column_panel = lax.dynamic_slice_in_dim(gathered, start, sigma_rows.shape[2], 0)
    applied = lax.psum_scatter(
        jnp.dot(
            sigma_rows[0],
            column_panel.reshape(sigma_rows.shape[2], count * width),
            preferred_element_type=jnp.float32,
        ),
        "pcol",
        scatter_dimension=0,
        tiled=True,
    ).reshape(height, count, width)
    half = applied.astype(jnp.bfloat16)
    sigma_panel = jnp.where(active[:, :, None], -half, jnp.zeros_like(half))[None]
    coupling = jnp.einsum(
        "vwg,vwe->wge",
        masked.astype(jnp.float32),
        applied,
        precision=lax.Precision.HIGHEST,
    )
    diagonal = jnp.einsum(
        "skp,skq->spq", inv_diag[0], inv_diag[0], preferred_element_type=jnp.float32
    )
    marginal = lax.psum(quad_weight[0] * (coupling + diagonal), ("hyp",) + prow + ("pcol",))
    return sigma_panel, marginal


def start_kernel(*refs):
    sources, (own, give, own_inverse, limits), pieces = refs[:4], refs[4:8], refs[8:-5]
    buffers, sems = refs[-5:-1], refs[-1]
    copies = [
        pltpu.make_async_copy(source, buffer, sems.at[index])
        for index, (source, buffer) in enumerate(zip(sources, buffers))
    ]
    for copy in copies:
        copy.start()
    for copy in copies[:3]:
        copy.wait()
    live, panel, inverse, matrix = buffers
    first = lax.axis_index("side") == 0
    row = lax.broadcasted_iota(jnp.int32, own.shape, 0)
    rows = panel[0]
    zero = jnp.zeros(own.shape, own.dtype)
    one, two = (jnp.where(row < live[s], rows[:, s, :], zero) for s in range(2))
    height = own.shape[0]
    own[...] = jnp.where(first, one, two)
    give[:height] = jnp.where(first, two, one)
    spare = jnp.zeros((own_inverse.shape[0] - inverse.shape[2], own.shape[1]), own.dtype)
    one, two = (jnp.concatenate([inverse[0, s], spare], 0) for s in range(2))
    own_inverse[...] = jnp.where(first, one, two)
    give[height:] = jnp.where(first, two, one)
    for s in range(limits.shape[0]):
        limits[s] = jnp.full(limits.shape[1:], live[s], limits.dtype)
    copies[3].wait()
    at = 0
    for piece in pieces:
        piece[...] = matrix[0, :, at : at + piece.shape[0]].T
        at += piece.shape[0]


def set_rows(blocks, rows):
    column, height = lax.axis_index("pcol"), blocks[0].shape[0]
    for step, block in zip((0, 2, 1, 3), blocks):
        spot = jnp.bitwise_xor(column, step)
        rows[pl.ds(pl.multiple_of(spot * height, height), height), :] = block[...]


def own_kernel(*refs):
    weight, blocks, pieces, (rows, applied, tile) = refs[0], refs[1:5], refs[5:-3], refs[-3:]
    tile[...] = jnp.full(tile.shape, weight[0], tile.dtype)
    set_rows(blocks, rows)
    at = 0
    for piece in pieces:
        applied[at : at + piece.shape[0]] = jnp.dot(piece[...], rows[...], preferred_element_type=jnp.float32)
        at += piece.shape[0]


def gather_kernel(*refs):
    blocks, (own_rows, rows, pack) = refs[:4], refs[4:]
    set_rows(blocks, rows)
    same = lax.axis_index("pcol") // 2 == lax.axis_index("side")
    pack[...] = jnp.where(same, own_rows[...], rows[...])


def apply_kernel(own, rows, *refs):
    count, at = len(refs) // 2, 0
    for piece, applied in zip(refs[:count], refs[count:]):
        lines = slice(at, at + piece.shape[0])
        applied[...] = own[lines] + jnp.dot(piece[...], rows[...], preferred_element_type=jnp.float32)
        at += piece.shape[0]


def couple_kernel(pack, got_pack, own_inverse, got_inverse, *refs):
    core, column = lax.axis_index("core"), lax.axis_index("pcol")
    parts, (keep, send, packed) = refs[:-3], refs[-3:]
    applied = jnp.concatenate([part[...] for part in parts], 0)
    high = applied.astype(jnp.bfloat16)
    low = (applied - high.astype(jnp.float32)).astype(jnp.bfloat16)
    rows = jnp.where(column % 2 == core, pack[...], got_pack[...])
    blocks = {}
    for first in range(BLOCKS):
        left, right = slice(first * LANES, (first + 1) * LANES), slice(first * LANES, None)
        total = transposed_dot(rows[:, left], high[:, right])
        total += transposed_dot(rows[:, left], low[:, right])
        for lines in (own_inverse, got_inverse):
            total += transposed_dot(lines[:, left], lines[:, right])
        for index in range(BLOCKS - first):
            blocks[first, first + index] = total[:, index * LANES : (index + 1) * LANES]
    held = [blocks[place] for place in ABOVE]
    held += hold_diagonal(*(blocks[i, i] for i in range(BLOCKS)))
    for index, block in enumerate(held):
        packed[index * LANES : (index + 1) * LANES, :] = block
    size = keep.shape[0]
    keep[...] = packed[pl.ds(pl.multiple_of(core * size, 8), size), :]
    send[...] = packed[pl.ds(pl.multiple_of((1 - core) * size, 8), size), :]


def halve_kernel(weight, mine, came, keep, send, whole):
    whole[...] = weight[:1] * (mine[...] + came[...])
    size, point = keep.shape[0], lax.axis_index("hyp")
    keep[...] = whole[pl.ds(pl.multiple_of(point * size, 8), size), :]
    send[...] = whole[pl.ds(pl.multiple_of((1 - point) * size, 8), size), :]


def output_kernel(*refs):
    parts, (out_near, out_far, half) = refs[:-3], refs[-3:]
    count, at = len(parts) // 2, 0
    for mine, other in zip(parts[:count], parts[count:]):
        half[at : at + mine.shape[0]] = -(mine[...] + other[...]).astype(jnp.bfloat16)
        at += mine.shape[0]
    height, side, core = out_near.shape[0], lax.axis_index("side"), lax.axis_index("core")
    for out, at in ((out_near, side), (out_far, 1 - side)):
        spot = at * 2 + core
        out[...] = half[pl.ds(pl.multiple_of(spot * height, height), height), :]


def add_kernel(mine, came, out):
    out[...] = mine[...] + came[...]


def rows_kernel(limits, near, far, out):
    row = lax.broadcasted_iota(jnp.int32, near.shape, 0)
    first = lax.axis_index("pcol") // 2 == 0
    pair = (jnp.where(first, near[...], far[...]), jnp.where(first, far[...], near[...]))
    for s, value in enumerate(pair):
        out[0, :, s, :] = jnp.where(row < limits[s, :1, :1], value, jnp.zeros(value.shape, value.dtype))


def add_four_kernel(a, b, c, d, out):
    out[...] = (a[...] + b[...]) + (c[...] + d[...])


def stack_kernel(*refs):
    for index, ref in enumerate(refs[:-1]):
        refs[-1][index] = ref[...]


def set_lines(parts, lines, first):
    point, side, size = lax.axis_index("hyp"), lax.axis_index("side"), parts.shape[1]
    for index in range(parts.shape[0]):
        node = 1 - side if index % 2 else side
        slot = 1 - point if index // 2 else point
        lines[node, pl.ds(pl.multiple_of(first + slot * size, 8), size), :] = parts[index]


def copy_out(areas, result, out, sems):
    copies = [
        pltpu.make_async_copy(result.at[area], out.at[area], sems.at[index]) for index, area in enumerate(areas)
    ]
    for copy in copies:
        copy.start()
    return copies


def first_core_blocks(lines, result, out, sems):
    first, rest = slice(0, LANES), slice(LANES, BLOCKS * LANES)
    areas = []
    for node in range(2):
        for index in range(2):
            place = slice((index + 1) * LANES, (index + 2) * LANES)
            tile = lines[node, index * LANES : (index + 1) * LANES, :]
            result[node, first, place] = tile
            result[node, place, first] = tile.T
        areas += [(node, first, rest), (node, rest, first)]
    return copy_out(areas, result, out, sems)


def second_core_blocks(lines, at, result, out, sems):
    areas = []
    for node in range(2):
        held = (lines[node, at + index * LANES : at + (index + 1) * LANES, :] for index in range(2))
        for index, tile in enumerate(restore_diagonal(*held)):
            place = slice(index * LANES, (index + 1) * LANES)
            result[node, place, place] = tile
            areas.append((node, place, place))
    return copy_out(areas, result, out, sems)


def early_kernel(own, rows, rows_out, out, lines, result, sems, rows_sem):
    store = pltpu.make_async_copy(rows, rows_out, rows_sem)
    store.start()
    core = lax.axis_index("core")
    set_lines(own, lines, 0)

    @pl.when(core == 0)
    def _():
        for copy in first_core_blocks(lines, result, out, sems):
            copy.wait()

    @pl.when(core == 1)
    def _():
        for copy in second_core_blocks(lines, LANES // 2, result, out, sems):
            copy.wait()

    store.wait()


def late_kernel(own, other, before, out, lines, result, sems, middle_sems):
    del before
    core, half = lax.axis_index("core"), lines.shape[1] // 2
    set_lines(own, lines, core * half)
    set_lines(other, lines, (1 - core) * half)
    middle, last = (slice(i * LANES, (i + 1) * LANES) for i in (1, 2))
    areas = []
    for node in range(2):
        tile = lines[node, 2 * LANES : 3 * LANES, :]
        result[node, middle, last] = tile
        result[node, last, middle] = tile.T
        areas += [(node, middle, last), (node, last, middle)]
    shared = copy_out(areas, result, out, middle_sems)

    @pl.when(core == 1)
    def _():
        for copy in first_core_blocks(lines, result, out, sems):
            copy.wait()

    @pl.when(core == 0)
    def _():
        for copy in second_core_blocks(lines, len(ABOVE) * LANES, result, out, sems):
            copy.wait()

    for copy in shared:
        copy.wait()


def square(sigma_rows, panel, live_block_rows, inv_diag, quad_weight):
    height, count, width = panel.shape[1:]
    grid = lax.axis_size("pcol")
    points = lax.axis_size("hyp")
    f32, bf16 = jnp.float32, jnp.bfloat16
    shape = jax.ShapeDtypeStruct
    dma = pltpu.SemaphoreType.DMA
    stay = functools.partial(pltpu.with_memory_space_constraint, memory_space=pltpu.HBM)
    devices = points * 2 * 2 * grid
    live = live_block_rows[:, 0]

    def swap(x, point=0, side=0, core=0, column=0):
        mask = ((point * 2 + side) * 2 + core) * grid + column
        return lax.ppermute(x, AXES, [(i, i ^ mask) for i in range(devices)])

    extent = sigma_rows.shape[2]
    block = shape((height, width), bf16)
    cuts = (extent // 2, extent // 2)
    size = pl.cdiv(inv_diag.shape[2], ROWS) * ROWS
    own, give, own_inverse, limits, *pieces = call(
        start_kernel,
        [block, shape((height + size, width), bf16), shape((size, width), bf16)]
        + [shape((count, 8, LANES), jnp.int32)]
        + [shape((lines, extent), bf16) for lines in cuts],
        [HBM] * 4,
        *map(stay, (live, panel, inv_diag, sigma_rows)),
        scratch=[pltpu.SMEM(live.shape, jnp.int32)]
        + [pltpu.VMEM(x.shape, bf16) for x in (panel, inv_diag, sigma_rows)]
        + [dma((4,))],
    )
    got = swap(give, side=1)
    got, got_inverse = got[:height], got[height:]
    blocks = []
    for one in (own, got):
        two = swap(one, column=2)
        blocks += [one, two, swap(one, column=1), swap(two, column=1)]
    far = [swap(piece, side=1) for piece in pieces]


    product, line_shape = shape((extent, width), f32), shape((extent, width), bf16)
    own_rows, own_product, weight = call(
        own_kernel, [line_shape, product, shape((8, LANES), f32)], [SMEM] + [VMEM] * (4 + len(cuts)),
        quad_weight, *blocks[:4], *pieces,
    )
    rows, pack = call(
        gather_kernel, [line_shape] * 2, [VMEM] * 5, *blocks[4:], own_rows, after=far
    )
    got_pack = swap(pack, core=1)
    mine = call(
        apply_kernel, [shape((lines, width), f32) for lines in cuts], [VMEM] * (2 + len(cuts)),
        own_product, rows, *far,
    )
    lines = HELD * LANES // 2
    part, half = shape((lines // 2, LANES), f32), shape((lines, LANES), f32)
    other = [swap(x, core=1) for x in mine]
    keep, send = call(
        couple_kernel, [half, half], [VMEM] * (4 + len(cuts)),
        pack, got_pack, own_inverse, got_inverse, *mine,
        scratch=[pltpu.VMEM((2 * lines, LANES), f32)],
    )
    keep, send = call(
        halve_kernel, [part, part], [VMEM] * 3, weight, keep, swap(send, core=1),
        scratch=[pltpu.VMEM((lines, LANES), f32)],
    )
    def deliver(x, flip):
        pairs = []
        for i in range(devices):
            h, s, k, c = i // (4 * grid), i // (2 * grid) % 2, i // grid % 2, i % grid
            pairs.append((i, (h * 4 + c) * grid + 2 * (s ^ flip) + k))
        return lax.ppermute(x, AXES, pairs)

    total = call(
        add_four_kernel, part, [VMEM] * 4,
        keep, swap(send, point=1), swap(keep, column=1), swap(send, point=1, column=1),
    )
    out_near, out_far = call(
        output_kernel, [block, block], [VMEM] * (2 * len(cuts)), *mine, *other,
        scratch=[pltpu.VMEM((extent, width), bf16)],
        after=[keep],
    )
    near, far = deliver(out_near, 0), deliver(out_far, 1)
    total = call(add_kernel, part, [VMEM] * 2, total, swap(total, column=2))
    quarters = [total, swap(total, side=1), swap(total, point=1), swap(total, side=1, point=1)]
    rows = call(
        rows_kernel, shape((1, height, count, width), bf16), [VMEM] * 3, limits, near, far
    )
    quarters = call(
        stack_kernel, shape((len(quarters), *part.shape), f32), [VMEM] * len(quarters), *quarters, after=[rows]
    )
    whole = shape((count, width, width), f32)
    sigma_panel, marginal = call(
        early_kernel, [shape(rows.shape, bf16), whole], [VMEM] * 2, quarters, rows,
        scratch=[pltpu.VMEM((count, lines, LANES), f32), pltpu.VMEM(whole.shape, f32), dma((6,)), dma(())],
        out_specs=[HBM, HBM],
    )
    marginal = call(
        late_kernel, whole, [VMEM, VMEM, HBM], quarters, swap(quarters, core=1), marginal,
        scratch=[pltpu.VMEM((count, 2 * lines, LANES), f32), pltpu.VMEM(whole.shape, f32), dma((6,)), dma((4,))],
        out_specs=HBM,
        alias={2: 0},
    )
    return sigma_panel, marginal


def solution(mesh):
    sizes = dict(mesh.shape)
    prow, pcol = ("prow",), ("pcol",)

    def on_device(sigma_rows, panel, live_block_rows, inv_diag, quad_weight):
        height, count, width = panel.shape[1:]
        fits = (
            split
            and sigma_rows.shape[1] == sigma_rows.shape[2] == sizes["pcol"] * height
            and height % LANES == 0
            and count == 2
            and width == BLOCKS * LANES
        )
        body = square if fits else functools.partial(general, prow)
        return body(sigma_rows, panel, live_block_rows, inv_diag, quad_weight)

    split = sizes["hyp"] == 2 and sizes["pcol"] == 4 and sizes["prow"] == 4
    if split:
        prow = ("side", "core")
        mesh = jax.sharding.Mesh(
            mesh.devices.reshape(sizes["hyp"], 2, 2, sizes["pcol"]),
            ("hyp", "side", "core", "pcol"),
        )
    in_specs = (
        P("hyp", prow, pcol),
        P("hyp", prow + pcol, None, None),
        P(None, prow + pcol),
        P("hyp", None, prow + pcol, None),
        P("hyp"),
    )
    out_specs = (P("hyp", prow + pcol, None, None), P())
    return jax.shard_map(
        on_device, mesh=mesh, in_specs=in_specs, out_specs=out_specs, check_vma=False
    )
```

```python
import functools

import jax
import jax.numpy as jnp
from jax import lax
from jax.experimental import pallas as pl
from jax.experimental.pallas import tpu as pltpu
from jax.sharding import PartitionSpec as P

LANES = 128
ROWS = 16
VMEM = pl.BlockSpec(memory_space=pltpu.VMEM)
SMEM = pl.BlockSpec(memory_space=pltpu.SMEM)
ANY = pl.BlockSpec(memory_space=pl.ANY)
HBM = pl.BlockSpec(memory_space=pltpu.HBM)
AXES = ("hyp", "side", "core", "pcol")


def call(kernel, outs, specs, *operands, scratch=(), out_specs=None, after=(), alias={}):
    many = isinstance(outs, (list, tuple))
    count = len(specs)

    def body(*refs):
        kernel(*refs[:count], *refs[count + len(after) :])

    if out_specs is None:
        out_specs = [VMEM] * len(outs) if many else VMEM
    return pl.pallas_call(
        body,
        out_shape=outs,
        in_specs=list(specs) + [ANY] * len(after),
        out_specs=out_specs,
        scratch_shapes=scratch,
        input_output_aliases=alias,
        compiler_params=pltpu.CompilerParams(vmem_limit_bytes=32 * 2**20),
    )(*operands, *after)


def transposed_dot(left, right):
    return lax.dot_general(
        left, right, (((0,), (0,)), ((), ())), preferred_element_type=jnp.float32
    )


BLOCKS = 3
ABOVE = ((0, 1), (0, 2), (1, 2))
HELD = len(ABOVE) + 2


def block_indices():
    shape = (LANES, LANES)
    return lax.broadcasted_iota(jnp.int32, shape, 0), lax.broadcasted_iota(jnp.int32, shape, 1)


def hold_diagonal(first, second, third):
    row, column = block_indices()
    line = jnp.sum(jnp.where(row == column, second, 0.0), axis=0, keepdims=True)
    last = line[:, LANES - 1 :]
    below = jnp.where(row == LANES - 1, line, jnp.where((row == LANES - 2) & (column == 0), last, 0.0))
    upper = column >= row
    return jnp.where(upper, first, second), jnp.where(upper, third, below)


def restore_diagonal(shared, single):
    row, column = block_indices()
    turned, upper = shared.T, column >= row
    line = jnp.where(column[:1] == LANES - 1, single[LANES - 2 : LANES - 1, :1], single[LANES - 1 :, :])
    second = jnp.where(row == column, line, jnp.where(upper, turned, shared))
    return jnp.where(upper, shared, turned), second, jnp.where(upper, single, single.T)


def general(prow, sigma_rows, panel, live_block_rows, inv_diag, quad_weight):
    height, count, width = panel.shape[1:]
    offsets = lax.broadcasted_iota(jnp.int32, (height, count), 0)
    active = offsets < live_block_rows[:, 0][None, :]
    masked = jnp.where(active[:, :, None], panel[0], jnp.zeros_like(panel[0]))
    gathered = lax.all_gather(masked, prow + ("pcol",), axis=0, tiled=True)
    start = lax.axis_index("pcol") * sigma_rows.shape[2]
    column_panel = lax.dynamic_slice_in_dim(gathered, start, sigma_rows.shape[2], 0)
    applied = lax.psum_scatter(
        jnp.dot(
            sigma_rows[0],
            column_panel.reshape(sigma_rows.shape[2], count * width),
            preferred_element_type=jnp.float32,
        ),
        "pcol",
        scatter_dimension=0,
        tiled=True,
    ).reshape(height, count, width)
    half = applied.astype(jnp.bfloat16)
    sigma_panel = jnp.where(active[:, :, None], -half, jnp.zeros_like(half))[None]
    coupling = jnp.einsum(
        "vwg,vwe->wge",
        masked.astype(jnp.float32),
        applied,
        precision=lax.Precision.HIGHEST,
    )
    diagonal = jnp.einsum(
        "skp,skq->spq", inv_diag[0], inv_diag[0], preferred_element_type=jnp.float32
    )
    marginal = lax.psum(quad_weight[0] * (coupling + diagonal), ("hyp",) + prow + ("pcol",))
    return sigma_panel, marginal


def start_kernel(*refs):
    sources, (own, give, own_inverse, limits), pieces = refs[:4], refs[4:8], refs[8:-5]
    buffers, sems = refs[-5:-1], refs[-1]
    copies = [
        pltpu.make_async_copy(source, buffer, sems.at[index])
        for index, (source, buffer) in enumerate(zip(sources, buffers))
    ]
    for copy in copies:
        copy.start()
    for copy in copies[:3]:
        copy.wait()
    live, panel, inverse, matrix = buffers
    first = lax.axis_index("side") == 0
    row = lax.broadcasted_iota(jnp.int32, own.shape, 0)
    rows = panel[0]
    zero = jnp.zeros(own.shape, own.dtype)
    one, two = (jnp.where(row < live[s], rows[:, s, :], zero) for s in range(2))
    height = own.shape[0]
    own[...] = jnp.where(first, one, two)
    give[:height] = jnp.where(first, two, one)
    spare = jnp.zeros((own_inverse.shape[0] - inverse.shape[2], own.shape[1]), own.dtype)
    one, two = (jnp.concatenate([inverse[0, s], spare], 0) for s in range(2))
    own_inverse[...] = jnp.where(first, one, two)
    give[height:] = jnp.where(first, two, one)
    for s in range(limits.shape[0]):
        limits[s] = jnp.full(limits.shape[1:], live[s], limits.dtype)
    copies[3].wait()
    at = 0
    for piece in pieces:
        piece[...] = matrix[0, :, at : at + piece.shape[0]].T
        at += piece.shape[0]


def set_rows(blocks, rows):
    column, height = lax.axis_index("pcol"), blocks[0].shape[0]
    for step, block in zip((0, 2, 1, 3), blocks):
        spot = jnp.bitwise_xor(column, step)
        rows[pl.ds(pl.multiple_of(spot * height, height), height), :] = block[...]


def own_kernel(*refs):
    weight, inverses, blocks, pieces = refs[0], refs[1:3], refs[3:7], refs[7:-4]
    rows, applied, tile, base = refs[-4:]
    tile[...] = jnp.full(tile.shape, weight[0], tile.dtype)
    base[...] = sum(transposed_dot(lines[...], lines[...]) for lines in inverses)
    set_rows(blocks, rows)
    at = 0
    for piece in pieces:
        applied[at : at + piece.shape[0]] = jnp.dot(piece[...], rows[...], preferred_element_type=jnp.float32)
        at += piece.shape[0]


def gather_kernel(*refs):
    blocks, (own_rows, rows, pack) = refs[:4], refs[4:]
    set_rows(blocks, rows)
    same = lax.axis_index("pcol") // 2 == lax.axis_index("side")
    pack[...] = jnp.where(same, own_rows[...], rows[...])


def apply_kernel(own, rows, *refs):
    pieces, outs, (high, low) = refs[: len(refs) // 2 - 1], refs[len(refs) // 2 - 1 : -2], refs[-2:]
    at = 0
    for piece, out in zip(pieces, outs):
        lines = slice(at, at + piece.shape[0])
        applied = own[lines] + jnp.dot(piece[...], rows[...], preferred_element_type=jnp.float32)
        out[...] = applied
        high[lines] = applied.astype(jnp.bfloat16)
        low[lines] = (applied - applied.astype(jnp.bfloat16).astype(jnp.float32)).astype(jnp.bfloat16)
        at += piece.shape[0]


def couple_kernel(pack, got_pack, high, low, base, keep, send, packed):
    core, column = lax.axis_index("core"), lax.axis_index("pcol")
    rows = jnp.where(column % 2 == core, pack[...], got_pack[...])
    blocks = {}
    for first in range(BLOCKS):
        left, right = slice(first * LANES, (first + 1) * LANES), slice(first * LANES, None)
        total = transposed_dot(rows[:, left], high[:, right])
        total += transposed_dot(rows[:, left], low[:, right])
        total += base[left, right]
        for index in range(BLOCKS - first):
            blocks[first, first + index] = total[:, index * LANES : (index + 1) * LANES]
    held = [blocks[place] for place in ABOVE]
    held += hold_diagonal(*(blocks[i, i] for i in range(BLOCKS)))
    for index, block in enumerate(held):
        packed[index * LANES : (index + 1) * LANES, :] = block
    size = keep.shape[0]
    keep[...] = packed[pl.ds(pl.multiple_of(core * size, 8), size), :]
    send[...] = packed[pl.ds(pl.multiple_of((1 - core) * size, 8), size), :]


def halve_kernel(weight, mine, came, keep, send, whole):
    whole[...] = weight[:1] * (mine[...] + came[...])
    size, point = keep.shape[0], lax.axis_index("hyp")
    keep[...] = whole[pl.ds(pl.multiple_of(point * size, 8), size), :]
    send[...] = whole[pl.ds(pl.multiple_of((1 - point) * size, 8), size), :]


def output_kernel(*refs):
    parts, (out_near, out_far, half) = refs[:-3], refs[-3:]
    count, at = len(parts) // 2, 0
    for mine, other in zip(parts[:count], parts[count:]):
        half[at : at + mine.shape[0]] = -(mine[...] + other[...]).astype(jnp.bfloat16)
        at += mine.shape[0]
    height, side, core = out_near.shape[0], lax.axis_index("side"), lax.axis_index("core")
    for out, at in ((out_near, side), (out_far, 1 - side)):
        spot = at * 2 + core
        out[...] = half[pl.ds(pl.multiple_of(spot * height, height), height), :]


def add_kernel(mine, came, out):
    out[...] = mine[...] + came[...]


def rows_kernel(limits, near, far, out):
    row = lax.broadcasted_iota(jnp.int32, near.shape, 0)
    first = lax.axis_index("pcol") // 2 == 0
    pair = (jnp.where(first, near[...], far[...]), jnp.where(first, far[...], near[...]))
    for s, value in enumerate(pair):
        out[0, :, s, :] = jnp.where(row < limits[s, :1, :1], value, jnp.zeros(value.shape, value.dtype))


def add_four_kernel(a, b, c, d, out):
    out[...] = (a[...] + b[...]) + (c[...] + d[...])


def stack_kernel(*refs):
    for index, ref in enumerate(refs[:-1]):
        refs[-1][index] = ref[...]


def set_lines(parts, lines, first):
    point, side, size = lax.axis_index("hyp"), lax.axis_index("side"), parts.shape[1]
    for index in range(parts.shape[0]):
        node = 1 - side if index % 2 else side
        slot = 1 - point if index // 2 else point
        lines[node, pl.ds(pl.multiple_of(first + slot * size, 8), size), :] = parts[index]


def copy_out(areas, result, out, sems):
    copies = [
        pltpu.make_async_copy(result.at[area], out.at[area], sems.at[index]) for index, area in enumerate(areas)
    ]
    for copy in copies:
        copy.start()
    return copies


def first_core_blocks(lines, result, out, sems):
    first, rest = slice(0, LANES), slice(LANES, BLOCKS * LANES)
    areas = []
    for node in range(2):
        for index in range(2):
            place = slice((index + 1) * LANES, (index + 2) * LANES)
            tile = lines[node, index * LANES : (index + 1) * LANES, :]
            result[node, first, place] = tile
            result[node, place, first] = tile.T
        areas += [(node, first, rest), (node, rest, first)]
    return copy_out(areas, result, out, sems)


def second_core_blocks(lines, at, result, out, sems):
    areas = []
    for node in range(2):
        held = (lines[node, at + index * LANES : at + (index + 1) * LANES, :] for index in range(2))
        for index, tile in enumerate(restore_diagonal(*held)):
            place = slice(index * LANES, (index + 1) * LANES)
            result[node, place, place] = tile
            areas.append((node, place, place))
    return copy_out(areas, result, out, sems)


def early_kernel(own, rows, rows_out, out, lines, result, sems, rows_sem):
    store = pltpu.make_async_copy(rows, rows_out, rows_sem)
    store.start()
    core = lax.axis_index("core")
    set_lines(own, lines, 0)

    @pl.when(core == 0)
    def _():
        for copy in first_core_blocks(lines, result, out, sems):
            copy.wait()

    @pl.when(core == 1)
    def _():
        for copy in second_core_blocks(lines, LANES // 2, result, out, sems):
            copy.wait()

    store.wait()


def late_kernel(own, other, before, out, lines, result, sems, middle_sems):
    del before
    core, half = lax.axis_index("core"), lines.shape[1] // 2
    set_lines(own, lines, core * half)
    set_lines(other, lines, (1 - core) * half)
    middle, last = (slice(i * LANES, (i + 1) * LANES) for i in (1, 2))
    areas = []
    for node in range(2):
        tile = lines[node, 2 * LANES : 3 * LANES, :]
        result[node, middle, last] = tile
        result[node, last, middle] = tile.T
        areas += [(node, middle, last), (node, last, middle)]
    shared = copy_out(areas, result, out, middle_sems)

    @pl.when(core == 1)
    def _():
        for copy in first_core_blocks(lines, result, out, sems):
            copy.wait()

    @pl.when(core == 0)
    def _():
        for copy in second_core_blocks(lines, len(ABOVE) * LANES, result, out, sems):
            copy.wait()

    for copy in shared:
        copy.wait()


def square(sigma_rows, panel, live_block_rows, inv_diag, quad_weight):
    height, count, width = panel.shape[1:]
    grid = lax.axis_size("pcol")
    points = lax.axis_size("hyp")
    f32, bf16 = jnp.float32, jnp.bfloat16
    shape = jax.ShapeDtypeStruct
    dma = pltpu.SemaphoreType.DMA
    stay = functools.partial(pltpu.with_memory_space_constraint, memory_space=pltpu.HBM)
    devices = points * 2 * 2 * grid
    live = live_block_rows[:, 0]

    def swap(x, point=0, side=0, core=0, column=0):
        mask = ((point * 2 + side) * 2 + core) * grid + column
        return lax.ppermute(x, AXES, [(i, i ^ mask) for i in range(devices)])

    extent = sigma_rows.shape[2]
    block = shape((height, width), bf16)
    cuts = (extent // 2, extent // 2)
    size = pl.cdiv(inv_diag.shape[2], ROWS) * ROWS
    own, give, own_inverse, limits, *pieces = call(
        start_kernel,
        [block, shape((height + size, width), bf16), shape((size, width), bf16)]
        + [shape((count, 8, LANES), jnp.int32)]
        + [shape((lines, extent), bf16) for lines in cuts],
        [HBM] * 4,
        *map(stay, (live, panel, inv_diag, sigma_rows)),
        scratch=[pltpu.SMEM(live.shape, jnp.int32)]
        + [pltpu.VMEM(x.shape, bf16) for x in (panel, inv_diag, sigma_rows)]
        + [dma((4,))],
    )
    got = swap(give, side=1)
    got, got_inverse = got[:height], got[height:]
    blocks = []
    for one in (own, got):
        two = swap(one, column=2)
        blocks += [one, two, swap(one, column=1), swap(two, column=1)]
    far = [swap(piece, side=1) for piece in pieces]


    product, line_shape = shape((extent, width), f32), shape((extent, width), bf16)
    own_rows, own_product, weight, base = call(
        own_kernel,
        [line_shape, product, shape((8, LANES), f32), shape((width, width), f32)],
        [SMEM] + [VMEM] * (6 + len(cuts)),
        quad_weight, own_inverse, got_inverse, *blocks[:4], *pieces,
    )
    rows, pack = call(
        gather_kernel, [line_shape] * 2, [VMEM] * 5, *blocks[4:], own_rows, after=far
    )
    got_pack = swap(pack, core=1)
    *mine, high, low = call(
        apply_kernel, [shape((lines, width), f32) for lines in cuts] + [line_shape] * 2, [VMEM] * (2 + len(cuts)),
        own_product, rows, *far,
    )
    lines = HELD * LANES // 2
    part, half = shape((lines // 2, LANES), f32), shape((lines, LANES), f32)
    other = [swap(x, core=1) for x in mine]
    keep, send = call(
        couple_kernel, [half, half], [VMEM] * 5,
        pack, got_pack, high, low, base,
        scratch=[pltpu.VMEM((2 * lines, LANES), f32)],
    )
    keep, send = call(
        halve_kernel, [part, part], [VMEM] * 3, weight, keep, swap(send, core=1),
        scratch=[pltpu.VMEM((lines, LANES), f32)],
    )
    def deliver(x, flip):
        pairs = []
        for i in range(devices):
            h, s, k, c = i // (4 * grid), i // (2 * grid) % 2, i // grid % 2, i % grid
            pairs.append((i, (h * 4 + c) * grid + 2 * (s ^ flip) + k))
        return lax.ppermute(x, AXES, pairs)

    total = call(
        add_four_kernel, part, [VMEM] * 4,
        keep, swap(send, point=1), swap(keep, column=1), swap(send, point=1, column=1),
    )
    out_near, out_far = call(
        output_kernel, [block, block], [VMEM] * (2 * len(cuts)), *mine, *other,
        scratch=[pltpu.VMEM((extent, width), bf16)],
        after=[keep],
    )
    near, far = deliver(out_near, 0), deliver(out_far, 1)
    total = call(add_kernel, part, [VMEM] * 2, total, swap(total, column=2))
    quarters = [total, swap(total, side=1), swap(total, point=1), swap(total, side=1, point=1)]
    rows = call(
        rows_kernel, shape((1, height, count, width), bf16), [VMEM] * 3, limits, near, far
    )
    quarters = call(
        stack_kernel, shape((len(quarters), *part.shape), f32), [VMEM] * len(quarters), *quarters, after=[rows]
    )
    whole = shape((count, width, width), f32)
    sigma_panel, marginal = call(
        early_kernel, [shape(rows.shape, bf16), whole], [VMEM] * 2, quarters, rows,
        scratch=[pltpu.VMEM((count, lines, LANES), f32), pltpu.VMEM(whole.shape, f32), dma((6,)), dma(())],
        out_specs=[HBM, HBM],
    )
    marginal = call(
        late_kernel, whole, [VMEM, VMEM, HBM], quarters, swap(quarters, core=1), marginal,
        scratch=[pltpu.VMEM((count, 2 * lines, LANES), f32), pltpu.VMEM(whole.shape, f32), dma((6,)), dma((4,))],
        out_specs=HBM,
        alias={2: 0},
    )
    return sigma_panel, marginal


def solution(mesh):
    sizes = dict(mesh.shape)
    prow, pcol = ("prow",), ("pcol",)

    def on_device(sigma_rows, panel, live_block_rows, inv_diag, quad_weight):
        height, count, width = panel.shape[1:]
        fits = (
            split
            and sigma_rows.shape[1] == sigma_rows.shape[2] == sizes["pcol"] * height
            and height % LANES == 0
            and count == 2
            and width == BLOCKS * LANES
        )
        body = square if fits else functools.partial(general, prow)
        return body(sigma_rows, panel, live_block_rows, inv_diag, quad_weight)

    split = sizes["hyp"] == 2 and sizes["pcol"] == 4 and sizes["prow"] == 4
    if split:
        prow = ("side", "core")
        mesh = jax.sharding.Mesh(
            mesh.devices.reshape(sizes["hyp"], 2, 2, sizes["pcol"]),
            ("hyp", "side", "core", "pcol"),
        )
    in_specs = (
        P("hyp", prow, pcol),
        P("hyp", prow + pcol, None, None),
        P(None, prow + pcol),
        P("hyp", None, prow + pcol, None),
        P("hyp"),
    )
    out_specs = (P("hyp", prow + pcol, None, None), P())
    return jax.shard_map(
        on_device, mesh=mesh, in_specs=in_specs, out_specs=out_specs, check_vma=False
    )
```

```python
import functools

import jax
import jax.numpy as jnp
from jax import lax
from jax.experimental import pallas as pl
from jax.experimental.pallas import tpu as pltpu
from jax.sharding import PartitionSpec as P

LANES = 128
ROWS = 16
VMEM = pl.BlockSpec(memory_space=pltpu.VMEM)
SMEM = pl.BlockSpec(memory_space=pltpu.SMEM)
ANY = pl.BlockSpec(memory_space=pl.ANY)
HBM = pl.BlockSpec(memory_space=pltpu.HBM)
AXES = ("hyp", "side", "core", "pcol")


def call(kernel, outs, specs, *operands, scratch=(), out_specs=None, after=(), alias={}):
    many = isinstance(outs, (list, tuple))
    count = len(specs)

    def body(*refs):
        kernel(*refs[:count], *refs[count + len(after) :])

    if out_specs is None:
        out_specs = [VMEM] * len(outs) if many else VMEM
    return pl.pallas_call(
        body,
        out_shape=outs,
        in_specs=list(specs) + [ANY] * len(after),
        out_specs=out_specs,
        scratch_shapes=scratch,
        input_output_aliases=alias,
        compiler_params=pltpu.CompilerParams(vmem_limit_bytes=32 * 2**20),
    )(*operands, *after)


def transposed_dot(left, right):
    return lax.dot_general(
        left, right, (((0,), (0,)), ((), ())), preferred_element_type=jnp.float32
    )


BLOCKS = 3
ABOVE = ((0, 1), (0, 2), (1, 2))
HELD = len(ABOVE) + 2


def block_indices():
    shape = (LANES, LANES)
    return lax.broadcasted_iota(jnp.int32, shape, 0), lax.broadcasted_iota(jnp.int32, shape, 1)


def hold_diagonal(first, second, third):
    row, column = block_indices()
    line = jnp.sum(jnp.where(row == column, second, 0.0), axis=0, keepdims=True)
    last = line[:, LANES - 1 :]
    below = jnp.where(row == LANES - 1, line, jnp.where((row == LANES - 2) & (column == 0), last, 0.0))
    upper = column >= row
    return jnp.where(upper, first, second), jnp.where(upper, third, below)


def restore_diagonal(shared, single):
    row, column = block_indices()
    turned, upper = shared.T, column >= row
    line = jnp.where(column[:1] == LANES - 1, single[LANES - 2 : LANES - 1, :1], single[LANES - 1 :, :])
    second = jnp.where(row == column, line, jnp.where(upper, turned, shared))
    return jnp.where(upper, shared, turned), second, jnp.where(upper, single, single.T)


def general(prow, sigma_rows, panel, live_block_rows, inv_diag, quad_weight):
    height, count, width = panel.shape[1:]
    offsets = lax.broadcasted_iota(jnp.int32, (height, count), 0)
    active = offsets < live_block_rows[:, 0][None, :]
    masked = jnp.where(active[:, :, None], panel[0], jnp.zeros_like(panel[0]))
    gathered = lax.all_gather(masked, prow + ("pcol",), axis=0, tiled=True)
    start = lax.axis_index("pcol") * sigma_rows.shape[2]
    column_panel = lax.dynamic_slice_in_dim(gathered, start, sigma_rows.shape[2], 0)
    applied = lax.psum_scatter(
        jnp.dot(
            sigma_rows[0],
            column_panel.reshape(sigma_rows.shape[2], count * width),
            preferred_element_type=jnp.float32,
        ),
        "pcol",
        scatter_dimension=0,
        tiled=True,
    ).reshape(height, count, width)
    half = applied.astype(jnp.bfloat16)
    sigma_panel = jnp.where(active[:, :, None], -half, jnp.zeros_like(half))[None]
    coupling = jnp.einsum(
        "vwg,vwe->wge",
        masked.astype(jnp.float32),
        applied,
        precision=lax.Precision.HIGHEST,
    )
    diagonal = jnp.einsum(
        "skp,skq->spq", inv_diag[0], inv_diag[0], preferred_element_type=jnp.float32
    )
    marginal = lax.psum(quad_weight[0] * (coupling + diagonal), ("hyp",) + prow + ("pcol",))
    return sigma_panel, marginal


def start_kernel(*refs):
    sources, (own, give, own_inverse, limits), pieces = refs[:4], refs[4:8], refs[8:-5]
    buffers, sems = refs[-5:-1], refs[-1]
    copies = [
        pltpu.make_async_copy(source, buffer, sems.at[index])
        for index, (source, buffer) in enumerate(zip(sources, buffers))
    ]
    for copy in copies:
        copy.start()
    for copy in copies[:3]:
        copy.wait()
    live, panel, inverse, matrix = buffers
    first = lax.axis_index("side") == 0
    row = lax.broadcasted_iota(jnp.int32, own.shape, 0)
    rows = panel[0]
    zero = jnp.zeros(own.shape, own.dtype)
    one, two = (jnp.where(row < live[s], rows[:, s, :], zero) for s in range(2))
    height = own.shape[0]
    own[...] = jnp.where(first, one, two)
    give[:height] = jnp.where(first, two, one)
    spare = jnp.zeros((own_inverse.shape[0] - inverse.shape[2], own.shape[1]), own.dtype)
    one, two = (jnp.concatenate([inverse[0, s], spare], 0) for s in range(2))
    own_inverse[...] = jnp.where(first, one, two)
    give[height:] = jnp.where(first, two, one)
    for s in range(limits.shape[0]):
        limits[s] = jnp.full(limits.shape[1:], live[s], limits.dtype)
    copies[3].wait()
    at = 0
    for piece in pieces:
        piece[...] = matrix[0, :, at : at + piece.shape[0]].T
        at += piece.shape[0]


def set_rows(blocks, rows):
    column, height = lax.axis_index("pcol"), blocks[0].shape[0]
    for step, block in zip((0, 2, 1, 3), blocks):
        spot = jnp.bitwise_xor(column, step)
        rows[pl.ds(pl.multiple_of(spot * height, height), height), :] = block[...]


def own_kernel(*refs):
    weight, inverses, blocks, pieces = refs[0], refs[1:3], refs[3:7], refs[7:-4]
    rows, applied, tile, base = refs[-4:]
    tile[...] = jnp.full(tile.shape, weight[0], tile.dtype)
    base[...] = sum(transposed_dot(lines[...], lines[...]) for lines in inverses)
    set_rows(blocks, rows)
    at = 0
    for piece in pieces:
        applied[at : at + piece.shape[0]] = jnp.dot(piece[...], rows[...], preferred_element_type=jnp.float32)
        at += piece.shape[0]


def select_kernel(*refs):
    blocks, (own_rows, pack) = refs[:4], refs[4:]
    same = lax.axis_index("pcol") // 2 == lax.axis_index("side")

    @pl.when(same)
    def _():
        pack[...] = own_rows[...]

    @pl.when(jnp.logical_not(same))
    def _():
        set_rows(blocks, pack)


def apply_kernel(own, *refs):
    blocks, refs, (high, low, rows) = refs[:4], refs[4:-3], refs[-3:]
    pieces, outs = refs[: len(refs) // 2], refs[len(refs) // 2 :]
    set_rows(blocks, rows)
    at = 0
    for piece, out in zip(pieces, outs):
        lines = slice(at, at + piece.shape[0])
        applied = own[lines] + jnp.dot(piece[...], rows[...], preferred_element_type=jnp.float32)
        out[...] = applied
        high[lines] = applied.astype(jnp.bfloat16)
        low[lines] = (applied - applied.astype(jnp.bfloat16).astype(jnp.float32)).astype(jnp.bfloat16)
        at += piece.shape[0]


def couple_kernel(pack, got_pack, high, low, base, keep, send, packed):
    core, column = lax.axis_index("core"), lax.axis_index("pcol")
    rows = jnp.where(column % 2 == core, pack[...], got_pack[...])
    blocks = {}
    for first in range(BLOCKS):
        left, right = slice(first * LANES, (first + 1) * LANES), slice(first * LANES, None)
        total = transposed_dot(rows[:, left], high[:, right])
        total += transposed_dot(rows[:, left], low[:, right])
        total += base[left, right]
        for index in range(BLOCKS - first):
            blocks[first, first + index] = total[:, index * LANES : (index + 1) * LANES]
    held = [blocks[place] for place in ABOVE]
    held += hold_diagonal(*(blocks[i, i] for i in range(BLOCKS)))
    for index, block in enumerate(held):
        packed[index * LANES : (index + 1) * LANES, :] = block
    size = keep.shape[0]
    keep[...] = packed[pl.ds(pl.multiple_of(core * size, 8), size), :]
    send[...] = packed[pl.ds(pl.multiple_of((1 - core) * size, 8), size), :]


def halve_kernel(weight, mine, came, keep, send, whole):
    whole[...] = weight[:1] * (mine[...] + came[...])
    size, point = keep.shape[0], lax.axis_index("hyp")
    keep[...] = whole[pl.ds(pl.multiple_of(point * size, 8), size), :]
    send[...] = whole[pl.ds(pl.multiple_of((1 - point) * size, 8), size), :]


def output_kernel(*refs):
    parts, (out_near, out_far, half) = refs[:-3], refs[-3:]
    count, at = len(parts) // 2, 0
    for mine, other in zip(parts[:count], parts[count:]):
        half[at : at + mine.shape[0]] = -(mine[...] + other[...]).astype(jnp.bfloat16)
        at += mine.shape[0]
    height, side, core = out_near.shape[0], lax.axis_index("side"), lax.axis_index("core")
    for out, at in ((out_near, side), (out_far, 1 - side)):
        spot = at * 2 + core
        out[...] = half[pl.ds(pl.multiple_of(spot * height, height), height), :]


def add_kernel(mine, came, out):
    out[...] = mine[...] + came[...]


def rows_kernel(limits, near, far, out):
    row = lax.broadcasted_iota(jnp.int32, near.shape, 0)
    first = lax.axis_index("pcol") // 2 == 0
    pair = (jnp.where(first, near[...], far[...]), jnp.where(first, far[...], near[...]))
    for s, value in enumerate(pair):
        out[0, :, s, :] = jnp.where(row < limits[s, :1, :1], value, jnp.zeros(value.shape, value.dtype))


def add_four_kernel(a, b, c, d, out):
    out[...] = (a[...] + b[...]) + (c[...] + d[...])


def stack_kernel(*refs):
    for index, ref in enumerate(refs[:-1]):
        refs[-1][index] = ref[...]


def set_lines(parts, lines, first):
    point, side, size = lax.axis_index("hyp"), lax.axis_index("side"), parts.shape[1]
    for index in range(parts.shape[0]):
        node = 1 - side if index % 2 else side
        slot = 1 - point if index // 2 else point
        lines[node, pl.ds(pl.multiple_of(first + slot * size, 8), size), :] = parts[index]


def copy_out(areas, result, out, sems):
    copies = [
        pltpu.make_async_copy(result.at[area], out.at[area], sems.at[index]) for index, area in enumerate(areas)
    ]
    for copy in copies:
        copy.start()
    return copies


def first_core_blocks(lines, result, out, sems):
    first, rest = slice(0, LANES), slice(LANES, BLOCKS * LANES)
    areas = []
    for node in range(2):
        for index in range(2):
            place = slice((index + 1) * LANES, (index + 2) * LANES)
            tile = lines[node, index * LANES : (index + 1) * LANES, :]
            result[node, first, place] = tile
            result[node, place, first] = tile.T
        areas += [(node, first, rest), (node, rest, first)]
    return copy_out(areas, result, out, sems)


def second_core_blocks(lines, at, result, out, sems):
    areas = []
    for node in range(2):
        held = (lines[node, at + index * LANES : at + (index + 1) * LANES, :] for index in range(2))
        for index, tile in enumerate(restore_diagonal(*held)):
            place = slice(index * LANES, (index + 1) * LANES)
            result[node, place, place] = tile
            areas.append((node, place, place))
    return copy_out(areas, result, out, sems)


def early_kernel(own, rows, rows_out, out, lines, result, sems, rows_sem):
    store = pltpu.make_async_copy(rows, rows_out, rows_sem)
    store.start()
    core = lax.axis_index("core")
    set_lines(own, lines, 0)

    @pl.when(core == 0)
    def _():
        for copy in first_core_blocks(lines, result, out, sems):
            copy.wait()

    @pl.when(core == 1)
    def _():
        for copy in second_core_blocks(lines, LANES // 2, result, out, sems):
            copy.wait()

    store.wait()


def late_kernel(own, other, before, out, lines, result, sems, middle_sems):
    del before
    core, half = lax.axis_index("core"), lines.shape[1] // 2
    set_lines(own, lines, core * half)
    set_lines(other, lines, (1 - core) * half)
    middle, last = (slice(i * LANES, (i + 1) * LANES) for i in (1, 2))
    areas = []
    for node in range(2):
        tile = lines[node, 2 * LANES : 3 * LANES, :]
        result[node, middle, last] = tile
        result[node, last, middle] = tile.T
        areas += [(node, middle, last), (node, last, middle)]
    shared = copy_out(areas, result, out, middle_sems)

    @pl.when(core == 1)
    def _():
        for copy in first_core_blocks(lines, result, out, sems):
            copy.wait()

    @pl.when(core == 0)
    def _():
        for copy in second_core_blocks(lines, len(ABOVE) * LANES, result, out, sems):
            copy.wait()

    for copy in shared:
        copy.wait()


def square(sigma_rows, panel, live_block_rows, inv_diag, quad_weight):
    height, count, width = panel.shape[1:]
    grid = lax.axis_size("pcol")
    points = lax.axis_size("hyp")
    f32, bf16 = jnp.float32, jnp.bfloat16
    shape = jax.ShapeDtypeStruct
    dma = pltpu.SemaphoreType.DMA
    stay = functools.partial(pltpu.with_memory_space_constraint, memory_space=pltpu.HBM)
    devices = points * 2 * 2 * grid
    live = live_block_rows[:, 0]

    def swap(x, point=0, side=0, core=0, column=0):
        mask = ((point * 2 + side) * 2 + core) * grid + column
        return lax.ppermute(x, AXES, [(i, i ^ mask) for i in range(devices)])

    extent = sigma_rows.shape[2]
    block = shape((height, width), bf16)
    cuts = (extent // 2, extent // 2)
    size = pl.cdiv(inv_diag.shape[2], ROWS) * ROWS
    own, give, own_inverse, limits, *pieces = call(
        start_kernel,
        [block, shape((height + size, width), bf16), shape((size, width), bf16)]
        + [shape((count, 8, LANES), jnp.int32)]
        + [shape((lines, extent), bf16) for lines in cuts],
        [HBM] * 4,
        *map(stay, (live, panel, inv_diag, sigma_rows)),
        scratch=[pltpu.SMEM(live.shape, jnp.int32)]
        + [pltpu.VMEM(x.shape, bf16) for x in (panel, inv_diag, sigma_rows)]
        + [dma((4,))],
    )
    got = swap(give, side=1)
    got, got_inverse = got[:height], got[height:]
    blocks = []
    for one in (own, got):
        two = swap(one, column=2)
        blocks += [one, two, swap(one, column=1), swap(two, column=1)]
    far = [swap(piece, side=1) for piece in pieces]


    product, line_shape = shape((extent, width), f32), shape((extent, width), bf16)
    own_rows, own_product, weight, base = call(
        own_kernel,
        [line_shape, product, shape((8, LANES), f32), shape((width, width), f32)],
        [SMEM] + [VMEM] * (6 + len(cuts)),
        quad_weight, own_inverse, got_inverse, *blocks[:4], *pieces,
    )
    pack = call(select_kernel, line_shape, [VMEM] * 5, *blocks[4:], own_rows, after=far)
    got_pack = swap(pack, core=1)
    *mine, high, low = call(
        apply_kernel, [shape((lines, width), f32) for lines in cuts] + [line_shape] * 2, [VMEM] * (5 + len(cuts)),
        own_product, *blocks[4:], *far,
        scratch=[pltpu.VMEM((extent, width), bf16)],
        after=[pack],
    )
    lines = HELD * LANES // 2
    part, half = shape((lines // 2, LANES), f32), shape((lines, LANES), f32)
    other = [swap(x, core=1) for x in mine]
    keep, send = call(
        couple_kernel, [half, half], [VMEM] * 5,
        pack, got_pack, high, low, base,
        scratch=[pltpu.VMEM((2 * lines, LANES), f32)],
    )
    keep, send = call(
        halve_kernel, [part, part], [VMEM] * 3, weight, keep, swap(send, core=1),
        scratch=[pltpu.VMEM((lines, LANES), f32)],
    )
    def deliver(x, flip):
        pairs = []
        for i in range(devices):
            h, s, k, c = i // (4 * grid), i // (2 * grid) % 2, i // grid % 2, i % grid
            pairs.append((i, (h * 4 + c) * grid + 2 * (s ^ flip) + k))
        return lax.ppermute(x, AXES, pairs)

    out_near, out_far = call(
        output_kernel, [block, block], [VMEM] * (2 * len(cuts)), *mine, *other,
        scratch=[pltpu.VMEM((extent, width), bf16)],
        after=[keep],
    )
    near, far = deliver(out_near, 0), deliver(out_far, 1)
    total = call(
        add_four_kernel, part, [VMEM] * 4,
        keep, swap(send, point=1), swap(keep, column=1), swap(send, point=1, column=1),
        after=[out_near],
    )
    total = call(add_kernel, part, [VMEM] * 2, total, swap(total, column=2))
    quarters = [total, swap(total, side=1), swap(total, point=1), swap(total, side=1, point=1)]
    rows = call(
        rows_kernel, shape((1, height, count, width), bf16), [VMEM] * 3, limits, near, far
    )
    quarters = call(
        stack_kernel, shape((len(quarters), *part.shape), f32), [VMEM] * len(quarters), *quarters, after=[rows]
    )
    whole = shape((count, width, width), f32)
    sigma_panel, marginal = call(
        early_kernel, [shape(rows.shape, bf16), whole], [VMEM] * 2, quarters, rows,
        scratch=[pltpu.VMEM((count, lines, LANES), f32), pltpu.VMEM(whole.shape, f32), dma((6,)), dma(())],
        out_specs=[HBM, HBM],
    )
    marginal = call(
        late_kernel, whole, [VMEM, VMEM, HBM], quarters, swap(quarters, core=1), marginal,
        scratch=[pltpu.VMEM((count, 2 * lines, LANES), f32), pltpu.VMEM(whole.shape, f32), dma((6,)), dma((4,))],
        out_specs=HBM,
        alias={2: 0},
    )
    return sigma_panel, marginal


def solution(mesh):
    sizes = dict(mesh.shape)
    prow, pcol = ("prow",), ("pcol",)

    def on_device(sigma_rows, panel, live_block_rows, inv_diag, quad_weight):
        height, count, width = panel.shape[1:]
        fits = (
            split
            and sigma_rows.shape[1] == sigma_rows.shape[2] == sizes["pcol"] * height
            and height % LANES == 0
            and count == 2
            and width == BLOCKS * LANES
        )
        body = square if fits else functools.partial(general, prow)
        return body(sigma_rows, panel, live_block_rows, inv_diag, quad_weight)

    split = sizes["hyp"] == 2 and sizes["pcol"] == 4 and sizes["prow"] == 4
    if split:
        prow = ("side", "core")
        mesh = jax.sharding.Mesh(
            mesh.devices.reshape(sizes["hyp"], 2, 2, sizes["pcol"]),
            ("hyp", "side", "core", "pcol"),
        )
    in_specs = (
        P("hyp", prow, pcol),
        P("hyp", prow + pcol, None, None),
        P(None, prow + pcol),
        P("hyp", None, prow + pcol, None),
        P("hyp"),
    )
    out_specs = (P("hyp", prow + pcol, None, None), P())
    return jax.shard_map(
        on_device, mesh=mesh, in_specs=in_specs, out_specs=out_specs, check_vma=False
    )
```

```python
import functools

import jax
import jax.numpy as jnp
from jax import lax
from jax.experimental import pallas as pl
from jax.experimental.pallas import tpu as pltpu
from jax.sharding import PartitionSpec as P

LANES = 128
ROWS = 16
VMEM = pl.BlockSpec(memory_space=pltpu.VMEM)
SMEM = pl.BlockSpec(memory_space=pltpu.SMEM)
ANY = pl.BlockSpec(memory_space=pl.ANY)
HBM = pl.BlockSpec(memory_space=pltpu.HBM)
AXES = ("hyp", "side", "core", "pcol")


def call(kernel, outs, specs, *operands, scratch=(), out_specs=None, after=(), alias={}):
    many = isinstance(outs, (list, tuple))
    count = len(specs)

    def body(*refs):
        kernel(*refs[:count], *refs[count + len(after) :])

    if out_specs is None:
        out_specs = [VMEM] * len(outs) if many else VMEM
    return pl.pallas_call(
        body,
        out_shape=outs,
        in_specs=list(specs) + [ANY] * len(after),
        out_specs=out_specs,
        scratch_shapes=scratch,
        input_output_aliases=alias,
        compiler_params=pltpu.CompilerParams(vmem_limit_bytes=32 * 2**20),
    )(*operands, *after)


def transposed_dot(left, right):
    return lax.dot_general(
        left, right, (((0,), (0,)), ((), ())), preferred_element_type=jnp.float32
    )


BLOCKS = 3
ABOVE = ((0, 1), (0, 2), (1, 2))
HELD = len(ABOVE) + 2


def block_indices():
    shape = (LANES, LANES)
    return lax.broadcasted_iota(jnp.int32, shape, 0), lax.broadcasted_iota(jnp.int32, shape, 1)


def hold_diagonal(first, second, third):
    row, column = block_indices()
    line = jnp.sum(jnp.where(row == column, second, 0.0), axis=0, keepdims=True)
    last = line[:, LANES - 1 :]
    below = jnp.where(row == LANES - 1, line, jnp.where((row == LANES - 2) & (column == 0), last, 0.0))
    upper = column >= row
    return jnp.where(upper, first, second), jnp.where(upper, third, below)


def restore_diagonal(shared, single):
    row, column = block_indices()
    turned, upper = shared.T, column >= row
    line = jnp.where(column[:1] == LANES - 1, single[LANES - 2 : LANES - 1, :1], single[LANES - 1 :, :])
    second = jnp.where(row == column, line, jnp.where(upper, turned, shared))
    return jnp.where(upper, shared, turned), second, jnp.where(upper, single, single.T)


def general(prow, sigma_rows, panel, live_block_rows, inv_diag, quad_weight):
    height, count, width = panel.shape[1:]
    offsets = lax.broadcasted_iota(jnp.int32, (height, count), 0)
    active = offsets < live_block_rows[:, 0][None, :]
    masked = jnp.where(active[:, :, None], panel[0], jnp.zeros_like(panel[0]))
    gathered = lax.all_gather(masked, prow + ("pcol",), axis=0, tiled=True)
    start = lax.axis_index("pcol") * sigma_rows.shape[2]
    column_panel = lax.dynamic_slice_in_dim(gathered, start, sigma_rows.shape[2], 0)
    applied = lax.psum_scatter(
        jnp.dot(
            sigma_rows[0],
            column_panel.reshape(sigma_rows.shape[2], count * width),
            preferred_element_type=jnp.float32,
        ),
        "pcol",
        scatter_dimension=0,
        tiled=True,
    ).reshape(height, count, width)
    half = applied.astype(jnp.bfloat16)
    sigma_panel = jnp.where(active[:, :, None], -half, jnp.zeros_like(half))[None]
    coupling = jnp.einsum(
        "vwg,vwe->wge",
        masked.astype(jnp.float32),
        applied,
        precision=lax.Precision.HIGHEST,
    )
    diagonal = jnp.einsum(
        "skp,skq->spq", inv_diag[0], inv_diag[0], preferred_element_type=jnp.float32
    )
    marginal = lax.psum(quad_weight[0] * (coupling + diagonal), ("hyp",) + prow + ("pcol",))
    return sigma_panel, marginal


def start_kernel(*refs):
    sources, (own, give, own_inverse, limits), pieces = refs[:4], refs[4:8], refs[8:-5]
    buffers, sems = refs[-5:-1], refs[-1]
    copies = [
        pltpu.make_async_copy(source, buffer, sems.at[index])
        for index, (source, buffer) in enumerate(zip(sources, buffers))
    ]
    for copy in copies:
        copy.start()
    for copy in copies[:3]:
        copy.wait()
    live, panel, inverse, matrix = buffers
    first = lax.axis_index("side") == 0
    row = lax.broadcasted_iota(jnp.int32, own.shape, 0)
    rows = panel[0]
    zero = jnp.zeros(own.shape, own.dtype)
    one, two = (jnp.where(row < live[s], rows[:, s, :], zero) for s in range(2))
    height = own.shape[0]
    own[...] = jnp.where(first, one, two)
    give[:height] = jnp.where(first, two, one)
    spare = jnp.zeros((own_inverse.shape[0] - inverse.shape[2], own.shape[1]), own.dtype)
    one, two = (jnp.concatenate([inverse[0, s], spare], 0) for s in range(2))
    own_inverse[...] = jnp.where(first, one, two)
    give[height:] = jnp.where(first, two, one)
    for s in range(limits.shape[0]):
        limits[s] = jnp.full(limits.shape[1:], live[s], limits.dtype)
    copies[3].wait()
    at = 0
    for piece in pieces:
        piece[...] = matrix[0, :, at : at + piece.shape[0]].T
        at += piece.shape[0]


def set_rows(blocks, rows):
    column, height = lax.axis_index("pcol"), blocks[0].shape[0]
    for step, block in zip((0, 2, 1, 3), blocks):
        spot = jnp.bitwise_xor(column, step)
        rows[pl.ds(pl.multiple_of(spot * height, height), height), :] = block[...]


def own_kernel(*refs):
    weight, inverses, blocks, pieces = refs[0], refs[1:3], refs[3:7], refs[7:-4]
    rows, applied, tile, base = refs[-4:]
    tile[...] = jnp.full(tile.shape, weight[0], tile.dtype)
    base[...] = sum(transposed_dot(lines[...], lines[...]) for lines in inverses)
    set_rows(blocks, rows)
    at = 0
    for piece in pieces:
        applied[at : at + piece.shape[0]] = jnp.dot(piece[...], rows[...], preferred_element_type=jnp.float32)
        at += piece.shape[0]


def select_kernel(*refs):
    blocks, (own_rows, pack) = refs[:4], refs[4:]
    same = lax.axis_index("pcol") // 2 == lax.axis_index("side")

    @pl.when(same)
    def _():
        pack[...] = own_rows[...]

    @pl.when(jnp.logical_not(same))
    def _():
        set_rows(blocks, pack)


def apply_kernel(own, *refs):
    blocks, refs, (high, low, rows) = refs[:4], refs[4:-3], refs[-3:]
    pieces, outs = refs[: len(refs) // 2], refs[len(refs) // 2 :]
    set_rows(blocks, rows)
    at = 0
    for piece, out in zip(pieces, outs):
        lines = slice(at, at + piece.shape[0])
        applied = own[lines] + jnp.dot(piece[...], rows[...], preferred_element_type=jnp.float32)
        out[...] = applied
        high[lines] = applied.astype(jnp.bfloat16)
        low[lines] = (applied - applied.astype(jnp.bfloat16).astype(jnp.float32)).astype(jnp.bfloat16)
        at += piece.shape[0]


def couple_kernel(pack, got_pack, high, low, base, keep, send, packed):
    core, column = lax.axis_index("core"), lax.axis_index("pcol")
    rows = jnp.where(column % 2 == core, pack[...], got_pack[...])
    blocks = {}
    for first in range(BLOCKS):
        left, right = slice(first * LANES, (first + 1) * LANES), slice(first * LANES, None)
        total = transposed_dot(rows[:, left], high[:, right])
        total += transposed_dot(rows[:, left], low[:, right])
        total += base[left, right]
        for index in range(BLOCKS - first):
            blocks[first, first + index] = total[:, index * LANES : (index + 1) * LANES]
    held = [blocks[place] for place in ABOVE]
    held += hold_diagonal(*(blocks[i, i] for i in range(BLOCKS)))
    for index, block in enumerate(held):
        packed[index * LANES : (index + 1) * LANES, :] = block
    size = keep.shape[0]
    keep[...] = packed[pl.ds(pl.multiple_of(core * size, 8), size), :]
    send[...] = packed[pl.ds(pl.multiple_of((1 - core) * size, 8), size), :]


def halve_kernel(weight, mine, came, keep, send, whole):
    whole[...] = weight[:1] * (mine[...] + came[...])
    size, point = keep.shape[0], lax.axis_index("hyp")
    keep[...] = whole[pl.ds(pl.multiple_of(point * size, 8), size), :]
    send[...] = whole[pl.ds(pl.multiple_of((1 - point) * size, 8), size), :]


def output_kernel(*refs):
    parts, (out_near, out_far, half) = refs[:-3], refs[-3:]
    count, at = len(parts) // 2, 0
    for mine, other in zip(parts[:count], parts[count:]):
        half[at : at + mine.shape[0]] = -(mine[...] + other[...]).astype(jnp.bfloat16)
        at += mine.shape[0]
    height, side, core = out_near.shape[0], lax.axis_index("side"), lax.axis_index("core")
    for out, at in ((out_near, side), (out_far, 1 - side)):
        spot = at * 2 + core
        out[...] = half[pl.ds(pl.multiple_of(spot * height, height), height), :]


def add_kernel(mine, came, out):
    out[...] = mine[...] + came[...]


def rows_kernel(limits, near, far, out):
    row = lax.broadcasted_iota(jnp.int32, near.shape, 0)
    first = lax.axis_index("pcol") // 2 == 0
    pair = (jnp.where(first, near[...], far[...]), jnp.where(first, far[...], near[...]))
    for s, value in enumerate(pair):
        out[0, :, s, :] = jnp.where(row < limits[s, :1, :1], value, jnp.zeros(value.shape, value.dtype))


def add_four_kernel(a, b, c, d, out):
    out[...] = (a[...] + b[...]) + (c[...] + d[...])


def stack_kernel(*refs):
    for index, ref in enumerate(refs[:-1]):
        refs[-1][index] = ref[...]


def set_lines(parts, lines, first):
    point, side, size = lax.axis_index("hyp"), lax.axis_index("side"), parts.shape[1]
    for index in range(parts.shape[0]):
        node = 1 - side if index % 2 else side
        slot = 1 - point if index // 2 else point
        lines[node, pl.ds(pl.multiple_of(first + slot * size, 8), size), :] = parts[index]


def copy_out(areas, result, out, sems):
    copies = [
        pltpu.make_async_copy(result.at[area], out.at[area], sems.at[index]) for index, area in enumerate(areas)
    ]
    for copy in copies:
        copy.start()
    return copies


def first_core_blocks(lines, result, out, sems):
    first, rest = slice(0, LANES), slice(LANES, BLOCKS * LANES)
    areas = []
    for node in range(2):
        for index in range(2):
            place = slice((index + 1) * LANES, (index + 2) * LANES)
            tile = lines[node, index * LANES : (index + 1) * LANES, :]
            result[node, first, place] = tile
            result[node, place, first] = tile.T
        areas += [(node, first, rest), (node, rest, first)]
    return copy_out(areas, result, out, sems)


def second_core_blocks(lines, at, result, out, sems):
    areas = []
    for node in range(2):
        held = (lines[node, at + index * LANES : at + (index + 1) * LANES, :] for index in range(2))
        for index, tile in enumerate(restore_diagonal(*held)):
            place = slice(index * LANES, (index + 1) * LANES)
            result[node, place, place] = tile
            areas.append((node, place, place))
    return copy_out(areas, result, out, sems)


def early_kernel(own, rows, rows_out, out, lines, result, sems, rows_sem):
    store = pltpu.make_async_copy(rows, rows_out, rows_sem)
    store.start()
    core = lax.axis_index("core")
    set_lines(own, lines, 0)

    @pl.when(core == 0)
    def _():
        for copy in first_core_blocks(lines, result, out, sems):
            copy.wait()

    @pl.when(core == 1)
    def _():
        for copy in second_core_blocks(lines, LANES // 2, result, out, sems):
            copy.wait()

    store.wait()


def late_kernel(own, other, before, out, lines, result, sems, middle_sems):
    del before
    core, half = lax.axis_index("core"), lines.shape[1] // 2
    set_lines(own, lines, core * half)
    set_lines(other, lines, (1 - core) * half)
    middle, last = (slice(i * LANES, (i + 1) * LANES) for i in (1, 2))
    areas = []
    for node in range(2):
        tile = lines[node, 2 * LANES : 3 * LANES, :]
        result[node, middle, last] = tile
        result[node, last, middle] = tile.T
        areas += [(node, middle, last), (node, last, middle)]
    shared = copy_out(areas, result, out, middle_sems)

    @pl.when(core == 1)
    def _():
        for copy in first_core_blocks(lines, result, out, sems):
            copy.wait()

    @pl.when(core == 0)
    def _():
        for copy in second_core_blocks(lines, len(ABOVE) * LANES, result, out, sems):
            copy.wait()

    for copy in shared:
        copy.wait()


def square(sigma_rows, panel, live_block_rows, inv_diag, quad_weight):
    height, count, width = panel.shape[1:]
    grid = lax.axis_size("pcol")
    points = lax.axis_size("hyp")
    f32, bf16 = jnp.float32, jnp.bfloat16
    shape = jax.ShapeDtypeStruct
    dma = pltpu.SemaphoreType.DMA
    stay = functools.partial(pltpu.with_memory_space_constraint, memory_space=pltpu.HBM)
    devices = points * 2 * 2 * grid
    live = live_block_rows[:, 0]

    def swap(x, point=0, side=0, core=0, column=0):
        mask = ((point * 2 + side) * 2 + core) * grid + column
        return lax.ppermute(x, AXES, [(i, i ^ mask) for i in range(devices)])

    extent = sigma_rows.shape[2]
    block = shape((height, width), bf16)
    cuts = (extent // 2, extent // 2)
    size = pl.cdiv(inv_diag.shape[2], ROWS) * ROWS
    own, give, own_inverse, limits, *pieces = call(
        start_kernel,
        [block, shape((height + size, width), bf16), shape((size, width), bf16)]
        + [shape((count, 8, LANES), jnp.int32)]
        + [shape((lines, extent), bf16) for lines in cuts],
        [HBM] * 4,
        *map(stay, (live, panel, inv_diag, sigma_rows)),
        scratch=[pltpu.SMEM(live.shape, jnp.int32)]
        + [pltpu.VMEM(x.shape, bf16) for x in (panel, inv_diag, sigma_rows)]
        + [dma((4,))],
    )
    got = swap(give, side=1)
    got, got_inverse = got[:height], got[height:]
    blocks = []
    for one in (own, got):
        two = swap(one, column=2)
        blocks += [one, two, swap(one, column=1), swap(two, column=1)]
    far = [swap(piece, side=1) for piece in pieces]


    product, line_shape = shape((extent, width), f32), shape((extent, width), bf16)
    own_rows, own_product, weight, base = call(
        own_kernel,
        [line_shape, product, shape((8, LANES), f32), shape((width, width), f32)],
        [SMEM] + [VMEM] * (6 + len(cuts)),
        quad_weight, own_inverse, got_inverse, *blocks[:4], *pieces,
    )
    pack = call(select_kernel, line_shape, [VMEM] * 5, *blocks[4:], own_rows, after=far)
    got_pack = swap(pack, core=1)
    *mine, high, low = call(
        apply_kernel, [shape((lines, width), f32) for lines in cuts] + [line_shape] * 2, [VMEM] * (5 + len(cuts)),
        own_product, *blocks[4:], *far,
        scratch=[pltpu.VMEM((extent, width), bf16)],
        after=[pack],
    )
    lines = HELD * LANES // 2
    part, half = shape((lines // 2, LANES), f32), shape((lines, LANES), f32)
    other = [swap(x, core=1) for x in mine]
    keep, send = call(
        couple_kernel, [half, half], [VMEM] * 5,
        pack, got_pack, high, low, base,
        scratch=[pltpu.VMEM((2 * lines, LANES), f32)],
    )
    keep, send = call(
        halve_kernel, [part, part], [VMEM] * 3, weight, keep, swap(send, core=1),
        scratch=[pltpu.VMEM((lines, LANES), f32)],
    )
    def deliver(x, flip):
        pairs = []
        for i in range(devices):
            h, s, k, c = i // (4 * grid), i // (2 * grid) % 2, i // grid % 2, i % grid
            pairs.append((i, (h * 4 + c) * grid + 2 * (s ^ flip) + k))
        return lax.ppermute(x, AXES, pairs)

    total = call(
        add_four_kernel, part, [VMEM] * 4,
        keep, swap(send, point=1), swap(keep, column=1), swap(send, point=1, column=1),
    )
    out_near, out_far = call(
        output_kernel, [block, block], [VMEM] * (2 * len(cuts)), *mine, *other,
        scratch=[pltpu.VMEM((extent, width), bf16)],
        after=[keep],
    )
    near, far = deliver(out_near, 0), deliver(out_far, 1)
    total = call(add_kernel, part, [VMEM] * 2, total, swap(total, column=2))
    quarters = [total, swap(total, side=1), swap(total, point=1), swap(total, side=1, point=1)]
    rows = call(
        rows_kernel, shape((1, height, count, width), bf16), [VMEM] * 3, limits, near, far
    )
    quarters = call(
        stack_kernel, shape((len(quarters), *part.shape), f32), [VMEM] * len(quarters), *quarters, after=[rows]
    )
    whole = shape((count, width, width), f32)
    sigma_panel, marginal = call(
        early_kernel, [shape(rows.shape, bf16), whole], [VMEM] * 2, quarters, rows,
        scratch=[pltpu.VMEM((count, lines, LANES), f32), pltpu.VMEM(whole.shape, f32), dma((6,)), dma(())],
        out_specs=[HBM, HBM],
    )
    marginal = call(
        late_kernel, whole, [VMEM, VMEM, HBM], quarters, swap(quarters, core=1), marginal,
        scratch=[pltpu.VMEM((count, 2 * lines, LANES), f32), pltpu.VMEM(whole.shape, f32), dma((6,)), dma((4,))],
        out_specs=HBM,
        alias={2: 0},
    )
    return sigma_panel, marginal


def solution(mesh):
    sizes = dict(mesh.shape)
    prow, pcol = ("prow",), ("pcol",)

    def on_device(sigma_rows, panel, live_block_rows, inv_diag, quad_weight):
        height, count, width = panel.shape[1:]
        fits = (
            split
            and sigma_rows.shape[1] == sigma_rows.shape[2] == sizes["pcol"] * height
            and height % LANES == 0
            and count == 2
            and width == BLOCKS * LANES
        )
        body = square if fits else functools.partial(general, prow)
        return body(sigma_rows, panel, live_block_rows, inv_diag, quad_weight)

    split = sizes["hyp"] == 2 and sizes["pcol"] == 4 and sizes["prow"] == 4
    if split:
        prow = ("side", "core")
        mesh = jax.sharding.Mesh(
            mesh.devices.reshape(sizes["hyp"], 2, 2, sizes["pcol"]),
            ("hyp", "side", "core", "pcol"),
        )
    in_specs = (
        P("hyp", prow, pcol),
        P("hyp", prow + pcol, None, None),
        P(None, prow + pcol),
        P("hyp", None, prow + pcol, None),
        P("hyp"),
    )
    out_specs = (P("hyp", prow + pcol, None, None), P())
    return jax.shard_map(
        on_device, mesh=mesh, in_specs=in_specs, out_specs=out_specs, check_vma=False
    )
```

```python
import functools

import jax
import jax.numpy as jnp
from jax import lax
from jax.experimental import pallas as pl
from jax.experimental.pallas import tpu as pltpu
from jax.sharding import PartitionSpec as P

LANES = 128
ROWS = 16
VMEM = pl.BlockSpec(memory_space=pltpu.VMEM)
SMEM = pl.BlockSpec(memory_space=pltpu.SMEM)
ANY = pl.BlockSpec(memory_space=pl.ANY)
HBM = pl.BlockSpec(memory_space=pltpu.HBM)
AXES = ("hyp", "side", "core", "pcol")


def call(kernel, outs, specs, *operands, scratch=(), out_specs=None, after=(), alias={}):
    many = isinstance(outs, (list, tuple))
    count = len(specs)

    def body(*refs):
        kernel(*refs[:count], *refs[count + len(after) :])

    if out_specs is None:
        out_specs = [VMEM] * len(outs) if many else VMEM
    return pl.pallas_call(
        body,
        out_shape=outs,
        in_specs=list(specs) + [ANY] * len(after),
        out_specs=out_specs,
        scratch_shapes=scratch,
        input_output_aliases=alias,
        compiler_params=pltpu.CompilerParams(vmem_limit_bytes=32 * 2**20),
    )(*operands, *after)


def transposed_dot(left, right):
    return lax.dot_general(
        left, right, (((0,), (0,)), ((), ())), preferred_element_type=jnp.float32
    )


BLOCKS = 3
ABOVE = ((0, 1), (0, 2), (1, 2))
HELD = len(ABOVE) + 2


def block_indices():
    shape = (LANES, LANES)
    return lax.broadcasted_iota(jnp.int32, shape, 0), lax.broadcasted_iota(jnp.int32, shape, 1)


def hold_diagonal(first, second, third):
    row, column = block_indices()
    line = jnp.sum(jnp.where(row == column, second, 0.0), axis=0, keepdims=True)
    last = line[:, LANES - 1 :]
    below = jnp.where(row == LANES - 1, line, jnp.where((row == LANES - 2) & (column == 0), last, 0.0))
    upper = column >= row
    return jnp.where(upper, first, second), jnp.where(upper, third, below)


def restore_diagonal(shared, single):
    row, column = block_indices()
    turned, upper = shared.T, column >= row
    line = jnp.where(column[:1] == LANES - 1, single[LANES - 2 : LANES - 1, :1], single[LANES - 1 :, :])
    second = jnp.where(row == column, line, jnp.where(upper, turned, shared))
    return jnp.where(upper, shared, turned), second, jnp.where(upper, single, single.T)


def general(prow, sigma_rows, panel, live_block_rows, inv_diag, quad_weight):
    height, count, width = panel.shape[1:]
    offsets = lax.broadcasted_iota(jnp.int32, (height, count), 0)
    active = offsets < live_block_rows[:, 0][None, :]
    masked = jnp.where(active[:, :, None], panel[0], jnp.zeros_like(panel[0]))
    gathered = lax.all_gather(masked, prow + ("pcol",), axis=0, tiled=True)
    start = lax.axis_index("pcol") * sigma_rows.shape[2]
    column_panel = lax.dynamic_slice_in_dim(gathered, start, sigma_rows.shape[2], 0)
    applied = lax.psum_scatter(
        jnp.dot(
            sigma_rows[0],
            column_panel.reshape(sigma_rows.shape[2], count * width),
            preferred_element_type=jnp.float32,
        ),
        "pcol",
        scatter_dimension=0,
        tiled=True,
    ).reshape(height, count, width)
    half = applied.astype(jnp.bfloat16)
    sigma_panel = jnp.where(active[:, :, None], -half, jnp.zeros_like(half))[None]
    coupling = jnp.einsum(
        "vwg,vwe->wge",
        masked.astype(jnp.float32),
        applied,
        precision=lax.Precision.HIGHEST,
    )
    diagonal = jnp.einsum(
        "skp,skq->spq", inv_diag[0], inv_diag[0], preferred_element_type=jnp.float32
    )
    marginal = lax.psum(quad_weight[0] * (coupling + diagonal), ("hyp",) + prow + ("pcol",))
    return sigma_panel, marginal


def start_kernel(*refs):
    sources, (own, give, own_inverse, limits), pieces = refs[:4], refs[4:8], refs[8:-5]
    buffers, sems = refs[-5:-1], refs[-1]
    copies = [
        pltpu.make_async_copy(source, buffer, sems.at[index])
        for index, (source, buffer) in enumerate(zip(sources, buffers))
    ]
    for copy in copies:
        copy.start()
    for copy in copies[:3]:
        copy.wait()
    live, panel, inverse, matrix = buffers
    first = lax.axis_index("side") == 0
    row = lax.broadcasted_iota(jnp.int32, own.shape, 0)
    rows = panel[0]
    zero = jnp.zeros(own.shape, own.dtype)
    one, two = (jnp.where(row < live[s], rows[:, s, :], zero) for s in range(2))
    height = own.shape[0]
    own[...] = jnp.where(first, one, two)
    give[:height] = jnp.where(first, two, one)
    spare = jnp.zeros((own_inverse.shape[0] - inverse.shape[2], own.shape[1]), own.dtype)
    one, two = (jnp.concatenate([inverse[0, s], spare], 0) for s in range(2))
    own_inverse[...] = jnp.where(first, one, two)
    give[height:] = jnp.where(first, two, one)
    for s in range(limits.shape[0]):
        limits[s] = jnp.full(limits.shape[1:], live[s], limits.dtype)
    copies[3].wait()
    at = 0
    for piece in pieces:
        piece[...] = matrix[0, :, at : at + piece.shape[0]].T
        at += piece.shape[0]


def set_rows(blocks, rows):
    column, height = lax.axis_index("pcol"), blocks[0].shape[0]
    for step, block in zip((0, 2, 1, 3), blocks):
        spot = jnp.bitwise_xor(column, step)
        rows[pl.ds(pl.multiple_of(spot * height, height), height), :] = block[...]


def own_kernel(*refs):
    weight, inverses, blocks, pieces = refs[0], refs[1:3], refs[3:7], refs[7:-4]
    rows, applied, tile, base = refs[-4:]
    tile[...] = jnp.full(tile.shape, weight[0], tile.dtype)
    base[...] = sum(transposed_dot(lines[...], lines[...]) for lines in inverses)
    set_rows(blocks, rows)
    at = 0
    for piece in pieces:
        applied[at : at + piece.shape[0]] = jnp.dot(piece[...], rows[...], preferred_element_type=jnp.float32)
        at += piece.shape[0]


def select_kernel(*refs):
    blocks, (own_rows, pack) = refs[:4], refs[4:]
    same = lax.axis_index("pcol") // 2 == lax.axis_index("side")

    @pl.when(same)
    def _():
        pack[...] = own_rows[...]

    @pl.when(jnp.logical_not(same))
    def _():
        set_rows(blocks, pack)


def apply_kernel(own, *refs):
    blocks, refs, (high, low, rows) = refs[:4], refs[4:-3], refs[-3:]
    pieces, outs = refs[: len(refs) // 2], refs[len(refs) // 2 :]
    set_rows(blocks, rows)
    at = 0
    for piece, out in zip(pieces, outs):
        lines = slice(at, at + piece.shape[0])
        applied = own[lines] + jnp.dot(piece[...], rows[...], preferred_element_type=jnp.float32)
        out[...] = applied
        high[lines] = applied.astype(jnp.bfloat16)
        low[lines] = (applied - applied.astype(jnp.bfloat16).astype(jnp.float32)).astype(jnp.bfloat16)
        at += piece.shape[0]


def couple_kernel(pack, got_pack, high, low, base, keep, send, packed):
    core, column = lax.axis_index("core"), lax.axis_index("pcol")
    rows = jnp.where(column % 2 == core, pack[...], got_pack[...])
    blocks = {}
    for first in range(BLOCKS):
        left, right = slice(first * LANES, (first + 1) * LANES), slice(first * LANES, None)
        total = transposed_dot(rows[:, left], high[:, right])
        total += transposed_dot(rows[:, left], low[:, right])
        total += base[left, right]
        for index in range(BLOCKS - first):
            blocks[first, first + index] = total[:, index * LANES : (index + 1) * LANES]
    held = [blocks[place] for place in ABOVE]
    held += hold_diagonal(*(blocks[i, i] for i in range(BLOCKS)))
    for index, block in enumerate(held):
        packed[index * LANES : (index + 1) * LANES, :] = block
    size = keep.shape[0]
    keep[...] = packed[pl.ds(pl.multiple_of(core * size, 8), size), :]
    send[...] = packed[pl.ds(pl.multiple_of((1 - core) * size, 8), size), :]


def halve_kernel(weight, mine, came, keep, send, whole):
    whole[...] = weight[:1] * (mine[...] + came[...])
    size, point = keep.shape[0], lax.axis_index("hyp")
    keep[...] = whole[pl.ds(pl.multiple_of(point * size, 8), size), :]
    send[...] = whole[pl.ds(pl.multiple_of((1 - point) * size, 8), size), :]


def output_kernel(*refs):
    parts, (out_near, out_far, half) = refs[:-3], refs[-3:]
    count, at = len(parts) // 2, 0
    for mine, other in zip(parts[:count], parts[count:]):
        half[at : at + mine.shape[0]] = -(mine[...] + other[...]).astype(jnp.bfloat16)
        at += mine.shape[0]
    height, side, core = out_near.shape[0], lax.axis_index("side"), lax.axis_index("core")
    for out, at in ((out_near, side), (out_far, 1 - side)):
        spot = at * 2 + core
        out[...] = half[pl.ds(pl.multiple_of(spot * height, height), height), :]


def add_kernel(mine, came, out):
    out[...] = mine[...] + came[...]


def rows_kernel(limits, near, far, out):
    row = lax.broadcasted_iota(jnp.int32, near.shape, 0)
    first = lax.axis_index("pcol") // 2 == 0
    pair = (jnp.where(first, near[...], far[...]), jnp.where(first, far[...], near[...]))
    for s, value in enumerate(pair):
        out[0, :, s, :] = jnp.where(row < limits[s, :1, :1], value, jnp.zeros(value.shape, value.dtype))


def add_four_kernel(a, b, c, d, out):
    out[...] = (a[...] + b[...]) + (c[...] + d[...])


def stack_kernel(*refs):
    for index, ref in enumerate(refs[:-1]):
        refs[-1][index] = ref[...]


def set_lines(parts, lines, first):
    point, side, size = lax.axis_index("hyp"), lax.axis_index("side"), parts.shape[1]
    for index in range(parts.shape[0]):
        node = 1 - side if index % 2 else side
        slot = 1 - point if index // 2 else point
        lines[node, pl.ds(pl.multiple_of(first + slot * size, 8), size), :] = parts[index]


def copy_out(areas, result, out, sems):
    copies = [
        pltpu.make_async_copy(result.at[area], out.at[area], sems.at[index]) for index, area in enumerate(areas)
    ]
    for copy in copies:
        copy.start()
    return copies


def first_core_blocks(lines, result, out, sems):
    first, rest = slice(0, LANES), slice(LANES, BLOCKS * LANES)
    areas = []
    for node in range(2):
        for index in range(2):
            place = slice((index + 1) * LANES, (index + 2) * LANES)
            tile = lines[node, index * LANES : (index + 1) * LANES, :]
            result[node, first, place] = tile
            result[node, place, first] = tile.T
        areas += [(node, first, rest), (node, rest, first)]
    return copy_out(areas, result, out, sems)


def second_core_blocks(lines, at, result, out, sems):
    areas = []
    for node in range(2):
        held = (lines[node, at + index * LANES : at + (index + 1) * LANES, :] for index in range(2))
        for index, tile in enumerate(restore_diagonal(*held)):
            place = slice(index * LANES, (index + 1) * LANES)
            result[node, place, place] = tile
            areas.append((node, place, place))
    return copy_out(areas, result, out, sems)


def early_kernel(own, rows, rows_out, out, lines, result, sems, rows_sem):
    store = pltpu.make_async_copy(rows, rows_out, rows_sem)
    store.start()
    core = lax.axis_index("core")
    set_lines(own, lines, 0)

    @pl.when(core == 0)
    def _():
        for copy in first_core_blocks(lines, result, out, sems):
            copy.wait()

    @pl.when(core == 1)
    def _():
        for copy in second_core_blocks(lines, LANES // 2, result, out, sems):
            copy.wait()

    store.wait()


def late_kernel(own, other, before, out, lines, result, sems, middle_sems):
    del before
    core, half = lax.axis_index("core"), lines.shape[1] // 2
    size, slot, side = own.shape[1], 1 - core, lax.axis_index("side")
    other_point = jnp.where(slot == lax.axis_index("hyp"), 0, 2)
    for index in range(2):
        start = pl.multiple_of(core * half + slot * size, 8)
        lines[jnp.bitwise_xor(side, index), pl.ds(start, size), :] = own[other_point + index]
    set_lines(other, lines, (1 - core) * half)
    middle, last = (slice(i * LANES, (i + 1) * LANES) for i in (1, 2))
    areas = []
    for node in range(2):
        tile = lines[node, 2 * LANES : 3 * LANES, :]
        result[node, middle, last] = tile
        result[node, last, middle] = tile.T
        areas += [(node, middle, last), (node, last, middle)]
    shared = copy_out(areas, result, out, middle_sems)

    @pl.when(core == 1)
    def _():
        for copy in first_core_blocks(lines, result, out, sems):
            copy.wait()

    @pl.when(core == 0)
    def _():
        for copy in second_core_blocks(lines, len(ABOVE) * LANES, result, out, sems):
            copy.wait()

    for copy in shared:
        copy.wait()


def square(sigma_rows, panel, live_block_rows, inv_diag, quad_weight):
    height, count, width = panel.shape[1:]
    grid = lax.axis_size("pcol")
    points = lax.axis_size("hyp")
    f32, bf16 = jnp.float32, jnp.bfloat16
    shape = jax.ShapeDtypeStruct
    dma = pltpu.SemaphoreType.DMA
    stay = functools.partial(pltpu.with_memory_space_constraint, memory_space=pltpu.HBM)
    devices = points * 2 * 2 * grid
    live = live_block_rows[:, 0]

    def swap(x, point=0, side=0, core=0, column=0):
        mask = ((point * 2 + side) * 2 + core) * grid + column
        return lax.ppermute(x, AXES, [(i, i ^ mask) for i in range(devices)])

    extent = sigma_rows.shape[2]
    block = shape((height, width), bf16)
    cuts = (extent // 2, extent // 2)
    size = pl.cdiv(inv_diag.shape[2], ROWS) * ROWS
    own, give, own_inverse, limits, *pieces = call(
        start_kernel,
        [block, shape((height + size, width), bf16), shape((size, width), bf16)]
        + [shape((count, 8, LANES), jnp.int32)]
        + [shape((lines, extent), bf16) for lines in cuts],
        [HBM] * 4,
        *map(stay, (live, panel, inv_diag, sigma_rows)),
        scratch=[pltpu.SMEM(live.shape, jnp.int32)]
        + [pltpu.VMEM(x.shape, bf16) for x in (panel, inv_diag, sigma_rows)]
        + [dma((4,))],
    )
    got = swap(give, side=1)
    got, got_inverse = got[:height], got[height:]
    blocks = []
    for one in (own, got):
        two = swap(one, column=2)
        blocks += [one, two, swap(one, column=1), swap(two, column=1)]
    far = [swap(piece, side=1) for piece in pieces]


    product, line_shape = shape((extent, width), f32), shape((extent, width), bf16)
    own_rows, own_product, weight, base = call(
        own_kernel,
        [line_shape, product, shape((8, LANES), f32), shape((width, width), f32)],
        [SMEM] + [VMEM] * (6 + len(cuts)),
        quad_weight, own_inverse, got_inverse, *blocks[:4], *pieces,
    )
    pack = call(select_kernel, line_shape, [VMEM] * 5, *blocks[4:], own_rows, after=far)
    got_pack = swap(pack, core=1)
    *mine, high, low = call(
        apply_kernel, [shape((lines, width), f32) for lines in cuts] + [line_shape] * 2, [VMEM] * (5 + len(cuts)),
        own_product, *blocks[4:], *far,
        scratch=[pltpu.VMEM((extent, width), bf16)],
        after=[pack],
    )
    lines = HELD * LANES // 2
    part, half = shape((lines // 2, LANES), f32), shape((lines, LANES), f32)
    other = [swap(x, core=1) for x in mine]
    keep, send = call(
        couple_kernel, [half, half], [VMEM] * 5,
        pack, got_pack, high, low, base,
        scratch=[pltpu.VMEM((2 * lines, LANES), f32)],
    )
    keep, send = call(
        halve_kernel, [part, part], [VMEM] * 3, weight, keep, swap(send, core=1),
        scratch=[pltpu.VMEM((lines, LANES), f32)],
    )
    def deliver(x, flip):
        pairs = []
        for i in range(devices):
            h, s, k, c = i // (4 * grid), i // (2 * grid) % 2, i // grid % 2, i % grid
            pairs.append((i, (h * 4 + c) * grid + 2 * (s ^ flip) + k))
        return lax.ppermute(x, AXES, pairs)

    total = call(
        add_four_kernel, part, [VMEM] * 4,
        keep, swap(send, point=1), swap(keep, column=1), swap(send, point=1, column=1),
    )
    out_near, out_far = call(
        output_kernel, [block, block], [VMEM] * (2 * len(cuts)), *mine, *other,
        scratch=[pltpu.VMEM((extent, width), bf16)],
        after=[keep],
    )
    near, far = deliver(out_near, 0), deliver(out_far, 1)
    total = call(add_kernel, part, [VMEM] * 2, total, swap(total, column=2))
    quarters = [total, swap(total, side=1), swap(total, point=1), swap(total, side=1, point=1)]
    rows = call(
        rows_kernel, shape((1, height, count, width), bf16), [VMEM] * 3, limits, near, far
    )
    quarters = call(
        stack_kernel, shape((len(quarters), *part.shape), f32), [VMEM] * len(quarters), *quarters, after=[rows]
    )
    whole = shape((count, width, width), f32)
    sigma_panel, marginal = call(
        early_kernel, [shape(rows.shape, bf16), whole], [VMEM] * 2, quarters, rows,
        scratch=[pltpu.VMEM((count, lines, LANES), f32), pltpu.VMEM(whole.shape, f32), dma((6,)), dma(())],
        out_specs=[HBM, HBM],
    )
    marginal = call(
        late_kernel, whole, [VMEM, VMEM, HBM], quarters, swap(quarters, core=1), marginal,
        scratch=[pltpu.VMEM((count, 2 * lines, LANES), f32), pltpu.VMEM(whole.shape, f32), dma((6,)), dma((4,))],
        out_specs=HBM,
        alias={2: 0},
    )
    return sigma_panel, marginal


def solution(mesh):
    sizes = dict(mesh.shape)
    prow, pcol = ("prow",), ("pcol",)

    def on_device(sigma_rows, panel, live_block_rows, inv_diag, quad_weight):
        height, count, width = panel.shape[1:]
        fits = (
            split
            and sigma_rows.shape[1] == sigma_rows.shape[2] == sizes["pcol"] * height
            and height % LANES == 0
            and count == 2
            and width == BLOCKS * LANES
        )
        body = square if fits else functools.partial(general, prow)
        return body(sigma_rows, panel, live_block_rows, inv_diag, quad_weight)

    split = sizes["hyp"] == 2 and sizes["pcol"] == 4 and sizes["prow"] == 4
    if split:
        prow = ("side", "core")
        mesh = jax.sharding.Mesh(
            mesh.devices.reshape(sizes["hyp"], 2, 2, sizes["pcol"]),
            ("hyp", "side", "core", "pcol"),
        )
    in_specs = (
        P("hyp", prow, pcol),
        P("hyp", prow + pcol, None, None),
        P(None, prow + pcol),
        P("hyp", None, prow + pcol, None),
        P("hyp"),
    )
    out_specs = (P("hyp", prow + pcol, None, None), P())
    return jax.shard_map(
        on_device, mesh=mesh, in_specs=in_specs, out_specs=out_specs, check_vma=False
    )
```
